32 devices in a mesh: dp: 8 (over y, x, core), mp: 4 (over z).
Axes of the slice: x: 2, y: 2, z: 4, core: 2. Of those that a mesh axis runs over, the one named last changes fastest.
Arguments:
- inputs: bfloat16 [8704, 1536], P(('dp', 'mp')), may hold values from -6 to 6
- cotangent: bfloat16 [8704, 1536], P(('dp', 'mp')), may hold values from -6 to 6
- token_mask: int32 [8704], P(('dp', 'mp')), may hold values 0 or 1
- order: int32 [8, 1088], P('dp'), may hold values from 0 to 1087, each once within a row
- lengths: int32 [8, 4], P('dp'), may hold values from 1 to 1024, 1088 in all within a row
- gains: bfloat16 [2, 1536], replicated, may hold values from 0.5 to 1.5
- w_in: bfloat16 [1536, 2048], P('dp', 'mp'), may hold values from -0.15625 to 0.15625
- w_gate: bfloat16 [1536, 2048], P('dp', 'mp'), may hold values from -0.15625 to 0.15625
- w_out: bfloat16 [2048, 1536], P('mp', 'dp'), may hold values from -0.5 to 0.5
- conv_weight: bfloat16 [4, 16, 128], P(None, 'mp', 'dp'), may hold values from -3 to 3
- chan_bias: bfloat16 [3, 16, 128], P(None, 'mp', 'dp'), may hold values from -3 to 3
- decay: bfloat16 [16, 128], P('mp', 'dp'), may hold values from -9 to -3
- gate_blocks: bfloat16 [2, 16, 128, 128], P(None, 'mp', 'dp'), may hold values from -0.5 to 0.5
- w_up: bfloat16 [1536, 4608], P('dp', 'mp'), may hold values from -0.15625 to 0.15625
- w_gate_ff: bfloat16 [1536, 4608], P('dp', 'mp'), may hold values from -0.15625 to 0.15625
- w_down: bfloat16 [4608, 1536], P('mp', 'dp'), may hold values from -0.1875 to 0.1875
Outputs:
- output: bfloat16 [8704, 1536], P(('dp', 'mp'))
- grad_inputs: bfloat16 [8704, 1536], P(('dp', 'mp'))
- grad_gains: float32 [2, 1536], P(None, ('dp', 'mp'))
- grad_w_in: float32 [1536, 2048], P('dp', 'mp')
- grad_w_gate: float32 [1536, 2048], P('dp', 'mp')
- grad_w_out: float32 [2048, 1536], P('mp', 'dp')
- grad_conv: float32 [4, 16, 128], P(None, 'mp', 'dp')
- grad_bias: float32 [3, 16, 128], P(None, 'mp', 'dp')
- grad_decay: float32 [16, 128], P('mp', 'dp')
- grad_gate_blocks: float32 [2, 16, 128, 128], P(None, 'mp', 'dp')
- grad_w_up: float32 [1536, 4608], P('dp', 'mp')
- grad_w_gate_ff: float32 [1536, 4608], P('dp', 'mp')
- grad_w_down: float32 [4608, 1536], P('mp', 'dp')
The draws below stay inside these ranges and needn't reach their ends.
Inputs may be any that keep to these rules, and one draw needn't show every extreme that they name: Each row of order holds each of 0 to 1087 once. `lengths`: each row sums to 1088; its largest entry is 1024.
All inputs are finite; a program needn't handle non-finite values. No bound on the sum of `token_mask` on one device may be relied on, other than what follows from the above.
Results may differ from the reference program's by a relative error of at most 0.02.
Values may be sent and summed in bfloat16 or wider, within the bound.
A program may use at most 256 MiB of HBM per device.

```python
import math
import jax
import jax.numpy as jnp
import numpy as np
from jax import lax

D = 1536
R = 2048
FF = 4608
BLOCKS = 16
CONV = 4
BLK = 4
MAXLEN = 1024
BW = 128
SLOT = 1088
NSEQ = 4
TOKENS = 8704
N_DP = 8


def draw_decay(key, part):
    key = jax.random.fold_in(key, 7)
    values = jax.random.uniform(key, (BLOCKS, BW), jnp.float32, -9.0, -3.0)
    return values.astype(jnp.bfloat16)


def set_ends(result, stream_key, low, top_value):
    shape = result.shape
    index_at = [jax.random.randint(jax.random.fold_in(stream_key, axis), (), 0, shape[axis]) for axis in range(len(shape))]
    result = result.at[tuple(index_at)].set(low)
    longest = shape.index(max(shape))
    index_at[longest] = (index_at[longest] + 1) % shape[longest]
    return result.at[tuple(index_at)].set(top_value)


def levels(own_key, shape, shards, smallest, high):
    loudness = 1.0
    for axis_at, shards_of in shards:
        draws = jax.random.uniform(jax.random.fold_in(jax.random.fold_in(own_key, 6), axis_at), (shards_of,), jnp.float32, smallest / len(shards), high / len(shards))
        loudness = loudness * jnp.repeat(jnp.exp(draws), shape[axis_at] // shards_of).reshape((-1,) + (1,) * (len(shape) - 1 - axis_at))
    return loudness


def length_profile(amount, total, most, skew):
    portions = [(1 << 20) // math.isqrt(rank ** skew) + 1 for rank in range(2, amount + 1)]
    rest, counts = total - most - (amount - 1), [1] * (amount - 1)
    while rest > 0:
        candidates = [i for i in range(amount - 1) if counts[i] < most]
        pool, budget = sum([portions[i] for i in candidates]), rest
        for i in candidates:
            more = min(most - counts[i], max(1, budget * portions[i] // pool), rest)
            counts[i] = counts[i] + more
            rest = rest - more
    return np.array([most] + counts)


def ragged_sizes(rng, count, total, bound, lean):
    if count == 2:
        one = jax.random.randint(rng, (), max(1, total - bound), min(bound, total - 1) + 1)
        return jnp.stack([one, total - one])
    sizes = jnp.asarray(length_profile(count, total, bound, lean), jnp.int32)
    couples = (count - 1) // 2
    giver, taker = sizes[1:1 + 2 * couples:2], sizes[2:2 + 2 * couples:2]
    margin = jnp.minimum(giver - 1, bound - taker)
    shifted = jax.random.randint(jax.random.fold_in(rng, 1), (couples,), 0, 1 << 20) % (margin + 1)
    sizes = sizes.at[1:1 + 2 * couples:2].set(giver - shifted).at[2:2 + 2 * couples:2].set(taker + shifted)
    return sizes[jax.random.permutation(jax.random.fold_in(rng, 2), count)]


def gaussian(key, extent, deviation, most, pieces=(), held_as=jnp.bfloat16):
    loudness = levels(key, extent, pieces, -0.22, 0.18) if pieces else 1.0
    entries = jax.random.normal(key, extent, jnp.float32) * deviation * loudness
    return jnp.minimum(jnp.maximum(entries, -most), most).astype(held_as)


def setup_inputs(seed: int = 0) -> dict:
    keys = jax.random.split(jax.random.key(seed), 17)
    return {
        "inputs": gaussian(keys[0], (TOKENS, D), 1.0, 6.0, ((0, 32),)),
        "cotangent": gaussian(keys[1], (TOKENS, D), 1.0, 6.0, ((0, 32),)),
        "token_mask": set_ends((jax.random.randint(keys[2], (TOKENS,), 0, 8) < 7).astype(jnp.int32), jax.random.fold_in(keys[2], 1), 0, 1),
        "order": jax.vmap(lambda own: jax.random.permutation(own, SLOT))(jax.random.split(keys[3], N_DP)).reshape((N_DP, SLOT)).astype(jnp.int32),
        "lengths": jax.vmap(lambda own: ragged_sizes(own, NSEQ, SLOT, MAXLEN, 2))(jax.random.split(keys[4], N_DP)).reshape((N_DP, NSEQ)).astype(jnp.int32),
        "gains": jnp.clip(1.0 + 0.1 * jax.random.normal(keys[5], (2, D), jnp.float32), 0.5, 1.5).astype(jnp.bfloat16),
        "w_in": gaussian(keys[6], (D, R), D ** -0.5, 0.15625, ((0, 8), (1, 4))),
        "w_gate": gaussian(keys[7], (D, R), D ** -0.5, 0.15625, ((0, 8), (1, 4))),
        "w_out": gaussian(keys[8], (R, D), (R // 16) ** -0.5, 0.5, ((0, 4), (1, 8))),
        "conv_weight": gaussian(keys[9], (CONV, BLOCKS, BW), CONV ** -0.5, 3.0, ((1, 4), (2, 8))),
        "chan_bias": gaussian(keys[10], (3, BLOCKS, BW), 0.5, 3.0, ((1, 4), (2, 8))),
        "decay": draw_decay(jax.random.fold_in(keys[16], 71), 0),
        "gate_blocks": gaussian(keys[12], (2, BLOCKS, BW, BW), BW ** -0.5, 0.5, ((1, 4), (2, 8))),
        "w_up": gaussian(keys[13], (D, FF), D ** -0.5, 0.15625, ((0, 8), (1, 4))),
        "w_gate_ff": gaussian(keys[14], (D, FF), D ** -0.5, 0.15625, ((0, 8), (1, 4))),
        "w_down": gaussian(keys[15], (FF, D), (FF // 4) ** -0.5, 0.1875, ((0, 4), (1, 8))),
    }


epsilon = 1e-06
highest = lax.Precision.HIGHEST

@jax.custom_vjp
def low(v):
    return lax.optimization_barrier(v.astype(jnp.bfloat16)).astype(jnp.float32)

@jax.custom_vjp
def low_back(v):
    return v

def low_keep(v):
    return (low(v), None)

def low_pass(kept, grad):
    return (grad,)

def back_keep(v):
    return (v, None)

def back_low(kept, grad):
    return (low(grad),)
low.defvjp(low_keep, low_pass)
low_back.defvjp(back_keep, back_low)

def mix_gelu(values):
    return jax.nn.gelu(values, approximate=True)

def rms_rows(values):
    return values * lax.rsqrt(lax.optimization_barrier(jnp.mean(values * values, axis=-1, keepdims=True)) + epsilon)

def segments(length_row, count):
    ends = jnp.cumsum(length_row, dtype=jnp.int32)
    places = jnp.arange(count, dtype=jnp.int32)
    return lax.optimization_barrier(jnp.sum((places[:, None] >= ends[None, :]).astype(jnp.int32), axis=1, dtype=jnp.int32))

def join(first, second):
    return (first[0] * second[0], second[0] * first[1] + second[1])

def block_scan(rate, drive):
    count, width = rate.shape
    rate_blocks = rate.reshape(count // BLK, BLK, width)
    drive_blocks = drive.reshape(count // BLK, BLK, width)
    prod_blocks, part_blocks = lax.associative_scan(join, (rate_blocks, drive_blocks), axis=1)
    _, block_ends = lax.associative_scan(join, (prod_blocks[:, -1], part_blocks[:, -1]), axis=0)
    carried = jnp.concatenate([jnp.zeros((1, width), rate.dtype), block_ends[:-1]], axis=0)
    states = prod_blocks * carried[:, None, :] + part_blocks
    return states.reshape(count, width)

def recurrence(gate_pre, branch, conv_w, conv_b, gate_b, decay_row, gate_w, segment_ids):
    count, width = branch.shape
    taps = conv_w.shape[0]
    mixed = conv_b + conv_w[0] * branch
    for shift_by in range(1, taps):
        earlier = jnp.concatenate([jnp.zeros((shift_by, width), branch.dtype), branch[:-shift_by]], axis=0)
        before = jnp.concatenate([jnp.full((shift_by,), -1, jnp.int32), segment_ids[:-shift_by]])
        same_seq = (before == segment_ids).astype(branch.dtype)
        mixed = mixed + conv_w[shift_by] * earlier * same_seq[:, None]
    heads = gate_w.shape[1]
    blocks = mixed.reshape(count, heads, width // heads)
    gate_in = jnp.einsum('shb,hbc->shc', blocks, gate_w[0], precision=highest).reshape(count, width) + gate_b[0]
    gate_rec = jnp.einsum('shb,hbc->shc', blocks, gate_w[1], precision=highest).reshape(count, width) + gate_b[1]
    log_rate = -8.0 * jax.nn.sigmoid(gate_rec) * jax.nn.softplus(decay_row)
    previous = jnp.concatenate([jnp.full((1,), -1, jnp.int32), segment_ids[:-1]])
    keep_state = (previous == segment_ids).astype(branch.dtype)
    rate = jnp.exp(log_rate) * keep_state[:, None]
    drive = jnp.sqrt(1.0 - jnp.exp(2.0 * log_rate) + 0.01) * jax.nn.sigmoid(gate_in) * mixed
    return mix_gelu(gate_pre) * block_scan(rate, drive)

def layer(xs, gains, w_in, w_gate, w_out, conv_weight, chan_bias, decay, gate_blocks, w_up, w_gate_ff, w_down, order, lengths):
    conv_flat = conv_weight.reshape(CONV, R)
    bias_flat = chan_bias.reshape(3, R)
    decay_flat = decay.reshape(R)

    def group(x_rows, order_row, length_row):
        segment_ids = segments(length_row, SLOT)
        norm_in = low(rms_rows(x_rows) * gains[0])
        packed = norm_in[order_row]
        branch = low_back(jnp.dot(packed, w_in, precision=highest))
        gate_pre = low_back(jnp.dot(packed, w_gate, precision=highest))
        mixed = low(recurrence(gate_pre, branch, conv_flat, bias_flat[0], bias_flat[1:], decay_flat, gate_blocks, segment_ids))
        back = low_back(jnp.dot(mixed, w_out, precision=highest))
        resid = x_rows + jnp.zeros_like(back).at[order_row].set(back)
        norm_mid = low(rms_rows(resid) * gains[1])
        up_proj = low_back(jnp.dot(norm_mid, w_up, precision=highest))
        gate_ff = low_back(jnp.dot(norm_mid, w_gate_ff, precision=highest))
        hidden = low(mix_gelu(gate_ff) * up_proj)
        return resid + low_back(jnp.dot(hidden, w_down, precision=highest))

    def step(carried, item):
        return (carried, group(item[0], item[1], item[2]))
    _, outs = lax.scan(jax.checkpoint(step), None, (xs, order, lengths))
    return outs

def reference(inputs, cotangent, token_mask, order, lengths, gains, w_in, w_gate, w_out, conv_weight, chan_bias, decay, gate_blocks, w_up, w_gate_ff, w_down):
    params = tuple((p.astype(jnp.float32) for p in (gains, w_in, w_gate, w_out, conv_weight, chan_bias, decay, gate_blocks, w_up, w_gate_ff, w_down)))
    xs = inputs.astype(jnp.float32).reshape(N_DP, SLOT, D)

    def forward(x_all, *weights):
        return layer(x_all, *weights, order, lengths)
    outs, pull = jax.vjp(forward, xs, *params)
    cot = cotangent.astype(jnp.float32) * token_mask.astype(jnp.float32)[:, None]
    grads = pull(cot.reshape(N_DP, SLOT, D))
    output = outs.reshape(TOKENS, D).astype(jnp.bfloat16)
    grad_inputs = grads[0].reshape(TOKENS, D).astype(jnp.bfloat16)
    return (output, grad_inputs, grads[1], grads[2], grads[3], grads[4], grads[5], grads[6], grads[7], grads[8], grads[9], grads[10], grads[11])
```

```python
import functools

import jax
import jax.numpy as jnp
from jax import lax
from jax.experimental import pallas as pl
from jax.experimental.pallas import tpu as pltpu
from jax.sharding import PartitionSpec as P

epsilon = 1e-06
LANE = 128
SUB = 8
TAIL = 24
ROWS = 272
VMEM_MB = 60
f32 = jnp.float32
bf16 = jnp.bfloat16
GELU_C = 0.7978845608028654
GELU_A = 0.044715


def rms_scale(values):
    return lax.rsqrt(jnp.mean(values * values, axis=-1, keepdims=True) + epsilon)


def dot(left, right):
    return lax.dot_general(left, right, (((1,), (0,)), ((), ())), preferred_element_type=f32)


def dot_last(left, right):
    return lax.dot_general(left, right, (((1,), (1,)), ((), ())), preferred_element_type=f32)


def dot_first(left, right):
    return lax.dot_general(left, right, (((0,), (0,)), ((), ())), preferred_element_type=f32)


def gelu_of(v):
    return 0.5 * v * (1.0 + jnp.tanh(GELU_C * (v + GELU_A * v * v * v)))


def gelu_both(v):
    square = v * v
    th = jnp.tanh(GELU_C * (v + GELU_A * v * square))
    half = 0.5 * (1.0 + th)
    slope = half + 0.5 * v * (1.0 - th * th) * (GELU_C * (1.0 + 3.0 * GELU_A * square))
    return v * half, slope


def sigmoid(v):
    return 0.5 * jnp.tanh(0.5 * v) + 0.5


def split(values):
    high = values.astype(bf16)
    return high, (values - high.astype(f32)).astype(bf16)


def rows_of(index, rows):
    return pl.ds(pl.multiple_of(index * rows, rows), rows)


def pick_rows(order_col, count):
    places = lax.broadcasted_iota(jnp.int32, (order_col.shape[0], count), 1)
    return (places == order_col).astype(f32).astype(bf16)


def put_rows(order_row, first, rows):
    places = lax.broadcasted_iota(jnp.int32, (rows, order_row.shape[1]), 0) + first
    return (places == order_row).astype(f32).astype(bf16)


def mixer_forward(
    tokens,
    ocol,
    orow,
    pos,
    w_in,
    w_gate,
    w_out,
    chan,
    blocks,
    gate_ref,
    branch_ref,
    conv_ref,
    gin_ref,
    grec_ref,
    state_ref,
    mixed_ref,
    out_ref,
    packed,
    rate,
    prod,
    before,
    low,
):
    count, _ = tokens.shape
    width = w_in.shape[1]
    steps = count // SUB
    heads = width // LANE

    def project(b, carry):
        at = rows_of(b, ROWS)
        packed[...] = dot(pick_rows(ocol[at, :], count), tokens[...]).astype(bf16)
        branch_ref[at, :] = dot(packed[...], w_in[...])
        gate_ref[at, :] = dot(packed[...], w_gate[...])
        return carry

    lax.fori_loop(0, count // ROWS, project, 0)

    for k in range(TAIL // SUB):
        last = branch_ref[pl.ds(count - TAIL + k * SUB, SUB), :]
        before[pl.ds(k * SUB, SUB), :] = pltpu.roll(last, 1, 0)
    before[pl.ds(TAIL, ROWS), :] = branch_ref[pl.ds(0, ROWS), :]

    def gates(b, carry):
        at = rows_of(b, ROWS)

        @pl.when(b > 0)
        def _():
            before[...] = branch_ref[pl.ds(pl.multiple_of(b * ROWS - TAIL, SUB), ROWS + TAIL), :]

        place = pos[at, :]
        for h in range(heads):
            lanes = pl.ds(h * LANE, LANE)
            par = chan[:, lanes]
            conv = par[4:5] + par[0:1] * before[pl.ds(TAIL, ROWS), lanes]
            for k in range(1, 4):
                earlier = before[pl.ds(TAIL - SUB * k, ROWS), lanes]
                conv = conv + par[k : k + 1] * jnp.where(place >= k, earlier, 0.0)
            high, rest = split(conv)
            pre = dot(jnp.concatenate([high, rest], axis=1), blocks[h])
            gate_in = sigmoid(pre[:, :LANE] + par[5:6])
            gate_rec = sigmoid(pre[:, LANE:] + par[6:7])
            kept = jnp.exp(-8.0 * gate_rec * par[7:8])
            drive = jnp.sqrt(1.0 - kept * kept + 0.01) * gate_in * conv
            conv_ref[at, lanes] = conv
            gin_ref[at, lanes] = gate_in
            grec_ref[at, lanes] = gate_rec
            rate[at, lanes] = jnp.where(place >= 1, kept, 0.0)
            state_ref[at, lanes] = drive
        return carry

    lax.fori_loop(0, count // ROWS, gates, 0)

    def scan(i, carry):
        held, passed = carry
        at = rows_of(i, SUB)
        a = rate[at, :]
        held = a * held + state_ref[at, :]
        passed = a * passed
        state_ref[at, :] = held
        prod[at, :] = passed
        return held, passed

    ends = lax.fori_loop(
        0, steps, scan, (jnp.zeros((SUB, width), f32), jnp.ones((SUB, width), f32)), unroll=8
    )
    first = lax.broadcasted_iota(jnp.int32, (SUB, width), 0) == 0
    carry_in = jnp.zeros((SUB, width), f32)
    for _ in range(SUB - 1):
        carry_in = jnp.where(first, 0.0, pltpu.roll(ends[0] + ends[1] * carry_in, 1, 0))

    def finish(i, carry):
        at = rows_of(i, 2 * SUB)
        twice = jnp.concatenate([carry_in, carry_in], axis=0)
        value = state_ref[at, :] + prod[at, :] * twice
        state_ref[at, :] = value
        low[at, :] = (gelu_of(gate_ref[at, :]) * value).astype(bf16)
        return carry

    lax.fori_loop(0, steps // 2, finish, 0, unroll=2)

    def leave(b, carry):
        at = rows_of(b, ROWS)
        mixed = dot(put_rows(orow[...], b * ROWS, ROWS), low[...]).astype(bf16)
        mixed_ref[at, :] = mixed
        out_ref[at, :] = dot(mixed, w_out[...]).astype(bf16)
        return carry

    lax.fori_loop(0, count // ROWS, leave, 0)


def ffn(
    tokens, cot, w_up, w_gate, w_down, part_ref, dnorm_ref, hidden_ref, dup_ref, dgate_ref
):
    def block(b, carry):
        at = rows_of(b, ROWS)
        up = dot(tokens[at, :], w_up[...])
        value, slope = gelu_both(dot(tokens[at, :], w_gate[...]))
        hidden = (value * up).astype(bf16)
        hidden_ref[at, :] = hidden
        d_hidden = dot_last(cot[at, :], w_down[...])
        d_up = (d_hidden * value).astype(bf16)
        d_gate = (d_hidden * up * slope).astype(bf16)
        dup_ref[at, :] = d_up
        dgate_ref[at, :] = d_gate
        dnorm_ref[at, :] = (dot_last(d_up, w_up[...]) + dot_last(d_gate, w_gate[...])).astype(bf16)
        part_ref[at, :] = dot(hidden, w_down[...]).astype(bf16)
        return carry

    lax.fori_loop(0, tokens.shape[0] // ROWS, block, 0)


def mixer_backward(
    back,
    norm,
    ocol,
    orow,
    pos,
    gain,
    w_in,
    w_gate,
    w_out,
    chan,
    blocks,
    gate_ref,
    branch_ref,
    conv_ref,
    gin_ref,
    grec_ref,
    state_ref,
    dcat_ref,
    dnorm_ref,
    small_ref,
    dblocks_ref,
    dgain_ref,
    dmix_arr,
    dmix,
    adj,
    prod,
    after,
    before,
    low,
):
    count, _ = back.shape
    width = w_in.shape[1]
    steps = count // SUB
    heads = width // LANE
    blocks_of = count // ROWS

    def enter(b, carry):
        at = rows_of(b, ROWS)
        dmix_arr[at, :] = dot_last(back[at, :], w_out[...]).astype(bf16)
        return carry

    lax.fori_loop(0, blocks_of, enter, 0)

    def pack(b, carry):
        at = rows_of(b, ROWS)
        d_mixed = dot(pick_rows(ocol[at, :], count), dmix_arr[...])
        value, slope = gelu_both(gate_ref[at, :])
        adj[at, :] = d_mixed * value
        low[at, pl.ds(width, width)] = (d_mixed * state_ref[at, :] * slope).astype(bf16)
        kept = jnp.exp(-8.0 * grec_ref[at, :] * chan[7:8, :])
        dmix[at, :] = jnp.where(pos[at, :] >= 1, kept, 0.0)
        return carry

    lax.fori_loop(0, blocks_of, pack, 0)

    def scan(i, carry):
        held, passed, following = carry
        at = rows_of(steps - 1 - i, SUB)
        held = following * held + adj[at, :]
        passed = following * passed
        adj[at, :] = held
        prod[at, :] = passed
        return held, passed, dmix[at, :]

    last = lax.broadcasted_iota(jnp.int32, (SUB, width), 0) == SUB - 1
    wrapped = jnp.where(last, 0.0, pltpu.roll(dmix[pl.ds(0, SUB), :], SUB - 1, 0))
    ends = lax.fori_loop(
        0,
        steps,
        scan,
        (jnp.zeros((SUB, width), f32), jnp.ones((SUB, width), f32), wrapped),
        unroll=8,
    )
    carry_in = jnp.zeros((SUB, width), f32)
    for _ in range(SUB - 1):
        carry_in = jnp.where(last, 0.0, pltpu.roll(ends[0] + ends[1] * carry_in, SUB - 1, 0))

    small_ref[...] = jnp.zeros_like(small_ref)
    dblocks_ref[...] = jnp.zeros_like(dblocks_ref)
    first = lax.broadcasted_iota(jnp.int32, (SUB, width), 0) == 0
    state_last = state_ref[pl.ds(count - SUB, SUB), :]
    before[pl.ds(TAIL - SUB, SUB), :] = jnp.where(first, 0.0, pltpu.roll(state_last, 1, 0))
    before[pl.ds(TAIL, ROWS), :] = state_ref[pl.ds(0, ROWS), :]
    wide_carry = jnp.concatenate([carry_in] * (ROWS // SUB), axis=0)

    def point(b, carry):
        at = rows_of(b, ROWS)

        @pl.when(b > 0)
        def _():
            before[...] = state_ref[pl.ds(pl.multiple_of(b * ROWS - TAIL, SUB), ROWS + TAIL), :]

        place = pos[at, :]
        for h in range(heads):
            lanes = pl.ds(h * LANE, LANE)
            par = chan[:, lanes]
            adjoint = adj[at, lanes] + prod[at, lanes] * wide_carry[:, h * LANE : (h + 1) * LANE]
            conv = conv_ref[at, lanes]
            gate_in = gin_ref[at, lanes]
            gate_rec = grec_ref[at, lanes]
            kept = jnp.exp(-8.0 * gate_rec * par[7:8])
            square = kept * kept
            inside = 1.0 - square + 0.01
            inverse = lax.rsqrt(inside)
            root = inside * inverse
            previous = before[pl.ds(TAIL - SUB, ROWS), lanes]
            d_log = adjoint * previous * dmix[at, lanes]
            scaled = adjoint * gate_in
            d_log = d_log - scaled * conv * square * inverse
            d_in = adjoint * root * conv * gate_in * (1.0 - gate_in)
            d_rec = d_log * (-8.0 * par[7:8]) * gate_rec * (1.0 - gate_rec)
            both = jnp.concatenate([d_in, d_rec], axis=1)
            high, rest = split(both)
            d_conv = scaled * root + dot_last(high, blocks[h]) + dot_last(rest, blocks[h])
            dblocks_ref[h] += dot_first(conv.astype(bf16), high)
            after[at, lanes] = d_conv
            small_ref[4:5, lanes] += jnp.sum(d_conv, axis=0, keepdims=True)
            small_ref[5:6, lanes] += jnp.sum(d_in, axis=0, keepdims=True)
            small_ref[6:7, lanes] += jnp.sum(d_rec, axis=0, keepdims=True)
            small_ref[7:8, lanes] += (
                jnp.sum(d_log * gate_rec, axis=0, keepdims=True) * (-8.0) * par[8:9]
            )
        return carry

    lax.fori_loop(0, blocks_of, point, 0)

    for k in range(TAIL // SUB):
        head = after[pl.ds(k * SUB, SUB), :]
        after[pl.ds(count + k * SUB, SUB), :] = pltpu.roll(head, SUB - 1, 0)
        tail = branch_ref[pl.ds(count - TAIL + k * SUB, SUB), :]
        before[pl.ds(k * SUB, SUB), :] = pltpu.roll(tail, 1, 0)
    before[pl.ds(TAIL, ROWS), :] = branch_ref[pl.ds(0, ROWS), :]

    def unmix(b, carry):
        at = rows_of(b, ROWS)

        @pl.when(b > 0)
        def _():
            before[...] = branch_ref[pl.ds(pl.multiple_of(b * ROWS - TAIL, SUB), ROWS + TAIL), :]

        place = pos[at, :]
        for h in range(heads):
            lanes = pl.ds(h * LANE, LANE)
            par = chan[:, lanes]
            d_conv = after[at, lanes]
            d_branch = par[0:1] * d_conv
            small_ref[0:1, lanes] += jnp.sum(
                d_conv * before[pl.ds(TAIL, ROWS), lanes], axis=0, keepdims=True
            )
            for k in range(1, 4):
                later = pl.ds(pl.multiple_of(b * ROWS + SUB * k, SUB), ROWS)
                d_branch = d_branch + par[k : k + 1] * jnp.where(
                    pos[later, :] >= k, after[later, lanes], 0.0
                )
                earlier = before[pl.ds(TAIL - SUB * k, ROWS), lanes]
                small_ref[k : k + 1, lanes] += jnp.sum(
                    jnp.where(place >= k, d_conv * earlier, 0.0), axis=0, keepdims=True
                )
            low[at, lanes] = d_branch.astype(bf16)
        return carry

    lax.fori_loop(0, blocks_of, unmix, 0)
    dgain_ref[...] = jnp.zeros_like(dgain_ref)

    def leave(b, carry):
        at = rows_of(b, ROWS)
        cat = dot(put_rows(orow[...], b * ROWS, ROWS), low[...]).astype(bf16)
        dcat_ref[at, :] = cat
        d_norm = dot_last(cat[:, :width], w_in[...]) + dot_last(cat[:, width:], w_gate[...])
        dgain_ref[...] += jnp.sum(d_norm * norm[at, :].astype(f32), axis=0, keepdims=True)
        dnorm_ref[at, :] = d_norm.astype(bf16)
        return carry

    lax.fori_loop(0, blocks_of, leave, 0)
    dgain_ref[...] = dgain_ref[...] / gain[...]


def local_call(body, outs, scratch, flops, args):
    whole = pl.BlockSpec(memory_space=pltpu.VMEM)
    moved = sum(a.size * a.dtype.itemsize for a in args)
    moved += sum(o.size * o.dtype.itemsize for o in outs)
    return pl.pallas_call(
        body,
        out_shape=outs,
        in_specs=[whole] * len(args),
        out_specs=[whole] * len(outs),
        scratch_shapes=scratch,
        compiler_params=pltpu.CompilerParams(vmem_limit_bytes=VMEM_MB << 20),
        cost_estimate=pl.CostEstimate(flops=flops, bytes_accessed=moved, transcendentals=0),
    )(*args)


def shape_of(dtype, *shape):
    return jax.ShapeDtypeStruct(shape, dtype)


def shards(
    inputs,
    cotangent,
    token_mask,
    order,
    lengths,
    gains,
    w_in,
    w_gate,
    w_out,
    conv_weight,
    chan_bias,
    decay,
    gate_blocks,
    w_up,
    w_gate_ff,
    w_down,
):
    n_dp = lax.axis_size("dp")
    local_rows, model = inputs.shape
    count = local_rows * lax.axis_size("mp")
    heads, piece = decay.shape
    width = heads * piece * n_dp
    hidden_width = w_up.shape[1]

    flat = jnp.concatenate(
        [conv_weight.reshape(-1, piece), chan_bias.reshape(-1, piece), decay]
        + [gate_blocks.transpose(0, 1, 3, 2).reshape(-1, piece)],
        axis=0,
    )
    small_all = lax.all_gather(flat, "dp", axis=1, tiled=True)
    full_in = lax.all_gather(w_in, "dp", axis=0, tiled=True)
    full_gate = lax.all_gather(w_gate, "dp", axis=0, tiled=True)
    full_out = lax.all_gather(w_out, "dp", axis=1, tiled=True)
    full_up = lax.all_gather(w_up, "dp", axis=0, tiled=True)
    full_gate_ff = lax.all_gather(w_gate_ff, "dp", axis=0, tiled=True)
    full_down = lax.all_gather(w_down, "dp", axis=1, tiled=True)

    params = small_all[: 8 * heads].astype(f32).reshape(8, width)
    decay_row = params[7:8]
    chan = jnp.concatenate(
        [params[:7], jax.nn.softplus(decay_row), jax.nn.sigmoid(decay_row), jnp.zeros((7, width), f32)],
        axis=0,
    )
    blocks = small_all[8 * heads :].reshape(2, heads, LANE, LANE)
    blocks = blocks.transpose(1, 3, 0, 2).reshape(heads, LANE, 2 * LANE)
    blocks_twice = jnp.concatenate([blocks, blocks], axis=1)

    steps = count // SUB
    ends = jnp.cumsum(lengths[0], dtype=jnp.int32)
    starts = ends - lengths[0]
    places = jnp.arange(count, dtype=jnp.int32)
    own_start = jnp.max(
        jnp.where(places[:, None] >= starts[None, :], starts[None, :], 0), axis=1
    )
    pos = (places - own_start).reshape(SUB, steps).T
    wrap = jnp.concatenate([pos[: TAIL // SUB, 1:], jnp.full((TAIL // SUB, 1), -1, jnp.int32)], axis=1)
    pos_col = jnp.concatenate([pos, wrap], axis=0).reshape(count + TAIL, 1)
    order_int = order[0].reshape(SUB, steps).T.reshape(count)
    ocol, orow = order_int.reshape(count, 1), order_int.reshape(1, count)

    gain_f = gains.astype(f32)
    x_local = inputs.astype(f32)
    norm_in = (x_local * rms_scale(x_local) * gain_f[0]).astype(bf16)
    norm_group = lax.all_gather(norm_in, "mp", axis=0, tiled=True)
    cot = cotangent.astype(f32) * token_mask.astype(f32)[:, None]
    cot_group = lax.all_gather(cot.astype(bf16), "mp", axis=0, tiled=True)

    wide = pltpu.VMEM((count, width), f32)
    saved = [shape_of(f32, count, width)] * 6
    *kept, mixed, back_part = local_call(
        mixer_forward,
        saved + [shape_of(bf16, count, width), shape_of(bf16, count, model)],
        [
            pltpu.VMEM((ROWS, model), bf16),
            wide,
            wide,
            pltpu.VMEM((ROWS + TAIL, width), f32),
            pltpu.VMEM((count, width), bf16),
        ],
        2 * count * (count * model + 3 * model * width),
        (norm_group, ocol, orow, pos_col, full_in, full_gate, full_out, chan, blocks_twice),
    )
    resid = x_local + lax.psum_scatter(back_part, "mp", scatter_dimension=0, tiled=True).astype(f32)
    rms_mid = rms_scale(resid)
    norm_mid = (resid * rms_mid * gain_f[1]).astype(bf16)
    norm_mid_group = lax.all_gather(norm_mid, "mp", axis=0, tiled=True)

    hid = shape_of(bf16, count, hidden_width)
    tok = shape_of(bf16, count, model)
    ffn_part, d_norm_part, hidden, d_up, d_gate_ff = local_call(
        ffn,
        [tok, tok, hid, hid, hid],
        [],
        12 * count * model * hidden_width,
        (norm_mid_group, cot_group, full_up, full_gate_ff, full_down),
    )
    d_norm_mid = lax.psum_scatter(d_norm_part, "mp", scatter_dimension=0, tiled=True).astype(f32)
    scaled = gain_f[1] * d_norm_mid
    gain_mid = jnp.sum(d_norm_mid * resid * rms_mid, axis=0)
    d_resid = (
        cot
        + rms_mid * scaled
        - resid * (rms_mid * rms_mid * rms_mid) * jnp.mean(resid * scaled, axis=-1, keepdims=True)
    )
    back_group = lax.all_gather(d_resid.astype(bf16), "mp", axis=0, tiled=True)
    output = (
        resid + lax.psum_scatter(ffn_part, "mp", scatter_dimension=0, tiled=True).astype(f32)
    ).astype(bf16)

    def reduced(grad, dimension):
        return lax.psum_scatter(grad.astype(bf16), "dp", scatter_dimension=dimension, tiled=True).astype(f32)

    grad_down = reduced(dot_first(hidden, cot_group), 1)
    grad_up = reduced(dot_first(norm_mid_group, d_up), 0)
    grad_gate_ff = reduced(dot_first(norm_mid_group, d_gate_ff), 0)

    d_cat, d_norm_back, small, d_blocks, gain_in = local_call(
        mixer_backward,
        [
            shape_of(bf16, count, 2 * width),
            tok,
            shape_of(f32, 8, width),
            shape_of(f32, heads, LANE, 2 * LANE),
            shape_of(f32, 1, model),
        ],
        [
            pltpu.VMEM((count, width), bf16),
            wide,
            wide,
            wide,
            pltpu.VMEM((count + TAIL, width), f32),
            pltpu.VMEM((ROWS + TAIL, width), f32),
            pltpu.VMEM((count, 2 * width), bf16),
        ],
        2 * count * (3 * count * width + 3 * model * width),
        (
            back_group,
            norm_group,
            ocol,
            orow,
            pos_col,
            gain_f[0:1],
            full_in,
            full_gate,
            full_out,
            chan,
            blocks,
            *kept,
        ),
    )
    d_norm_in = lax.psum_scatter(d_norm_back, "mp", scatter_dimension=0, tiled=True).astype(f32)
    grad_out = reduced(dot_first(mixed, back_group), 1)
    grad_cat = dot_first(norm_group, d_cat)
    grad_in = reduced(grad_cat[:, :width], 0)
    grad_gate = reduced(grad_cat[:, width:], 0)

    d_blocks_rows = d_blocks.reshape(heads, n_dp, piece, 2, LANE).transpose(1, 3, 0, 2, 4)
    small_rows = small.reshape(8 * heads, n_dp, piece).transpose(1, 0, 2)
    packed_small = jnp.concatenate(
        [small_rows.reshape(n_dp, -1), d_blocks_rows.reshape(n_dp, -1)], axis=1
    )
    small_own = lax.psum_scatter(packed_small, "dp", scatter_dimension=0, tiled=True)[0]
    split_at = 8 * heads * piece
    rows = small_own[:split_at].reshape(8, heads, piece)
    grad_blocks = small_own[split_at:].reshape(2, heads, piece, LANE)

    rms_in = rms_scale(x_local)
    e_in = gain_f[0] * d_norm_in
    grad_inputs = (
        d_resid
        + rms_in * e_in
        - x_local * (rms_in * rms_in * rms_in) * jnp.mean(x_local * e_in, axis=-1, keepdims=True)
    ).astype(bf16)
    grad_gains = lax.psum_scatter(
        jnp.stack([gain_in[0], gain_mid]), ("dp", "mp"), scatter_dimension=1, tiled=True
    )
    return (
        output,
        grad_inputs,
        grad_gains,
        grad_in,
        grad_gate,
        grad_out,
        rows[0:4],
        rows[4:7],
        rows[7],
        grad_blocks,
        grad_up,
        grad_gate_ff,
        grad_down,
    )


def solution(mesh):
    row, col = P("dp", "mp"), P("mp", "dp")
    tok = P(("dp", "mp"), None)
    chan = P(None, "mp", "dp")
    gate = P(None, "mp", "dp", None)
    return jax.shard_map(
        shards,
        mesh=mesh,
        in_specs=(
            tok, tok, P(("dp", "mp")), P("dp", None), P("dp", None), P(),
            row, row, col, chan, chan, col, gate, row, row, col,
        ),
        out_specs=(
            tok, tok, P(None, ("dp", "mp")), row, row, col, chan, chan, col, gate, row, row, col,
        ),
        check_vma=False,
    )
```

```python
import functools

import jax
import jax.numpy as jnp
from jax import lax
from jax.experimental import pallas as pl
from jax.experimental.pallas import tpu as pltpu
from jax.sharding import PartitionSpec as P

epsilon = 1e-06
LANE = 128
SUB = 8
TAIL = 24
ROWS = 272
VMEM_MB = 60
f32 = jnp.float32
bf16 = jnp.bfloat16
GELU_C = 0.7978845608028654
GELU_A = 0.044715


def rms_scale(values):
    return lax.rsqrt(jnp.mean(values * values, axis=-1, keepdims=True) + epsilon)


def dot(left, right):
    return lax.dot_general(left, right, (((1,), (0,)), ((), ())), preferred_element_type=f32)


def dot_last(left, right):
    return lax.dot_general(left, right, (((1,), (1,)), ((), ())), preferred_element_type=f32)


def dot_first(left, right):
    return lax.dot_general(left, right, (((0,), (0,)), ((), ())), preferred_element_type=f32)


def gelu_of(v):
    return 0.5 * v * (1.0 + jnp.tanh(GELU_C * (v + GELU_A * v * v * v)))


def gelu_both(v):
    square = v * v
    th = jnp.tanh(GELU_C * (v + GELU_A * v * square))
    half = 0.5 * (1.0 + th)
    slope = half + 0.5 * v * (1.0 - th * th) * (GELU_C * (1.0 + 3.0 * GELU_A * square))
    return v * half, slope


def sigmoid(v):
    return 0.5 * jnp.tanh(0.5 * v) + 0.5


def split(values):
    high = values.astype(bf16)
    return high, (values - high.astype(f32)).astype(bf16)


def rows_of(index, rows):
    return pl.ds(pl.multiple_of(index * rows, rows), rows)


def pick_rows(order_col, count):
    places = lax.broadcasted_iota(jnp.int32, (order_col.shape[0], count), 1)
    return (places == order_col).astype(f32).astype(bf16)


def put_rows(order_row, first, rows):
    places = lax.broadcasted_iota(jnp.int32, (rows, order_row.shape[1]), 0) + first
    return (places == order_row).astype(f32).astype(bf16)


def mixer_forward(
    tokens,
    ocol,
    orow,
    pos,
    w_in,
    w_gate,
    w_out,
    chan,
    blocks,
    gate_ref,
    branch_ref,
    conv_ref,
    gin_ref,
    grec_ref,
    state_ref,
    mixed_ref,
    out_ref,
    packed,
    rate,
    prod,
    before,
    low,
):
    count, _ = tokens.shape
    width = w_in.shape[1]
    steps = count // SUB
    heads = width // LANE

    def project(b, carry):
        at = rows_of(b, ROWS)
        packed[...] = dot(pick_rows(ocol[at, :], count), tokens[...]).astype(bf16)
        branch_ref[at, :] = dot(packed[...], w_in[...])
        gate_ref[at, :] = dot(packed[...], w_gate[...])
        return carry

    lax.fori_loop(0, count // ROWS, project, 0)

    for k in range(TAIL // SUB):
        last = branch_ref[pl.ds(count - TAIL + k * SUB, SUB), :]
        before[pl.ds(k * SUB, SUB), :] = pltpu.roll(last, 1, 0)
    before[pl.ds(TAIL, ROWS), :] = branch_ref[pl.ds(0, ROWS), :]

    def gates(b, carry):
        at = rows_of(b, ROWS)

        @pl.when(b > 0)
        def _():
            before[...] = branch_ref[pl.ds(pl.multiple_of(b * ROWS - TAIL, SUB), ROWS + TAIL), :]

        place = pos[at, :]
        for h in range(heads):
            lanes = pl.ds(h * LANE, LANE)
            par = chan[:, lanes]
            conv = par[4:5] + par[0:1] * before[pl.ds(TAIL, ROWS), lanes]
            for k in range(1, 4):
                earlier = before[pl.ds(TAIL - SUB * k, ROWS), lanes]
                conv = conv + par[k : k + 1] * jnp.where(place >= k, earlier, 0.0)
            high, rest = split(conv)
            pre = dot(jnp.concatenate([high, rest], axis=1), blocks[h])
            gate_in = sigmoid(pre[:, :LANE] + par[5:6])
            gate_rec = sigmoid(pre[:, LANE:] + par[6:7])
            kept = jnp.exp(-8.0 * gate_rec * par[7:8])
            drive = jnp.sqrt(1.0 - kept * kept + 0.01) * gate_in * conv
            conv_ref[at, lanes] = conv
            gin_ref[at, lanes] = gate_in
            grec_ref[at, lanes] = gate_rec
            rate[at, lanes] = jnp.where(place >= 1, kept, 0.0)
            state_ref[at, lanes] = drive
        return carry

    lax.fori_loop(0, count // ROWS, gates, 0)

    def scan(i, carry):
        held, passed = carry
        at = rows_of(i, SUB)
        a = rate[at, :]
        held = a * held + state_ref[at, :]
        passed = a * passed
        state_ref[at, :] = held
        prod[at, :] = passed
        return held, passed

    ends = lax.fori_loop(
        0, steps, scan, (jnp.zeros((SUB, width), f32), jnp.ones((SUB, width), f32)), unroll=8
    )
    first = lax.broadcasted_iota(jnp.int32, (SUB, width), 0) == 0
    carry_in = jnp.zeros((SUB, width), f32)
    for _ in range(SUB - 1):
        carry_in = jnp.where(first, 0.0, pltpu.roll(ends[0] + ends[1] * carry_in, 1, 0))

    def finish(i, carry):
        at = rows_of(i, 2 * SUB)
        twice = jnp.concatenate([carry_in, carry_in], axis=0)
        value = state_ref[at, :] + prod[at, :] * twice
        state_ref[at, :] = value
        low[at, :] = (gelu_of(gate_ref[at, :]) * value).astype(bf16)
        return carry

    lax.fori_loop(0, steps // 2, finish, 0, unroll=2)

    def leave(b, carry):
        at = rows_of(b, ROWS)
        mixed = dot(put_rows(orow[...], b * ROWS, ROWS), low[...]).astype(bf16)
        mixed_ref[at, :] = mixed
        out_ref[at, :] = dot(mixed, w_out[...]).astype(bf16)
        return carry

    lax.fori_loop(0, count // ROWS, leave, 0)


def ffn(
    tokens, cot, w_up, w_gate, w_down, part_ref, dnorm_ref, hidden_ref, dup_ref, dgate_ref
):
    def block(b, carry):
        at = rows_of(b, ROWS)
        up = dot(tokens[at, :], w_up[...])
        value, slope = gelu_both(dot(tokens[at, :], w_gate[...]))
        hidden = (value * up).astype(bf16)
        hidden_ref[at, :] = hidden
        d_hidden = dot_last(cot[at, :], w_down[...])
        d_up = (d_hidden * value).astype(bf16)
        d_gate = (d_hidden * up * slope).astype(bf16)
        dup_ref[at, :] = d_up
        dgate_ref[at, :] = d_gate
        dnorm_ref[at, :] = (dot_last(d_up, w_up[...]) + dot_last(d_gate, w_gate[...])).astype(bf16)
        part_ref[at, :] = dot(hidden, w_down[...]).astype(bf16)
        return carry

    lax.fori_loop(0, tokens.shape[0] // ROWS, block, 0)


def mixer_backward(
    back,
    norm,
    ocol,
    orow,
    pos,
    gain,
    w_in,
    w_gate,
    w_out,
    chan,
    blocks,
    gate_ref,
    branch_ref,
    conv_ref,
    gin_ref,
    grec_ref,
    state_ref,
    dcat_ref,
    dnorm_ref,
    small_ref,
    dblocks_ref,
    dgain_ref,
    dmix_arr,
    dmix,
    adj,
    prod,
    after,
    before,
    low,
):
    count, _ = back.shape
    width = w_in.shape[1]
    steps = count // SUB
    heads = width // LANE
    blocks_of = count // ROWS

    def enter(b, carry):
        at = rows_of(b, ROWS)
        dmix_arr[at, :] = dot_last(back[at, :], w_out[...]).astype(bf16)
        return carry

    lax.fori_loop(0, blocks_of, enter, 0)

    def pack(b, carry):
        at = rows_of(b, ROWS)
        d_mixed = dot(pick_rows(ocol[at, :], count), dmix_arr[...])
        value, slope = gelu_both(gate_ref[at, :])
        adj[at, :] = d_mixed * value
        low[at, pl.ds(width, width)] = (d_mixed * state_ref[at, :] * slope).astype(bf16)
        kept = jnp.exp(-8.0 * grec_ref[at, :] * chan[7:8, :])
        dmix[at, :] = jnp.where(pos[at, :] >= 1, kept, 0.0)
        return carry

    lax.fori_loop(0, blocks_of, pack, 0)

    def scan(i, carry):
        held, passed, following = carry
        at = rows_of(steps - 1 - i, SUB)
        held = following * held + adj[at, :]
        passed = following * passed
        adj[at, :] = held
        prod[at, :] = passed
        return held, passed, dmix[at, :]

    last = lax.broadcasted_iota(jnp.int32, (SUB, width), 0) == SUB - 1
    wrapped = jnp.where(last, 0.0, pltpu.roll(dmix[pl.ds(0, SUB), :], SUB - 1, 0))
    ends = lax.fori_loop(
        0,
        steps,
        scan,
        (jnp.zeros((SUB, width), f32), jnp.ones((SUB, width), f32), wrapped),
        unroll=8,
    )
    carry_in = jnp.zeros((SUB, width), f32)
    for _ in range(SUB - 1):
        carry_in = jnp.where(last, 0.0, pltpu.roll(ends[0] + ends[1] * carry_in, SUB - 1, 0))

    small_ref[...] = jnp.zeros_like(small_ref)
    dblocks_ref[...] = jnp.zeros_like(dblocks_ref)
    first = lax.broadcasted_iota(jnp.int32, (SUB, width), 0) == 0
    state_last = state_ref[pl.ds(count - SUB, SUB), :]
    before[pl.ds(TAIL - SUB, SUB), :] = jnp.where(first, 0.0, pltpu.roll(state_last, 1, 0))
    before[pl.ds(TAIL, ROWS), :] = state_ref[pl.ds(0, ROWS), :]
    wide_carry = jnp.concatenate([carry_in] * (ROWS // SUB), axis=0)

    def point(b, carry):
        at = rows_of(b, ROWS)

        @pl.when(b > 0)
        def _():
            before[...] = state_ref[pl.ds(pl.multiple_of(b * ROWS - TAIL, SUB), ROWS + TAIL), :]

        place = pos[at, :]
        for h in range(heads):
            lanes = pl.ds(h * LANE, LANE)
            par = chan[:, lanes]
            adjoint = adj[at, lanes] + prod[at, lanes] * wide_carry[:, h * LANE : (h + 1) * LANE]
            conv = conv_ref[at, lanes]
            gate_in = gin_ref[at, lanes]
            gate_rec = grec_ref[at, lanes]
            kept = jnp.exp(-8.0 * gate_rec * par[7:8])
            square = kept * kept
            inside = 1.0 - square + 0.01
            inverse = lax.rsqrt(inside)
            root = inside * inverse
            previous = before[pl.ds(TAIL - SUB, ROWS), lanes]
            d_log = adjoint * previous * dmix[at, lanes]
            scaled = adjoint * gate_in
            d_log = d_log - scaled * conv * square * inverse
            d_in = adjoint * root * conv * gate_in * (1.0 - gate_in)
            d_rec = d_log * (-8.0 * par[7:8]) * gate_rec * (1.0 - gate_rec)
            both = jnp.concatenate([d_in, d_rec], axis=1)
            high, rest = split(both)
            d_conv = scaled * root + dot_last(high, blocks[h]) + dot_last(rest, blocks[h])
            dblocks_ref[h] += dot_first(conv.astype(bf16), high)
            after[at, lanes] = d_conv
            small_ref[4:5, lanes] += jnp.sum(d_conv, axis=0, keepdims=True)
            small_ref[5:6, lanes] += jnp.sum(d_in, axis=0, keepdims=True)
            small_ref[6:7, lanes] += jnp.sum(d_rec, axis=0, keepdims=True)
            small_ref[7:8, lanes] += (
                jnp.sum(d_log * gate_rec, axis=0, keepdims=True) * (-8.0) * par[8:9]
            )
        return carry

    lax.fori_loop(0, blocks_of, point, 0)

    for k in range(TAIL // SUB):
        head = after[pl.ds(k * SUB, SUB), :]
        after[pl.ds(count + k * SUB, SUB), :] = pltpu.roll(head, SUB - 1, 0)
        tail = branch_ref[pl.ds(count - TAIL + k * SUB, SUB), :]
        before[pl.ds(k * SUB, SUB), :] = pltpu.roll(tail, 1, 0)
    before[pl.ds(TAIL, ROWS), :] = branch_ref[pl.ds(0, ROWS), :]

    def unmix(b, carry):
        at = rows_of(b, ROWS)

        @pl.when(b > 0)
        def _():
            before[...] = branch_ref[pl.ds(pl.multiple_of(b * ROWS - TAIL, SUB), ROWS + TAIL), :]

        place = pos[at, :]
        for h in range(heads):
            lanes = pl.ds(h * LANE, LANE)
            par = chan[:, lanes]
            d_conv = after[at, lanes]
            d_branch = par[0:1] * d_conv
            small_ref[0:1, lanes] += jnp.sum(
                d_conv * before[pl.ds(TAIL, ROWS), lanes], axis=0, keepdims=True
            )
            for k in range(1, 4):
                later = pl.ds(pl.multiple_of(b * ROWS + SUB * k, SUB), ROWS)
                d_branch = d_branch + par[k : k + 1] * jnp.where(
                    pos[later, :] >= k, after[later, lanes], 0.0
                )
                earlier = before[pl.ds(TAIL - SUB * k, ROWS), lanes]
                small_ref[k : k + 1, lanes] += jnp.sum(
                    jnp.where(place >= k, d_conv * earlier, 0.0), axis=0, keepdims=True
                )
            low[at, lanes] = d_branch.astype(bf16)
        return carry

    lax.fori_loop(0, blocks_of, unmix, 0)
    dgain_ref[...] = jnp.zeros_like(dgain_ref)

    def leave(b, carry):
        at = rows_of(b, ROWS)
        cat = dot(put_rows(orow[...], b * ROWS, ROWS), low[...]).astype(bf16)
        dcat_ref[at, :] = cat
        d_norm = dot_last(cat[:, :width], w_in[...]) + dot_last(cat[:, width:], w_gate[...])
        dgain_ref[...] += jnp.sum(d_norm * norm[at, :].astype(f32), axis=0, keepdims=True)
        dnorm_ref[at, :] = d_norm.astype(bf16)
        return carry

    lax.fori_loop(0, blocks_of, leave, 0)
    dgain_ref[...] = dgain_ref[...] / gain[...]


MESH = pl.DeviceIdType.MESH
TILE = 16
PIECES = 4


def cut_rows(rows, parts):
    tiles = rows // TILE
    ends = [tiles * (k + 1) // parts for k in range(parts)]
    return [(TILE * a, TILE * (b - a)) for a, b in zip([0] + ends[:-1], ends)]


class Line:
    def __init__(self, n, local, part, arrived, whole, sums, alls):
        self.n, self.local, self.part, self.arrived, self.whole = n, local, part, arrived, whole
        self.sums, self.alls = sums, alls
        self.me = lax.axis_index("mp")
        self.pieces = cut_rows(local, PIECES)
        self.has = (self.me > 0, self.me < n - 1)

    def greet(self):
        barrier = pltpu.get_barrier_semaphore()
        for has, other in zip(self.has, (self.me - 1, self.me + 1)):

            @pl.when(has)
            def _():
                pl.semaphore_signal(barrier, inc=1, device_id={"mp": other}, device_id_type=MESH)

        both = self.has[0] & self.has[1]

        @pl.when(both)
        def _():
            pl.semaphore_wait(barrier, 2)

        @pl.when(jnp.logical_not(both))
        def _():
            pl.semaphore_wait(barrier, 1)

    def rows_at(self, owner, k):
        first, rows = self.pieces[k]
        return pl.ds(pl.multiple_of(owner * self.local + first, TILE), rows)

    def copy(self, source, target, sems, way, owner, k):
        return pltpu.make_async_remote_copy(
            src_ref=source,
            dst_ref=target,
            send_sem=sems[0].at[way, owner, k],
            recv_sem=sems[1].at[way, owner, k],
            device_id={"mp": self.me + 1 - 2 * way},
            device_id_type=MESH,
        )

    def sum_copy(self, way, owner, k, first=False):
        at = self.rows_at(owner, k)
        landed = self.arrived[way].at[at]
        return self.copy(self.part.at[at] if first else landed, landed, self.sums, way, owner, k)

    def all_copy(self, way, owner, k):
        block = self.whole.at[self.rows_at(owner, k)]
        return self.copy(block, block, self.alls, way, owner, k)

    def relay(self, k):
        for away in range(self.n - 1):
            for way in range(2):
                owner = away if way else self.n - 1 - away
                beyond = self.me > owner if way else self.me < owner

                @pl.when(beyond & jnp.logical_not(self.has[way]))
                def _():
                    self.sum_copy(way, owner, k, True).start()

                @pl.when(beyond & self.has[way])
                def _():
                    self.sum_copy(way, owner, k).wait_recv()
                    at = self.rows_at(owner, k)
                    landed = self.arrived[way]
                    landed[at, :] = (landed[at, :].astype(f32) + self.part[at, :].astype(f32)).astype(bf16)
                    self.sum_copy(way, owner, k).start()

    def total(self, k, into):
        at = self.rows_at(self.me, k)
        rows = pl.ds(0, self.pieces[k][1])
        into[rows, :] = self.part[at, :].astype(f32)
        for way in range(2):

            @pl.when(self.has[way])
            def _():
                self.sum_copy(way, self.me, k).wait_recv()
                into[rows, :] += self.arrived[way][at, :].astype(f32)

    def spread(self, k):
        for way in range(2):

            @pl.when(self.has[1 - way])
            def _():
                self.all_copy(way, self.me, k).start()

    def forward(self, k):
        for away in range(self.n - 1):
            for way in range(2):
                owner = self.n - 1 - away if way else away
                below = self.me < owner if way else self.me > owner

                @pl.when(below)
                def _():
                    self.all_copy(way, owner, k).wait_recv()

                @pl.when(below & self.has[1 - way])
                def _():
                    self.all_copy(way, owner, k).start()

    def finish(self):
        for k in range(PIECES):
            for owner in range(self.n):
                for way in range(2):
                    if self.part is not None:

                        @pl.when(self.me > owner if way else self.me < owner)
                        def _():
                            self.sum_copy(way, owner, k).wait_send()

                    if self.whole is not None:
                        reached = self.me <= owner if way else self.me >= owner

                        @pl.when(reached & self.has[1 - way])
                        def _():
                            self.all_copy(way, owner, k).wait_send()

    def run(self, point):
        for k in range(PIECES + 2):
            if k < PIECES and self.part is not None:
                self.relay(k)
            if 1 <= k <= PIECES:
                point(k - 1)
                if self.whole is not None:
                    self.spread(k - 1)
            if k >= 2 and self.whole is not None:
                self.forward(k - 2)
        self.finish()

    def tiles(self, k, body):
        first, rows = self.pieces[k]

        def one(i, carry):
            body(
                pl.ds(pl.multiple_of(i * TILE, TILE), TILE),
                pl.ds(pl.multiple_of(first + i * TILE, TILE), TILE),
                pl.ds(pl.multiple_of(self.me * self.local + first + i * TILE, TILE), TILE),
            )
            return carry

        lax.fori_loop(0, rows // TILE, one, 0)


def gather_norm(n, x, gain, whole, send, recv):
    line = Line(n, x.shape[0], None, None, whole, None, (send, recv))
    line.greet()

    def point(k):
        def one(_, own, at):
            v = x[own, :].astype(f32)
            whole[at, :] = (v * rms_scale(v) * gain[...]).astype(bf16)

        line.tiles(k, one)

    line.run(point)


def sum_norm_gather(n, x, gain, part, resid, whole, left, right, total, ss, sr, send, recv):
    line = Line(n, x.shape[0], part, (left, right), whole, (ss, sr), (send, recv))
    line.greet()

    def point(k):
        line.total(k, total)

        def one(here, own, at):
            v = x[own, :].astype(f32) + total[here, :]
            resid[own, :] = v
            whole[at, :] = (v * rms_scale(v) * gain[...]).astype(bf16)

        line.tiles(k, one)

    line.run(point)


def norm_back(value, gain, grad):
    scale = rms_scale(value)
    e = gain * grad
    slope = scale * scale * scale * jnp.mean(value * e, axis=-1, keepdims=True)
    return scale * e - value * slope, grad * value * scale


def sum_back_gather(
    n, resid, cot, gain, part, d_resid, gain_grad, whole, left, right, total, ss, sr, send, recv
):
    line = Line(n, resid.shape[0], part, (left, right), whole, (ss, sr), (send, recv))
    line.greet()
    gain_grad[...] = jnp.zeros_like(gain_grad)

    def point(k):
        line.total(k, total)

        def one(here, own, at):
            back, terms = norm_back(resid[own, :], gain[...], total[here, :])
            gain_grad[...] += jnp.sum(terms, axis=0, keepdims=True)
            value = cot[own, :].astype(f32) + back
            d_resid[own, :] = value
            whole[at, :] = value.astype(bf16)

        line.tiles(k, one)

    line.run(point)


def sum_back(n, x, d_resid, gain, part, grad_x, left, right, total, ss, sr):
    line = Line(n, x.shape[0], part, (left, right), None, (ss, sr), None)
    line.greet()

    def point(k):
        line.total(k, total)

        def one(here, own, at):
            back, _ = norm_back(x[own, :].astype(f32), gain[...], total[here, :])
            grad_x[own, :] = (d_resid[own, :] + back).astype(bf16)

        line.tiles(k, one)

    line.run(point)


def line_call(body, n, identity, outs, sums, alls, args):
    whole = pl.BlockSpec(memory_space=pltpu.VMEM)
    local, model = args[0].shape
    sem = pltpu.SemaphoreType.DMA((2, n, PIECES))
    scratch = []
    if sums:
        scratch += [pltpu.VMEM((n * local, model), bf16)] * 2
        scratch += [pltpu.VMEM((max(rows for _, rows in cut_rows(local, PIECES)), model), f32)]
        scratch += [sem, sem]
    if alls:
        scratch += [sem, sem]
    moved = sum(a.size * a.dtype.itemsize for a in args)
    return pl.pallas_call(
        functools.partial(body, n),
        out_shape=outs,
        in_specs=[whole] * len(args),
        out_specs=[whole] * len(outs),
        scratch_shapes=scratch,
        compiler_params=pltpu.CompilerParams(
            vmem_limit_bytes=VMEM_MB << 20, collective_id=identity, has_side_effects=True
        ),
        cost_estimate=pl.CostEstimate(flops=0, bytes_accessed=100 * moved, transcendentals=0),
    )(*args)


def local_call(body, outs, scratch, flops, args):
    whole = pl.BlockSpec(memory_space=pltpu.VMEM)
    moved = sum(a.size * a.dtype.itemsize for a in args)
    moved += sum(o.size * o.dtype.itemsize for o in outs)
    return pl.pallas_call(
        body,
        out_shape=outs,
        in_specs=[whole] * len(args),
        out_specs=[whole] * len(outs),
        scratch_shapes=scratch,
        compiler_params=pltpu.CompilerParams(vmem_limit_bytes=VMEM_MB << 20),
        cost_estimate=pl.CostEstimate(flops=flops, bytes_accessed=moved, transcendentals=0),
    )(*args)


def shape_of(dtype, *shape):
    return jax.ShapeDtypeStruct(shape, dtype)


def shards(
    inputs,
    cotangent,
    token_mask,
    order,
    lengths,
    gains,
    w_in,
    w_gate,
    w_out,
    conv_weight,
    chan_bias,
    decay,
    gate_blocks,
    w_up,
    w_gate_ff,
    w_down,
):
    n_dp = lax.axis_size("dp")
    local_rows, model = inputs.shape
    count = local_rows * lax.axis_size("mp")
    heads, piece = decay.shape
    width = heads * piece * n_dp
    hidden_width = w_up.shape[1]

    flat = jnp.concatenate(
        [conv_weight.reshape(-1, piece), chan_bias.reshape(-1, piece), decay]
        + [gate_blocks.transpose(0, 1, 3, 2).reshape(-1, piece)],
        axis=0,
    )
    small_all = lax.all_gather(flat, "dp", axis=1, tiled=True)
    full_in = lax.all_gather(w_in, "dp", axis=0, tiled=True)
    full_gate = lax.all_gather(w_gate, "dp", axis=0, tiled=True)
    full_out = lax.all_gather(w_out, "dp", axis=1, tiled=True)
    full_up = lax.all_gather(w_up, "dp", axis=0, tiled=True)
    full_gate_ff = lax.all_gather(w_gate_ff, "dp", axis=0, tiled=True)
    full_down = lax.all_gather(w_down, "dp", axis=1, tiled=True)

    params = small_all[: 8 * heads].astype(f32).reshape(8, width)
    decay_row = params[7:8]
    chan = jnp.concatenate(
        [params[:7], jax.nn.softplus(decay_row), jax.nn.sigmoid(decay_row), jnp.zeros((7, width), f32)],
        axis=0,
    )
    blocks = small_all[8 * heads :].reshape(2, heads, LANE, LANE)
    blocks = blocks.transpose(1, 3, 0, 2).reshape(heads, LANE, 2 * LANE)
    blocks_twice = jnp.concatenate([blocks, blocks], axis=1)

    steps = count // SUB
    ends = jnp.cumsum(lengths[0], dtype=jnp.int32)
    starts = ends - lengths[0]
    places = jnp.arange(count, dtype=jnp.int32)
    own_start = jnp.max(
        jnp.where(places[:, None] >= starts[None, :], starts[None, :], 0), axis=1
    )
    pos = (places - own_start).reshape(SUB, steps).T
    wrap = jnp.concatenate([pos[: TAIL // SUB, 1:], jnp.full((TAIL // SUB, 1), -1, jnp.int32)], axis=1)
    pos_col = jnp.concatenate([pos, wrap], axis=0).reshape(count + TAIL, 1)
    order_int = order[0].reshape(SUB, steps).T.reshape(count)
    ocol, orow = order_int.reshape(count, 1), order_int.reshape(1, count)

    gain_f = gains.astype(f32)
    n_mp = lax.axis_size("mp")
    tok = shape_of(bf16, count, model)
    own = shape_of(f32, local_rows, model)
    (norm_group,) = line_call(gather_norm, n_mp, 0, [tok], False, True, (inputs, gain_f[0:1]))
    cot = cotangent * token_mask.astype(bf16)[:, None]
    cot_group = lax.all_gather(cot, "mp", axis=0, tiled=True)

    wide = pltpu.VMEM((count, width), f32)
    saved = [shape_of(f32, count, width)] * 6
    *kept, mixed, back_part = local_call(
        mixer_forward,
        saved + [shape_of(bf16, count, width), shape_of(bf16, count, model)],
        [
            pltpu.VMEM((ROWS, model), bf16),
            wide,
            wide,
            pltpu.VMEM((ROWS + TAIL, width), f32),
            pltpu.VMEM((count, width), bf16),
        ],
        2 * count * (count * model + 3 * model * width),
        (norm_group, ocol, orow, pos_col, full_in, full_gate, full_out, chan, blocks_twice),
    )
    resid, norm_mid_group = line_call(
        sum_norm_gather, n_mp, 1, [own, tok], True, True, (inputs, gain_f[1:2], back_part)
    )

    hid = shape_of(bf16, count, hidden_width)
    ffn_part, d_norm_part, hidden, d_up, d_gate_ff = local_call(
        ffn,
        [tok, tok, hid, hid, hid],
        [],
        12 * count * model * hidden_width,
        (norm_mid_group, cot_group, full_up, full_gate_ff, full_down),
    )
    d_resid, gain_mid, back_group = line_call(
        sum_back_gather,
        n_mp,
        2,
        [own, shape_of(f32, 1, model), tok],
        True,
        True,
        (resid, cot, gain_f[1:2], d_norm_part),
    )
    output = (
        resid + lax.psum_scatter(ffn_part, "mp", scatter_dimension=0, tiled=True).astype(f32)
    ).astype(bf16)

    def reduced(grad, dimension):
        return lax.psum_scatter(grad.astype(bf16), "dp", scatter_dimension=dimension, tiled=True).astype(f32)

    grad_down = reduced(dot_first(hidden, cot_group), 1)
    grad_up = reduced(dot_first(norm_mid_group, d_up), 0)
    grad_gate_ff = reduced(dot_first(norm_mid_group, d_gate_ff), 0)

    d_cat, d_norm_back, small, d_blocks, gain_in = local_call(
        mixer_backward,
        [
            shape_of(bf16, count, 2 * width),
            tok,
            shape_of(f32, 8, width),
            shape_of(f32, heads, LANE, 2 * LANE),
            shape_of(f32, 1, model),
        ],
        [
            pltpu.VMEM((count, width), bf16),
            wide,
            wide,
            wide,
            pltpu.VMEM((count + TAIL, width), f32),
            pltpu.VMEM((ROWS + TAIL, width), f32),
            pltpu.VMEM((count, 2 * width), bf16),
        ],
        2 * count * (3 * count * width + 3 * model * width),
        (
            back_group,
            norm_group,
            ocol,
            orow,
            pos_col,
            gain_f[0:1],
            full_in,
            full_gate,
            full_out,
            chan,
            blocks,
            *kept,
        ),
    )
    (grad_inputs,) = line_call(
        sum_back,
        n_mp,
        3,
        [shape_of(bf16, local_rows, model)],
        True,
        False,
        (inputs, d_resid, gain_f[0:1], d_norm_back),
    )
    grad_out = reduced(dot_first(mixed, back_group), 1)
    grad_cat = dot_first(norm_group, d_cat)
    grad_in = reduced(grad_cat[:, :width], 0)
    grad_gate = reduced(grad_cat[:, width:], 0)

    d_blocks_rows = d_blocks.reshape(heads, n_dp, piece, 2, LANE).transpose(1, 3, 0, 2, 4)
    small_rows = small.reshape(8 * heads, n_dp, piece).transpose(1, 0, 2)
    packed_small = jnp.concatenate(
        [small_rows.reshape(n_dp, -1), d_blocks_rows.reshape(n_dp, -1)], axis=1
    )
    small_own = lax.psum_scatter(packed_small, "dp", scatter_dimension=0, tiled=True)[0]
    split_at = 8 * heads * piece
    rows = small_own[:split_at].reshape(8, heads, piece)
    grad_blocks = small_own[split_at:].reshape(2, heads, piece, LANE)

    grad_gains = lax.psum_scatter(
        jnp.concatenate([gain_in, gain_mid], axis=0), ("dp", "mp"), scatter_dimension=1, tiled=True
    )
    return (
        output,
        grad_inputs,
        grad_gains,
        grad_in,
        grad_gate,
        grad_out,
        rows[0:4],
        rows[4:7],
        rows[7],
        grad_blocks,
        grad_up,
        grad_gate_ff,
        grad_down,
    )


def solution(mesh):
    row, col = P("dp", "mp"), P("mp", "dp")
    tok = P(("dp", "mp"), None)
    chan = P(None, "mp", "dp")
    gate = P(None, "mp", "dp", None)
    return jax.shard_map(
        shards,
        mesh=mesh,
        in_specs=(
            tok, tok, P(("dp", "mp")), P("dp", None), P("dp", None), P(),
            row, row, col, chan, chan, col, gate, row, row, col,
        ),
        out_specs=(
            tok, tok, P(None, ("dp", "mp")), row, row, col, chan, chan, col, gate, row, row, col,
        ),
        check_vma=False,
    )
```

```python
import functools

import jax
import jax.numpy as jnp
from jax import lax
from jax.experimental import pallas as pl
from jax.experimental.pallas import tpu as pltpu
from jax.sharding import PartitionSpec as P

epsilon = 1e-06
LANE = 128
SUB = 8
TAIL = 24
ROWS = 272
VMEM_MB = 62
f32 = jnp.float32
bf16 = jnp.bfloat16
GELU_C = 0.7978845608028654
GELU_A = 0.044715


def rms_scale(values):
    return lax.rsqrt(jnp.mean(values * values, axis=-1, keepdims=True) + epsilon)


def dot(left, right):
    return lax.dot_general(left, right, (((1,), (0,)), ((), ())), preferred_element_type=f32)


def dot_last(left, right):
    return lax.dot_general(left, right, (((1,), (1,)), ((), ())), preferred_element_type=f32)


def dot_first(left, right):
    return lax.dot_general(left, right, (((0,), (0,)), ((), ())), preferred_element_type=f32)


def gelu_of(v):
    return 0.5 * v * (1.0 + jnp.tanh(GELU_C * (v + GELU_A * v * v * v)))


def gelu_both(v):
    square = v * v
    th = jnp.tanh(GELU_C * (v + GELU_A * v * square))
    half = 0.5 * (1.0 + th)
    slope = half + 0.5 * v * (1.0 - th * th) * (GELU_C * (1.0 + 3.0 * GELU_A * square))
    return v * half, slope


def sigmoid(v):
    return 0.5 * jnp.tanh(0.5 * v) + 0.5


def split(values):
    high = values.astype(bf16)
    return high, (values - high.astype(f32)).astype(bf16)


def rows_of(index, rows):
    return pl.ds(pl.multiple_of(index * rows, rows), rows)


def pick_rows(order_col, count):
    places = lax.broadcasted_iota(jnp.int32, (order_col.shape[0], count), 1)
    return (places == order_col).astype(f32).astype(bf16)


def put_rows(order_row, first, rows):
    places = lax.broadcasted_iota(jnp.int32, (rows, order_row.shape[1]), 0) + first
    return (places == order_row).astype(f32).astype(bf16)


def mixer_forward(
    tokens,
    ocol,
    orow,
    pos,
    w_in,
    w_gate,
    w_out,
    chan,
    blocks,
    gate_ref,
    branch_ref,
    conv_ref,
    gin_ref,
    grec_ref,
    state_ref,
    mixed_ref,
    out_ref,
    packed,
    rate,
    prod,
    before,
    low,
):
    count, _ = tokens.shape
    width = w_in.shape[1]
    steps = count // SUB
    heads = width // LANE

    def project(b, carry):
        at = rows_of(b, ROWS)
        packed[...] = dot(pick_rows(ocol[at, :], count), tokens[...]).astype(bf16)
        branch_ref[at, :] = dot(packed[...], w_in[...])
        gate_ref[at, :] = dot(packed[...], w_gate[...])
        return carry

    lax.fori_loop(0, count // ROWS, project, 0)

    for k in range(TAIL // SUB):
        last = branch_ref[pl.ds(count - TAIL + k * SUB, SUB), :]
        before[pl.ds(k * SUB, SUB), :] = pltpu.roll(last, 1, 0)
    before[pl.ds(TAIL, ROWS), :] = branch_ref[pl.ds(0, ROWS), :]

    def gates(b, carry):
        at = rows_of(b, ROWS)

        @pl.when(b > 0)
        def _():
            before[...] = branch_ref[pl.ds(pl.multiple_of(b * ROWS - TAIL, SUB), ROWS + TAIL), :]

        place = pos[at, :]
        for h in range(heads):
            lanes = pl.ds(h * LANE, LANE)
            par = chan[:, lanes]
            conv = par[4:5] + par[0:1] * before[pl.ds(TAIL, ROWS), lanes]
            for k in range(1, 4):
                earlier = before[pl.ds(TAIL - SUB * k, ROWS), lanes]
                conv = conv + par[k : k + 1] * jnp.where(place >= k, earlier, 0.0)
            high, rest = split(conv)
            pair = jnp.concatenate([blocks[h], blocks[heads + h]], axis=1)
            pre = dot(
                jnp.concatenate([high, rest], axis=1), jnp.concatenate([pair, pair], axis=0)
            )
            gate_in = sigmoid(pre[:, :LANE] + par[5:6])
            gate_rec = sigmoid(pre[:, LANE:] + par[6:7])
            kept = jnp.exp(-8.0 * gate_rec * par[7:8])
            drive = jnp.sqrt(1.0 - kept * kept + 0.01) * gate_in * conv
            conv_ref[at, lanes] = conv
            gin_ref[at, lanes] = gate_in
            grec_ref[at, lanes] = gate_rec
            rate[at, lanes] = jnp.where(place >= 1, kept, 0.0)
            state_ref[at, lanes] = drive
        return carry

    lax.fori_loop(0, count // ROWS, gates, 0)

    def scan(i, carry):
        held, passed = carry
        at = rows_of(i, SUB)
        a = rate[at, :]
        held = a * held + state_ref[at, :]
        passed = a * passed
        state_ref[at, :] = held
        prod[at, :] = passed
        return held, passed

    ends = lax.fori_loop(
        0, steps, scan, (jnp.zeros((SUB, width), f32), jnp.ones((SUB, width), f32)), unroll=8
    )
    first = lax.broadcasted_iota(jnp.int32, (SUB, width), 0) == 0
    carry_in = jnp.zeros((SUB, width), f32)
    for _ in range(SUB - 1):
        carry_in = jnp.where(first, 0.0, pltpu.roll(ends[0] + ends[1] * carry_in, 1, 0))

    def finish(i, carry):
        at = rows_of(i, 2 * SUB)
        twice = jnp.concatenate([carry_in, carry_in], axis=0)
        value = state_ref[at, :] + prod[at, :] * twice
        state_ref[at, :] = value
        low[at, :] = (gelu_of(gate_ref[at, :]) * value).astype(bf16)
        return carry

    lax.fori_loop(0, steps // 2, finish, 0, unroll=2)

    def leave(b, carry):
        at = rows_of(b, ROWS)
        mixed = dot(put_rows(orow[...], b * ROWS, ROWS), low[...]).astype(bf16)
        mixed_ref[at, :] = mixed
        out_ref[at, :] = dot_last(mixed, w_out[...]).astype(bf16)
        return carry

    lax.fori_loop(0, count // ROWS, leave, 0)


def ffn(
    tokens, cot, w_up, w_gate, w_down, part_ref, dnorm_ref, hidden_ref, dup_ref, dgate_ref
):
    def block(b, carry):
        at = rows_of(b, ROWS)
        up = dot(tokens[at, :], w_up[...])
        value, slope = gelu_both(dot(tokens[at, :], w_gate[...]))
        hidden = (value * up).astype(bf16)
        hidden_ref[at, :] = hidden
        d_hidden = dot(cot[at, :], w_down[...])
        d_up = (d_hidden * value).astype(bf16)
        d_gate = (d_hidden * up * slope).astype(bf16)
        dup_ref[at, :] = d_up
        dgate_ref[at, :] = d_gate
        dnorm_ref[at, :] = (dot_last(d_up, w_up[...]) + dot_last(d_gate, w_gate[...])).astype(bf16)
        part_ref[at, :] = dot_last(hidden, w_down[...]).astype(bf16)
        return carry

    lax.fori_loop(0, tokens.shape[0] // ROWS, block, 0)


def mixer_backward(
    back,
    norm,
    ocol,
    orow,
    pos,
    gain,
    w_in,
    w_gate,
    w_out,
    chan,
    blocks,
    gate_ref,
    branch_ref,
    conv_ref,
    gin_ref,
    grec_ref,
    state_ref,
    dcat_ref,
    dnorm_ref,
    small_ref,
    dblocks_ref,
    dgain_ref,
    dmix_arr,
    dmix,
    adj,
    prod,
    after,
    before,
    low,
):
    count, _ = back.shape
    width = w_in.shape[1]
    steps = count // SUB
    heads = width // LANE
    blocks_of = count // ROWS

    def enter(b, carry):
        at = rows_of(b, ROWS)
        dmix_arr[at, :] = dot(back[at, :], w_out[...]).astype(bf16)
        return carry

    lax.fori_loop(0, blocks_of, enter, 0)

    def pack(b, carry):
        at = rows_of(b, ROWS)
        d_mixed = dot(pick_rows(ocol[at, :], count), dmix_arr[...])
        value, slope = gelu_both(gate_ref[at, :])
        adj[at, :] = d_mixed * value
        low[at, pl.ds(width, width)] = (d_mixed * state_ref[at, :] * slope).astype(bf16)
        kept = jnp.exp(-8.0 * grec_ref[at, :] * chan[7:8, :])
        dmix[at, :] = jnp.where(pos[at, :] >= 1, kept, 0.0)
        return carry

    lax.fori_loop(0, blocks_of, pack, 0)

    def scan(i, carry):
        held, passed, following = carry
        at = rows_of(steps - 1 - i, SUB)
        held = following * held + adj[at, :]
        passed = following * passed
        adj[at, :] = held
        prod[at, :] = passed
        return held, passed, dmix[at, :]

    last = lax.broadcasted_iota(jnp.int32, (SUB, width), 0) == SUB - 1
    wrapped = jnp.where(last, 0.0, pltpu.roll(dmix[pl.ds(0, SUB), :], SUB - 1, 0))
    ends = lax.fori_loop(
        0,
        steps,
        scan,
        (jnp.zeros((SUB, width), f32), jnp.ones((SUB, width), f32), wrapped),
        unroll=8,
    )
    carry_in = jnp.zeros((SUB, width), f32)
    for _ in range(SUB - 1):
        carry_in = jnp.where(last, 0.0, pltpu.roll(ends[0] + ends[1] * carry_in, SUB - 1, 0))

    small_ref[...] = jnp.zeros_like(small_ref)
    dblocks_ref[...] = jnp.zeros_like(dblocks_ref)
    first = lax.broadcasted_iota(jnp.int32, (SUB, width), 0) == 0
    state_last = state_ref[pl.ds(count - SUB, SUB), :]
    before[pl.ds(TAIL - SUB, SUB), :] = jnp.where(first, 0.0, pltpu.roll(state_last, 1, 0))
    before[pl.ds(TAIL, ROWS), :] = state_ref[pl.ds(0, ROWS), :]
    wide_carry = jnp.concatenate([carry_in] * (ROWS // SUB), axis=0)

    def point(b, carry):
        at = rows_of(b, ROWS)

        @pl.when(b > 0)
        def _():
            before[...] = state_ref[pl.ds(pl.multiple_of(b * ROWS - TAIL, SUB), ROWS + TAIL), :]

        place = pos[at, :]
        for h in range(heads):
            lanes = pl.ds(h * LANE, LANE)
            par = chan[:, lanes]
            adjoint = adj[at, lanes] + prod[at, lanes] * wide_carry[:, h * LANE : (h + 1) * LANE]
            conv = conv_ref[at, lanes]
            gate_in = gin_ref[at, lanes]
            gate_rec = grec_ref[at, lanes]
            kept = jnp.exp(-8.0 * gate_rec * par[7:8])
            square = kept * kept
            inside = 1.0 - square + 0.01
            inverse = lax.rsqrt(inside)
            root = inside * inverse
            previous = before[pl.ds(TAIL - SUB, ROWS), lanes]
            d_log = adjoint * previous * dmix[at, lanes]
            scaled = adjoint * gate_in
            d_log = d_log - scaled * conv * square * inverse
            d_in = adjoint * root * conv * gate_in * (1.0 - gate_in)
            d_rec = d_log * (-8.0 * par[7:8]) * gate_rec * (1.0 - gate_rec)
            both = jnp.concatenate([d_in, d_rec], axis=1)
            high, rest = split(both)
            pair = jnp.concatenate([blocks[h], blocks[heads + h]], axis=1)
            d_conv = scaled * root + dot_last(high, pair) + dot_last(rest, pair)
            dblocks_ref[h] += dot_first(conv.astype(bf16), high)
            after[at, lanes] = d_conv
            small_ref[4:5, lanes] += jnp.sum(d_conv, axis=0, keepdims=True)
            small_ref[5:6, lanes] += jnp.sum(d_in, axis=0, keepdims=True)
            small_ref[6:7, lanes] += jnp.sum(d_rec, axis=0, keepdims=True)
            small_ref[7:8, lanes] += (
                jnp.sum(d_log * gate_rec, axis=0, keepdims=True) * (-8.0) * par[8:9]
            )
        return carry

    lax.fori_loop(0, blocks_of, point, 0)

    for k in range(TAIL // SUB):
        head = after[pl.ds(k * SUB, SUB), :]
        after[pl.ds(count + k * SUB, SUB), :] = pltpu.roll(head, SUB - 1, 0)
        tail = branch_ref[pl.ds(count - TAIL + k * SUB, SUB), :]
        before[pl.ds(k * SUB, SUB), :] = pltpu.roll(tail, 1, 0)
    before[pl.ds(TAIL, ROWS), :] = branch_ref[pl.ds(0, ROWS), :]

    def unmix(b, carry):
        at = rows_of(b, ROWS)

        @pl.when(b > 0)
        def _():
            before[...] = branch_ref[pl.ds(pl.multiple_of(b * ROWS - TAIL, SUB), ROWS + TAIL), :]

        place = pos[at, :]
        for h in range(heads):
            lanes = pl.ds(h * LANE, LANE)
            par = chan[:, lanes]
            d_conv = after[at, lanes]
            d_branch = par[0:1] * d_conv
            small_ref[0:1, lanes] += jnp.sum(
                d_conv * before[pl.ds(TAIL, ROWS), lanes], axis=0, keepdims=True
            )
            for k in range(1, 4):
                later = pl.ds(pl.multiple_of(b * ROWS + SUB * k, SUB), ROWS)
                d_branch = d_branch + par[k : k + 1] * jnp.where(
                    pos[later, :] >= k, after[later, lanes], 0.0
                )
                earlier = before[pl.ds(TAIL - SUB * k, ROWS), lanes]
                small_ref[k : k + 1, lanes] += jnp.sum(
                    jnp.where(place >= k, d_conv * earlier, 0.0), axis=0, keepdims=True
                )
            low[at, lanes] = d_branch.astype(bf16)
        return carry

    lax.fori_loop(0, blocks_of, unmix, 0)
    dgain_ref[...] = jnp.zeros_like(dgain_ref)

    def leave(b, carry):
        at = rows_of(b, ROWS)
        cat = dot(put_rows(orow[...], b * ROWS, ROWS), low[...]).astype(bf16)
        dcat_ref[at, :] = cat
        d_norm = dot_last(cat[:, :width], w_in[...]) + dot_last(cat[:, width:], w_gate[...])
        dgain_ref[...] += jnp.sum(d_norm * norm[at, :].astype(f32), axis=0, keepdims=True)
        dnorm_ref[at, :] = d_norm.astype(bf16)
        return carry

    lax.fori_loop(0, blocks_of, leave, 0)
    dgain_ref[...] = dgain_ref[...] / gain[...]


MESH = pl.DeviceIdType.MESH
TILE = 16
PIECES = 4


def cut_rows(rows, parts):
    tiles = rows // TILE
    ends = [tiles * (k + 1) // parts for k in range(parts)]
    return [(TILE * a, TILE * (b - a)) for a, b in zip([0] + ends[:-1], ends)]


class Line:
    def __init__(self, n, local, part, arrived, whole, sums, alls):
        self.n, self.local, self.part, self.arrived, self.whole = n, local, part, arrived, whole
        self.sums, self.alls = sums, alls
        self.me = lax.axis_index("mp")
        self.pieces = cut_rows(local, PIECES)
        self.has = (self.me > 0, self.me < n - 1)

    def greet(self, plane=None):
        barrier = pltpu.get_barrier_semaphore()
        more = 0
        if plane is not None:
            for bit in plane.bits:
                more += 1
                pl.semaphore_signal(
                    barrier, inc=1, device_id={"dp": plane.other(bit)}, device_id_type=MESH
                )
        for has, other in zip(self.has, (self.me - 1, self.me + 1)):

            @pl.when(has)
            def _():
                pl.semaphore_signal(barrier, inc=1, device_id={"mp": other}, device_id_type=MESH)

        both = self.has[0] & self.has[1]

        @pl.when(both)
        def _():
            pl.semaphore_wait(barrier, more + 2)

        @pl.when(jnp.logical_not(both))
        def _():
            pl.semaphore_wait(barrier, more + 1)

    def rows_at(self, owner, k):
        first, rows = self.pieces[k]
        return pl.ds(pl.multiple_of(owner * self.local + first, TILE), rows)

    def copy(self, source, target, sems, way, owner, k):
        return pltpu.make_async_remote_copy(
            src_ref=source,
            dst_ref=target,
            send_sem=sems[0].at[way, owner, k],
            recv_sem=sems[1].at[way, owner, k],
            device_id={"mp": self.me + 1 - 2 * way},
            device_id_type=MESH,
        )

    def sum_copy(self, way, owner, k, first=False):
        at = self.rows_at(owner, k)
        landed = self.arrived[way].at[at]
        return self.copy(self.part.at[at] if first else landed, landed, self.sums, way, owner, k)

    def all_copy(self, way, owner, k):
        block = self.whole.at[self.rows_at(owner, k)]
        return self.copy(block, block, self.alls, way, owner, k)

    def first(self, k):
        for away in range(self.n - 1):
            for way in range(2):
                owner = away if way else self.n - 1 - away

                @pl.when(jnp.logical_not(self.has[way]))
                def _():
                    self.sum_copy(way, owner, k, True).start()

    def relay(self, k, stage):
        for way in range(2):
            late = stage - (self.n - 1 - self.me if way else self.me)
            owner = late if way else self.n - 1 - late

            @pl.when(self.has[way] & (late >= 0))
            def _():
                self.sum_copy(way, owner, k).wait_recv()
                at = self.rows_at(owner, k)
                landed = self.arrived[way]
                landed[at, :] = (landed[at, :].astype(f32) + self.part[at, :].astype(f32)).astype(bf16)
                self.sum_copy(way, owner, k).start()

    def total(self, k, into):
        at = self.rows_at(self.me, k)
        rows = pl.ds(0, self.pieces[k][1])
        into[rows, :] = self.part[at, :].astype(f32)
        for way in range(2):

            @pl.when(self.has[way])
            def _():
                self.sum_copy(way, self.me, k).wait_recv()
                into[rows, :] += self.arrived[way][at, :].astype(f32)

    def spread(self, k):
        for way in range(2):

            @pl.when(self.has[1 - way])
            def _():
                self.all_copy(way, self.me, k).start()

    def forward(self, k, stage):
        for way in range(2):
            owner = self.me + stage if way else self.me - stage
            there = owner < self.n if way else owner >= 0

            @pl.when(there)
            def _():
                self.all_copy(way, owner, k).wait_recv()

            @pl.when(there & self.has[1 - way])
            def _():
                self.all_copy(way, owner, k).start()

    def finish(self):
        for k in range(PIECES):
            for owner in range(self.n):
                for way in range(2):
                    if self.part is not None:

                        @pl.when(self.me > owner if way else self.me < owner)
                        def _():
                            self.sum_copy(way, owner, k).wait_send()

                    if self.whole is not None:
                        reached = self.me <= owner if way else self.me >= owner

                        @pl.when(reached & self.has[1 - way])
                        def _():
                            self.all_copy(way, owner, k).wait_send()

    def run(self, point, tasks=()):
        tasks = iter(tasks)
        sums, alls = self.part is not None, self.whole is not None
        if sums:
            self.first(0)
        else:
            for k in range(PIECES):
                point(k)
                self.spread(k)
        for step in range(PIECES + (1 if alls and sums else 0)):
            gathered = step - 1 if sums else step
            if sums and alls and step > 0:
                self.spread(gathered)
            if sums and step + 1 < PIECES:
                self.first(step + 1)
            for stage in range(1, self.n):
                next(tasks, idle)()
                if alls and gathered >= 0:
                    self.forward(gathered, stage)
                if sums and step < PIECES and stage < self.n - 1:
                    self.relay(step, stage)
            if sums and step < PIECES:
                point(step)
        for task in tasks:
            task()
        self.finish()

    def tiles(self, k, body):
        first, rows = self.pieces[k]

        def one(i, carry):
            body(
                pl.ds(pl.multiple_of(i * TILE, TILE), TILE),
                pl.ds(pl.multiple_of(first + i * TILE, TILE), TILE),
                pl.ds(pl.multiple_of(self.me * self.local + first + i * TILE, TILE), TILE),
            )
            return carry

        lax.fori_loop(0, rows // TILE, one, 0)


def idle():
    pass


class Plane:
    bits = (1, 2, 4)
    orders = ((4, 2, 1), (2, 4, 1))

    def __init__(self):
        self.me = lax.axis_index("dp")

    def bit(self, bit):
        return lax.rem(self.me // bit, 2)

    def other(self, *bits):
        return self.me + sum(bit * (1 - 2 * self.bit(bit)) for bit in bits)

    def gather_copies(self, item, view, halves, stage, sems):
        copies = []
        for half in halves:
            order = self.orders[half]
            for combo in range(1 << stage):
                flipped = [bit for i, bit in enumerate(order[:stage]) if combo >> i & 1]
                block = view(self.other(*flipped), half)
                slot = (1 << stage) - 1 + combo
                copies.append(
                    pltpu.make_async_remote_copy(
                        src_ref=block,
                        dst_ref=block,
                        send_sem=sems[0].at[item, half, slot],
                        recv_sem=sems[1].at[item, half, slot],
                        device_id={"dp": self.other(order[stage])},
                        device_id_type=MESH,
                    )
                )
        return copies


class Reduce(Plane):
    def __init__(self, index, left, right, lanes, mine, theirs, got, second, third, out, sems):
        super().__init__()
        self.index, self.left, self.right, self.lanes = index, left, right, lanes
        self.mine, self.theirs, self.got = mine.at[index], theirs.at[index], got.at[index]
        self.second, self.third, self.out = second.at[index], third.at[index], out
        self.sems = sems
        self.rows = out.shape[0]
        self.half = self.rows // 2

    def copy(self, source, target, slot, bit):
        return pltpu.make_async_remote_copy(
            src_ref=source,
            dst_ref=target,
            send_sem=self.sems[0].at[self.index, slot],
            recv_sem=self.sems[1].at[self.index, slot],
            device_id={"dp": self.other(bit)},
            device_id_type=MESH,
        )

    def core_copy(self, t):
        return self.copy(self.theirs.at[t], self.got.at[t], t, 1)

    def second_copy(self, half, j):
        x, y = self.bit(2), self.bit(4)
        block = (1 - y) * 2 + j if half else j * 2 + 1 - x
        rows = self.mine.at[block, pl.ds(half * self.half, self.half)]
        return self.copy(rows, self.second.at[half, j], 4 + 2 * half + j, 4 if half else 2)

    def third_block(self, half):
        x, y = self.bit(2), self.bit(4)
        return y * 2 + 1 - x if half else (1 - y) * 2 + x

    def third_copy(self, half):
        rows = self.mine.at[self.third_block(half), pl.ds(half * self.half, self.half)]
        return self.copy(rows, self.third.at[half], 8 + half, 2 if half else 4)

    def product(self, t):
        def task():
            core = self.bit(1)
            pair = pl.ds(t * 2 * self.rows, 2 * self.rows)
            both = dot_first(self.left[:, pair], self.right[:, self.lanes])
            low, high = both[: self.rows], both[self.rows :]
            self.mine[t] = jnp.where(core == 0, low, high).astype(bf16)
            self.theirs[t] = jnp.where(core == 0, high, low).astype(bf16)
            self.core_copy(t).start()

        return task

    def add_core(self):
        for t in range(4):
            self.core_copy(t).wait_recv()
            self.mine[t] = (self.mine[t].astype(f32) + self.got[t].astype(f32)).astype(bf16)
        for half in range(2):
            for j in range(2):
                self.second_copy(half, j).start()

    def add_second(self):
        for half in range(2):
            for j in range(2):
                self.second_copy(half, j).wait_recv()
        for half in range(2):
            block, at = self.third_block(half), pl.ds(half * self.half, self.half)
            far = 1 - self.bit(2 if half else 4)
            self.mine[block, at] = (
                self.mine[block, at].astype(f32) + self.second[half, far].astype(f32)
            ).astype(bf16)
            self.third_copy(half).start()

    def add_third(self):
        own = self.bit(4) * 2 + self.bit(2)
        for half in range(2):
            self.third_copy(half).wait_recv()
            at = pl.ds(half * self.half, self.half)
            near = self.bit(2 if half else 4)
            self.out[at, :] = (
                self.mine[own, at].astype(f32)
                + self.second[half, near].astype(f32)
                + self.third[half].astype(f32)
            )

    def finish(self):
        for t in range(4):
            self.core_copy(t).wait_send()
        for half in range(2):
            for j in range(2):
                self.second_copy(half, j).wait_send()
            self.third_copy(half).wait_send()


def reduce_tasks(parts):
    tasks = [part.product(t) for part in parts for t in range(4)]

    def also(at, extra):
        while len(tasks) <= at:
            tasks.append(idle)
        before = tasks[at]

        def both():
            extra()
            before()

        tasks[at] = both

    for i, part in enumerate(parts):
        also(4 * i + 5, part.add_core)
        also(4 * i + 8, part.add_second)
        also(4 * i + 10, part.add_third)

    def finish():
        for part in parts:
            part.finish()

    return tasks + [finish]


def reduce_scratch(arrays, rows, width):
    block = pltpu.VMEM((arrays, 4, rows, width), bf16)
    sem = pltpu.SemaphoreType.DMA((arrays, 10))
    return [
        block,
        block,
        block,
        pltpu.VMEM((arrays, 2, 2, rows // 2, width), bf16),
        pltpu.VMEM((arrays, 2, rows // 2, width), bf16),
        sem,
        sem,
    ]


def gather_norm(n, x, gain, whole, send, recv):
    line = Line(n, x.shape[0], None, None, whole, None, (send, recv))
    line.greet()

    def point(k):
        def one(_, own, at):
            v = x[own, :].astype(f32)
            whole[at, :] = (v * rms_scale(v) * gain[...]).astype(bf16)

        line.tiles(k, one)

    line.run(point)


def gather_weights(
    n,
    x,
    gain,
    w_in,
    w_gate,
    w_out,
    blocks,
    chan,
    whole,
    all_in,
    all_gate,
    all_out,
    all_blocks,
    all_chan,
    send,
    recv,
    raw,
    plane_send,
    plane_recv,
):
    line = Line(n, x.shape[0], None, None, whole, None, (send, recv))
    plane = Plane()
    line.greet(plane)
    sems = plane_send, plane_recv
    rows, piece = w_in.shape[0], blocks.shape[1]
    lines = chan.shape[0]

    def view_of(array):
        def view(owner, half):
            first = owner * rows + half * (rows // 2)
            return array.at[pl.ds(pl.multiple_of(first, TILE), rows // 2)]

        return view

    def blocks_view(owner, half):
        return all_blocks.at[:, pl.ds(pl.multiple_of(owner * piece, TILE), piece)]

    def chan_view(owner, half):
        return raw.at[pl.ds(pl.multiple_of(owner * lines, TILE), lines)]

    items = [(view_of(array), (0, 1)) for array in (all_in, all_gate, all_out)]
    items += [(blocks_view, (0,)), (chan_view, (1,))]

    def copies(stage):
        return [
            copy
            for item, (view, halves) in enumerate(items)
            for copy in plane.gather_copies(item, view, halves, stage, sems)
        ]

    def stage_task(stage):
        def task():
            if stage:
                for copy in copies(stage - 1):
                    copy.wait_recv()
            for copy in copies(stage):
                copy.start()

        return task

    def last():
        for copy in copies(2):
            copy.wait_recv()
        lane = lax.broadcasted_iota(jnp.int32, (LANE, LANE), 1)
        row = lax.broadcasted_iota(jnp.int32, (LANE, LANE), 0)
        total = jnp.zeros((lines, LANE), f32)
        for owner in range(LANE // piece):
            moved = ((row < piece) & (row + owner * piece == lane)).astype(f32).astype(bf16)
            total = total + dot(raw[pl.ds(owner * lines, lines), :], moved)
        for h in range(lines // SUB):
            par = total[h * SUB : (h + 1) * SUB]
            lanes = pl.ds(h * LANE, LANE)
            all_chan[0:SUB, lanes] = par
            decay = par[SUB - 1 : SUB]
            small = jnp.exp(-jnp.abs(decay))
            one_more = 1.0 + small
            rest = jnp.where(one_more == 1.0, 1.0, one_more - 1.0)
            log_one_more = jnp.where(one_more == 1.0, small, jnp.log(one_more) * (small / rest))
            all_chan[SUB - 1 : SUB, lanes] = jnp.maximum(decay, 0.0) + log_one_more
            all_chan[SUB : 2 * SUB, lanes] = jnp.broadcast_to(sigmoid(decay), (SUB, LANE))
        for stage in range(3):
            for copy in copies(stage):
                copy.wait_send()

    own = pl.ds(pl.multiple_of(plane.me * rows, TILE), rows)
    all_in[own, :] = w_in[...]
    all_gate[own, :] = w_gate[...]
    all_out[own, :] = w_out[...]
    all_blocks[:, pl.ds(pl.multiple_of(plane.me * piece, TILE), piece), :] = blocks[...]
    raw[pl.ds(pl.multiple_of(plane.me * lines, TILE), lines), :] = chan[...]

    def point(k):
        def one(_, own, at):
            v = x[own, :].astype(f32)
            whole[at, :] = (v * rms_scale(v) * gain[...]).astype(bf16)

        line.tiles(k, one)

    tasks = [idle, stage_task(1), idle, idle, stage_task(2), idle, idle, last]
    stage_task(0)()
    line.run(point, tasks)


def sum_norm_gather(n, x, gain, part, resid, whole, left, right, total, ss, sr, send, recv):
    line = Line(n, x.shape[0], part, (left, right), whole, (ss, sr), (send, recv))
    line.greet()

    def point(k):
        line.total(k, total)

        def one(here, own, at):
            v = x[own, :].astype(f32) + total[here, :]
            resid[own, :] = v
            whole[at, :] = (v * rms_scale(v) * gain[...]).astype(bf16)

        line.tiles(k, one)

    line.run(point)


def norm_back(value, gain, grad):
    scale = rms_scale(value)
    e = gain * grad
    slope = scale * scale * scale * jnp.mean(value * e, axis=-1, keepdims=True)
    return scale * e - value * slope, grad * value * scale


def sum_back_gather(n, resid, cot, gain, part, *rest):
    if len(rest) > 10:
        norm, cots, d_up, d_gate, hidden, *rest = rest
        d_resid, gain_grad, whole, *outs = rest[:6]
        left, right, total, ss, sr, send, recv, *reduce = rest[6:]
        every = slice(None)
        sides = ((norm, d_up, every), (norm, d_gate, every), (cots, hidden, every))
    else:
        d_resid, gain_grad, whole, left, right, total, ss, sr, send, recv = rest
        sides = ()
    line = Line(n, resid.shape[0], part, (left, right), whole, (ss, sr), (send, recv))
    line.greet(Plane() if sides else None)
    gain_grad[...] = jnp.zeros_like(gain_grad)

    def point(k):
        line.total(k, total)

        def one(here, own, at):
            back, terms = norm_back(resid[own, :], gain[...], total[here, :])
            gain_grad[...] += jnp.sum(terms, axis=0, keepdims=True)
            value = cot[own, :].astype(f32) + back
            d_resid[own, :] = value
            whole[at, :] = value.astype(bf16)

        line.tiles(k, one)

    if sides:
        tasks = reduce_tasks(
            [
                Reduce(i, *side, *reduce[:5], out, reduce[5:])
                for i, (side, out) in enumerate(zip(sides, outs))
            ]
        )
        line.run(point, tasks)
    else:
        line.run(point)


def sum_back(n, x, d_resid, gain, part, *rest):
    if len(rest) > 6:
        norm, back_all, cat, mixed, *rest = rest
        grad_x, *outs = rest[:4]
        left, right, total, ss, sr, *reduce = rest[4:]
        width = mixed.shape[1]
        sides = (
            (norm, cat, slice(0, width)),
            (norm, cat, slice(width, 2 * width)),
            (back_all, mixed, slice(None)),
        )
    else:
        grad_x, left, right, total, ss, sr = rest
        sides = ()
    line = Line(n, x.shape[0], part, (left, right), None, (ss, sr), None)
    line.greet(Plane() if sides else None)

    def point(k):
        line.total(k, total)

        def one(here, own, at):
            back, _ = norm_back(x[own, :].astype(f32), gain[...], total[here, :])
            grad_x[own, :] = (d_resid[own, :] + back).astype(bf16)

        line.tiles(k, one)

    if sides:
        tasks = reduce_tasks(
            [
                Reduce(i, *side, *reduce[:5], out, reduce[5:])
                for i, (side, out) in enumerate(zip(sides, outs))
            ]
        )
        line.run(point, tasks)
    else:
        line.run(point)


def line_call(body, n, identity, outs, sums, alls, args, more=()):
    whole = pl.BlockSpec(memory_space=pltpu.VMEM)
    local, model = args[0].shape
    sem = pltpu.SemaphoreType.DMA((2, n, PIECES))
    scratch = []
    if sums:
        scratch += [pltpu.VMEM((n * local, model), bf16)] * 2
        scratch += [pltpu.VMEM((max(rows for _, rows in cut_rows(local, PIECES)), model), f32)]
        scratch += [sem, sem]
    if alls:
        scratch += [sem, sem]
    scratch += more
    moved = sum(a.size * a.dtype.itemsize for a in args)
    return pl.pallas_call(
        functools.partial(body, n),
        out_shape=outs,
        in_specs=[whole] * len(args),
        out_specs=[whole] * len(outs),
        scratch_shapes=scratch,
        compiler_params=pltpu.CompilerParams(
            vmem_limit_bytes=VMEM_MB << 20, collective_id=identity, has_side_effects=True
        ),
        cost_estimate=pl.CostEstimate(flops=0, bytes_accessed=100 * moved, transcendentals=0),
    )(*args)


def local_call(body, outs, scratch, flops, args):
    whole = pl.BlockSpec(memory_space=pltpu.VMEM)
    moved = sum(a.size * a.dtype.itemsize for a in args)
    moved += sum(o.size * o.dtype.itemsize for o in outs)
    return pl.pallas_call(
        body,
        out_shape=outs,
        in_specs=[whole] * len(args),
        out_specs=[whole] * len(outs),
        scratch_shapes=scratch,
        compiler_params=pltpu.CompilerParams(vmem_limit_bytes=VMEM_MB << 20),
        cost_estimate=pl.CostEstimate(flops=flops, bytes_accessed=moved, transcendentals=0),
    )(*args)


def shape_of(dtype, *shape):
    return jax.ShapeDtypeStruct(shape, dtype)


def shards(
    inputs,
    cotangent,
    token_mask,
    order,
    lengths,
    gains,
    w_in,
    w_gate,
    w_out,
    conv_weight,
    chan_bias,
    decay,
    gate_blocks,
    w_up,
    w_gate_ff,
    w_down,
):
    n_dp = lax.axis_size("dp")
    local_rows, model = inputs.shape
    count = local_rows * lax.axis_size("mp")
    heads, piece = decay.shape
    width = heads * piece * n_dp
    hidden_width = w_up.shape[1]

    fused = n_dp == 8
    rows = model // n_dp
    out_rows, down_rows = w_out.T, w_down.T
    full_up = lax.all_gather(w_up, "dp", axis=0, tiled=True)
    full_gate_ff = lax.all_gather(w_gate_ff, "dp", axis=0, tiled=True)
    full_down = lax.all_gather(down_rows, "dp", axis=0, tiled=True)
    lines = jnp.concatenate([conv_weight, chan_bias, decay[None]], axis=0).transpose(1, 0, 2)
    lines = lines.reshape(SUB * heads, piece)

    steps = count // SUB
    ends = jnp.cumsum(lengths[0], dtype=jnp.int32)
    starts = ends - lengths[0]
    places = jnp.arange(count, dtype=jnp.int32)
    own_start = jnp.max(
        jnp.where(places[:, None] >= starts[None, :], starts[None, :], 0), axis=1
    )
    pos = (places - own_start).reshape(SUB, steps).T
    wrap = jnp.concatenate([pos[: TAIL // SUB, 1:], jnp.full((TAIL // SUB, 1), -1, jnp.int32)], axis=1)
    pos_col = jnp.concatenate([pos, wrap], axis=0).reshape(count + TAIL, 1)
    order_int = order[0].reshape(SUB, steps).T.reshape(count)
    ocol, orow = order_int.reshape(count, 1), order_int.reshape(1, count)

    gain_f = gains.astype(f32)
    n_mp = lax.axis_size("mp")
    tok = shape_of(bf16, count, model)
    own = shape_of(f32, local_rows, model)
    if fused:
        grown = shape_of(bf16, model, width)
        norm_group, full_in, full_gate, full_out, blocks, chan = line_call(
            gather_weights,
            n_mp,
            0,
            [tok, grown, grown, grown, shape_of(bf16, 2 * heads, LANE, LANE), shape_of(f32, 16, width)],
            False,
            True,
            (
                inputs,
                gain_f[0:1],
                w_in,
                w_gate,
                out_rows,
                gate_blocks.reshape(2 * heads, piece, LANE),
                jnp.pad(lines, ((0, 0), (0, LANE - piece))),
            ),
            [pltpu.VMEM((n_dp * SUB * heads, LANE), bf16)] + [pltpu.SemaphoreType.DMA((5, 2, 7))] * 2,
        )
    else:
        (norm_group,) = line_call(gather_norm, n_mp, 0, [tok], False, True, (inputs, gain_f[0:1]))
        full_in = lax.all_gather(w_in, "dp", axis=0, tiled=True)
        full_gate = lax.all_gather(w_gate, "dp", axis=0, tiled=True)
        full_out = lax.all_gather(out_rows, "dp", axis=0, tiled=True)
        blocks = lax.all_gather(gate_blocks, "dp", axis=2, tiled=True).reshape(2 * heads, LANE, LANE)
        params = lax.all_gather(lines, "dp", axis=1, tiled=True).astype(f32)
        params = params.reshape(heads, SUB, LANE).transpose(1, 0, 2).reshape(SUB, width)
        decay_row = params[7:8]
        chan = jnp.concatenate(
            [params[:7], jax.nn.softplus(decay_row)] + [jax.nn.sigmoid(decay_row)] * SUB, axis=0
        )
    cot = cotangent * token_mask.astype(bf16)[:, None]
    cot_group = lax.all_gather(cot, "mp", axis=0, tiled=True)

    wide = pltpu.VMEM((count, width), f32)
    saved = [shape_of(f32, count, width)] * 6
    *kept, mixed, back_part = local_call(
        mixer_forward,
        saved + [shape_of(bf16, count, width), shape_of(bf16, count, model)],
        [
            pltpu.VMEM((ROWS, model), bf16),
            wide,
            wide,
            pltpu.VMEM((ROWS + TAIL, width), f32),
            pltpu.VMEM((count, width), bf16),
        ],
        2 * count * (count * model + 3 * model * width),
        (norm_group, ocol, orow, pos_col, full_in, full_gate, full_out, chan, blocks),
    )
    resid, norm_mid_group = line_call(
        sum_norm_gather, n_mp, 1, [own, tok], True, True, (inputs, gain_f[1:2], back_part)
    )

    hid = shape_of(bf16, count, hidden_width)
    ffn_part, d_norm_part, hidden, d_up, d_gate_ff = local_call(
        ffn,
        [tok, tok, hid, hid, hid],
        [],
        12 * count * model * hidden_width,
        (norm_mid_group, cot_group, full_up, full_gate_ff, full_down),
    )
    d_resid, gain_mid, back_group, *ffn_grads = line_call(
        sum_back_gather,
        n_mp,
        2,
        [own, shape_of(f32, 1, model), tok] + [shape_of(f32, rows, hidden_width)] * (3 * fused),
        True,
        True,
        (resid, cot, gain_f[1:2], d_norm_part)
        + ((norm_mid_group, cot_group, d_up, d_gate_ff, hidden) if fused else ()),
        reduce_scratch(3, rows, hidden_width) if fused else (),
    )
    output = (
        resid + lax.psum_scatter(ffn_part, "mp", scatter_dimension=0, tiled=True).astype(f32)
    ).astype(bf16)

    def reduced(left, right):
        grad = dot_first(left, right).astype(bf16)
        return lax.psum_scatter(grad, "dp", scatter_dimension=0, tiled=True).astype(f32)

    if not fused:
        ffn_grads = [
            reduced(norm_mid_group, d_up),
            reduced(norm_mid_group, d_gate_ff),
            reduced(cot_group, hidden),
        ]

    d_cat, d_norm_back, small, d_blocks, gain_in = local_call(
        mixer_backward,
        [
            shape_of(bf16, count, 2 * width),
            tok,
            shape_of(f32, 8, width),
            shape_of(f32, heads, LANE, 2 * LANE),
            shape_of(f32, 1, model),
        ],
        [
            pltpu.VMEM((count, width), bf16),
            wide,
            wide,
            wide,
            pltpu.VMEM((count + TAIL, width), f32),
            pltpu.VMEM((ROWS + TAIL, width), f32),
            pltpu.VMEM((count, 2 * width), bf16),
        ],
        2 * count * (3 * count * width + 3 * model * width),
        (
            back_group,
            norm_group,
            ocol,
            orow,
            pos_col,
            gain_f[0:1],
            full_in,
            full_gate,
            full_out,
            chan,
            blocks,
            *kept,
        ),
    )
    grad_inputs, *mix_grads = line_call(
        sum_back,
        n_mp,
        3,
        [shape_of(bf16, local_rows, model)] + [shape_of(f32, rows, width)] * (3 * fused),
        True,
        False,
        (inputs, d_resid, gain_f[0:1], d_norm_back)
        + ((norm_group, back_group, d_cat, mixed) if fused else ()),
        reduce_scratch(3, rows, width) if fused else (),
    )
    if not fused:
        mix_grads = [
            reduced(norm_group, d_cat[:, :width]),
            reduced(norm_group, d_cat[:, width:]),
            reduced(back_group, mixed),
        ]

    d_blocks_rows = d_blocks.reshape(heads, n_dp, piece, 2, LANE).transpose(1, 3, 0, 2, 4)
    small_rows = small.reshape(8 * heads, n_dp, piece).transpose(1, 0, 2)
    packed_small = jnp.concatenate(
        [small_rows.reshape(n_dp, -1), d_blocks_rows.reshape(n_dp, -1)], axis=1
    )
    pad = -packed_small.shape[1] % (SUB * LANE)
    packed_small = jnp.pad(packed_small, ((0, 0), (0, pad))).reshape(-1, LANE)
    small_own = lax.psum_scatter(packed_small, "dp", scatter_dimension=0, tiled=True).reshape(-1)
    split_at = 8 * heads * piece
    lines_own = small_own[:split_at].reshape(8, heads, piece)
    grad_blocks = small_own[split_at : split_at + gate_blocks.size].reshape(gate_blocks.shape)

    owners = n_dp * n_mp
    gain_parts = jnp.concatenate([gain_in, gain_mid], axis=0).reshape(2, owners, -1).transpose(1, 0, 2)
    gain_parts = jnp.pad(
        gain_parts.reshape(owners, -1), ((0, 0), (0, SUB * LANE - 2 * model // owners))
    ).reshape(-1, LANE)
    gain_own = lax.psum_scatter(gain_parts, ("dp", "mp"), scatter_dimension=0, tiled=True)
    grad_gains = gain_own.reshape(-1)[: 2 * model // owners].reshape(2, -1)
    return (
        output,
        grad_inputs,
        grad_gains,
        mix_grads[0],
        mix_grads[1],
        mix_grads[2].T,
        lines_own[0:4],
        lines_own[4:7],
        lines_own[7],
        grad_blocks,
        ffn_grads[0],
        ffn_grads[1],
        ffn_grads[2].T,
    )


def solution(mesh):
    row, col = P("dp", "mp"), P("mp", "dp")
    tok = P(("dp", "mp"), None)
    chan = P(None, "mp", "dp")
    gate = P(None, "mp", "dp", None)
    return jax.shard_map(
        shards,
        mesh=mesh,
        in_specs=(
            tok, tok, P(("dp", "mp")), P("dp", None), P("dp", None), P(),
            row, row, col, chan, chan, col, gate, row, row, col,
        ),
        out_specs=(
            tok, tok, P(None, ("dp", "mp")), row, row, col, chan, chan, col, gate, row, row, col,
        ),
        check_vma=False,
    )
```

```python
import functools

import jax
import jax.numpy as jnp
from jax import lax
from jax.experimental import pallas as pl
from jax.experimental.pallas import tpu as pltpu
from jax.sharding import PartitionSpec as P

epsilon = 1e-06
LANE = 128
SUB = 8
TAIL = 24
ROWS = 272
VMEM_MB = 62
f32 = jnp.float32
bf16 = jnp.bfloat16
GELU_C = 0.7978845608028654
GELU_A = 0.044715


def rms_scale(values):
    return lax.rsqrt(jnp.mean(values * values, axis=-1, keepdims=True) + epsilon)


def dot(left, right):
    return lax.dot_general(left, right, (((1,), (0,)), ((), ())), preferred_element_type=f32)


def dot_last(left, right):
    return lax.dot_general(left, right, (((1,), (1,)), ((), ())), preferred_element_type=f32)


def dot_first(left, right):
    return lax.dot_general(left, right, (((0,), (0,)), ((), ())), preferred_element_type=f32)


def gelu_of(v):
    return 0.5 * v * (1.0 + jnp.tanh(GELU_C * (v + GELU_A * v * v * v)))


def gelu_both(v):
    square = v * v
    th = jnp.tanh(GELU_C * (v + GELU_A * v * square))
    half = 0.5 * (1.0 + th)
    slope = half + 0.5 * v * (1.0 - th * th) * (GELU_C * (1.0 + 3.0 * GELU_A * square))
    return v * half, slope


def sigmoid(v):
    return 0.5 * jnp.tanh(0.5 * v) + 0.5


def split(values):
    high = values.astype(bf16)
    return high, (values - high.astype(f32)).astype(bf16)


def rows_of(index, rows):
    return pl.ds(pl.multiple_of(index * rows, rows), rows)


def pick_rows(order_col, count):
    places = lax.broadcasted_iota(jnp.int32, (order_col.shape[0], count), 1)
    return (places == order_col).astype(f32).astype(bf16)


def put_rows(order_row, first, rows):
    places = lax.broadcasted_iota(jnp.int32, (rows, order_row.shape[1]), 0) + first
    return (places == order_row).astype(f32).astype(bf16)


def mixer_forward(
    tokens,
    ocol,
    orow,
    pos,
    w_in,
    w_gate,
    w_out,
    chan,
    blocks,
    gate_ref,
    branch_ref,
    conv_ref,
    gin_ref,
    grec_ref,
    state_ref,
    mixed_ref,
    out_ref,
    packed,
    rate,
    prod,
    before,
    low,
):
    count, _ = tokens.shape
    width = w_in.shape[1]
    steps = count // SUB
    heads = width // LANE

    def project(b, carry):
        at = rows_of(b, ROWS)
        packed[...] = dot(pick_rows(ocol[at, :], count), tokens[...]).astype(bf16)
        branch_ref[at, :] = dot(packed[...], w_in[...])
        gate_ref[at, :] = dot(packed[...], w_gate[...])
        return carry

    lax.fori_loop(0, count // ROWS, project, 0)

    for k in range(TAIL // SUB):
        last = branch_ref[pl.ds(count - TAIL + k * SUB, SUB), :]
        before[pl.ds(k * SUB, SUB), :] = pltpu.roll(last, 1, 0)
    before[pl.ds(TAIL, ROWS), :] = branch_ref[pl.ds(0, ROWS), :]

    def gates(b, carry):
        at = rows_of(b, ROWS)

        @pl.when(b > 0)
        def _():
            before[...] = branch_ref[pl.ds(pl.multiple_of(b * ROWS - TAIL, SUB), ROWS + TAIL), :]

        place = pos[at, :]
        for h in range(heads):
            lanes = pl.ds(h * LANE, LANE)
            par = chan[:, lanes]
            conv = par[4:5] + par[0:1] * before[pl.ds(TAIL, ROWS), lanes]
            for k in range(1, 4):
                earlier = before[pl.ds(TAIL - SUB * k, ROWS), lanes]
                conv = conv + par[k : k + 1] * jnp.where(place >= k, earlier, 0.0)
            high, rest = split(conv)
            pair = jnp.concatenate([blocks[h], blocks[heads + h]], axis=1)
            pre = dot(
                jnp.concatenate([high, rest], axis=1), jnp.concatenate([pair, pair], axis=0)
            )
            gate_in = sigmoid(pre[:, :LANE] + par[5:6])
            gate_rec = sigmoid(pre[:, LANE:] + par[6:7])
            kept = jnp.exp(-8.0 * gate_rec * par[7:8])
            drive = jnp.sqrt(1.0 - kept * kept + 0.01) * gate_in * conv
            conv_ref[at, lanes] = conv
            gin_ref[at, lanes] = gate_in
            grec_ref[at, lanes] = gate_rec
            rate[at, lanes] = jnp.where(place >= 1, kept, 0.0)
            state_ref[at, lanes] = drive
        return carry

    lax.fori_loop(0, count // ROWS, gates, 0)

    def scan(i, carry):
        held, passed = carry
        at = rows_of(i, SUB)
        a = rate[at, :]
        held = a * held + state_ref[at, :]
        passed = a * passed
        state_ref[at, :] = held
        prod[at, :] = passed
        return held, passed

    ends = lax.fori_loop(
        0, steps, scan, (jnp.zeros((SUB, width), f32), jnp.ones((SUB, width), f32)), unroll=8
    )
    first = lax.broadcasted_iota(jnp.int32, (SUB, width), 0) == 0
    carry_in = jnp.zeros((SUB, width), f32)
    for _ in range(SUB - 1):
        carry_in = jnp.where(first, 0.0, pltpu.roll(ends[0] + ends[1] * carry_in, 1, 0))

    def finish(i, carry):
        at = rows_of(i, 2 * SUB)
        twice = jnp.concatenate([carry_in, carry_in], axis=0)
        value = state_ref[at, :] + prod[at, :] * twice
        state_ref[at, :] = value
        low[at, :] = (gelu_of(gate_ref[at, :]) * value).astype(bf16)
        return carry

    lax.fori_loop(0, steps // 2, finish, 0, unroll=2)

    def leave(b, carry):
        at = rows_of(b, ROWS)
        mixed = dot(put_rows(orow[...], b * ROWS, ROWS), low[...]).astype(bf16)
        mixed_ref[at, :] = mixed
        out_ref[at, :] = dot_last(mixed, w_out[...]).astype(bf16)
        return carry

    lax.fori_loop(0, count // ROWS, leave, 0)


def ffn(
    tokens, cot, w_up, w_gate, w_down, part_ref, dnorm_ref, hidden_ref, dup_ref, dgate_ref
):
    def block(b, carry):
        at = rows_of(b, ROWS)
        up = dot(tokens[at, :], w_up[...])
        value, slope = gelu_both(dot(tokens[at, :], w_gate[...]))
        hidden = (value * up).astype(bf16)
        hidden_ref[at, :] = hidden
        d_hidden = dot(cot[at, :], w_down[...])
        d_up = (d_hidden * value).astype(bf16)
        d_gate = (d_hidden * up * slope).astype(bf16)
        dup_ref[at, :] = d_up
        dgate_ref[at, :] = d_gate
        dnorm_ref[at, :] = (dot_last(d_up, w_up[...]) + dot_last(d_gate, w_gate[...])).astype(bf16)
        part_ref[at, :] = dot_last(hidden, w_down[...]).astype(bf16)
        return carry

    lax.fori_loop(0, tokens.shape[0] // ROWS, block, 0)


def mixer_backward(
    back,
    norm,
    ocol,
    orow,
    pos,
    gain,
    w_in,
    w_gate,
    w_out,
    chan,
    blocks,
    gate_ref,
    branch_ref,
    conv_ref,
    gin_ref,
    grec_ref,
    state_ref,
    dcat_ref,
    dnorm_ref,
    little_ref,
    dgain_ref,
    dmix_arr,
    dmix,
    adj,
    prod,
    after,
    before,
    low,
    small_ref,
    dblocks_ref,
):
    count, _ = back.shape
    width = w_in.shape[1]
    steps = count // SUB
    heads = width // LANE
    blocks_of = count // ROWS

    def enter(b, carry):
        at = rows_of(b, ROWS)
        dmix_arr[at, :] = dot(back[at, :], w_out[...]).astype(bf16)
        return carry

    lax.fori_loop(0, blocks_of, enter, 0)

    def pack(b, carry):
        at = rows_of(b, ROWS)
        d_mixed = dot(pick_rows(ocol[at, :], count), dmix_arr[...])
        value, slope = gelu_both(gate_ref[at, :])
        adj[at, :] = d_mixed * value
        low[at, pl.ds(width, width)] = (d_mixed * state_ref[at, :] * slope).astype(bf16)
        kept = jnp.exp(-8.0 * grec_ref[at, :] * chan[7:8, :])
        dmix[at, :] = jnp.where(pos[at, :] >= 1, kept, 0.0)
        return carry

    lax.fori_loop(0, blocks_of, pack, 0)

    def scan(i, carry):
        held, passed, following = carry
        at = rows_of(steps - 1 - i, SUB)
        held = following * held + adj[at, :]
        passed = following * passed
        adj[at, :] = held
        prod[at, :] = passed
        return held, passed, dmix[at, :]

    last = lax.broadcasted_iota(jnp.int32, (SUB, width), 0) == SUB - 1
    wrapped = jnp.where(last, 0.0, pltpu.roll(dmix[pl.ds(0, SUB), :], SUB - 1, 0))
    ends = lax.fori_loop(
        0,
        steps,
        scan,
        (jnp.zeros((SUB, width), f32), jnp.ones((SUB, width), f32), wrapped),
        unroll=8,
    )
    carry_in = jnp.zeros((SUB, width), f32)
    for _ in range(SUB - 1):
        carry_in = jnp.where(last, 0.0, pltpu.roll(ends[0] + ends[1] * carry_in, SUB - 1, 0))

    small_ref[...] = jnp.zeros_like(small_ref)
    dblocks_ref[...] = jnp.zeros_like(dblocks_ref)
    first = lax.broadcasted_iota(jnp.int32, (SUB, width), 0) == 0
    state_last = state_ref[pl.ds(count - SUB, SUB), :]
    before[pl.ds(TAIL - SUB, SUB), :] = jnp.where(first, 0.0, pltpu.roll(state_last, 1, 0))
    before[pl.ds(TAIL, ROWS), :] = state_ref[pl.ds(0, ROWS), :]
    wide_carry = jnp.concatenate([carry_in] * (ROWS // SUB), axis=0)

    def point(b, carry):
        at = rows_of(b, ROWS)

        @pl.when(b > 0)
        def _():
            before[...] = state_ref[pl.ds(pl.multiple_of(b * ROWS - TAIL, SUB), ROWS + TAIL), :]

        place = pos[at, :]
        for h in range(heads):
            lanes = pl.ds(h * LANE, LANE)
            par = chan[:, lanes]
            adjoint = adj[at, lanes] + prod[at, lanes] * wide_carry[:, h * LANE : (h + 1) * LANE]
            conv = conv_ref[at, lanes]
            gate_in = gin_ref[at, lanes]
            gate_rec = grec_ref[at, lanes]
            kept = jnp.exp(-8.0 * gate_rec * par[7:8])
            square = kept * kept
            inside = 1.0 - square + 0.01
            inverse = lax.rsqrt(inside)
            root = inside * inverse
            previous = before[pl.ds(TAIL - SUB, ROWS), lanes]
            d_log = adjoint * previous * dmix[at, lanes]
            scaled = adjoint * gate_in
            d_log = d_log - scaled * conv * square * inverse
            d_in = adjoint * root * conv * gate_in * (1.0 - gate_in)
            d_rec = d_log * (-8.0 * par[7:8]) * gate_rec * (1.0 - gate_rec)
            both = jnp.concatenate([d_in, d_rec], axis=1)
            high, rest = split(both)
            pair = jnp.concatenate([blocks[h], blocks[heads + h]], axis=1)
            d_conv = scaled * root + dot_last(high, pair) + dot_last(rest, pair)
            dblocks_ref[h] += dot_first(conv.astype(bf16), high)
            after[at, lanes] = d_conv
            small_ref[4:5, lanes] += jnp.sum(d_conv, axis=0, keepdims=True)
            small_ref[5:6, lanes] += jnp.sum(d_in, axis=0, keepdims=True)
            small_ref[6:7, lanes] += jnp.sum(d_rec, axis=0, keepdims=True)
            small_ref[7:8, lanes] += (
                jnp.sum(d_log * gate_rec, axis=0, keepdims=True) * (-8.0) * par[8:9]
            )
        return carry

    lax.fori_loop(0, blocks_of, point, 0)

    for k in range(TAIL // SUB):
        head = after[pl.ds(k * SUB, SUB), :]
        after[pl.ds(count + k * SUB, SUB), :] = pltpu.roll(head, SUB - 1, 0)
        tail = branch_ref[pl.ds(count - TAIL + k * SUB, SUB), :]
        before[pl.ds(k * SUB, SUB), :] = pltpu.roll(tail, 1, 0)
    before[pl.ds(TAIL, ROWS), :] = branch_ref[pl.ds(0, ROWS), :]

    def unmix(b, carry):
        at = rows_of(b, ROWS)

        @pl.when(b > 0)
        def _():
            before[...] = branch_ref[pl.ds(pl.multiple_of(b * ROWS - TAIL, SUB), ROWS + TAIL), :]

        place = pos[at, :]
        for h in range(heads):
            lanes = pl.ds(h * LANE, LANE)
            par = chan[:, lanes]
            d_conv = after[at, lanes]
            d_branch = par[0:1] * d_conv
            small_ref[0:1, lanes] += jnp.sum(
                d_conv * before[pl.ds(TAIL, ROWS), lanes], axis=0, keepdims=True
            )
            for k in range(1, 4):
                later = pl.ds(pl.multiple_of(b * ROWS + SUB * k, SUB), ROWS)
                d_branch = d_branch + par[k : k + 1] * jnp.where(
                    pos[later, :] >= k, after[later, lanes], 0.0
                )
                earlier = before[pl.ds(TAIL - SUB * k, ROWS), lanes]
                small_ref[k : k + 1, lanes] += jnp.sum(
                    jnp.where(place >= k, d_conv * earlier, 0.0), axis=0, keepdims=True
                )
            low[at, lanes] = d_branch.astype(bf16)
        return carry

    lax.fori_loop(0, blocks_of, unmix, 0)
    lines = [small_ref[0:SUB, h * LANE : (h + 1) * LANE] for h in range(heads)]
    lines.append(jnp.zeros((LANE - SUB * heads, LANE), f32))
    little_ref[:, pl.ds(2 * width, LANE)] = jnp.concatenate(lines, axis=0).T
    for h in range(heads):
        little_ref[:, pl.ds(2 * h * LANE, 2 * LANE)] = dblocks_ref[h]
    dgain_ref[...] = jnp.zeros_like(dgain_ref)

    def leave(b, carry):
        at = rows_of(b, ROWS)
        cat = dot(put_rows(orow[...], b * ROWS, ROWS), low[...]).astype(bf16)
        dcat_ref[at, :] = cat
        d_norm = dot_last(cat[:, :width], w_in[...]) + dot_last(cat[:, width:], w_gate[...])
        dgain_ref[...] += jnp.sum(d_norm * norm[at, :].astype(f32), axis=0, keepdims=True)
        dnorm_ref[at, :] = d_norm.astype(bf16)
        return carry

    lax.fori_loop(0, blocks_of, leave, 0)
    dgain_ref[...] = dgain_ref[...] / gain[...]


MESH = pl.DeviceIdType.MESH
TILE = 16
PIECES = 4


def cut_rows(rows, parts):
    tiles = rows // TILE
    ends = [tiles * (k + 1) // parts for k in range(parts)]
    return [(TILE * a, TILE * (b - a)) for a, b in zip([0] + ends[:-1], ends)]


class Line:
    def __init__(self, n, local, part, arrived, whole, sums, alls):
        self.n, self.local, self.part, self.arrived, self.whole = n, local, part, arrived, whole
        self.sums, self.alls = sums, alls
        self.me = lax.axis_index("mp")
        self.pieces = cut_rows(local, PIECES)
        self.has = (self.me > 0, self.me < n - 1)

    def greet(self, plane=None):
        barrier = pltpu.get_barrier_semaphore()
        more = 0
        if plane is not None:
            for bit in plane.bits:
                more += 1
                pl.semaphore_signal(
                    barrier, inc=1, device_id={"dp": plane.other(bit)}, device_id_type=MESH
                )
        for has, other in zip(self.has, (self.me - 1, self.me + 1)):

            @pl.when(has)
            def _():
                pl.semaphore_signal(barrier, inc=1, device_id={"mp": other}, device_id_type=MESH)

        both = self.has[0] & self.has[1]

        @pl.when(both)
        def _():
            pl.semaphore_wait(barrier, more + 2)

        @pl.when(jnp.logical_not(both))
        def _():
            pl.semaphore_wait(barrier, more + 1)

    def rows_at(self, owner, k):
        first, rows = self.pieces[k]
        return pl.ds(pl.multiple_of(owner * self.local + first, TILE), rows)

    def copy(self, source, target, sems, way, owner, k):
        return pltpu.make_async_remote_copy(
            src_ref=source,
            dst_ref=target,
            send_sem=sems[0].at[way, owner, k],
            recv_sem=sems[1].at[way, owner, k],
            device_id={"mp": self.me + 1 - 2 * way},
            device_id_type=MESH,
        )

    def sum_copy(self, way, owner, k, first=False):
        at = self.rows_at(owner, k)
        landed = self.arrived[way].at[at]
        return self.copy(self.part.at[at] if first else landed, landed, self.sums, way, owner, k)

    def all_copy(self, way, owner, k):
        block = self.whole.at[self.rows_at(owner, k)]
        return self.copy(block, block, self.alls, way, owner, k)

    def first(self, k):
        for away in range(self.n - 1):
            for way in range(2):
                owner = away if way else self.n - 1 - away

                @pl.when(jnp.logical_not(self.has[way]))
                def _():
                    self.sum_copy(way, owner, k, True).start()

    def relay(self, k, stage):
        for way in range(2):
            late = stage - (self.n - 1 - self.me if way else self.me)
            owner = late if way else self.n - 1 - late

            @pl.when(self.has[way] & (late >= 0))
            def _():
                self.sum_copy(way, owner, k).wait_recv()
                at = self.rows_at(owner, k)
                landed = self.arrived[way]
                landed[at, :] = (landed[at, :].astype(f32) + self.part[at, :].astype(f32)).astype(bf16)
                self.sum_copy(way, owner, k).start()

    def total(self, k, into):
        at = self.rows_at(self.me, k)
        rows = pl.ds(0, self.pieces[k][1])
        into[rows, :] = self.part[at, :].astype(f32)
        for way in range(2):

            @pl.when(self.has[way])
            def _():
                self.sum_copy(way, self.me, k).wait_recv()
                into[rows, :] += self.arrived[way][at, :].astype(f32)

    def spread(self, k):
        for way in range(2):

            @pl.when(self.has[1 - way])
            def _():
                self.all_copy(way, self.me, k).start()

    def forward(self, k, stage):
        for way in range(2):
            owner = self.me + stage if way else self.me - stage
            there = owner < self.n if way else owner >= 0

            @pl.when(there)
            def _():
                self.all_copy(way, owner, k).wait_recv()

            @pl.when(there & self.has[1 - way])
            def _():
                self.all_copy(way, owner, k).start()

    def finish(self):
        for k in range(PIECES):
            for owner in range(self.n):
                for way in range(2):
                    if self.part is not None:

                        @pl.when(self.me > owner if way else self.me < owner)
                        def _():
                            self.sum_copy(way, owner, k).wait_send()

                    if self.whole is not None:
                        reached = self.me <= owner if way else self.me >= owner

                        @pl.when(reached & self.has[1 - way])
                        def _():
                            self.all_copy(way, owner, k).wait_send()

    def run(self, point, tasks=()):
        tasks = iter(tasks)
        sums, alls = self.part is not None, self.whole is not None
        if sums:
            self.first(0)
        else:
            for k in range(PIECES):
                point(k)
                self.spread(k)
        for step in range(PIECES + (1 if alls and sums else 0)):
            gathered = step - 1 if sums else step
            if sums and alls and step > 0:
                self.spread(gathered)
            if sums and step + 1 < PIECES:
                self.first(step + 1)
            for stage in range(1, self.n):
                next(tasks, idle)()
                if alls and gathered >= 0:
                    self.forward(gathered, stage)
                if sums and step < PIECES and stage < self.n - 1:
                    self.relay(step, stage)
            if sums and step < PIECES:
                point(step)
        for task in tasks:
            task()
        self.finish()

    def tiles(self, k, body):
        first, rows = self.pieces[k]

        def one(i, carry):
            body(
                pl.ds(pl.multiple_of(i * TILE, TILE), TILE),
                pl.ds(pl.multiple_of(first + i * TILE, TILE), TILE),
                pl.ds(pl.multiple_of(self.me * self.local + first + i * TILE, TILE), TILE),
            )
            return carry

        lax.fori_loop(0, rows // TILE, one, 0)


def idle():
    pass


class Plane:
    bits = (1, 2, 4)
    orders = ((4, 2, 1), (2, 4, 1))

    def __init__(self):
        self.me = lax.axis_index("dp")

    def bit(self, bit):
        return lax.rem(self.me // bit, 2)

    def other(self, *bits):
        return self.me + sum(bit * (1 - 2 * self.bit(bit)) for bit in bits)

    def gather_copies(self, item, view, halves, stage, sems):
        copies = []
        for half in halves:
            order = self.orders[half]
            for combo in range(1 << stage):
                flipped = [bit for i, bit in enumerate(order[:stage]) if combo >> i & 1]
                block = view(self.other(*flipped), half)
                slot = (1 << stage) - 1 + combo
                copies.append(
                    pltpu.make_async_remote_copy(
                        src_ref=block,
                        dst_ref=block,
                        send_sem=sems[0].at[item, half, slot],
                        recv_sem=sems[1].at[item, half, slot],
                        device_id={"dp": self.other(order[stage])},
                        device_id_type=MESH,
                    )
                )
        return copies


class Reduce(Plane):
    def __init__(self, index, left, right, lanes, mine, theirs, got, second, third, out, sems):
        super().__init__()
        self.index, self.left, self.right, self.lanes = index, left, right, lanes
        self.mine, self.theirs, self.got = mine.at[index], theirs.at[index], got.at[index]
        self.second, self.third, self.out = second.at[index], third.at[index], out
        self.sems = sems
        self.rows = out.shape[0]
        self.half = self.rows // 2

    def copy(self, source, target, slot, bit):
        return pltpu.make_async_remote_copy(
            src_ref=source,
            dst_ref=target,
            send_sem=self.sems[0].at[self.index, slot],
            recv_sem=self.sems[1].at[self.index, slot],
            device_id={"dp": self.other(bit)},
            device_id_type=MESH,
        )

    def core_copy(self, t):
        return self.copy(self.theirs.at[t], self.got.at[t], t, 1)

    def second_copy(self, half, j):
        x, y = self.bit(2), self.bit(4)
        block = (1 - y) * 2 + j if half else j * 2 + 1 - x
        rows = self.mine.at[block, pl.ds(half * self.half, self.half)]
        return self.copy(rows, self.second.at[half, j], 4 + 2 * half + j, 4 if half else 2)

    def third_block(self, half):
        x, y = self.bit(2), self.bit(4)
        return y * 2 + 1 - x if half else (1 - y) * 2 + x

    def third_copy(self, half):
        rows = self.mine.at[self.third_block(half), pl.ds(half * self.half, self.half)]
        return self.copy(rows, self.third.at[half], 8 + half, 2 if half else 4)

    def product(self, t):
        def task():
            core = self.bit(1)
            pair = pl.ds(t * 2 * self.rows, 2 * self.rows)
            both = dot_first(self.left[:, pair], self.right[:, self.lanes])
            low, high = both[: self.rows], both[self.rows :]
            self.mine[t] = jnp.where(core == 0, low, high).astype(bf16)
            self.theirs[t] = jnp.where(core == 0, high, low).astype(bf16)
            self.core_copy(t).start()

        return task

    def keep(self, t):
        return self.mine[t]

    def add_core(self):
        for t in range(4):
            self.core_copy(t).wait_recv()
            self.mine[t] = (self.keep(t).astype(f32) + self.got[t].astype(f32)).astype(self.mine.dtype)
        for half in range(2):
            for j in range(2):
                self.second_copy(half, j).start()

    def add_second(self):
        for half in range(2):
            for j in range(2):
                self.second_copy(half, j).wait_recv()
        for half in range(2):
            block, at = self.third_block(half), pl.ds(half * self.half, self.half)
            far = 1 - self.bit(2 if half else 4)
            self.mine[block, at] = (
                self.mine[block, at].astype(f32) + self.second[half, far].astype(f32)
            ).astype(self.mine.dtype)
            self.third_copy(half).start()

    def add_third(self):
        own = self.bit(4) * 2 + self.bit(2)
        for half in range(2):
            self.third_copy(half).wait_recv()
            at = pl.ds(half * self.half, self.half)
            near = self.bit(2 if half else 4)
            self.out[at, :] = (
                self.mine[own, at].astype(f32)
                + self.second[half, near].astype(f32)
                + self.third[half].astype(f32)
            )

    def finish(self):
        for t in range(4):
            self.core_copy(t).wait_send()
        for half in range(2):
            for j in range(2):
                self.second_copy(half, j).wait_send()
            self.third_copy(half).wait_send()


class Given(Reduce):
    def __init__(self, given, mine, got, second, third, out, sems):
        super().__init__(0, None, None, None, mine, mine, got, second, third, out, sems)
        self.given = given

    def rows_of(self, t, core):
        return pl.ds(pl.multiple_of((2 * t + core) * self.rows, self.rows), self.rows)

    def core_copy(self, t):
        return self.copy(self.given.at[self.rows_of(t, 1 - self.bit(1))], self.got.at[t], t, 1)

    def start(self):
        for t in range(4):
            self.core_copy(t).start()

    def keep(self, t):
        return self.given[self.rows_of(t, self.bit(1)), :]


def reduce_tasks(parts, given=None):
    tasks = [part.product(t) for part in parts for t in range(4)]

    def also(at, extra):
        while len(tasks) <= at:
            tasks.append(idle)
        before = tasks[at]

        def both():
            extra()
            before()

        tasks[at] = both

    for i, part in enumerate(parts):
        also(4 * i + 5, part.add_core)
        also(4 * i + 8, part.add_second)
        also(4 * i + 10, part.add_third)

    if given is not None:
        also(0, given.start)
        also(2, given.add_core)
        also(4, given.add_second)
        also(6, given.add_third)

    def finish():
        for part in parts + ([] if given is None else [given]):
            part.finish()

    return tasks + [finish]


def given_scratch(rows, width):
    sem = pltpu.SemaphoreType.DMA((1, 10))
    return [
        pltpu.VMEM((1, 4, rows, width), f32),
        pltpu.VMEM((1, 4, rows, width), f32),
        pltpu.VMEM((1, 2, 2, rows // 2, width), f32),
        pltpu.VMEM((1, 2, rows // 2, width), f32),
        sem,
        sem,
    ]


def reduce_scratch(arrays, rows, width):
    block = pltpu.VMEM((arrays, 4, rows, width), bf16)
    sem = pltpu.SemaphoreType.DMA((arrays, 10))
    return [
        block,
        block,
        block,
        pltpu.VMEM((arrays, 2, 2, rows // 2, width), bf16),
        pltpu.VMEM((arrays, 2, rows // 2, width), bf16),
        sem,
        sem,
    ]


def gather_norm(n, x, gain, whole, send, recv):
    line = Line(n, x.shape[0], None, None, whole, None, (send, recv))
    line.greet()

    def point(k):
        def one(_, own, at):
            v = x[own, :].astype(f32)
            whole[at, :] = (v * rms_scale(v) * gain[...]).astype(bf16)

        line.tiles(k, one)

    line.run(point)


def gather_weights(
    n,
    x,
    gain,
    w_in,
    w_gate,
    w_out,
    blocks,
    chan,
    whole,
    all_in,
    all_gate,
    all_out,
    all_blocks,
    all_chan,
    send,
    recv,
    raw,
    plane_send,
    plane_recv,
):
    line = Line(n, x.shape[0], None, None, whole, None, (send, recv))
    plane = Plane()
    line.greet(plane)
    sems = plane_send, plane_recv
    rows, piece = w_in.shape[0], blocks.shape[1]
    lines = chan.shape[0]

    def view_of(array):
        def view(owner, half):
            first = owner * rows + half * (rows // 2)
            return array.at[pl.ds(pl.multiple_of(first, TILE), rows // 2)]

        return view

    def blocks_view(owner, half):
        return all_blocks.at[:, pl.ds(pl.multiple_of(owner * piece, TILE), piece)]

    def chan_view(owner, half):
        return raw.at[pl.ds(pl.multiple_of(owner * lines, TILE), lines)]

    items = [(view_of(array), (0, 1)) for array in (all_in, all_gate, all_out)]
    items += [(blocks_view, (0,)), (chan_view, (1,))]

    def copies(stage):
        return [
            copy
            for item, (view, halves) in enumerate(items)
            for copy in plane.gather_copies(item, view, halves, stage, sems)
        ]

    def stage_task(stage):
        def task():
            if stage:
                for copy in copies(stage - 1):
                    copy.wait_recv()
            for copy in copies(stage):
                copy.start()

        return task

    def last():
        for copy in copies(2):
            copy.wait_recv()
        lane = lax.broadcasted_iota(jnp.int32, (LANE, LANE), 1)
        row = lax.broadcasted_iota(jnp.int32, (LANE, LANE), 0)
        total = jnp.zeros((lines, LANE), f32)
        for owner in range(LANE // piece):
            moved = ((row < piece) & (row + owner * piece == lane)).astype(f32).astype(bf16)
            total = total + dot(raw[pl.ds(owner * lines, lines), :], moved)
        for h in range(lines // SUB):
            par = total[h * SUB : (h + 1) * SUB]
            lanes = pl.ds(h * LANE, LANE)
            all_chan[0:SUB, lanes] = par
            decay = par[SUB - 1 : SUB]
            small = jnp.exp(-jnp.abs(decay))
            one_more = 1.0 + small
            rest = jnp.where(one_more == 1.0, 1.0, one_more - 1.0)
            log_one_more = jnp.where(one_more == 1.0, small, jnp.log(one_more) * (small / rest))
            all_chan[SUB - 1 : SUB, lanes] = jnp.maximum(decay, 0.0) + log_one_more
            all_chan[SUB : 2 * SUB, lanes] = jnp.broadcast_to(sigmoid(decay), (SUB, LANE))
        for stage in range(3):
            for copy in copies(stage):
                copy.wait_send()

    own = pl.ds(pl.multiple_of(plane.me * rows, TILE), rows)
    all_in[own, :] = w_in[...]
    all_gate[own, :] = w_gate[...]
    all_out[own, :] = w_out[...]
    all_blocks[:, pl.ds(pl.multiple_of(plane.me * piece, TILE), piece), :] = blocks[...]
    raw[pl.ds(pl.multiple_of(plane.me * lines, TILE), lines), :] = chan[...]

    def point(k):
        def one(_, own, at):
            v = x[own, :].astype(f32)
            whole[at, :] = (v * rms_scale(v) * gain[...]).astype(bf16)

        line.tiles(k, one)

    tasks = [idle, stage_task(1), idle, idle, stage_task(2), idle, idle, last]
    stage_task(0)()
    line.run(point, tasks)


def sum_norm_gather(n, x, gain, part, resid, whole, left, right, total, ss, sr, send, recv):
    line = Line(n, x.shape[0], part, (left, right), whole, (ss, sr), (send, recv))
    line.greet()

    def point(k):
        line.total(k, total)

        def one(here, own, at):
            v = x[own, :].astype(f32) + total[here, :]
            resid[own, :] = v
            whole[at, :] = (v * rms_scale(v) * gain[...]).astype(bf16)

        line.tiles(k, one)

    line.run(point)


def norm_back(value, gain, grad):
    scale = rms_scale(value)
    e = gain * grad
    slope = scale * scale * scale * jnp.mean(value * e, axis=-1, keepdims=True)
    return scale * e - value * slope, grad * value * scale


def sum_back_gather(n, resid, cot, gain, part, *rest):
    if len(rest) > 10:
        norm, cots, d_up, d_gate, hidden, *rest = rest
        d_resid, gain_grad, whole, *outs = rest[:6]
        left, right, total, ss, sr, send, recv, *reduce = rest[6:]
        every = slice(None)
        sides = ((norm, d_up, every), (norm, d_gate, every), (cots, hidden, every))
    else:
        d_resid, gain_grad, whole, left, right, total, ss, sr, send, recv = rest
        sides = ()
    line = Line(n, resid.shape[0], part, (left, right), whole, (ss, sr), (send, recv))
    line.greet(Plane() if sides else None)
    gain_grad[...] = jnp.zeros_like(gain_grad)

    def point(k):
        line.total(k, total)

        def one(here, own, at):
            back, terms = norm_back(resid[own, :], gain[...], total[here, :])
            gain_grad[...] += jnp.sum(terms, axis=0, keepdims=True)
            value = cot[own, :].astype(f32) + back
            d_resid[own, :] = value
            whole[at, :] = value.astype(bf16)

        line.tiles(k, one)

    if sides:
        tasks = reduce_tasks(
            [
                Reduce(i, *side, *reduce[:5], out, reduce[5:])
                for i, (side, out) in enumerate(zip(sides, outs))
            ]
        )
        line.run(point, tasks)
    else:
        line.run(point)


def sum_back(n, x, d_resid, gain, part, *rest):
    if len(rest) > 6:
        norm, back_all, cat, mixed, little, *rest = rest
        grad_x, *outs, little_out = rest[:5]
        left, right, total, ss, sr, *reduce = rest[5:]
        given = Given(little, *reduce[7:11], little_out, reduce[11:])
        width = mixed.shape[1]
        sides = (
            (norm, cat, slice(0, width)),
            (norm, cat, slice(width, 2 * width)),
            (back_all, mixed, slice(None)),
        )
    else:
        grad_x, left, right, total, ss, sr = rest
        sides = ()
    line = Line(n, x.shape[0], part, (left, right), None, (ss, sr), None)
    line.greet(Plane() if sides else None)

    def point(k):
        line.total(k, total)

        def one(here, own, at):
            back, _ = norm_back(x[own, :].astype(f32), gain[...], total[here, :])
            grad_x[own, :] = (d_resid[own, :] + back).astype(bf16)

        line.tiles(k, one)

    if sides:
        tasks = reduce_tasks(
            [
                Reduce(i, *side, *reduce[:5], out, reduce[5:7])
                for i, (side, out) in enumerate(zip(sides, outs))
            ],
            given,
        )
        line.run(point, tasks)
    else:
        line.run(point)


def line_call(body, n, identity, outs, sums, alls, args, more=()):
    whole = pl.BlockSpec(memory_space=pltpu.VMEM)
    local, model = args[0].shape
    sem = pltpu.SemaphoreType.DMA((2, n, PIECES))
    scratch = []
    if sums:
        scratch += [pltpu.VMEM((n * local, model), bf16)] * 2
        scratch += [pltpu.VMEM((max(rows for _, rows in cut_rows(local, PIECES)), model), f32)]
        scratch += [sem, sem]
    if alls:
        scratch += [sem, sem]
    scratch += more
    moved = sum(a.size * a.dtype.itemsize for a in args)
    return pl.pallas_call(
        functools.partial(body, n),
        out_shape=outs,
        in_specs=[whole] * len(args),
        out_specs=[whole] * len(outs),
        scratch_shapes=scratch,
        compiler_params=pltpu.CompilerParams(
            vmem_limit_bytes=VMEM_MB << 20, collective_id=identity, has_side_effects=True
        ),
        cost_estimate=pl.CostEstimate(flops=0, bytes_accessed=100 * moved, transcendentals=0),
    )(*args)


def local_call(body, outs, scratch, flops, args):
    whole = pl.BlockSpec(memory_space=pltpu.VMEM)
    moved = sum(a.size * a.dtype.itemsize for a in args)
    moved += sum(o.size * o.dtype.itemsize for o in outs)
    return pl.pallas_call(
        body,
        out_shape=outs,
        in_specs=[whole] * len(args),
        out_specs=[whole] * len(outs),
        scratch_shapes=scratch,
        compiler_params=pltpu.CompilerParams(vmem_limit_bytes=VMEM_MB << 20),
        cost_estimate=pl.CostEstimate(flops=flops, bytes_accessed=moved, transcendentals=0),
    )(*args)


def shape_of(dtype, *shape):
    return jax.ShapeDtypeStruct(shape, dtype)


def shards(
    inputs,
    cotangent,
    token_mask,
    order,
    lengths,
    gains,
    w_in,
    w_gate,
    w_out,
    conv_weight,
    chan_bias,
    decay,
    gate_blocks,
    w_up,
    w_gate_ff,
    w_down,
):
    n_dp = lax.axis_size("dp")
    local_rows, model = inputs.shape
    count = local_rows * lax.axis_size("mp")
    heads, piece = decay.shape
    width = heads * piece * n_dp
    hidden_width = w_up.shape[1]

    fused = n_dp == 8
    rows = model // n_dp
    out_rows, down_rows = w_out.T, w_down.T
    full_up = lax.all_gather(w_up, "dp", axis=0, tiled=True)
    full_gate_ff = lax.all_gather(w_gate_ff, "dp", axis=0, tiled=True)
    full_down = lax.all_gather(down_rows, "dp", axis=0, tiled=True)
    lines = jnp.concatenate([conv_weight, chan_bias, decay[None]], axis=0).transpose(1, 0, 2)
    lines = lines.reshape(SUB * heads, piece)

    steps = count // SUB
    ends = jnp.cumsum(lengths[0], dtype=jnp.int32)
    starts = ends - lengths[0]
    places = jnp.arange(count, dtype=jnp.int32)
    own_start = jnp.max(
        jnp.where(places[:, None] >= starts[None, :], starts[None, :], 0), axis=1
    )
    pos = (places - own_start).reshape(SUB, steps).T
    wrap = jnp.concatenate([pos[: TAIL // SUB, 1:], jnp.full((TAIL // SUB, 1), -1, jnp.int32)], axis=1)
    pos_col = jnp.concatenate([pos, wrap], axis=0).reshape(count + TAIL, 1)
    order_int = order[0].reshape(SUB, steps).T.reshape(count)
    ocol, orow = order_int.reshape(count, 1), order_int.reshape(1, count)

    gain_f = gains.astype(f32)
    n_mp = lax.axis_size("mp")
    tok = shape_of(bf16, count, model)
    own = shape_of(f32, local_rows, model)
    if fused:
        grown = shape_of(bf16, model, width)
        norm_group, full_in, full_gate, full_out, blocks, chan = line_call(
            gather_weights,
            n_mp,
            0,
            [tok, grown, grown, grown, shape_of(bf16, 2 * heads, LANE, LANE), shape_of(f32, 16, width)],
            False,
            True,
            (
                inputs,
                gain_f[0:1],
                w_in,
                w_gate,
                out_rows,
                gate_blocks.reshape(2 * heads, piece, LANE),
                jnp.pad(lines, ((0, 0), (0, LANE - piece))),
            ),
            [pltpu.VMEM((n_dp * SUB * heads, LANE), bf16)] + [pltpu.SemaphoreType.DMA((5, 2, 7))] * 2,
        )
    else:
        (norm_group,) = line_call(gather_norm, n_mp, 0, [tok], False, True, (inputs, gain_f[0:1]))
        full_in = lax.all_gather(w_in, "dp", axis=0, tiled=True)
        full_gate = lax.all_gather(w_gate, "dp", axis=0, tiled=True)
        full_out = lax.all_gather(out_rows, "dp", axis=0, tiled=True)
        blocks = lax.all_gather(gate_blocks, "dp", axis=2, tiled=True).reshape(2 * heads, LANE, LANE)
        params = lax.all_gather(lines, "dp", axis=1, tiled=True).astype(f32)
        params = params.reshape(heads, SUB, LANE).transpose(1, 0, 2).reshape(SUB, width)
        decay_row = params[7:8]
        chan = jnp.concatenate(
            [params[:7], jax.nn.softplus(decay_row)] + [jax.nn.sigmoid(decay_row)] * SUB, axis=0
        )
    cot = cotangent * token_mask.astype(bf16)[:, None]
    cot_late, norm_group = lax.optimization_barrier((cot, norm_group))
    cot_group = lax.all_gather(cot_late, "mp", axis=0, tiled=True)

    wide = pltpu.VMEM((count, width), f32)
    saved = [shape_of(f32, count, width)] * 6
    *kept, mixed, back_part = local_call(
        mixer_forward,
        saved + [shape_of(bf16, count, width), shape_of(bf16, count, model)],
        [
            pltpu.VMEM((ROWS, model), bf16),
            wide,
            wide,
            pltpu.VMEM((ROWS + TAIL, width), f32),
            pltpu.VMEM((count, width), bf16),
        ],
        2 * count * (count * model + 3 * model * width),
        (norm_group, ocol, orow, pos_col, full_in, full_gate, full_out, chan, blocks),
    )
    resid, norm_mid_group = line_call(
        sum_norm_gather, n_mp, 1, [own, tok], True, True, (inputs, gain_f[1:2], back_part)
    )

    hid = shape_of(bf16, count, hidden_width)
    ffn_part, d_norm_part, hidden, d_up, d_gate_ff = local_call(
        ffn,
        [tok, tok, hid, hid, hid],
        [],
        12 * count * model * hidden_width,
        (norm_mid_group, cot_group, full_up, full_gate_ff, full_down),
    )
    d_resid, gain_mid, back_group, *ffn_grads = line_call(
        sum_back_gather,
        n_mp,
        2,
        [own, shape_of(f32, 1, model), tok] + [shape_of(f32, rows, hidden_width)] * (3 * fused),
        True,
        True,
        (resid, cot, gain_f[1:2], d_norm_part)
        + ((norm_mid_group, cot_group, d_up, d_gate_ff, hidden) if fused else ()),
        reduce_scratch(3, rows, hidden_width) if fused else (),
    )
    def reduced(left, right):
        grad = dot_first(left, right).astype(bf16)
        return lax.psum_scatter(grad, "dp", scatter_dimension=0, tiled=True).astype(f32)

    if not fused:
        ffn_grads = [
            reduced(norm_mid_group, d_up),
            reduced(norm_mid_group, d_gate_ff),
            reduced(cot_group, hidden),
        ]

    d_cat, d_norm_back, little, gain_in = local_call(
        mixer_backward,
        [
            shape_of(bf16, count, 2 * width),
            tok,
            shape_of(f32, LANE, 2 * width + LANE),
            shape_of(f32, 1, model),
        ],
        [
            pltpu.VMEM((count, width), bf16),
            wide,
            wide,
            wide,
            pltpu.VMEM((count + TAIL, width), f32),
            pltpu.VMEM((ROWS + TAIL, width), f32),
            pltpu.VMEM((count, 2 * width), bf16),
            pltpu.VMEM((SUB, width), f32),
            pltpu.VMEM((heads, LANE, 2 * LANE), f32),
        ],
        2 * count * (3 * count * width + 3 * model * width),
        (
            back_group,
            norm_group,
            ocol,
            orow,
            pos_col,
            gain_f[0:1],
            full_in,
            full_gate,
            full_out,
            chan,
            blocks,
            *kept,
        ),
    )
    ffn_sum = lax.psum_scatter(ffn_part, "mp", scatter_dimension=0, tiled=True)
    ffn_sum, d_norm_back = lax.optimization_barrier((ffn_sum, d_norm_back))
    output = (resid + ffn_sum.astype(f32)).astype(bf16)
    grad_inputs, *mix_grads = line_call(
        sum_back,
        n_mp,
        3,
        [shape_of(bf16, local_rows, model)]
        + ([shape_of(f32, rows, width)] * 3 + [shape_of(f32, piece, little.shape[1])]) * fused,
        True,
        False,
        (inputs, d_resid, gain_f[0:1], d_norm_back)
        + ((norm_group, back_group, d_cat, mixed, little) if fused else ()),
        reduce_scratch(3, rows, width) + given_scratch(piece, little.shape[1]) if fused else (),
    )
    if fused:
        *mix_grads, little_own = mix_grads
    else:
        mix_grads = [
            reduced(norm_group, d_cat[:, :width]),
            reduced(norm_group, d_cat[:, width:]),
            reduced(back_group, mixed),
        ]
        little_own = lax.psum_scatter(little, "dp", scatter_dimension=0, tiled=True)
    lines_own = little_own[:, 2 * width : 2 * width + SUB * heads].reshape(piece, heads, SUB)
    lines_own = lines_own.transpose(2, 1, 0)
    grad_blocks = little_own[:, : 2 * width].reshape(piece, heads, 2, LANE).transpose(2, 1, 0, 3)

    owners = n_dp * n_mp
    gain_parts = jnp.concatenate([gain_in, gain_mid], axis=0).reshape(2, owners, -1).transpose(1, 0, 2)
    gain_parts = jnp.pad(
        gain_parts.reshape(owners, -1), ((0, 0), (0, SUB * LANE - 2 * model // owners))
    ).reshape(-1, LANE)
    gain_own = lax.psum_scatter(gain_parts, ("dp", "mp"), scatter_dimension=0, tiled=True)
    grad_gains = gain_own.reshape(-1)[: 2 * model // owners].reshape(2, -1)
    return (
        output,
        grad_inputs,
        grad_gains,
        mix_grads[0],
        mix_grads[1],
        mix_grads[2].T,
        lines_own[0:4],
        lines_own[4:7],
        lines_own[7],
        grad_blocks,
        ffn_grads[0],
        ffn_grads[1],
        ffn_grads[2].T,
    )


def solution(mesh):
    row, col = P("dp", "mp"), P("mp", "dp")
    tok = P(("dp", "mp"), None)
    chan = P(None, "mp", "dp")
    gate = P(None, "mp", "dp", None)
    return jax.shard_map(
        shards,
        mesh=mesh,
        in_specs=(
            tok, tok, P(("dp", "mp")), P("dp", None), P("dp", None), P(),
            row, row, col, chan, chan, col, gate, row, row, col,
        ),
        out_specs=(
            tok, tok, P(None, ("dp", "mp")), row, row, col, chan, chan, col, gate, row, row, col,
        ),
        check_vma=False,
    )
```

```python
import functools

import jax
import jax.numpy as jnp
from jax import lax
from jax.experimental import pallas as pl
from jax.experimental.pallas import tpu as pltpu
from jax.sharding import PartitionSpec as P

epsilon = 1e-06
LANE = 128
SUB = 8
TAIL = 24
ROWS = 272
VMEM_MB = 62
f32 = jnp.float32
bf16 = jnp.bfloat16
GELU_C = 0.7978845608028654
GELU_A = 0.044715


def rms_scale(values):
    return lax.rsqrt(jnp.mean(values * values, axis=-1, keepdims=True) + epsilon)


def dot(left, right):
    return lax.dot_general(left, right, (((1,), (0,)), ((), ())), preferred_element_type=f32)


def dot_last(left, right):
    return lax.dot_general(left, right, (((1,), (1,)), ((), ())), preferred_element_type=f32)


def dot_first(left, right):
    return lax.dot_general(left, right, (((0,), (0,)), ((), ())), preferred_element_type=f32)


def gelu_of(v):
    return 0.5 * v * (1.0 + jnp.tanh(GELU_C * (v + GELU_A * v * v * v)))


def gelu_both(v):
    square = v * v
    th = jnp.tanh(GELU_C * (v + GELU_A * v * square))
    half = 0.5 * (1.0 + th)
    slope = half + 0.5 * v * (1.0 - th * th) * (GELU_C * (1.0 + 3.0 * GELU_A * square))
    return v * half, slope


def sigmoid(v):
    return 0.5 * jnp.tanh(0.5 * v) + 0.5


def split(values):
    high = values.astype(bf16)
    return high, (values - high.astype(f32)).astype(bf16)


def rows_of(index, rows):
    return pl.ds(pl.multiple_of(index * rows, rows), rows)


def pick_rows(order_col, count):
    places = lax.broadcasted_iota(jnp.int32, (order_col.shape[0], count), 1)
    return (places == order_col).astype(f32).astype(bf16)


def put_rows(order_row, first, rows):
    places = lax.broadcasted_iota(jnp.int32, (rows, order_row.shape[1]), 0) + first
    return (places == order_row).astype(f32).astype(bf16)


def mixer_forward(
    tokens,
    ocol,
    orow,
    pos,
    w_in,
    w_gate,
    w_out,
    chan,
    blocks,
    gate_ref,
    branch_ref,
    conv_ref,
    gin_ref,
    grec_ref,
    state_ref,
    mixed_ref,
    out_ref,
    packed,
    rate,
    prod,
    before,
    low,
):
    count, _ = tokens.shape
    width = w_in.shape[1]
    steps = count // SUB
    heads = width // LANE

    def project(b, carry):
        at = rows_of(b, ROWS)
        packed[...] = dot(pick_rows(ocol[at, :], count), tokens[...]).astype(bf16)
        branch_ref[at, :] = dot(packed[...], w_in[...])
        gate_ref[at, :] = dot(packed[...], w_gate[...])
        return carry

    lax.fori_loop(0, count // ROWS, project, 0)

    for k in range(TAIL // SUB):
        last = branch_ref[pl.ds(count - TAIL + k * SUB, SUB), :]
        before[pl.ds(k * SUB, SUB), :] = pltpu.roll(last, 1, 0)
    before[pl.ds(TAIL, ROWS), :] = branch_ref[pl.ds(0, ROWS), :]

    def gates(b, carry):
        at = rows_of(b, ROWS)

        @pl.when(b > 0)
        def _():
            before[...] = branch_ref[pl.ds(pl.multiple_of(b * ROWS - TAIL, SUB), ROWS + TAIL), :]

        place = pos[at, :]
        for h in range(heads):
            lanes = pl.ds(h * LANE, LANE)
            par = chan[:, lanes]
            conv = par[4:5] + par[0:1] * before[pl.ds(TAIL, ROWS), lanes]
            for k in range(1, 4):
                earlier = before[pl.ds(TAIL - SUB * k, ROWS), lanes]
                conv = conv + par[k : k + 1] * jnp.where(place >= k, earlier, 0.0)
            high, rest = split(conv)
            pair = jnp.concatenate([blocks[h], blocks[heads + h]], axis=1)
            pre = dot(
                jnp.concatenate([high, rest], axis=1), jnp.concatenate([pair, pair], axis=0)
            )
            gate_in = sigmoid(pre[:, :LANE] + par[5:6])
            gate_rec = sigmoid(pre[:, LANE:] + par[6:7])
            kept = jnp.exp(-8.0 * gate_rec * par[7:8])
            drive = jnp.sqrt(1.0 - kept * kept + 0.01) * gate_in * conv
            conv_ref[at, lanes] = conv
            gin_ref[at, lanes] = gate_in
            grec_ref[at, lanes] = gate_rec
            rate[at, lanes] = jnp.where(place >= 1, kept, 0.0)
            state_ref[at, lanes] = drive
        return carry

    lax.fori_loop(0, count // ROWS, gates, 0)

    def scan(i, carry):
        held, passed = carry
        at = rows_of(i, SUB)
        a = rate[at, :]
        held = a * held + state_ref[at, :]
        passed = a * passed
        state_ref[at, :] = held
        prod[at, :] = passed
        return held, passed

    ends = lax.fori_loop(
        0, steps, scan, (jnp.zeros((SUB, width), f32), jnp.ones((SUB, width), f32)), unroll=8
    )
    first = lax.broadcasted_iota(jnp.int32, (SUB, width), 0) == 0
    carry_in = jnp.zeros((SUB, width), f32)
    for _ in range(SUB - 1):
        carry_in = jnp.where(first, 0.0, pltpu.roll(ends[0] + ends[1] * carry_in, 1, 0))

    def finish(i, carry):
        at = rows_of(i, 2 * SUB)
        twice = jnp.concatenate([carry_in, carry_in], axis=0)
        value = state_ref[at, :] + prod[at, :] * twice
        state_ref[at, :] = value
        low[at, :] = (gelu_of(gate_ref[at, :]) * value).astype(bf16)
        return carry

    lax.fori_loop(0, steps // 2, finish, 0, unroll=2)

    def leave(b, carry):
        at = rows_of(b, ROWS)
        mixed = dot(put_rows(orow[...], b * ROWS, ROWS), low[...]).astype(bf16)
        mixed_ref[at, :] = mixed
        out_ref[at, :] = dot_last(mixed, w_out[...]).astype(bf16)
        return carry

    lax.fori_loop(0, count // ROWS, leave, 0)


def ffn(
    tokens, cot, w_up, w_gate, w_down, part_ref, dnorm_ref, hidden_ref, dup_ref, dgate_ref
):
    def block(b, carry):
        at = rows_of(b, ROWS)
        up = dot(tokens[at, :], w_up[...])
        value, slope = gelu_both(dot(tokens[at, :], w_gate[...]))
        hidden = (value * up).astype(bf16)
        hidden_ref[at, :] = hidden
        d_hidden = dot(cot[at, :], w_down[...])
        d_up = (d_hidden * value).astype(bf16)
        d_gate = (d_hidden * up * slope).astype(bf16)
        dup_ref[at, :] = d_up
        dgate_ref[at, :] = d_gate
        dnorm_ref[at, :] = (dot_last(d_up, w_up[...]) + dot_last(d_gate, w_gate[...])).astype(bf16)
        part_ref[at, :] = dot_last(hidden, w_down[...]).astype(bf16)
        return carry

    lax.fori_loop(0, tokens.shape[0] // ROWS, block, 0)


def mixer_backward(
    back,
    norm,
    ocol,
    orow,
    pos,
    gain,
    w_in,
    w_gate,
    w_out,
    chan,
    blocks,
    gate_ref,
    branch_ref,
    conv_ref,
    gin_ref,
    grec_ref,
    state_ref,
    dcat_ref,
    dnorm_ref,
    little_ref,
    dgain_ref,
    dmix_arr,
    dmix,
    adj,
    prod,
    after,
    before,
    low,
    small_ref,
    dblocks_ref,
):
    count, _ = back.shape
    width = w_in.shape[1]
    steps = count // SUB
    heads = width // LANE
    blocks_of = count // ROWS

    def enter(b, carry):
        at = rows_of(b, ROWS)
        dmix_arr[at, :] = dot(back[at, :], w_out[...]).astype(bf16)
        return carry

    lax.fori_loop(0, blocks_of, enter, 0)

    def pack(b, carry):
        at = rows_of(b, ROWS)
        d_mixed = dot(pick_rows(ocol[at, :], count), dmix_arr[...])
        value, slope = gelu_both(gate_ref[at, :])
        adj[at, :] = d_mixed * value
        low[at, pl.ds(width, width)] = (d_mixed * state_ref[at, :] * slope).astype(bf16)
        kept = jnp.exp(-8.0 * grec_ref[at, :] * chan[7:8, :])
        dmix[at, :] = jnp.where(pos[at, :] >= 1, kept, 0.0)
        return carry

    lax.fori_loop(0, blocks_of, pack, 0)

    def scan(i, carry):
        held, passed, following = carry
        at = rows_of(steps - 1 - i, SUB)
        held = following * held + adj[at, :]
        passed = following * passed
        adj[at, :] = held
        prod[at, :] = passed
        return held, passed, dmix[at, :]

    last = lax.broadcasted_iota(jnp.int32, (SUB, width), 0) == SUB - 1
    wrapped = jnp.where(last, 0.0, pltpu.roll(dmix[pl.ds(0, SUB), :], SUB - 1, 0))
    ends = lax.fori_loop(
        0,
        steps,
        scan,
        (jnp.zeros((SUB, width), f32), jnp.ones((SUB, width), f32), wrapped),
        unroll=8,
    )
    carry_in = jnp.zeros((SUB, width), f32)
    for _ in range(SUB - 1):
        carry_in = jnp.where(last, 0.0, pltpu.roll(ends[0] + ends[1] * carry_in, SUB - 1, 0))

    small_ref[...] = jnp.zeros_like(small_ref)
    dblocks_ref[...] = jnp.zeros_like(dblocks_ref)
    first = lax.broadcasted_iota(jnp.int32, (SUB, width), 0) == 0
    state_last = state_ref[pl.ds(count - SUB, SUB), :]
    before[pl.ds(TAIL - SUB, SUB), :] = jnp.where(first, 0.0, pltpu.roll(state_last, 1, 0))
    before[pl.ds(TAIL, ROWS), :] = state_ref[pl.ds(0, ROWS), :]
    wide_carry = jnp.concatenate([carry_in] * (ROWS // SUB), axis=0)

    def point(b, carry):
        at = rows_of(b, ROWS)

        @pl.when(b > 0)
        def _():
            before[...] = state_ref[pl.ds(pl.multiple_of(b * ROWS - TAIL, SUB), ROWS + TAIL), :]

        place = pos[at, :]
        for h in range(heads):
            lanes = pl.ds(h * LANE, LANE)
            par = chan[:, lanes]
            adjoint = adj[at, lanes] + prod[at, lanes] * wide_carry[:, h * LANE : (h + 1) * LANE]
            conv = conv_ref[at, lanes]
            gate_in = gin_ref[at, lanes]
            gate_rec = grec_ref[at, lanes]
            kept = jnp.exp(-8.0 * gate_rec * par[7:8])
            square = kept * kept
            inside = 1.0 - square + 0.01
            inverse = lax.rsqrt(inside)
            root = inside * inverse
            previous = before[pl.ds(TAIL - SUB, ROWS), lanes]
            d_log = adjoint * previous * dmix[at, lanes]
            scaled = adjoint * gate_in
            d_log = d_log - scaled * conv * square * inverse
            d_in = adjoint * root * conv * gate_in * (1.0 - gate_in)
            d_rec = d_log * (-8.0 * par[7:8]) * gate_rec * (1.0 - gate_rec)
            both = jnp.concatenate([d_in, d_rec], axis=1)
            high, rest = split(both)
            pair = jnp.concatenate([blocks[h], blocks[heads + h]], axis=1)
            d_conv = scaled * root + dot_last(high, pair) + dot_last(rest, pair)
            dblocks_ref[h] += dot_first(conv.astype(bf16), high)
            after[at, lanes] = d_conv
            small_ref[4:5, lanes] += jnp.sum(d_conv, axis=0, keepdims=True)
            small_ref[5:6, lanes] += jnp.sum(d_in, axis=0, keepdims=True)
            small_ref[6:7, lanes] += jnp.sum(d_rec, axis=0, keepdims=True)
            small_ref[7:8, lanes] += (
                jnp.sum(d_log * gate_rec, axis=0, keepdims=True) * (-8.0) * par[8:9]
            )
        return carry

    lax.fori_loop(0, blocks_of, point, 0)

    for k in range(TAIL // SUB):
        head = after[pl.ds(k * SUB, SUB), :]
        after[pl.ds(count + k * SUB, SUB), :] = pltpu.roll(head, SUB - 1, 0)
        tail = branch_ref[pl.ds(count - TAIL + k * SUB, SUB), :]
        before[pl.ds(k * SUB, SUB), :] = pltpu.roll(tail, 1, 0)
    before[pl.ds(TAIL, ROWS), :] = branch_ref[pl.ds(0, ROWS), :]

    def unmix(b, carry):
        at = rows_of(b, ROWS)

        @pl.when(b > 0)
        def _():
            before[...] = branch_ref[pl.ds(pl.multiple_of(b * ROWS - TAIL, SUB), ROWS + TAIL), :]

        place = pos[at, :]
        for h in range(heads):
            lanes = pl.ds(h * LANE, LANE)
            par = chan[:, lanes]
            d_conv = after[at, lanes]
            d_branch = par[0:1] * d_conv
            small_ref[0:1, lanes] += jnp.sum(
                d_conv * before[pl.ds(TAIL, ROWS), lanes], axis=0, keepdims=True
            )
            for k in range(1, 4):
                later = pl.ds(pl.multiple_of(b * ROWS + SUB * k, SUB), ROWS)
                d_branch = d_branch + par[k : k + 1] * jnp.where(
                    pos[later, :] >= k, after[later, lanes], 0.0
                )
                earlier = before[pl.ds(TAIL - SUB * k, ROWS), lanes]
                small_ref[k : k + 1, lanes] += jnp.sum(
                    jnp.where(place >= k, d_conv * earlier, 0.0), axis=0, keepdims=True
                )
            low[at, lanes] = d_branch.astype(bf16)
        return carry

    lax.fori_loop(0, blocks_of, unmix, 0)
    lines = [small_ref[0:SUB, h * LANE : (h + 1) * LANE] for h in range(heads)]
    lines.append(jnp.zeros((LANE - SUB * heads, LANE), f32))
    little_ref[:, pl.ds(2 * width, LANE)] = jnp.concatenate(lines, axis=0).T
    for h in range(heads):
        little_ref[:, pl.ds(2 * h * LANE, 2 * LANE)] = dblocks_ref[h]
    dgain_ref[...] = jnp.zeros_like(dgain_ref)

    def leave(b, carry):
        at = rows_of(b, ROWS)
        cat = dot(put_rows(orow[...], b * ROWS, ROWS), low[...]).astype(bf16)
        dcat_ref[at, :] = cat
        d_norm = dot_last(cat[:, :width], w_in[...]) + dot_last(cat[:, width:], w_gate[...])
        dgain_ref[...] += jnp.sum(d_norm * norm[at, :].astype(f32), axis=0, keepdims=True)
        dnorm_ref[at, :] = d_norm.astype(bf16)
        return carry

    lax.fori_loop(0, blocks_of, leave, 0)
    dgain_ref[...] = dgain_ref[...] / gain[...]


MESH = pl.DeviceIdType.MESH
TILE = 16
PIECES = 4


def cut_rows(rows, parts):
    tiles = rows // TILE
    ends = [tiles * (k + 1) // parts for k in range(parts)]
    return [(TILE * a, TILE * (b - a)) for a, b in zip([0] + ends[:-1], ends)]


class Line:
    def __init__(self, n, local, part, arrived, whole, sums, alls):
        self.n, self.local, self.part, self.arrived, self.whole = n, local, part, arrived, whole
        self.sums, self.alls = sums, alls
        self.me = lax.axis_index("mp")
        self.pieces = cut_rows(local, PIECES)
        self.has = (self.me > 0, self.me < n - 1)

    def greet(self, plane=None):
        barrier = pltpu.get_barrier_semaphore()
        more = 0
        if plane is not None:
            for bit in plane.bits:
                more += 1
                pl.semaphore_signal(
                    barrier, inc=1, device_id={"dp": plane.other(bit)}, device_id_type=MESH
                )
        for away in range(1, self.n):
            more += 1
            pl.semaphore_signal(
                barrier,
                inc=1,
                device_id={"mp": lax.rem(self.me + away, self.n)},
                device_id_type=MESH,
            )
        pl.semaphore_wait(barrier, more)

    def rows_at(self, owner, k):
        first, rows = self.pieces[k]
        return pl.ds(pl.multiple_of(owner * self.local + first, TILE), rows)

    def copy(self, source, target, sems, way, owner, k):
        return pltpu.make_async_remote_copy(
            src_ref=source,
            dst_ref=target,
            send_sem=sems[0].at[way, owner, k],
            recv_sem=sems[1].at[way, owner, k],
            device_id={"mp": self.me + 1 - 2 * way},
            device_id_type=MESH,
        )

    def sum_copy(self, way, owner, k, first=False):
        at = self.rows_at(owner, k)
        landed = self.arrived[way].at[at]
        return self.copy(self.part.at[at] if first else landed, landed, self.sums, way, owner, k)

    def all_copy(self, way, owner, k):
        block = self.whole.at[self.rows_at(owner, k)]
        return self.copy(block, block, self.alls, way, owner, k)

    def first(self, k):
        for away in range(self.n - 1):
            for way in range(2):
                owner = away if way else self.n - 1 - away

                @pl.when(jnp.logical_not(self.has[way]))
                def _():
                    self.sum_copy(way, owner, k, True).start()

    def relay(self, k, stage):
        for way in range(2):
            late = stage - (self.n - 1 - self.me if way else self.me)
            owner = late if way else self.n - 1 - late

            @pl.when(self.has[way] & (late >= 0))
            def _():
                self.sum_copy(way, owner, k).wait_recv()
                at = self.rows_at(owner, k)
                landed = self.arrived[way]
                landed[at, :] = (landed[at, :].astype(f32) + self.part[at, :].astype(f32)).astype(bf16)
                self.sum_copy(way, owner, k).start()

    def total(self, k, into):
        at = self.rows_at(self.me, k)
        rows = pl.ds(0, self.pieces[k][1])
        into[rows, :] = self.part[at, :].astype(f32)
        for way in range(2):

            @pl.when(self.has[way])
            def _():
                self.sum_copy(way, self.me, k).wait_recv()
                into[rows, :] += self.arrived[way][at, :].astype(f32)

    def spread(self, k):
        for way in range(2):

            @pl.when(self.has[1 - way])
            def _():
                self.all_copy(way, self.me, k).start()

    def forward(self, k, stage):
        for way in range(2):
            owner = self.me + stage if way else self.me - stage
            there = owner < self.n if way else owner >= 0

            @pl.when(there)
            def _():
                self.all_copy(way, owner, k).wait_recv()

            @pl.when(there & self.has[1 - way])
            def _():
                self.all_copy(way, owner, k).start()

    def finish(self):
        for k in range(PIECES):
            for owner in range(self.n):
                for way in range(2):
                    if self.part is not None:

                        @pl.when(self.me > owner if way else self.me < owner)
                        def _():
                            self.sum_copy(way, owner, k).wait_send()

                    if self.whole is not None:
                        reached = self.me <= owner if way else self.me >= owner

                        @pl.when(reached & self.has[1 - way])
                        def _():
                            self.all_copy(way, owner, k).wait_send()

    def run(self, point, tasks=()):
        tasks = iter(tasks)
        sums, alls = self.part is not None, self.whole is not None
        if sums:
            self.first(0)
        else:
            for k in range(PIECES):
                point(k)
                self.spread(k)
        for step in range(PIECES + (1 if alls and sums else 0)):
            gathered = step - 1 if sums else step
            if sums and alls and step > 0:
                self.spread(gathered)
            if sums and step + 1 < PIECES:
                self.first(step + 1)
            for stage in range(1, self.n):
                next(tasks, idle)()
                if alls and gathered >= 0:
                    self.forward(gathered, stage)
                if sums and step < PIECES and stage < self.n - 1:
                    self.relay(step, stage)
            if sums and step < PIECES:
                point(step)
        for task in tasks:
            task()
        self.finish()

    def tiles(self, k, body):
        first, rows = self.pieces[k]

        def one(i, carry):
            body(
                pl.ds(pl.multiple_of(i * TILE, TILE), TILE),
                pl.ds(pl.multiple_of(first + i * TILE, TILE), TILE),
                pl.ds(pl.multiple_of(self.me * self.local + first + i * TILE, TILE), TILE),
            )
            return carry

        lax.fori_loop(0, rows // TILE, one, 0)


def idle():
    pass


def all_of(tasks):
    for task in tasks:
        task()


class Plane:
    bits = (1, 2, 4)
    orders = ((4, 2, 1), (2, 4, 1))

    def __init__(self):
        self.me = lax.axis_index("dp")

    def bit(self, bit):
        return lax.rem(self.me // bit, 2)

    def other(self, *bits):
        return self.me + sum(bit * (1 - 2 * self.bit(bit)) for bit in bits)

    def gather_copies(self, item, view, halves, stage, sems):
        copies = []
        for half in halves:
            order = self.orders[half]
            for combo in range(1 << stage):
                flipped = [bit for i, bit in enumerate(order[:stage]) if combo >> i & 1]
                block = view(self.other(*flipped), half)
                slot = (1 << stage) - 1 + combo
                copies.append(
                    pltpu.make_async_remote_copy(
                        src_ref=block,
                        dst_ref=block,
                        send_sem=sems[0].at[item, half, slot],
                        recv_sem=sems[1].at[item, half, slot],
                        device_id={"dp": self.other(order[stage])},
                        device_id_type=MESH,
                    )
                )
        return copies


class Reduce(Plane):
    def __init__(self, index, left, right, lanes, mine, theirs, got, second, third, out, sems):
        super().__init__()
        self.index, self.left, self.right, self.lanes = index, left, right, lanes
        self.mine, self.theirs, self.got = mine.at[index], theirs.at[index], got.at[index]
        self.second, self.third, self.out = second.at[index], third.at[index], out
        self.sems = sems
        self.rows = out.shape[0]
        self.half = self.rows // 2

    def copy(self, source, target, slot, bit):
        return pltpu.make_async_remote_copy(
            src_ref=source,
            dst_ref=target,
            send_sem=self.sems[0].at[self.index, slot],
            recv_sem=self.sems[1].at[self.index, slot],
            device_id={"dp": self.other(bit)},
            device_id_type=MESH,
        )

    def core_copy(self, t):
        return self.copy(self.theirs.at[t], self.got.at[t], t, 1)

    def second_copy(self, half, j):
        x, y = self.bit(2), self.bit(4)
        block = (1 - y) * 2 + j if half else j * 2 + 1 - x
        rows = self.mine.at[block, pl.ds(half * self.half, self.half)]
        return self.copy(rows, self.second.at[half, j], 4 + 2 * half + j, 4 if half else 2)

    def third_block(self, half):
        x, y = self.bit(2), self.bit(4)
        return y * 2 + 1 - x if half else (1 - y) * 2 + x

    def third_copy(self, half):
        rows = self.mine.at[self.third_block(half), pl.ds(half * self.half, self.half)]
        return self.copy(rows, self.third.at[half], 8 + half, 2 if half else 4)

    def product(self, t):
        def task():
            core = self.bit(1)
            pair = pl.ds(t * 2 * self.rows, 2 * self.rows)
            both = dot_first(self.left[:, pair], self.right[:, self.lanes])
            low, high = both[: self.rows], both[self.rows :]
            self.mine[t] = jnp.where(core == 0, low, high).astype(bf16)
            self.theirs[t] = jnp.where(core == 0, high, low).astype(bf16)
            self.core_copy(t).start()

        return task

    def keep(self, t):
        return self.mine[t]

    def add_core(self):
        for t in range(4):
            self.core_copy(t).wait_recv()
            self.mine[t] = (self.keep(t).astype(f32) + self.got[t].astype(f32)).astype(self.mine.dtype)
        for half in range(2):
            for j in range(2):
                self.second_copy(half, j).start()

    def add_second(self):
        for half in range(2):
            for j in range(2):
                self.second_copy(half, j).wait_recv()
        for half in range(2):
            block, at = self.third_block(half), pl.ds(half * self.half, self.half)
            far = 1 - self.bit(2 if half else 4)
            self.mine[block, at] = (
                self.mine[block, at].astype(f32) + self.second[half, far].astype(f32)
            ).astype(self.mine.dtype)
            self.third_copy(half).start()

    def add_third(self):
        own = self.bit(4) * 2 + self.bit(2)
        for half in range(2):
            self.third_copy(half).wait_recv()
            at = pl.ds(half * self.half, self.half)
            near = self.bit(2 if half else 4)
            self.out[at, :] = (
                self.mine[own, at].astype(f32)
                + self.second[half, near].astype(f32)
                + self.third[half].astype(f32)
            )

    def finish(self):
        for t in range(4):
            self.core_copy(t).wait_send()
        for half in range(2):
            for j in range(2):
                self.second_copy(half, j).wait_send()
            self.third_copy(half).wait_send()


class Given(Reduce):
    def __init__(self, given, mine, got, second, third, out, sems):
        super().__init__(0, None, None, None, mine, mine, got, second, third, out, sems)
        self.given = given

    def rows_of(self, t, core):
        return pl.ds(pl.multiple_of((2 * t + core) * self.rows, self.rows), self.rows)

    def core_copy(self, t):
        return self.copy(self.given.at[self.rows_of(t, 1 - self.bit(1))], self.got.at[t], t, 1)

    def start(self):
        for t in range(4):
            self.core_copy(t).start()

    def keep(self, t):
        return self.given[self.rows_of(t, self.bit(1)), :]


def reduce_tasks(parts, given=()):
    tasks = [part.product(t) for part in parts for t in range(4)]

    def also(at, extra):
        while len(tasks) <= at:
            tasks.append(idle)
        before = tasks[at]

        def both():
            extra()
            before()

        tasks[at] = both

    for i, part in enumerate(parts):
        also(4 * i + 5, part.add_core)
        also(4 * i + 8, part.add_second)
        also(4 * i + 10, part.add_third)

    for part in given:
        also(0, part.start)
        also(2, part.add_core)
        also(4, part.add_second)
        also(6, part.add_third)

    def finish():
        for part in [*parts, *given]:
            part.finish()

    return tasks + [finish]


def given_scratch(rows, width):
    sem = pltpu.SemaphoreType.DMA((1, 10))
    return [
        pltpu.VMEM((1, 4, rows, width), f32),
        pltpu.VMEM((1, 4, rows, width), f32),
        pltpu.VMEM((1, 2, 2, rows // 2, width), f32),
        pltpu.VMEM((1, 2, rows // 2, width), f32),
        sem,
        sem,
    ]


def reduce_scratch(arrays, rows, width):
    block = pltpu.VMEM((arrays, 4, rows, width), bf16)
    sem = pltpu.SemaphoreType.DMA((arrays, 10))
    return [
        block,
        block,
        block,
        pltpu.VMEM((arrays, 2, 2, rows // 2, width), bf16),
        pltpu.VMEM((arrays, 2, rows // 2, width), bf16),
        sem,
        sem,
    ]


def gather_norm(n, x, gain, whole, send, recv):
    line = Line(n, x.shape[0], None, None, whole, None, (send, recv))
    line.greet()

    def point(k):
        def one(_, own, at):
            v = x[own, :].astype(f32)
            whole[at, :] = (v * rms_scale(v) * gain[...]).astype(bf16)

        line.tiles(k, one)

    line.run(point)


def gather_weights(
    n,
    x,
    gain,
    w_in,
    w_gate,
    w_out,
    blocks,
    chan,
    whole,
    all_in,
    all_gate,
    all_out,
    all_blocks,
    all_chan,
    send,
    recv,
    raw,
    plane_send,
    plane_recv,
):
    line = Line(n, x.shape[0], None, None, whole, None, (send, recv))
    plane = Plane()
    line.greet(plane)
    sems = plane_send, plane_recv
    rows, piece = w_in.shape[0], blocks.shape[1]
    lines = chan.shape[0]

    def view_of(array):
        def view(owner, half):
            first = owner * rows + half * (rows // 2)
            return array.at[pl.ds(pl.multiple_of(first, TILE), rows // 2)]

        return view

    def blocks_view(owner, half):
        return all_blocks.at[:, pl.ds(pl.multiple_of(owner * piece, TILE), piece)]

    def chan_view(owner, half):
        return raw.at[pl.ds(pl.multiple_of(owner * lines, TILE), lines)]

    items = [(view_of(array), (0, 1)) for array in (all_in, all_gate, all_out)]
    items += [(blocks_view, (0,)), (chan_view, (1,))]

    def copies(stage):
        return [
            copy
            for item, (view, halves) in enumerate(items)
            for copy in plane.gather_copies(item, view, halves, stage, sems)
        ]

    def stage_task(stage):
        def task():
            if stage:
                for copy in copies(stage - 1):
                    copy.wait_recv()
            for copy in copies(stage):
                copy.start()

        return task

    def last():
        for copy in copies(2):
            copy.wait_recv()
        lane = lax.broadcasted_iota(jnp.int32, (LANE, LANE), 1)
        row = lax.broadcasted_iota(jnp.int32, (LANE, LANE), 0)
        total = jnp.zeros((lines, LANE), f32)
        for owner in range(LANE // piece):
            moved = ((row < piece) & (row + owner * piece == lane)).astype(f32).astype(bf16)
            total = total + dot(raw[pl.ds(owner * lines, lines), :], moved)
        for h in range(lines // SUB):
            par = total[h * SUB : (h + 1) * SUB]
            lanes = pl.ds(h * LANE, LANE)
            all_chan[0:SUB, lanes] = par
            decay = par[SUB - 1 : SUB]
            small = jnp.exp(-jnp.abs(decay))
            one_more = 1.0 + small
            rest = jnp.where(one_more == 1.0, 1.0, one_more - 1.0)
            log_one_more = jnp.where(one_more == 1.0, small, jnp.log(one_more) * (small / rest))
            all_chan[SUB - 1 : SUB, lanes] = jnp.maximum(decay, 0.0) + log_one_more
            all_chan[SUB : 2 * SUB, lanes] = jnp.broadcast_to(sigmoid(decay), (SUB, LANE))
        for stage in range(3):
            for copy in copies(stage):
                copy.wait_send()

    own = pl.ds(pl.multiple_of(plane.me * rows, TILE), rows)
    all_in[own, :] = w_in[...]
    all_gate[own, :] = w_gate[...]
    all_out[own, :] = w_out[...]
    all_blocks[:, pl.ds(pl.multiple_of(plane.me * piece, TILE), piece), :] = blocks[...]
    raw[pl.ds(pl.multiple_of(plane.me * lines, TILE), lines), :] = chan[...]

    def point(k):
        def one(_, own, at):
            v = x[own, :].astype(f32)
            whole[at, :] = (v * rms_scale(v) * gain[...]).astype(bf16)

        line.tiles(k, one)

    tasks = [idle, stage_task(1), idle, idle, stage_task(2), idle, idle, last]
    stage_task(0)()
    line.run(point, tasks)


def sum_norm_gather(
    n, x, cot, gain, part, resid, whole, cots, left, right, total, ss, sr, send, recv, cot_send, cot_recv
):
    line = Line(n, x.shape[0], part, (left, right), whole, (ss, sr), (send, recv))
    other = Line(n, x.shape[0], None, None, cots, None, (cot_send, cot_recv))
    line.greet()

    def keep(_, own, at):
        cots[at, :] = cot[own, :]

    for k in range(PIECES):
        other.tiles(k, keep)

    def point(k):
        line.total(k, total)

        def one(here, own, at):
            v = x[own, :].astype(f32) + total[here, :]
            resid[own, :] = v
            whole[at, :] = (v * rms_scale(v) * gain[...]).astype(bf16)

        line.tiles(k, one)

    tasks = []
    for k in range(PIECES):
        for stage in range(n):
            at = k * (n - 1) + stage
            task = functools.partial(other.forward, k, stage) if stage else functools.partial(other.spread, k)
            tasks += [[] for _ in range(at + 1 - len(tasks))]
            tasks[at].append(task)
    line.run(point, [functools.partial(all_of, group) for group in tasks])
    other.finish()


def norm_back(value, gain, grad):
    scale = rms_scale(value)
    e = gain * grad
    slope = scale * scale * scale * jnp.mean(value * e, axis=-1, keepdims=True)
    return scale * e - value * slope, grad * value * scale


def sum_back_gather(n, resid, cot, gain, part, *rest):
    if len(rest) > 10:
        norm, cots, d_up, d_gate, hidden, *rest = rest
        d_resid, gain_grad, whole, *outs = rest[:6]
        left, right, total, ss, sr, send, recv, *reduce = rest[6:]
        every = slice(None)
        sides = ((norm, d_up, every), (norm, d_gate, every), (cots, hidden, every))
    else:
        d_resid, gain_grad, whole, left, right, total, ss, sr, send, recv = rest
        sides = ()
    line = Line(n, resid.shape[0], part, (left, right), whole, (ss, sr), (send, recv))
    line.greet(Plane() if sides else None)
    gain_grad[...] = jnp.zeros_like(gain_grad)

    def point(k):
        line.total(k, total)

        def one(here, own, at):
            back, terms = norm_back(resid[own, :], gain[...], total[here, :])
            gain_grad[...] += jnp.sum(terms, axis=0, keepdims=True)
            value = cot[own, :].astype(f32) + back
            d_resid[own, :] = value
            whole[at, :] = value.astype(bf16)

        line.tiles(k, one)

    if sides:
        tasks = reduce_tasks(
            [
                Reduce(i, *side, *reduce[:5], out, reduce[5:])
                for i, (side, out) in enumerate(zip(sides, outs))
            ]
        )
        line.run(point, tasks)
    else:
        line.run(point)


def sum_back(n, x, d_resid, gain, part, *rest):
    if len(rest) > 6:
        norm, back_all, cat, mixed, little, gains, *rest = rest
        grad_x, *outs, little_out, gains_out = rest[:6]
        left, right, total, ss, sr, *reduce = rest[6:]
        given = [
            Given(little, *reduce[7:11], little_out, reduce[11:13]),
            Given(gains, *reduce[13:17], gains_out, reduce[17:19]),
        ]
        met, met_send, met_recv = reduce[19:]
        width = mixed.shape[1]
        sides = (
            (norm, cat, slice(0, width)),
            (norm, cat, slice(width, 2 * width)),
            (back_all, mixed, slice(None)),
        )
    else:
        grad_x, left, right, total, ss, sr = rest
        sides = ()
    line = Line(n, x.shape[0], part, (left, right), None, (ss, sr), None)
    line.greet(Plane() if sides else None)

    def point(k):
        line.total(k, total)

        def one(here, own, at):
            back, _ = norm_back(x[own, :].astype(f32), gain[...], total[here, :])
            grad_x[own, :] = (d_resid[own, :] + back).astype(bf16)

        line.tiles(k, one)

    if sides:
        tasks = reduce_tasks(
            [
                Reduce(i, *side, *reduce[:5], out, reduce[5:7])
                for i, (side, out) in enumerate(zip(sides, outs))
            ],
            given,
        )
        me = lax.axis_index("mp")

        def meet(away):
            return pltpu.make_async_remote_copy(
                src_ref=gains_out,
                dst_ref=met.at[away - 1],
                send_sem=met_send.at[away - 1],
                recv_sem=met_recv.at[away - 1],
                device_id={"mp": lax.rem(me + away, n)},
                device_id_type=MESH,
            )

        def send_gains():
            for away in range(1, n):
                meet(away).start()

        def add_gains():
            for away in range(1, n):
                meet(away).wait()
            gains_out[...] += sum(met[away] for away in range(n - 1))

        tasks[7:7] = [send_gains]
        tasks.append(add_gains)
        line.run(point, tasks)
    else:
        line.run(point)


def line_call(body, n, identity, outs, sums, alls, args, more=()):
    whole = pl.BlockSpec(memory_space=pltpu.VMEM)
    local, model = args[0].shape
    sem = pltpu.SemaphoreType.DMA((2, n, PIECES))
    scratch = []
    if sums:
        scratch += [pltpu.VMEM((n * local, model), bf16)] * 2
        scratch += [pltpu.VMEM((max(rows for _, rows in cut_rows(local, PIECES)), model), f32)]
        scratch += [sem, sem]
    if alls:
        scratch += [sem, sem]
    scratch += more
    moved = sum(a.size * a.dtype.itemsize for a in args)
    return pl.pallas_call(
        functools.partial(body, n),
        out_shape=outs,
        in_specs=[whole] * len(args),
        out_specs=[whole] * len(outs),
        scratch_shapes=scratch,
        compiler_params=pltpu.CompilerParams(
            vmem_limit_bytes=VMEM_MB << 20, collective_id=identity, has_side_effects=True
        ),
        cost_estimate=pl.CostEstimate(flops=0, bytes_accessed=100 * moved, transcendentals=0),
    )(*args)


def local_call(body, outs, scratch, flops, args):
    whole = pl.BlockSpec(memory_space=pltpu.VMEM)
    moved = sum(a.size * a.dtype.itemsize for a in args)
    moved += sum(o.size * o.dtype.itemsize for o in outs)
    return pl.pallas_call(
        body,
        out_shape=outs,
        in_specs=[whole] * len(args),
        out_specs=[whole] * len(outs),
        scratch_shapes=scratch,
        compiler_params=pltpu.CompilerParams(vmem_limit_bytes=VMEM_MB << 20),
        cost_estimate=pl.CostEstimate(flops=flops, bytes_accessed=moved, transcendentals=0),
    )(*args)


def shape_of(dtype, *shape):
    return jax.ShapeDtypeStruct(shape, dtype)


def shards(
    inputs,
    cotangent,
    token_mask,
    order,
    lengths,
    gains,
    w_in,
    w_gate,
    w_out,
    conv_weight,
    chan_bias,
    decay,
    gate_blocks,
    w_up,
    w_gate_ff,
    w_down,
):
    n_dp = lax.axis_size("dp")
    local_rows, model = inputs.shape
    count = local_rows * lax.axis_size("mp")
    heads, piece = decay.shape
    width = heads * piece * n_dp
    hidden_width = w_up.shape[1]

    fused = n_dp == 8
    rows = model // n_dp
    out_rows, down_rows = w_out.T, w_down.T
    full_up = lax.all_gather(w_up, "dp", axis=0, tiled=True)
    full_gate_ff = lax.all_gather(w_gate_ff, "dp", axis=0, tiled=True)
    full_down = lax.all_gather(down_rows, "dp", axis=0, tiled=True)
    lines = jnp.concatenate([conv_weight, chan_bias, decay[None]], axis=0).transpose(1, 0, 2)
    lines = lines.reshape(SUB * heads, piece)

    steps = count // SUB
    ends = jnp.cumsum(lengths[0], dtype=jnp.int32)
    starts = ends - lengths[0]
    places = jnp.arange(count, dtype=jnp.int32)
    own_start = jnp.max(
        jnp.where(places[:, None] >= starts[None, :], starts[None, :], 0), axis=1
    )
    pos = (places - own_start).reshape(SUB, steps).T
    wrap = jnp.concatenate([pos[: TAIL // SUB, 1:], jnp.full((TAIL // SUB, 1), -1, jnp.int32)], axis=1)
    pos_col = jnp.concatenate([pos, wrap], axis=0).reshape(count + TAIL, 1)
    order_int = order[0].reshape(SUB, steps).T.reshape(count)
    ocol, orow = order_int.reshape(count, 1), order_int.reshape(1, count)

    gain_f = gains.astype(f32)
    n_mp = lax.axis_size("mp")
    tok = shape_of(bf16, count, model)
    own = shape_of(f32, local_rows, model)
    if fused:
        grown = shape_of(bf16, model, width)
        norm_group, full_in, full_gate, full_out, blocks, chan = line_call(
            gather_weights,
            n_mp,
            0,
            [tok, grown, grown, grown, shape_of(bf16, 2 * heads, LANE, LANE), shape_of(f32, 16, width)],
            False,
            True,
            (
                inputs,
                gain_f[0:1],
                w_in,
                w_gate,
                out_rows,
                gate_blocks.reshape(2 * heads, piece, LANE),
                jnp.pad(lines, ((0, 0), (0, LANE - piece))),
            ),
            [pltpu.VMEM((n_dp * SUB * heads, LANE), bf16)] + [pltpu.SemaphoreType.DMA((5, 2, 7))] * 2,
        )
    else:
        (norm_group,) = line_call(gather_norm, n_mp, 0, [tok], False, True, (inputs, gain_f[0:1]))
        full_in = lax.all_gather(w_in, "dp", axis=0, tiled=True)
        full_gate = lax.all_gather(w_gate, "dp", axis=0, tiled=True)
        full_out = lax.all_gather(out_rows, "dp", axis=0, tiled=True)
        blocks = lax.all_gather(gate_blocks, "dp", axis=2, tiled=True).reshape(2 * heads, LANE, LANE)
        params = lax.all_gather(lines, "dp", axis=1, tiled=True).astype(f32)
        params = params.reshape(heads, SUB, LANE).transpose(1, 0, 2).reshape(SUB, width)
        decay_row = params[7:8]
        chan = jnp.concatenate(
            [params[:7], jax.nn.softplus(decay_row)] + [jax.nn.sigmoid(decay_row)] * SUB, axis=0
        )
    cot = cotangent * token_mask.astype(bf16)[:, None]

    wide = pltpu.VMEM((count, width), f32)
    saved = [shape_of(f32, count, width)] * 6
    *kept, mixed, back_part = local_call(
        mixer_forward,
        saved + [shape_of(bf16, count, width), shape_of(bf16, count, model)],
        [
            pltpu.VMEM((ROWS, model), bf16),
            wide,
            wide,
            pltpu.VMEM((ROWS + TAIL, width), f32),
            pltpu.VMEM((count, width), bf16),
        ],
        2 * count * (count * model + 3 * model * width),
        (norm_group, ocol, orow, pos_col, full_in, full_gate, full_out, chan, blocks),
    )
    resid, norm_mid_group, cot_group = line_call(
        sum_norm_gather,
        n_mp,
        1,
        [own, tok, tok],
        True,
        True,
        (inputs, cot, gain_f[1:2], back_part),
        [pltpu.SemaphoreType.DMA((2, n_mp, PIECES))] * 2,
    )

    hid = shape_of(bf16, count, hidden_width)
    ffn_part, d_norm_part, hidden, d_up, d_gate_ff = local_call(
        ffn,
        [tok, tok, hid, hid, hid],
        [],
        12 * count * model * hidden_width,
        (norm_mid_group, cot_group, full_up, full_gate_ff, full_down),
    )
    d_resid, gain_mid, back_group, *ffn_grads = line_call(
        sum_back_gather,
        n_mp,
        2,
        [own, shape_of(f32, 1, model), tok] + [shape_of(f32, rows, hidden_width)] * (3 * fused),
        True,
        True,
        (resid, cot, gain_f[1:2], d_norm_part)
        + ((norm_mid_group, cot_group, d_up, d_gate_ff, hidden) if fused else ()),
        reduce_scratch(3, rows, hidden_width) if fused else (),
    )
    def reduced(left, right):
        grad = dot_first(left, right).astype(bf16)
        return lax.psum_scatter(grad, "dp", scatter_dimension=0, tiled=True).astype(f32)

    if not fused:
        ffn_grads = [
            reduced(norm_mid_group, d_up),
            reduced(norm_mid_group, d_gate_ff),
            reduced(cot_group, hidden),
        ]

    d_cat, d_norm_back, little, gain_in = local_call(
        mixer_backward,
        [
            shape_of(bf16, count, 2 * width),
            tok,
            shape_of(f32, LANE, 2 * width + LANE),
            shape_of(f32, 1, model),
        ],
        [
            pltpu.VMEM((count, width), bf16),
            wide,
            wide,
            wide,
            pltpu.VMEM((count + TAIL, width), f32),
            pltpu.VMEM((ROWS + TAIL, width), f32),
            pltpu.VMEM((count, 2 * width), bf16),
            pltpu.VMEM((SUB, width), f32),
            pltpu.VMEM((heads, LANE, 2 * LANE), f32),
        ],
        2 * count * (3 * count * width + 3 * model * width),
        (
            back_group,
            norm_group,
            ocol,
            orow,
            pos_col,
            gain_f[0:1],
            full_in,
            full_gate,
            full_out,
            chan,
            blocks,
            *kept,
        ),
    )
    share = model // (n_dp * n_mp)
    gain_parts = jnp.concatenate([gain_in, gain_mid], axis=0).reshape(2, n_dp, n_mp, share)
    gain_parts = gain_parts.transpose(1, 2, 0, 3).reshape(n_dp, 2 * n_mp, share)
    gain_parts = jnp.pad(gain_parts, ((0, 0), (0, 2 * SUB - 2 * n_mp), (0, LANE - share)))
    gain_parts = gain_parts.reshape(2 * SUB * n_dp, LANE)
    ffn_sum = lax.psum_scatter(ffn_part, "mp", scatter_dimension=0, tiled=True)
    ffn_sum, d_norm_back = lax.optimization_barrier((ffn_sum, d_norm_back))
    output = (resid + ffn_sum.astype(f32)).astype(bf16)
    grad_inputs, *mix_grads = line_call(
        sum_back,
        n_mp,
        3,
        [shape_of(bf16, local_rows, model)]
        + (
            [shape_of(f32, rows, width)] * 3
            + [shape_of(f32, piece, little.shape[1]), shape_of(f32, 2 * SUB, LANE)]
        )
        * fused,
        True,
        False,
        (inputs, d_resid, gain_f[0:1], d_norm_back)
        + ((norm_group, back_group, d_cat, mixed, little, gain_parts) if fused else ()),
        reduce_scratch(3, rows, width)
        + given_scratch(piece, little.shape[1])
        + given_scratch(2 * SUB, LANE)
        + [pltpu.VMEM((n_mp - 1, 2 * SUB, LANE), f32)]
        + [pltpu.SemaphoreType.DMA((n_mp - 1,))] * 2
        if fused
        else (),
    )
    if fused:
        *mix_grads, little_own, gain_own = mix_grads
    else:
        mix_grads = [
            reduced(norm_group, d_cat[:, :width]),
            reduced(norm_group, d_cat[:, width:]),
            reduced(back_group, mixed),
        ]
        little_own = lax.psum_scatter(little, "dp", scatter_dimension=0, tiled=True)
        gain_own = lax.psum(lax.psum_scatter(gain_parts, "dp", scatter_dimension=0, tiled=True), "mp")
    grad_gains = lax.dynamic_slice_in_dim(gain_own, 2 * lax.axis_index("mp"), 2, axis=0)[:, :share]
    lines_own = little_own[:, 2 * width : 2 * width + SUB * heads].reshape(piece, heads, SUB)
    lines_own = lines_own.transpose(2, 1, 0)
    grad_blocks = little_own[:, : 2 * width].reshape(piece, heads, 2, LANE).transpose(2, 1, 0, 3)

    return (
        output,
        grad_inputs,
        grad_gains,
        mix_grads[0],
        mix_grads[1],
        mix_grads[2].T,
        lines_own[0:4],
        lines_own[4:7],
        lines_own[7],
        grad_blocks,
        ffn_grads[0],
        ffn_grads[1],
        ffn_grads[2].T,
    )


def solution(mesh):
    row, col = P("dp", "mp"), P("mp", "dp")
    tok = P(("dp", "mp"), None)
    chan = P(None, "mp", "dp")
    gate = P(None, "mp", "dp", None)
    return jax.shard_map(
        shards,
        mesh=mesh,
        in_specs=(
            tok, tok, P(("dp", "mp")), P("dp", None), P("dp", None), P(),
            row, row, col, chan, chan, col, gate, row, row, col,
        ),
        out_specs=(
            tok, tok, P(None, ("dp", "mp")), row, row, col, chan, chan, col, gate, row, row, col,
        ),
        check_vma=False,
    )
```

```python
import functools

import jax
import jax.numpy as jnp
from jax import lax
from jax.experimental import pallas as pl
from jax.experimental.pallas import tpu as pltpu
from jax.sharding import PartitionSpec as P

epsilon = 1e-06
LANE = 128
SUB = 8
TAIL = 24
ROWS = 272
VMEM_MB = 62
f32 = jnp.float32
bf16 = jnp.bfloat16
GELU_C = 0.7978845608028654
GELU_A = 0.044715


def rms_scale(values):
    return lax.rsqrt(jnp.mean(values * values, axis=-1, keepdims=True) + epsilon)


def dot(left, right):
    return lax.dot_general(left, right, (((1,), (0,)), ((), ())), preferred_element_type=f32)


def dot_last(left, right):
    return lax.dot_general(left, right, (((1,), (1,)), ((), ())), preferred_element_type=f32)


def dot_first(left, right):
    return lax.dot_general(left, right, (((0,), (0,)), ((), ())), preferred_element_type=f32)


def gelu_of(v):
    return 0.5 * v * (1.0 + jnp.tanh(GELU_C * (v + GELU_A * v * v * v)))


def gelu_both(v):
    square = v * v
    th = jnp.tanh(GELU_C * (v + GELU_A * v * square))
    half = 0.5 * (1.0 + th)
    slope = half + 0.5 * v * (1.0 - th * th) * (GELU_C * (1.0 + 3.0 * GELU_A * square))
    return v * half, slope


def sigmoid(v):
    return 0.5 * jnp.tanh(0.5 * v) + 0.5


def split(values):
    high = values.astype(bf16)
    return high, (values - high.astype(f32)).astype(bf16)


def rows_of(index, rows):
    return pl.ds(pl.multiple_of(index * rows, rows), rows)


def pick_rows(order_col, count):
    places = lax.broadcasted_iota(jnp.int32, (order_col.shape[0], count), 1)
    return (places == order_col).astype(f32).astype(bf16)


def put_rows(order_row, first, rows):
    places = lax.broadcasted_iota(jnp.int32, (rows, order_row.shape[1]), 0) + first
    return (places == order_row).astype(f32).astype(bf16)


def mixer_forward(
    tokens,
    ocol,
    orow,
    pos,
    w_in,
    w_gate,
    w_out,
    chan,
    blocks,
    gate_ref,
    branch_ref,
    conv_ref,
    gin_ref,
    grec_ref,
    state_ref,
    mixed_ref,
    out_ref,
    packed,
    rate,
    prod,
    before,
    low,
):
    count, _ = tokens.shape
    width = w_in.shape[1]
    steps = count // SUB
    heads = width // LANE

    def project(b, carry):
        at = rows_of(b, ROWS)
        packed[...] = dot(pick_rows(ocol[at, :], count), tokens[...]).astype(bf16)
        branch_ref[at, :] = dot(packed[...], w_in[...])
        gate_ref[at, :] = dot(packed[...], w_gate[...])
        return carry

    lax.fori_loop(0, count // ROWS, project, 0)

    for k in range(TAIL // SUB):
        last = branch_ref[pl.ds(count - TAIL + k * SUB, SUB), :]
        before[pl.ds(k * SUB, SUB), :] = pltpu.roll(last, 1, 0)
    before[pl.ds(TAIL, ROWS), :] = branch_ref[pl.ds(0, ROWS), :]

    def gates(b, carry):
        at = rows_of(b, ROWS)

        @pl.when(b > 0)
        def _():
            before[...] = branch_ref[pl.ds(pl.multiple_of(b * ROWS - TAIL, SUB), ROWS + TAIL), :]

        place = pos[at, :]
        for h in range(heads):
            lanes = pl.ds(h * LANE, LANE)
            par = chan[:, lanes]
            conv = par[4:5] + par[0:1] * before[pl.ds(TAIL, ROWS), lanes]
            for k in range(1, 4):
                earlier = before[pl.ds(TAIL - SUB * k, ROWS), lanes]
                conv = conv + par[k : k + 1] * jnp.where(place >= k, earlier, 0.0)
            high, rest = split(conv)
            pair = jnp.concatenate([blocks[h], blocks[heads + h]], axis=1)
            pre = dot(
                jnp.concatenate([high, rest], axis=1), jnp.concatenate([pair, pair], axis=0)
            )
            gate_in = sigmoid(pre[:, :LANE] + par[5:6])
            gate_rec = sigmoid(pre[:, LANE:] + par[6:7])
            kept = jnp.exp(-8.0 * gate_rec * par[7:8])
            drive = jnp.sqrt(1.0 - kept * kept + 0.01) * gate_in * conv
            conv_ref[at, lanes] = conv
            gin_ref[at, lanes] = gate_in
            grec_ref[at, lanes] = gate_rec
            rate[at, lanes] = jnp.where(place >= 1, kept, 0.0)
            state_ref[at, lanes] = drive
        return carry

    lax.fori_loop(0, count // ROWS, gates, 0)

    def scan(i, carry):
        held, passed = carry
        at = rows_of(i, SUB)
        a = rate[at, :]
        held = a * held + state_ref[at, :]
        passed = a * passed
        state_ref[at, :] = held
        prod[at, :] = passed
        return held, passed

    ends = lax.fori_loop(
        0, steps, scan, (jnp.zeros((SUB, width), f32), jnp.ones((SUB, width), f32)), unroll=8
    )
    first = lax.broadcasted_iota(jnp.int32, (SUB, width), 0) == 0
    carry_in = jnp.zeros((SUB, width), f32)
    for _ in range(SUB - 1):
        carry_in = jnp.where(first, 0.0, pltpu.roll(ends[0] + ends[1] * carry_in, 1, 0))

    def finish(i, carry):
        at = rows_of(i, 2 * SUB)
        twice = jnp.concatenate([carry_in, carry_in], axis=0)
        value = state_ref[at, :] + prod[at, :] * twice
        state_ref[at, :] = value
        low[at, :] = (gelu_of(gate_ref[at, :]) * value).astype(bf16)
        return carry

    lax.fori_loop(0, steps // 2, finish, 0, unroll=2)

    def leave(b, carry):
        at = rows_of(b, ROWS)
        mixed = dot(put_rows(orow[...], b * ROWS, ROWS), low[...]).astype(bf16)
        mixed_ref[at, :] = mixed
        out_ref[at, :] = dot_last(mixed, w_out[...]).astype(bf16)
        return carry

    lax.fori_loop(0, count // ROWS, leave, 0)


def ffn(
    tokens, cot, w_up, w_gate, w_down, dnorm_ref, hidden_ref, dup_ref, dgate_ref
):
    def block(b, carry):
        at = rows_of(b, ROWS)
        up = dot(tokens[at, :], w_up[...])
        value, slope = gelu_both(dot(tokens[at, :], w_gate[...]))
        hidden = (value * up).astype(bf16)
        hidden_ref[at, :] = hidden
        d_hidden = dot(cot[at, :], w_down[...])
        d_up = (d_hidden * value).astype(bf16)
        d_gate = (d_hidden * up * slope).astype(bf16)
        dup_ref[at, :] = d_up
        dgate_ref[at, :] = d_gate
        dnorm_ref[at, :] = (dot_last(d_up, w_up[...]) + dot_last(d_gate, w_gate[...])).astype(bf16)
        return carry

    lax.fori_loop(0, tokens.shape[0] // ROWS, block, 0)


def mixer_backward(
    back,
    norm,
    ocol,
    orow,
    pos,
    gain,
    w_in,
    w_gate,
    w_out,
    chan,
    blocks,
    gate_ref,
    branch_ref,
    conv_ref,
    gin_ref,
    grec_ref,
    state_ref,
    dcat_ref,
    dnorm_ref,
    little_ref,
    dgain_ref,
    dmix_arr,
    dmix,
    adj,
    prod,
    after,
    before,
    low,
    small_ref,
    dblocks_ref,
):
    count, _ = back.shape
    width = w_in.shape[1]
    steps = count // SUB
    heads = width // LANE
    blocks_of = count // ROWS

    def enter(b, carry):
        at = rows_of(b, ROWS)
        dmix_arr[at, :] = dot(back[at, :], w_out[...]).astype(bf16)
        return carry

    lax.fori_loop(0, blocks_of, enter, 0)

    def pack(b, carry):
        at = rows_of(b, ROWS)
        d_mixed = dot(pick_rows(ocol[at, :], count), dmix_arr[...])
        value, slope = gelu_both(gate_ref[at, :])
        adj[at, :] = d_mixed * value
        low[at, pl.ds(width, width)] = (d_mixed * state_ref[at, :] * slope).astype(bf16)
        kept = jnp.exp(-8.0 * grec_ref[at, :] * chan[7:8, :])
        dmix[at, :] = jnp.where(pos[at, :] >= 1, kept, 0.0)
        return carry

    lax.fori_loop(0, blocks_of, pack, 0)

    def scan(i, carry):
        held, passed, following = carry
        at = rows_of(steps - 1 - i, SUB)
        held = following * held + adj[at, :]
        passed = following * passed
        adj[at, :] = held
        prod[at, :] = passed
        return held, passed, dmix[at, :]

    last = lax.broadcasted_iota(jnp.int32, (SUB, width), 0) == SUB - 1
    wrapped = jnp.where(last, 0.0, pltpu.roll(dmix[pl.ds(0, SUB), :], SUB - 1, 0))
    ends = lax.fori_loop(
        0,
        steps,
        scan,
        (jnp.zeros((SUB, width), f32), jnp.ones((SUB, width), f32), wrapped),
        unroll=8,
    )
    carry_in = jnp.zeros((SUB, width), f32)
    for _ in range(SUB - 1):
        carry_in = jnp.where(last, 0.0, pltpu.roll(ends[0] + ends[1] * carry_in, SUB - 1, 0))

    small_ref[...] = jnp.zeros_like(small_ref)
    dblocks_ref[...] = jnp.zeros_like(dblocks_ref)
    first = lax.broadcasted_iota(jnp.int32, (SUB, width), 0) == 0
    state_last = state_ref[pl.ds(count - SUB, SUB), :]
    before[pl.ds(TAIL - SUB, SUB), :] = jnp.where(first, 0.0, pltpu.roll(state_last, 1, 0))
    before[pl.ds(TAIL, ROWS), :] = state_ref[pl.ds(0, ROWS), :]
    wide_carry = jnp.concatenate([carry_in] * (ROWS // SUB), axis=0)

    def point(b, carry):
        at = rows_of(b, ROWS)

        @pl.when(b > 0)
        def _():
            before[...] = state_ref[pl.ds(pl.multiple_of(b * ROWS - TAIL, SUB), ROWS + TAIL), :]

        place = pos[at, :]
        for h in range(heads):
            lanes = pl.ds(h * LANE, LANE)
            par = chan[:, lanes]
            adjoint = adj[at, lanes] + prod[at, lanes] * wide_carry[:, h * LANE : (h + 1) * LANE]
            conv = conv_ref[at, lanes]
            gate_in = gin_ref[at, lanes]
            gate_rec = grec_ref[at, lanes]
            kept = jnp.exp(-8.0 * gate_rec * par[7:8])
            square = kept * kept
            inside = 1.0 - square + 0.01
            inverse = lax.rsqrt(inside)
            root = inside * inverse
            previous = before[pl.ds(TAIL - SUB, ROWS), lanes]
            d_log = adjoint * previous * dmix[at, lanes]
            scaled = adjoint * gate_in
            d_log = d_log - scaled * conv * square * inverse
            d_in = adjoint * root * conv * gate_in * (1.0 - gate_in)
            d_rec = d_log * (-8.0 * par[7:8]) * gate_rec * (1.0 - gate_rec)
            both = jnp.concatenate([d_in, d_rec], axis=1)
            high, rest = split(both)
            pair = jnp.concatenate([blocks[h], blocks[heads + h]], axis=1)
            d_conv = scaled * root + dot_last(high, pair) + dot_last(rest, pair)
            dblocks_ref[h] += dot_first(conv.astype(bf16), high)
            after[at, lanes] = d_conv
            small_ref[4:5, lanes] += jnp.sum(d_conv, axis=0, keepdims=True)
            small_ref[5:6, lanes] += jnp.sum(d_in, axis=0, keepdims=True)
            small_ref[6:7, lanes] += jnp.sum(d_rec, axis=0, keepdims=True)
            small_ref[7:8, lanes] += (
                jnp.sum(d_log * gate_rec, axis=0, keepdims=True) * (-8.0) * par[8:9]
            )
        return carry

    lax.fori_loop(0, blocks_of, point, 0)

    for k in range(TAIL // SUB):
        head = after[pl.ds(k * SUB, SUB), :]
        after[pl.ds(count + k * SUB, SUB), :] = pltpu.roll(head, SUB - 1, 0)
        tail = branch_ref[pl.ds(count - TAIL + k * SUB, SUB), :]
        before[pl.ds(k * SUB, SUB), :] = pltpu.roll(tail, 1, 0)
    before[pl.ds(TAIL, ROWS), :] = branch_ref[pl.ds(0, ROWS), :]

    def unmix(b, carry):
        at = rows_of(b, ROWS)

        @pl.when(b > 0)
        def _():
            before[...] = branch_ref[pl.ds(pl.multiple_of(b * ROWS - TAIL, SUB), ROWS + TAIL), :]

        place = pos[at, :]
        for h in range(heads):
            lanes = pl.ds(h * LANE, LANE)
            par = chan[:, lanes]
            d_conv = after[at, lanes]
            d_branch = par[0:1] * d_conv
            small_ref[0:1, lanes] += jnp.sum(
                d_conv * before[pl.ds(TAIL, ROWS), lanes], axis=0, keepdims=True
            )
            for k in range(1, 4):
                later = pl.ds(pl.multiple_of(b * ROWS + SUB * k, SUB), ROWS)
                d_branch = d_branch + par[k : k + 1] * jnp.where(
                    pos[later, :] >= k, after[later, lanes], 0.0
                )
                earlier = before[pl.ds(TAIL - SUB * k, ROWS), lanes]
                small_ref[k : k + 1, lanes] += jnp.sum(
                    jnp.where(place >= k, d_conv * earlier, 0.0), axis=0, keepdims=True
                )
            low[at, lanes] = d_branch.astype(bf16)
        return carry

    lax.fori_loop(0, blocks_of, unmix, 0)
    lines = [small_ref[0:SUB, h * LANE : (h + 1) * LANE] for h in range(heads)]
    lines.append(jnp.zeros((LANE - SUB * heads, LANE), f32))
    little_ref[:, pl.ds(2 * width, LANE)] = jnp.concatenate(lines, axis=0).T
    for h in range(heads):
        little_ref[:, pl.ds(2 * h * LANE, 2 * LANE)] = dblocks_ref[h]
    dgain_ref[...] = jnp.zeros_like(dgain_ref)

    def leave(b, carry):
        at = rows_of(b, ROWS)
        cat = dot(put_rows(orow[...], b * ROWS, ROWS), low[...]).astype(bf16)
        dcat_ref[at, :] = cat
        d_norm = dot_last(cat[:, :width], w_in[...]) + dot_last(cat[:, width:], w_gate[...])
        dgain_ref[...] += jnp.sum(d_norm * norm[at, :].astype(f32), axis=0, keepdims=True)
        dnorm_ref[at, :] = d_norm.astype(bf16)
        return carry

    lax.fori_loop(0, blocks_of, leave, 0)
    dgain_ref[...] = dgain_ref[...] / gain[...]


MESH = pl.DeviceIdType.MESH
TILE = 16
PIECES = 8
HOP = 1
AFTER = 1


def cut_rows(rows, parts):
    tiles = rows // TILE
    ends = [tiles * (k + 1) // parts for k in range(parts)]
    return [(TILE * a, TILE * (b - a)) for a, b in zip([0] + ends[:-1], ends)]


class Line:
    def __init__(self, n, local, part, arrived, whole, sums, alls):
        self.n, self.local, self.part, self.arrived, self.whole = n, local, part, arrived, whole
        self.sums, self.alls = sums, alls
        self.me = lax.axis_index("mp")
        self.pieces = cut_rows(local, PIECES)
        self.has = (self.me > 0, self.me < n - 1)

    def greet(self, plane=None):
        barrier = pltpu.get_barrier_semaphore()
        more = 0
        if plane is not None:
            for bit in plane.bits:
                more += 1
                pl.semaphore_signal(
                    barrier, inc=1, device_id={"dp": plane.other(bit)}, device_id_type=MESH
                )
        for away in range(1, self.n):
            more += 1
            pl.semaphore_signal(
                barrier,
                inc=1,
                device_id={"mp": lax.rem(self.me + away, self.n)},
                device_id_type=MESH,
            )
        pl.semaphore_wait(barrier, more)

    def rows_at(self, owner, k):
        first, rows = self.pieces[k]
        return pl.ds(pl.multiple_of(owner * self.local + first, TILE), rows)

    def copy(self, source, target, sems, way, owner, k):
        return pltpu.make_async_remote_copy(
            src_ref=source,
            dst_ref=target,
            send_sem=sems[0].at[way, owner, k],
            recv_sem=sems[1].at[way, owner, k],
            device_id={"mp": self.me + 1 - 2 * way},
            device_id_type=MESH,
        )

    def sum_copy(self, way, owner, k, first=False):
        at = self.rows_at(owner, k)
        landed = self.arrived[way].at[at]
        return self.copy(self.part.at[at] if first else landed, landed, self.sums, way, owner, k)

    def all_copy(self, way, owner, k):
        block = self.whole.at[self.rows_at(owner, k)]
        return self.copy(block, block, self.alls, way, owner, k)

    def first(self, k):
        for away in range(self.n - 1):
            for way in range(2):
                owner = away if way else self.n - 1 - away

                @pl.when(jnp.logical_not(self.has[way]))
                def _():
                    self.sum_copy(way, owner, k, True).start()

    def relay(self, k, stage):
        for way in range(2):
            late = stage - (self.n - 1 - self.me if way else self.me)
            owner = late if way else self.n - 1 - late

            @pl.when(self.has[way] & (late >= 0))
            def _():
                self.sum_copy(way, owner, k).wait_recv()
                at = self.rows_at(owner, k)
                landed = self.arrived[way]
                landed[at, :] = (landed[at, :].astype(f32) + self.part[at, :].astype(f32)).astype(bf16)
                self.sum_copy(way, owner, k).start()

    def total(self, k, into):
        at = self.rows_at(self.me, k)
        rows = pl.ds(0, self.pieces[k][1])
        into[rows, :] = self.part[at, :].astype(f32)
        for way in range(2):

            @pl.when(self.has[way])
            def _():
                self.sum_copy(way, self.me, k).wait_recv()
                into[rows, :] += self.arrived[way][at, :].astype(f32)

    def spread(self, k):
        for way in range(2):

            @pl.when(self.has[1 - way])
            def _():
                self.all_copy(way, self.me, k).start()

    def forward(self, k, stage):
        for way in range(2):
            owner = self.me + stage if way else self.me - stage
            there = owner < self.n if way else owner >= 0

            @pl.when(there)
            def _():
                self.all_copy(way, owner, k).wait_recv()

            @pl.when(there & self.has[1 - way])
            def _():
                self.all_copy(way, owner, k).start()

    def finish(self):
        for k in range(PIECES):
            for owner in range(self.n):
                for way in range(2):
                    if self.part is not None:

                        @pl.when(self.me > owner if way else self.me < owner)
                        def _():
                            self.sum_copy(way, owner, k).wait_send()

                    if self.whole is not None:
                        reached = self.me <= owner if way else self.me >= owner

                        @pl.when(reached & self.has[1 - way])
                        def _():
                            self.all_copy(way, owner, k).wait_send()

    def run(self, point, tasks=()):
        sums, alls = self.part is not None, self.whole is not None
        slots = [[] for _ in range(PIECES + (HOP + AFTER) * (self.n - 1) + 1)]
        for k in range(PIECES):
            done = k + HOP * (self.n - 1) if sums else 0
            if sums:
                slots[k].append((0, functools.partial(self.first, k)))
                for stage in range(1, self.n - 1):
                    slots[k + HOP * stage].append((2, functools.partial(self.relay, k, stage)))
            slots[done].append((3, functools.partial(point, k)))
            if alls:
                slots[done].append((4, functools.partial(self.spread, k)))
                for stage in range(1, self.n):
                    at = (done if sums else k) + AFTER * stage
                    slots[at].append((1, functools.partial(self.forward, k, stage)))
        tasks = iter(tasks)
        for slot in slots:
            for step, (_, work) in enumerate(sorted(slot, key=lambda entry: entry[0])):
                if step in (0, 3):
                    next(tasks, idle)()
                work()
        for task in tasks:
            task()
        self.finish()

    def tiles(self, k, body):
        first, rows = self.pieces[k]

        def one(i, carry):
            body(
                pl.ds(pl.multiple_of(i * TILE, TILE), TILE),
                pl.ds(pl.multiple_of(first + i * TILE, TILE), TILE),
                pl.ds(pl.multiple_of(self.me * self.local + first + i * TILE, TILE), TILE),
            )
            return carry

        lax.fori_loop(0, rows // TILE, one, 0)


def idle():
    pass


class Late:
    def __init__(self, source, ref, sem):
        self.ref = ref
        self.copy = pltpu.make_async_copy(source, ref, sem)
        self.pending = True
        self.copy.start()

    def ready(self):
        if self.pending:
            self.copy.wait()
        self.pending = False


def late_all(sources, refs, sems):
    return [Late(source, ref, sems.at[i]) for i, (source, ref) in enumerate(zip(sources, refs))]


class Plane:
    bits = (1, 2, 4)
    orders = ((4, 2, 1), (2, 4, 1))

    def __init__(self):
        self.me = lax.axis_index("dp")

    def bit(self, bit):
        return lax.rem(self.me // bit, 2)

    def other(self, *bits):
        return self.me + sum(bit * (1 - 2 * self.bit(bit)) for bit in bits)

    def gather_copies(self, item, view, halves, stage, sems):
        copies = []
        for half in halves:
            order = self.orders[half]
            for combo in range(1 << stage):
                flipped = [bit for i, bit in enumerate(order[:stage]) if combo >> i & 1]
                block = view(self.other(*flipped), half)
                slot = (1 << stage) - 1 + combo
                copies.append(
                    pltpu.make_async_remote_copy(
                        src_ref=block,
                        dst_ref=block,
                        send_sem=sems[0].at[item, half, slot],
                        recv_sem=sems[1].at[item, half, slot],
                        device_id={"dp": self.other(order[stage])},
                        device_id_type=MESH,
                    )
                )
        return copies


class Reduce(Plane):
    def __init__(self, index, left, right, lanes, sent, mine, theirs, got, second, third, out, sems):
        super().__init__()
        self.sent, self.theirs = sent, theirs
        self.index, self.left, self.right, self.lanes = index, left, right, lanes
        self.mine, self.got = mine.at[index], got.at[index]
        self.second, self.third, self.out = second.at[index], third.at[index], out
        self.sems = sems
        self.rows = out.shape[0]
        self.half = self.rows // 2

    def copy(self, source, target, slot, bit):
        return pltpu.make_async_remote_copy(
            src_ref=source,
            dst_ref=target,
            send_sem=self.sems[0].at[self.index, slot],
            recv_sem=self.sems[1].at[self.index, slot],
            device_id={"dp": self.other(bit)},
            device_id_type=MESH,
        )

    def core_copy(self, t):
        return self.copy(self.theirs.at[(4 * self.index + t) % 2], self.got.at[t], t, 1)

    def second_copy(self, half, j):
        x, y = self.bit(2), self.bit(4)
        block = (1 - y) * 2 + j if half else j * 2 + 1 - x
        rows = self.mine.at[block, pl.ds(half * self.half, self.half)]
        return self.copy(rows, self.second.at[half, j], 4 + 2 * half + j, 4 if half else 2)

    def third_block(self, half):
        x, y = self.bit(2), self.bit(4)
        return y * 2 + 1 - x if half else (1 - y) * 2 + x

    def third_copy(self, half):
        rows = self.mine.at[self.third_block(half), pl.ds(half * self.half, self.half)]
        return self.copy(rows, self.third.at[half], 8 + half, 2 if half else 4)

    def product(self, t):
        def task():
            core = self.bit(1)
            pair = pl.ds(t * 2 * self.rows, 2 * self.rows)
            if t == 0:
                self.left.ready()
                self.right.ready()
            if len(self.sent) > 1:
                self.sent[-2].wait_send()
            both = dot_first(self.left.ref[:, pair], self.right.ref[:, self.lanes])
            low, high = both[: self.rows], both[self.rows :]
            self.mine[t] = jnp.where(core == 0, low, high).astype(bf16)
            self.theirs[(4 * self.index + t) % 2] = jnp.where(core == 0, high, low).astype(bf16)
            self.sent.append(self.core_copy(t))
            self.sent[-1].start()

        return task

    def keep(self, t):
        return self.mine[t]

    def add_core(self):
        for t in range(4):
            self.core_copy(t).wait_recv()
            self.mine[t] = (self.keep(t).astype(f32) + self.got[t].astype(f32)).astype(self.mine.dtype)
        for half in range(2):
            for j in range(2):
                self.second_copy(half, j).start()

    def add_second(self):
        for half in range(2):
            for j in range(2):
                self.second_copy(half, j).wait_recv()
        for half in range(2):
            block, at = self.third_block(half), pl.ds(half * self.half, self.half)
            far = 1 - self.bit(2 if half else 4)
            self.mine[block, at] = (
                self.mine[block, at].astype(f32) + self.second[half, far].astype(f32)
            ).astype(self.mine.dtype)
            self.third_copy(half).start()

    def add_third(self):
        own = self.bit(4) * 2 + self.bit(2)
        for half in range(2):
            self.third_copy(half).wait_recv()
            at = pl.ds(half * self.half, self.half)
            near = self.bit(2 if half else 4)
            self.out[at, :] = (
                self.mine[own, at].astype(f32)
                + self.second[half, near].astype(f32)
                + self.third[half].astype(f32)
            )

    def finish(self):
        for half in range(2):
            for j in range(2):
                self.second_copy(half, j).wait_send()
            self.third_copy(half).wait_send()


class Given(Reduce):
    def __init__(self, given, mine, got, second, third, out, sems):
        super().__init__(0, None, None, None, None, mine, None, got, second, third, out, sems)
        self.given = given

    def rows_of(self, t, core):
        return pl.ds(pl.multiple_of((2 * t + core) * self.rows, self.rows), self.rows)

    def core_copy(self, t):
        return self.copy(self.given.at[self.rows_of(t, 1 - self.bit(1))], self.got.at[t], t, 1)

    def start(self):
        for t in range(4):
            self.core_copy(t).start()

    def finish(self):
        for t in range(4):
            self.core_copy(t).wait_send()
        super().finish()

    def keep(self, t):
        return self.given[self.rows_of(t, self.bit(1)), :]


def reduce_tasks(parts, given=()):
    tasks = [part.product(t) for part in parts for t in range(4)]

    def also(at, extra):
        while len(tasks) <= at:
            tasks.append(idle)
        before = tasks[at]

        def both():
            extra()
            before()

        tasks[at] = both

    for i, part in enumerate(parts):
        also(4 * i + 5, part.add_core)
        also(4 * i + 8, part.add_second)
        also(4 * i + 10, part.add_third)

    for part in given:
        also(0, part.start)
        also(2, part.add_core)
        also(4, part.add_second)
        also(6, part.add_third)

    def finish():
        for copy in parts[0].sent[-2:]:
            copy.wait_send()
        for part in [*parts, *given]:
            part.finish()

    return tasks, finish


def given_scratch(rows, width):
    sem = pltpu.SemaphoreType.DMA((1, 10))
    return [
        pltpu.VMEM((1, 4, rows, width), f32),
        pltpu.VMEM((1, 4, rows, width), f32),
        pltpu.VMEM((1, 2, 2, rows // 2, width), f32),
        pltpu.VMEM((1, 2, rows // 2, width), f32),
        sem,
        sem,
    ]


def reduce_scratch(arrays, rows, width):
    block = pltpu.VMEM((arrays, 4, rows, width), bf16)
    sem = pltpu.SemaphoreType.DMA((arrays, 10))
    return [
        block,
        pltpu.VMEM((2, rows, width), bf16),
        block,
        pltpu.VMEM((arrays, 2, 2, rows // 2, width), bf16),
        pltpu.VMEM((arrays, 2, rows // 2, width), bf16),
        sem,
        sem,
    ]


def gather_norm(n, x, gain, whole, send, recv):
    line = Line(n, x.shape[0], None, None, whole, None, (send, recv))
    line.greet()

    def point(k):
        def one(_, own, at):
            v = x[own, :].astype(f32)
            whole[at, :] = (v * rms_scale(v) * gain[...]).astype(bf16)

        line.tiles(k, one)

    line.run(point)


def row_view(array, rows):
    def view(owner, half):
        first = owner * rows + half * (rows // 2)
        return array.at[pl.ds(pl.multiple_of(first, TILE), rows // 2)]

    return view


def gather_tasks(plane, items, sems):
    def copies(stage):
        return [
            copy
            for item, (view, halves) in enumerate(items)
            for copy in plane.gather_copies(item, view, halves, stage, sems)
        ]

    def stage_task(stage):
        def task():
            if stage:
                for copy in copies(stage - 1):
                    copy.wait_recv()
            for copy in copies(stage):
                copy.start()

        return task

    def last():
        for copy in copies(2):
            copy.wait_recv()
        for stage in range(3):
            for copy in copies(stage):
                copy.wait_send()

    return stage_task(0), stage_task(1), stage_task(2), last


def gather_weights(
    n,
    x,
    gain,
    w_in,
    w_gate,
    w_out,
    blocks,
    chan,
    whole,
    all_in,
    all_gate,
    all_out,
    all_blocks,
    all_chan,
    send,
    recv,
    raw,
    plane_send,
    plane_recv,
):
    line = Line(n, x.shape[0], None, None, whole, None, (send, recv))
    plane = Plane()
    line.greet(plane)
    sems = plane_send, plane_recv
    rows, piece = w_in.shape[0], blocks.shape[1]
    lines = chan.shape[0]

    def blocks_view(owner, half):
        return all_blocks.at[:, pl.ds(pl.multiple_of(owner * piece, TILE), piece)]

    def chan_view(owner, half):
        return raw.at[pl.ds(pl.multiple_of(owner * lines, TILE), lines)]

    items = [(row_view(array, rows), (0, 1)) for array in (all_in, all_gate, all_out)]
    items += [(blocks_view, (0,)), (chan_view, (1,))]

    first, second, third, finish = gather_tasks(plane, items, sems)

    def last():
        finish()
        lane = lax.broadcasted_iota(jnp.int32, (LANE, LANE), 1)
        row = lax.broadcasted_iota(jnp.int32, (LANE, LANE), 0)
        total = jnp.zeros((lines, LANE), f32)
        for owner in range(LANE // piece):
            moved = ((row < piece) & (row + owner * piece == lane)).astype(f32).astype(bf16)
            total = total + dot(raw[pl.ds(owner * lines, lines), :], moved)
        for h in range(lines // SUB):
            par = total[h * SUB : (h + 1) * SUB]
            lanes = pl.ds(h * LANE, LANE)
            all_chan[0:SUB, lanes] = par
            decay = par[SUB - 1 : SUB]
            small = jnp.exp(-jnp.abs(decay))
            one_more = 1.0 + small
            rest = jnp.where(one_more == 1.0, 1.0, one_more - 1.0)
            log_one_more = jnp.where(one_more == 1.0, small, jnp.log(one_more) * (small / rest))
            all_chan[SUB - 1 : SUB, lanes] = jnp.maximum(decay, 0.0) + log_one_more
            all_chan[SUB : 2 * SUB, lanes] = jnp.broadcast_to(sigmoid(decay), (SUB, LANE))

    own = pl.ds(pl.multiple_of(plane.me * rows, TILE), rows)
    all_in[own, :] = w_in[...]
    all_gate[own, :] = w_gate[...]
    all_out[own, :] = w_out[...]
    all_blocks[:, pl.ds(pl.multiple_of(plane.me * piece, TILE), piece), :] = blocks[...]
    raw[pl.ds(pl.multiple_of(plane.me * lines, TILE), lines), :] = chan[...]

    def point(k):
        def one(_, own, at):
            v = x[own, :].astype(f32)
            whole[at, :] = (v * rms_scale(v) * gain[...]).astype(bf16)

        line.tiles(k, one)

    first()
    line.run(point, [idle] * 4 + [second] + [idle] * 3 + [third] + [idle] * 3 + [last])


def sum_norm_gather(n, x, gain, part, *rest):
    if len(rest) > 9:
        shares, rest = rest[:3], rest[3:]
        resid, whole, *alls = rest[:5]
        left, right, total, ss, sr, send, recv, plane_send, plane_recv = rest[5:]
        plane = Plane()
    else:
        resid, whole, left, right, total, ss, sr, send, recv = rest
        plane = None
    line = Line(n, x.shape[0], part, (left, right), whole, (ss, sr), (send, recv))
    line.greet(plane)
    tasks = []
    if plane is not None:
        rows = shares[0].shape[0]
        own = pl.ds(pl.multiple_of(plane.me * rows, TILE), rows)
        for share, array in zip(shares, alls):
            array[own, :] = share[...]
        items = [(row_view(array, rows), (0, 1)) for array in alls]
        first, second, third, last = gather_tasks(plane, items, (plane_send, plane_recv))
        tasks = [first] + [idle] * 5 + [second] + [idle] * 9 + [third] + [idle] * 6 + [last]

    def point(k):
        line.total(k, total)

        def one(here, own, at):
            v = x[own, :].astype(f32) + total[here, :]
            resid[own, :] = v
            whole[at, :] = (v * rms_scale(v) * gain[...]).astype(bf16)

        line.tiles(k, one)

    line.run(point, tasks)


def norm_back(value, gain, grad):
    scale = rms_scale(value)
    e = gain * grad
    slope = scale * scale * scale * jnp.mean(value * e, axis=-1, keepdims=True)
    return scale * e - value * slope, grad * value * scale


def sum_back_gather(n, resid, cot, gain, part, *rest):
    if len(rest) > 10:
        sources, rest = rest[:6], rest[6:]
        d_resid, gain_grad, whole, ffn_part, *outs = rest[:7]
        left, right, total, ss, sr, send, recv, *reduce = rest[7:]
        reduce, refs, late_sems = reduce[:7], reduce[7:13], reduce[13]
    else:
        d_resid, gain_grad, whole, left, right, total, ss, sr, send, recv = rest
        sources = ()
    line = Line(n, resid.shape[0], part, (left, right), whole, (ss, sr), (send, recv))
    line.greet(Plane() if sources else None)
    gain_grad[...] = jnp.zeros_like(gain_grad)

    def point(k):
        line.total(k, total)

        def one(here, own, at):
            back, terms = norm_back(resid[own, :], gain[...], total[here, :])
            gain_grad[...] += jnp.sum(terms, axis=0, keepdims=True)
            value = cot[own, :].astype(f32) + back
            d_resid[own, :] = value
            whole[at, :] = value.astype(bf16)

        line.tiles(k, one)

    if not sources:
        line.run(point)
        return
    norm, cots, d_up, d_gate, hidden, w_down = late_all(sources, refs, late_sems)
    sent = []
    tasks, finish = reduce_tasks(
        [
            Reduce(i, *side, slice(None), sent, *reduce[:5], out, reduce[5:])
            for i, (side, out) in enumerate(
                zip(((norm, d_up), (norm, d_gate), (cots, hidden)), outs)
            )
        ]
    )

    def project(b):
        w_down.ready()
        at = pl.ds(b * ROWS, ROWS)
        ffn_part[at, :] = dot_last(hidden.ref[at, :], w_down.ref[...]).astype(bf16)

    for b in range(part.shape[0] // ROWS):
        tasks.insert(12 + b, functools.partial(project, b))
    line.run(point, tasks)
    finish()


def sum_back(n, x, d_resid, gain, part, *rest):
    if len(rest) > 6:
        little, gains, *rest = rest
        sources, rest = rest[:4], rest[4:]
        grad_x, *outs, little_out, gains_out = rest[:6]
        left, right, total, ss, sr, *reduce = rest[6:]
        refs, late_sems = reduce[22:26], reduce[26]
        given = [
            Given(little, *reduce[7:11], little_out, reduce[11:13]),
            Given(gains, *reduce[13:17], gains_out, reduce[17:19]),
        ]
        met, met_send, met_recv = reduce[19:22]
    else:
        grad_x, left, right, total, ss, sr = rest
        sources = ()
    line = Line(n, x.shape[0], part, (left, right), None, (ss, sr), None)
    line.greet(Plane() if sources else None)

    def point(k):
        line.total(k, total)

        def one(here, own, at):
            back, _ = norm_back(x[own, :].astype(f32), gain[...], total[here, :])
            grad_x[own, :] = (d_resid[own, :] + back).astype(bf16)

        line.tiles(k, one)

    if not sources:
        line.run(point)
        return
    norm, back_all, cat, mixed = late_all(sources, refs, late_sems)
    width = mixed.ref.shape[1]
    sent = []
    sides = (
        (norm, cat, slice(0, width)),
        (norm, cat, slice(width, 2 * width)),
        (back_all, mixed, slice(None)),
    )
    tasks, finish = reduce_tasks(
        [
            Reduce(i, *side, sent, *reduce[:5], out, reduce[5:7])
            for i, (side, out) in enumerate(zip(sides, outs))
        ],
        given,
    )
    me = lax.axis_index("mp")

    def meet(away):
        return pltpu.make_async_remote_copy(
            src_ref=gains_out,
            dst_ref=met.at[away - 1],
            send_sem=met_send.at[away - 1],
            recv_sem=met_recv.at[away - 1],
            device_id={"mp": lax.rem(me + away, n)},
            device_id_type=MESH,
        )

    def send_gains():
        for away in range(1, n):
            meet(away).start()

    def add_gains():
        for away in range(1, n):
            meet(away).wait()
        gains_out[...] += sum(met[away] for away in range(n - 1))

    tasks[7:7] = [send_gains]
    line.run(point, tasks)
    finish()
    add_gains()


def line_call(body, n, identity, outs, sums, alls, args, more=(), late=0):
    whole = pl.BlockSpec(memory_space=pltpu.VMEM)
    local, model = args[0].shape
    sem = pltpu.SemaphoreType.DMA((2, n, PIECES))
    scratch = []
    if sums:
        scratch += [pltpu.VMEM((n * local, model), bf16)] * 2
        scratch += [pltpu.VMEM((max(rows for _, rows in cut_rows(local, PIECES)), model), f32)]
        scratch += [sem, sem]
    if alls:
        scratch += [sem, sem]
    scratch += more
    if late:
        scratch += [pltpu.VMEM(a.shape, a.dtype) for a in args[-late:]]
        scratch += [pltpu.SemaphoreType.DMA((late,))]
    moved = sum(a.size * a.dtype.itemsize for a in args)
    return pl.pallas_call(
        functools.partial(body, n),
        out_shape=outs,
        in_specs=[whole] * (len(args) - late) + [pl.BlockSpec(memory_space=pl.ANY)] * late,
        out_specs=[whole] * len(outs),
        scratch_shapes=scratch,
        compiler_params=pltpu.CompilerParams(
            vmem_limit_bytes=VMEM_MB << 20, collective_id=identity, has_side_effects=True
        ),
        cost_estimate=pl.CostEstimate(flops=0, bytes_accessed=100 * moved, transcendentals=0),
    )(*args)


def local_call(body, outs, scratch, flops, args):
    whole = pl.BlockSpec(memory_space=pltpu.VMEM)
    moved = sum(a.size * a.dtype.itemsize for a in args)
    moved += sum(o.size * o.dtype.itemsize for o in outs)
    return pl.pallas_call(
        body,
        out_shape=outs,
        in_specs=[whole] * len(args),
        out_specs=[whole] * len(outs),
        scratch_shapes=scratch,
        compiler_params=pltpu.CompilerParams(vmem_limit_bytes=VMEM_MB << 20),
        cost_estimate=pl.CostEstimate(flops=flops, bytes_accessed=moved, transcendentals=0),
    )(*args)


def shape_of(dtype, *shape):
    return jax.ShapeDtypeStruct(shape, dtype)


def shards(
    inputs,
    cotangent,
    token_mask,
    order,
    lengths,
    gains,
    w_in,
    w_gate,
    w_out,
    conv_weight,
    chan_bias,
    decay,
    gate_blocks,
    w_up,
    w_gate_ff,
    w_down,
):
    n_dp = lax.axis_size("dp")
    local_rows, model = inputs.shape
    count = local_rows * lax.axis_size("mp")
    heads, piece = decay.shape
    width = heads * piece * n_dp
    hidden_width = w_up.shape[1]

    fused = n_dp == 8
    rows = model // n_dp
    out_rows, down_rows = w_out.T, w_down.T
    lines = jnp.concatenate([conv_weight, chan_bias, decay[None]], axis=0).transpose(1, 0, 2)
    lines = lines.reshape(SUB * heads, piece)

    steps = count // SUB
    ends = jnp.cumsum(lengths[0], dtype=jnp.int32)
    starts = ends - lengths[0]
    places = jnp.arange(count, dtype=jnp.int32)
    own_start = jnp.max(
        jnp.where(places[:, None] >= starts[None, :], starts[None, :], 0), axis=1
    )
    pos = (places - own_start).reshape(SUB, steps).T
    wrap = jnp.concatenate([pos[: TAIL // SUB, 1:], jnp.full((TAIL // SUB, 1), -1, jnp.int32)], axis=1)
    pos_col = jnp.concatenate([pos, wrap], axis=0).reshape(count + TAIL, 1)
    order_int = order[0].reshape(SUB, steps).T.reshape(count)
    ocol, orow = order_int.reshape(count, 1), order_int.reshape(1, count)

    gain_f = gains.astype(f32)
    n_mp = lax.axis_size("mp")
    tok = shape_of(bf16, count, model)
    own = shape_of(f32, local_rows, model)
    if fused:
        grown = shape_of(bf16, model, width)
        norm_group, full_in, full_gate, full_out, blocks, chan = line_call(
            gather_weights,
            n_mp,
            0,
            [tok, grown, grown, grown, shape_of(bf16, 2 * heads, LANE, LANE), shape_of(f32, 16, width)],
            False,
            True,
            (
                inputs,
                gain_f[0:1],
                w_in,
                w_gate,
                out_rows,
                gate_blocks.reshape(2 * heads, piece, LANE),
                jnp.pad(lines, ((0, 0), (0, LANE - piece))),
            ),
            [pltpu.VMEM((n_dp * SUB * heads, LANE), bf16)] + [pltpu.SemaphoreType.DMA((5, 2, 7))] * 2,
        )
    else:
        (norm_group,) = line_call(gather_norm, n_mp, 0, [tok], False, True, (inputs, gain_f[0:1]))
        full_in = lax.all_gather(w_in, "dp", axis=0, tiled=True)
        full_gate = lax.all_gather(w_gate, "dp", axis=0, tiled=True)
        full_out = lax.all_gather(out_rows, "dp", axis=0, tiled=True)
        blocks = lax.all_gather(gate_blocks, "dp", axis=2, tiled=True).reshape(2 * heads, LANE, LANE)
        params = lax.all_gather(lines, "dp", axis=1, tiled=True).astype(f32)
        params = params.reshape(heads, SUB, LANE).transpose(1, 0, 2).reshape(SUB, width)
        decay_row = params[7:8]
        chan = jnp.concatenate(
            [params[:7], jax.nn.softplus(decay_row)] + [jax.nn.sigmoid(decay_row)] * SUB, axis=0
        )
    cot = cotangent * token_mask.astype(bf16)[:, None]

    cot_late, norm_group = lax.optimization_barrier((cot, norm_group))
    cot_group = lax.all_gather(cot_late, "mp", axis=0, tiled=True)

    wide = pltpu.VMEM((count, width), f32)
    saved = [shape_of(f32, count, width)] * 6
    *kept, mixed, back_part = local_call(
        mixer_forward,
        saved + [shape_of(bf16, count, width), shape_of(bf16, count, model)],
        [
            pltpu.VMEM((ROWS, model), bf16),
            wide,
            wide,
            pltpu.VMEM((ROWS + TAIL, width), f32),
            pltpu.VMEM((count, width), bf16),
        ],
        2 * count * (count * model + 3 * model * width),
        (norm_group, ocol, orow, pos_col, full_in, full_gate, full_out, chan, blocks),
    )
    shares = (w_up, w_gate_ff, down_rows)
    resid, norm_mid_group, *ffn_weights = line_call(
        sum_norm_gather,
        n_mp,
        1,
        [own, tok] + [shape_of(bf16, model, hidden_width)] * (3 * fused),
        True,
        True,
        (inputs, gain_f[1:2], back_part) + (shares if fused else ()),
        [pltpu.SemaphoreType.DMA((3, 2, 7))] * (2 * fused),
    )
    if not fused:
        ffn_weights = [lax.all_gather(share, "dp", axis=0, tiled=True) for share in shares]
    full_up, full_gate_ff, full_down = ffn_weights

    hid = shape_of(bf16, count, hidden_width)
    d_norm_part, hidden, d_up, d_gate_ff = local_call(
        ffn,
        [tok, hid, hid, hid],
        [],
        10 * count * model * hidden_width,
        (norm_mid_group, cot_group, full_up, full_gate_ff, full_down),
    )
    d_resid, gain_mid, back_group, *ffn_grads = line_call(
        sum_back_gather,
        n_mp,
        2,
        [own, shape_of(f32, 1, model), tok]
        + ([tok] + [shape_of(f32, rows, hidden_width)] * 3) * fused,
        True,
        True,
        (resid, cot, gain_f[1:2], d_norm_part)
        + ((norm_mid_group, cot_group, d_up, d_gate_ff, hidden, full_down) if fused else ()),
        reduce_scratch(3, rows, hidden_width) if fused else (),
        6 * fused,
    )
    def reduced(left, right):
        grad = dot_first(left, right).astype(bf16)
        return lax.psum_scatter(grad, "dp", scatter_dimension=0, tiled=True).astype(f32)

    if fused:
        ffn_part, *ffn_grads = ffn_grads
    else:
        ffn_part = dot_last(hidden, full_down).astype(bf16)
        ffn_grads = [
            reduced(norm_mid_group, d_up),
            reduced(norm_mid_group, d_gate_ff),
            reduced(cot_group, hidden),
        ]

    d_cat, d_norm_back, little, gain_in = local_call(
        mixer_backward,
        [
            shape_of(bf16, count, 2 * width),
            tok,
            shape_of(f32, LANE, 2 * width + LANE),
            shape_of(f32, 1, model),
        ],
        [
            pltpu.VMEM((count, width), bf16),
            wide,
            wide,
            wide,
            pltpu.VMEM((count + TAIL, width), f32),
            pltpu.VMEM((ROWS + TAIL, width), f32),
            pltpu.VMEM((count, 2 * width), bf16),
            pltpu.VMEM((SUB, width), f32),
            pltpu.VMEM((heads, LANE, 2 * LANE), f32),
        ],
        2 * count * (3 * count * width + 3 * model * width),
        (
            back_group,
            norm_group,
            ocol,
            orow,
            pos_col,
            gain_f[0:1],
            full_in,
            full_gate,
            full_out,
            chan,
            blocks,
            *kept,
        ),
    )
    share = model // (n_dp * n_mp)
    gain_parts = jnp.concatenate([gain_in, gain_mid], axis=0).reshape(2, n_dp, n_mp, share)
    gain_parts = gain_parts.transpose(1, 2, 0, 3).reshape(n_dp, 2 * n_mp, share)
    gain_parts = jnp.pad(gain_parts, ((0, 0), (0, 2 * SUB - 2 * n_mp), (0, LANE - share)))
    gain_parts = gain_parts.reshape(2 * SUB * n_dp, LANE)
    ffn_sum = lax.psum_scatter(ffn_part, "mp", scatter_dimension=0, tiled=True)
    ffn_sum, d_norm_back = lax.optimization_barrier((ffn_sum, d_norm_back))
    output = (resid + ffn_sum.astype(f32)).astype(bf16)
    grad_inputs, *mix_grads = line_call(
        sum_back,
        n_mp,
        3,
        [shape_of(bf16, local_rows, model)]
        + (
            [shape_of(f32, rows, width)] * 3
            + [shape_of(f32, piece, little.shape[1]), shape_of(f32, 2 * SUB, LANE)]
        )
        * fused,
        True,
        False,
        (inputs, d_resid, gain_f[0:1], d_norm_back)
        + ((little, gain_parts, norm_group, back_group, d_cat, mixed) if fused else ()),
        reduce_scratch(3, rows, width)
        + given_scratch(piece, little.shape[1])
        + given_scratch(2 * SUB, LANE)
        + [pltpu.VMEM((n_mp - 1, 2 * SUB, LANE), f32)]
        + [pltpu.SemaphoreType.DMA((n_mp - 1,))] * 2
        if fused
        else (),
        4 * fused,
    )
    if fused:
        *mix_grads, little_own, gain_own = mix_grads
    else:
        mix_grads = [
            reduced(norm_group, d_cat[:, :width]),
            reduced(norm_group, d_cat[:, width:]),
            reduced(back_group, mixed),
        ]
        little_own = lax.psum_scatter(little, "dp", scatter_dimension=0, tiled=True)
        gain_own = lax.psum(lax.psum_scatter(gain_parts, "dp", scatter_dimension=0, tiled=True), "mp")
    grad_gains = lax.dynamic_slice_in_dim(gain_own, 2 * lax.axis_index("mp"), 2, axis=0)[:, :share]
    lines_own = little_own[:, 2 * width : 2 * width + SUB * heads].reshape(piece, heads, SUB)
    lines_own = lines_own.transpose(2, 1, 0)
    grad_blocks = little_own[:, : 2 * width].reshape(piece, heads, 2, LANE).transpose(2, 1, 0, 3)

    return (
        output,
        grad_inputs,
        grad_gains,
        mix_grads[0],
        mix_grads[1],
        mix_grads[2].T,
        lines_own[0:4],
        lines_own[4:7],
        lines_own[7],
        grad_blocks,
        ffn_grads[0],
        ffn_grads[1],
        ffn_grads[2].T,
    )


def solution(mesh):
    row, col = P("dp", "mp"), P("mp", "dp")
    tok = P(("dp", "mp"), None)
    chan = P(None, "mp", "dp")
    gate = P(None, "mp", "dp", None)
    return jax.shard_map(
        shards,
        mesh=mesh,
        in_specs=(
            tok, tok, P(("dp", "mp")), P("dp", None), P("dp", None), P(),
            row, row, col, chan, chan, col, gate, row, row, col,
        ),
        out_specs=(
            tok, tok, P(None, ("dp", "mp")), row, row, col, chan, chan, col, gate, row, row, col,
        ),
        check_vma=False,
    )
```

```python
import functools

import jax
import jax.numpy as jnp
from jax import lax
from jax.experimental import pallas as pl
from jax.experimental.pallas import tpu as pltpu
from jax.sharding import PartitionSpec as P

epsilon = 1e-06
LANE = 128
SUB = 8
TAIL = 24
ROWS = 272
VMEM_MB = 62
f32 = jnp.float32
bf16 = jnp.bfloat16
GELU_C = 0.7978845608028654
GELU_A = 0.044715


def rms_scale(values):
    return lax.rsqrt(jnp.mean(values * values, axis=-1, keepdims=True) + epsilon)


def dot(left, right):
    return lax.dot_general(left, right, (((1,), (0,)), ((), ())), preferred_element_type=f32)


def dot_last(left, right):
    return lax.dot_general(left, right, (((1,), (1,)), ((), ())), preferred_element_type=f32)


def dot_first(left, right):
    return lax.dot_general(left, right, (((0,), (0,)), ((), ())), preferred_element_type=f32)


def gelu_of(v):
    return 0.5 * v * (1.0 + jnp.tanh(GELU_C * (v + GELU_A * v * v * v)))


def gelu_both(v):
    square = v * v
    th = jnp.tanh(GELU_C * (v + GELU_A * v * square))
    half = 0.5 * (1.0 + th)
    slope = half + 0.5 * v * (1.0 - th * th) * (GELU_C * (1.0 + 3.0 * GELU_A * square))
    return v * half, slope


def sigmoid(v):
    return 0.5 * jnp.tanh(0.5 * v) + 0.5


def split(values):
    high = values.astype(bf16)
    return high, (values - high.astype(f32)).astype(bf16)


def rows_of(index, rows):
    return pl.ds(pl.multiple_of(index * rows, rows), rows)


def pick_rows(order_col, count):
    places = lax.broadcasted_iota(jnp.int32, (order_col.shape[0], count), 1)
    return (places == order_col).astype(f32).astype(bf16)


def put_rows(order_row, first, rows):
    places = lax.broadcasted_iota(jnp.int32, (rows, order_row.shape[1]), 0) + first
    return (places == order_row).astype(f32).astype(bf16)


def mixer_forward(tokens, ocol, orow, pos, w_in, w_gate, chan, blocks, w_out_far, *rest):
    far, rest = rest[:8], rest[8:]
    packed, rate, prod, before, low, w_out, *near, late_sem, held_sem = rest
    gate_ref, branch_ref, conv_ref, gin_ref, grec_ref, state_ref, mixed_ref, out_ref = near
    (late_out,) = late_all([w_out_far], [w_out], late_sem)
    leaving = [
        pltpu.make_async_copy(source, target, held_sem.at[i, 0])
        for i, (source, target) in enumerate(zip(near, far))
    ]
    count, _ = tokens.shape
    width = w_in.shape[1]
    steps = count // SUB
    heads = width // LANE

    def project(b, carry):
        at = rows_of(b, ROWS)
        packed[...] = dot(pick_rows(ocol[at, :], count), tokens[...]).astype(bf16)
        branch_ref[at, :] = dot(packed[...], w_in[...])
        gate_ref[at, :] = dot(packed[...], w_gate[...])
        return carry

    lax.fori_loop(0, count // ROWS, project, 0)
    leaving[0].start()
    leaving[1].start()

    for k in range(TAIL // SUB):
        last = branch_ref[pl.ds(count - TAIL + k * SUB, SUB), :]
        before[pl.ds(k * SUB, SUB), :] = pltpu.roll(last, 1, 0)
    before[pl.ds(TAIL, ROWS), :] = branch_ref[pl.ds(0, ROWS), :]

    def gates(b, carry):
        at = rows_of(b, ROWS)

        @pl.when(b > 0)
        def _():
            before[...] = branch_ref[pl.ds(pl.multiple_of(b * ROWS - TAIL, SUB), ROWS + TAIL), :]

        place = pos[at, :]
        for h in range(heads):
            lanes = pl.ds(h * LANE, LANE)
            par = chan[:, lanes]
            conv = par[4:5] + par[0:1] * before[pl.ds(TAIL, ROWS), lanes]
            for k in range(1, 4):
                earlier = before[pl.ds(TAIL - SUB * k, ROWS), lanes]
                conv = conv + par[k : k + 1] * jnp.where(place >= k, earlier, 0.0)
            high, rest = split(conv)
            pair = jnp.concatenate([blocks[h], blocks[heads + h]], axis=1)
            pre = dot(
                jnp.concatenate([high, rest], axis=1), jnp.concatenate([pair, pair], axis=0)
            )
            gate_in = sigmoid(pre[:, :LANE] + par[5:6])
            gate_rec = sigmoid(pre[:, LANE:] + par[6:7])
            kept = jnp.exp(-8.0 * gate_rec * par[7:8])
            drive = jnp.sqrt(1.0 - kept * kept + 0.01) * gate_in * conv
            conv_ref[at, lanes] = conv
            gin_ref[at, lanes] = gate_in
            grec_ref[at, lanes] = gate_rec
            rate[at, lanes] = jnp.where(place >= 1, kept, 0.0)
            state_ref[at, lanes] = drive
        return carry

    lax.fori_loop(0, count // ROWS, gates, 0)
    for copy in leaving[2:5]:
        copy.start()

    def scan(i, carry):
        held, passed = carry
        at = rows_of(i, SUB)
        a = rate[at, :]
        held = a * held + state_ref[at, :]
        passed = a * passed
        state_ref[at, :] = held
        prod[at, :] = passed
        return held, passed

    ends = lax.fori_loop(
        0, steps, scan, (jnp.zeros((SUB, width), f32), jnp.ones((SUB, width), f32)), unroll=8
    )
    first = lax.broadcasted_iota(jnp.int32, (SUB, width), 0) == 0
    carry_in = jnp.zeros((SUB, width), f32)
    for _ in range(SUB - 1):
        carry_in = jnp.where(first, 0.0, pltpu.roll(ends[0] + ends[1] * carry_in, 1, 0))

    def finish(i, carry):
        at = rows_of(i, 2 * SUB)
        twice = jnp.concatenate([carry_in, carry_in], axis=0)
        value = state_ref[at, :] + prod[at, :] * twice
        state_ref[at, :] = value
        low[at, :] = (gelu_of(gate_ref[at, :]) * value).astype(bf16)
        return carry

    lax.fori_loop(0, steps // 2, finish, 0, unroll=2)
    leaving[5].start()
    late_out.ready()

    def leave(b, carry):
        at = rows_of(b, ROWS)
        mixed = dot(put_rows(orow[...], b * ROWS, ROWS), low[...]).astype(bf16)
        mixed_ref[at, :] = mixed
        out_ref[at, :] = dot_last(mixed, w_out[...]).astype(bf16)
        return carry

    lax.fori_loop(0, count // ROWS, leave, 0)
    for copy in leaving[6:]:
        copy.start()
    for copy in leaving:
        copy.wait()


def ffn(tokens, w_up, w_gate_far, cot_far, w_down_far, *rest):
    far, rest = rest[:4], rest[4:]
    w_gate, cot, w_down, *near, late_sem, held_sem = rest
    dnorm_ref, hidden_ref, dup_ref, dgate_ref = near
    late = late_all([w_gate_far, cot_far, w_down_far], [w_gate, cot, w_down], late_sem)
    blocks_of = tokens.shape[0] // ROWS

    def leaving(b):
        at = rows_of(b, ROWS)
        return [
            pltpu.make_async_copy(source.at[at], target.at[at], held_sem.at[i, b])
            for i, (source, target) in enumerate(zip(near, far))
        ]

    def block(b, carry):
        at = rows_of(b, ROWS)
        up = dot(tokens[at, :], w_up[...])

        @pl.when(b == 0)
        def _():
            for array in late:
                array.copy.wait()

        value, slope = gelu_both(dot(tokens[at, :], w_gate[...]))
        hidden_ref[at, :] = (value * up).astype(bf16)
        d_hidden = dot(cot[at, :], w_down[...])
        d_up = (d_hidden * value).astype(bf16)
        d_gate = (d_hidden * up * slope).astype(bf16)
        dup_ref[at, :] = d_up
        dgate_ref[at, :] = d_gate
        dnorm_ref[at, :] = (dot_last(d_up, w_up[...]) + dot_last(d_gate, w_gate[...])).astype(bf16)
        for copy in leaving(b):
            copy.start()
        return carry

    lax.fori_loop(0, blocks_of, block, 0)
    for b in range(blocks_of):
        for copy in leaving(b):
            copy.wait()


def mixer_backward(back, w_out, ocol, orow, pos, gain, chan, blocks, *rest):
    far, (dcat_ref, dnorm_ref, little_ref, dgain_ref), rest = rest[:9], rest[9:13], rest[13:]
    dmix_arr, dmix, adj, prod, after, before, low, small_ref, dblocks_ref, *rest = rest
    gate_ref, grec_ref, state_ref, conv_ref, gin_ref, branch_ref, norm, w_in, w_gate, late_sem = rest
    late = late_all(far, rest[:9], late_sem)
    count, _ = back.shape
    width = w_in.shape[1]
    steps = count // SUB
    heads = width // LANE
    blocks_of = count // ROWS

    def enter(b, carry):
        at = rows_of(b, ROWS)
        dmix_arr[at, :] = dot(back[at, :], w_out[...]).astype(bf16)
        return carry

    lax.fori_loop(0, blocks_of, enter, 0)
    for array in late[:3]:
        array.ready()

    def pack(b, carry):
        at = rows_of(b, ROWS)
        d_mixed = dot(pick_rows(ocol[at, :], count), dmix_arr[...])
        value, slope = gelu_both(gate_ref[at, :])
        adj[at, :] = d_mixed * value
        low[at, pl.ds(width, width)] = (d_mixed * state_ref[at, :] * slope).astype(bf16)
        kept = jnp.exp(-8.0 * grec_ref[at, :] * chan[7:8, :])
        dmix[at, :] = jnp.where(pos[at, :] >= 1, kept, 0.0)
        return carry

    lax.fori_loop(0, blocks_of, pack, 0)
    for array in late:
        array.ready()

    def scan(i, carry):
        held, passed, following = carry
        at = rows_of(steps - 1 - i, SUB)
        held = following * held + adj[at, :]
        passed = following * passed
        adj[at, :] = held
        prod[at, :] = passed
        return held, passed, dmix[at, :]

    last = lax.broadcasted_iota(jnp.int32, (SUB, width), 0) == SUB - 1
    wrapped = jnp.where(last, 0.0, pltpu.roll(dmix[pl.ds(0, SUB), :], SUB - 1, 0))
    ends = lax.fori_loop(
        0,
        steps,
        scan,
        (jnp.zeros((SUB, width), f32), jnp.ones((SUB, width), f32), wrapped),
        unroll=8,
    )
    carry_in = jnp.zeros((SUB, width), f32)
    for _ in range(SUB - 1):
        carry_in = jnp.where(last, 0.0, pltpu.roll(ends[0] + ends[1] * carry_in, SUB - 1, 0))

    small_ref[...] = jnp.zeros_like(small_ref)
    dblocks_ref[...] = jnp.zeros_like(dblocks_ref)
    first = lax.broadcasted_iota(jnp.int32, (SUB, width), 0) == 0
    state_last = state_ref[pl.ds(count - SUB, SUB), :]
    before[pl.ds(TAIL - SUB, SUB), :] = jnp.where(first, 0.0, pltpu.roll(state_last, 1, 0))
    before[pl.ds(TAIL, ROWS), :] = state_ref[pl.ds(0, ROWS), :]
    wide_carry = jnp.concatenate([carry_in] * (ROWS // SUB), axis=0)

    def point(b, carry):
        at = rows_of(b, ROWS)

        @pl.when(b > 0)
        def _():
            before[...] = state_ref[pl.ds(pl.multiple_of(b * ROWS - TAIL, SUB), ROWS + TAIL), :]

        place = pos[at, :]
        for h in range(heads):
            lanes = pl.ds(h * LANE, LANE)
            par = chan[:, lanes]
            adjoint = adj[at, lanes] + prod[at, lanes] * wide_carry[:, h * LANE : (h + 1) * LANE]
            conv = conv_ref[at, lanes]
            gate_in = gin_ref[at, lanes]
            gate_rec = grec_ref[at, lanes]
            kept = jnp.exp(-8.0 * gate_rec * par[7:8])
            square = kept * kept
            inside = 1.0 - square + 0.01
            inverse = lax.rsqrt(inside)
            root = inside * inverse
            previous = before[pl.ds(TAIL - SUB, ROWS), lanes]
            d_log = adjoint * previous * dmix[at, lanes]
            scaled = adjoint * gate_in
            d_log = d_log - scaled * conv * square * inverse
            d_in = adjoint * root * conv * gate_in * (1.0 - gate_in)
            d_rec = d_log * (-8.0 * par[7:8]) * gate_rec * (1.0 - gate_rec)
            both = jnp.concatenate([d_in, d_rec], axis=1)
            high, rest = split(both)
            pair = jnp.concatenate([blocks[h], blocks[heads + h]], axis=1)
            d_conv = scaled * root + dot_last(high, pair) + dot_last(rest, pair)
            dblocks_ref[h] += dot_first(conv.astype(bf16), high)
            after[at, lanes] = d_conv
            small_ref[4:5, lanes] += jnp.sum(d_conv, axis=0, keepdims=True)
            small_ref[5:6, lanes] += jnp.sum(d_in, axis=0, keepdims=True)
            small_ref[6:7, lanes] += jnp.sum(d_rec, axis=0, keepdims=True)
            small_ref[7:8, lanes] += (
                jnp.sum(d_log * gate_rec, axis=0, keepdims=True) * (-8.0) * par[8:9]
            )
        return carry

    lax.fori_loop(0, blocks_of, point, 0)

    for k in range(TAIL // SUB):
        head = after[pl.ds(k * SUB, SUB), :]
        after[pl.ds(count + k * SUB, SUB), :] = pltpu.roll(head, SUB - 1, 0)
        tail = branch_ref[pl.ds(count - TAIL + k * SUB, SUB), :]
        before[pl.ds(k * SUB, SUB), :] = pltpu.roll(tail, 1, 0)
    before[pl.ds(TAIL, ROWS), :] = branch_ref[pl.ds(0, ROWS), :]

    def unmix(b, carry):
        at = rows_of(b, ROWS)

        @pl.when(b > 0)
        def _():
            before[...] = branch_ref[pl.ds(pl.multiple_of(b * ROWS - TAIL, SUB), ROWS + TAIL), :]

        place = pos[at, :]
        for h in range(heads):
            lanes = pl.ds(h * LANE, LANE)
            par = chan[:, lanes]
            d_conv = after[at, lanes]
            d_branch = par[0:1] * d_conv
            small_ref[0:1, lanes] += jnp.sum(
                d_conv * before[pl.ds(TAIL, ROWS), lanes], axis=0, keepdims=True
            )
            for k in range(1, 4):
                later = pl.ds(pl.multiple_of(b * ROWS + SUB * k, SUB), ROWS)
                d_branch = d_branch + par[k : k + 1] * jnp.where(
                    pos[later, :] >= k, after[later, lanes], 0.0
                )
                earlier = before[pl.ds(TAIL - SUB * k, ROWS), lanes]
                small_ref[k : k + 1, lanes] += jnp.sum(
                    jnp.where(place >= k, d_conv * earlier, 0.0), axis=0, keepdims=True
                )
            low[at, lanes] = d_branch.astype(bf16)
        return carry

    lax.fori_loop(0, blocks_of, unmix, 0)
    lines = [small_ref[0:SUB, h * LANE : (h + 1) * LANE] for h in range(heads)]
    lines.append(jnp.zeros((LANE - SUB * heads, LANE), f32))
    little_ref[:, pl.ds(2 * width, LANE)] = jnp.concatenate(lines, axis=0).T
    for h in range(heads):
        little_ref[:, pl.ds(2 * h * LANE, 2 * LANE)] = dblocks_ref[h]
    dgain_ref[...] = jnp.zeros_like(dgain_ref)

    def leave(b, carry):
        at = rows_of(b, ROWS)
        cat = dot(put_rows(orow[...], b * ROWS, ROWS), low[...]).astype(bf16)
        dcat_ref[at, :] = cat
        d_norm = dot_last(cat[:, :width], w_in[...]) + dot_last(cat[:, width:], w_gate[...])
        dgain_ref[...] += jnp.sum(d_norm * norm[at, :].astype(f32), axis=0, keepdims=True)
        dnorm_ref[at, :] = d_norm.astype(bf16)
        return carry

    lax.fori_loop(0, blocks_of, leave, 0)
    dgain_ref[...] = dgain_ref[...] / gain[...]


MESH = pl.DeviceIdType.MESH
TILE = 16
PIECES = 8
HOP = 1
AFTER = 1


def cut_rows(rows, parts):
    tiles = rows // TILE
    ends = [tiles * (k + 1) // parts for k in range(parts)]
    return [(TILE * a, TILE * (b - a)) for a, b in zip([0] + ends[:-1], ends)]


class Line:
    def __init__(self, n, local, part, arrived, whole, sums, alls):
        self.n, self.local, self.part, self.arrived, self.whole = n, local, part, arrived, whole
        self.sums, self.alls = sums, alls
        self.me = lax.axis_index("mp")
        self.pieces = cut_rows(local, PIECES)
        self.has = (self.me > 0, self.me < n - 1)

    def greet(self, plane=None):
        barrier = pltpu.get_barrier_semaphore()
        more = 0
        if plane is not None:
            for bit in plane.bits:
                more += 1
                pl.semaphore_signal(
                    barrier, inc=1, device_id={"dp": plane.other(bit)}, device_id_type=MESH
                )
        for away in range(1, self.n):
            more += 1
            pl.semaphore_signal(
                barrier,
                inc=1,
                device_id={"mp": lax.rem(self.me + away, self.n)},
                device_id_type=MESH,
            )
        pl.semaphore_wait(barrier, more)

    def rows_at(self, owner, k):
        first, rows = self.pieces[k]
        return pl.ds(pl.multiple_of(owner * self.local + first, TILE), rows)

    def copy(self, source, target, sems, way, owner, k):
        return pltpu.make_async_remote_copy(
            src_ref=source,
            dst_ref=target,
            send_sem=sems[0].at[way, owner, k],
            recv_sem=sems[1].at[way, owner, k],
            device_id={"mp": self.me + 1 - 2 * way},
            device_id_type=MESH,
        )

    def sum_copy(self, way, owner, k, first=False):
        at = self.rows_at(owner, k)
        landed = self.arrived[way].at[at]
        return self.copy(self.part.at[at] if first else landed, landed, self.sums, way, owner, k)

    def all_copy(self, way, owner, k):
        block = self.whole.at[self.rows_at(owner, k)]
        return self.copy(block, block, self.alls, way, owner, k)

    def first(self, k):
        for away in range(self.n - 1):
            for way in range(2):
                owner = away if way else self.n - 1 - away

                @pl.when(jnp.logical_not(self.has[way]))
                def _():
                    self.sum_copy(way, owner, k, True).start()

    def relay(self, k, stage):
        for way in range(2):
            late = stage - (self.n - 1 - self.me if way else self.me)
            owner = late if way else self.n - 1 - late

            @pl.when(self.has[way] & (late >= 0))
            def _():
                self.sum_copy(way, owner, k).wait_recv()
                at = self.rows_at(owner, k)
                landed = self.arrived[way]
                landed[at, :] = (landed[at, :].astype(f32) + self.part[at, :].astype(f32)).astype(bf16)
                self.sum_copy(way, owner, k).start()

    def total(self, k, into):
        at = self.rows_at(self.me, k)
        rows = pl.ds(0, self.pieces[k][1])
        into[rows, :] = self.part[at, :].astype(f32)
        for way in range(2):

            @pl.when(self.has[way])
            def _():
                self.sum_copy(way, self.me, k).wait_recv()
                into[rows, :] += self.arrived[way][at, :].astype(f32)

    def spread(self, k):
        for way in range(2):

            @pl.when(self.has[1 - way])
            def _():
                self.all_copy(way, self.me, k).start()

    def forward(self, k, stage):
        for way in range(2):
            owner = self.me + stage if way else self.me - stage
            there = owner < self.n if way else owner >= 0

            @pl.when(there)
            def _():
                self.all_copy(way, owner, k).wait_recv()

            @pl.when(there & self.has[1 - way])
            def _():
                self.all_copy(way, owner, k).start()

    def finish(self):
        for k in range(PIECES):
            for owner in range(self.n):
                for way in range(2):
                    if self.part is not None:

                        @pl.when(self.me > owner if way else self.me < owner)
                        def _():
                            self.sum_copy(way, owner, k).wait_send()

                    if self.whole is not None:
                        reached = self.me <= owner if way else self.me >= owner

                        @pl.when(reached & self.has[1 - way])
                        def _():
                            self.all_copy(way, owner, k).wait_send()

    def run(self, point, tasks=()):
        sums, alls = self.part is not None, self.whole is not None
        slots = [[] for _ in range(PIECES + (HOP + AFTER) * (self.n - 1) + 1)]
        for k in range(PIECES):
            done = k + HOP * (self.n - 1) if sums else 0
            if sums:
                slots[k].append((0, functools.partial(self.first, k)))
                for stage in range(1, self.n - 1):
                    slots[k + HOP * stage].append((2, functools.partial(self.relay, k, stage)))
            slots[done].append((3, functools.partial(point, k)))
            if alls:
                slots[done].append((4, functools.partial(self.spread, k)))
                for stage in range(1, self.n):
                    at = (done if sums else k) + AFTER * stage
                    slots[at].append((1, functools.partial(self.forward, k, stage)))
        tasks = iter(tasks)
        for slot in slots:
            for step, (_, work) in enumerate(sorted(slot, key=lambda entry: entry[0])):
                if step in (0, 3):
                    next(tasks, idle)()
                work()
        for task in tasks:
            task()
        self.finish()

    def tiles(self, k, body):
        first, rows = self.pieces[k]

        def one(i, carry):
            body(
                pl.ds(pl.multiple_of(i * TILE, TILE), TILE),
                pl.ds(pl.multiple_of(first + i * TILE, TILE), TILE),
                pl.ds(pl.multiple_of(self.me * self.local + first + i * TILE, TILE), TILE),
            )
            return carry

        lax.fori_loop(0, rows // TILE, one, 0)


def idle():
    pass


class Late:
    def __init__(self, source, ref, sem):
        self.ref = ref
        self.copy = pltpu.make_async_copy(source, ref, sem)
        self.pending = True
        self.copy.start()

    def ready(self):
        if self.pending:
            self.copy.wait()
        self.pending = False


def late_all(sources, refs, sems):
    return [Late(source, ref, sems.at[i]) for i, (source, ref) in enumerate(zip(sources, refs))]


class Plane:
    bits = (1, 2, 4)
    orders = ((4, 2, 1), (2, 4, 1))

    def __init__(self):
        self.me = lax.axis_index("dp")

    def bit(self, bit):
        return lax.rem(self.me // bit, 2)

    def other(self, *bits):
        return self.me + sum(bit * (1 - 2 * self.bit(bit)) for bit in bits)

    def gather_copies(self, item, view, halves, stage, sems):
        copies = []
        for half in halves:
            order = self.orders[half]
            for combo in range(1 << stage):
                flipped = [bit for i, bit in enumerate(order[:stage]) if combo >> i & 1]
                block = view(self.other(*flipped), half)
                slot = (1 << stage) - 1 + combo
                copies.append(
                    pltpu.make_async_remote_copy(
                        src_ref=block,
                        dst_ref=block,
                        send_sem=sems[0].at[item, half, slot],
                        recv_sem=sems[1].at[item, half, slot],
                        device_id={"dp": self.other(order[stage])},
                        device_id_type=MESH,
                    )
                )
        return copies


class Reduce(Plane):
    def __init__(self, index, left, right, lanes, sent, mine, theirs, got, second, third, out, sems):
        super().__init__()
        self.sent, self.theirs = sent, theirs
        self.index, self.left, self.right, self.lanes = index, left, right, lanes
        self.mine, self.got = mine.at[index], got.at[index]
        self.second, self.third, self.out = second.at[index], third.at[index], out
        self.sems = sems
        self.rows = out.shape[0]
        self.half = self.rows // 2

    def copy(self, source, target, slot, bit):
        return pltpu.make_async_remote_copy(
            src_ref=source,
            dst_ref=target,
            send_sem=self.sems[0].at[self.index, slot],
            recv_sem=self.sems[1].at[self.index, slot],
            device_id={"dp": self.other(bit)},
            device_id_type=MESH,
        )

    def core_copy(self, t):
        return self.copy(self.theirs.at[(4 * self.index + t) % 2], self.got.at[t], t, 1)

    def second_copy(self, half, j):
        x, y = self.bit(2), self.bit(4)
        block = (1 - y) * 2 + j if half else j * 2 + 1 - x
        rows = self.mine.at[block, pl.ds(half * self.half, self.half)]
        return self.copy(rows, self.second.at[half, j], 4 + 2 * half + j, 4 if half else 2)

    def third_block(self, half):
        x, y = self.bit(2), self.bit(4)
        return y * 2 + 1 - x if half else (1 - y) * 2 + x

    def third_copy(self, half):
        rows = self.mine.at[self.third_block(half), pl.ds(half * self.half, self.half)]
        return self.copy(rows, self.third.at[half], 8 + half, 2 if half else 4)

    def product(self, t):
        def task():
            core = self.bit(1)
            pair = pl.ds(t * 2 * self.rows, 2 * self.rows)
            if t == 0:
                self.left.ready()
                self.right.ready()
            if len(self.sent) > 1:
                self.sent[-2].wait_send()
            both = dot_first(self.left.ref[:, pair], self.right.ref[:, self.lanes])
            low, high = both[: self.rows], both[self.rows :]
            self.mine[t] = jnp.where(core == 0, low, high).astype(bf16)
            self.theirs[(4 * self.index + t) % 2] = jnp.where(core == 0, high, low).astype(bf16)
            self.sent.append(self.core_copy(t))
            self.sent[-1].start()

        return task

    def keep(self, t):
        return self.mine[t]

    def add_core(self):
        for t in range(4):
            self.core_copy(t).wait_recv()
            self.mine[t] = (self.keep(t).astype(f32) + self.got[t].astype(f32)).astype(self.mine.dtype)
        for half in range(2):
            for j in range(2):
                self.second_copy(half, j).start()

    def add_second(self):
        for half in range(2):
            for j in range(2):
                self.second_copy(half, j).wait_recv()
        for half in range(2):
            block, at = self.third_block(half), pl.ds(half * self.half, self.half)
            far = 1 - self.bit(2 if half else 4)
            self.mine[block, at] = (
                self.mine[block, at].astype(f32) + self.second[half, far].astype(f32)
            ).astype(self.mine.dtype)
            self.third_copy(half).start()

    def add_third(self):
        own = self.bit(4) * 2 + self.bit(2)
        for half in range(2):
            self.third_copy(half).wait_recv()
            at = pl.ds(half * self.half, self.half)
            near = self.bit(2 if half else 4)
            self.out[at, :] = (
                self.mine[own, at].astype(f32)
                + self.second[half, near].astype(f32)
                + self.third[half].astype(f32)
            )

    def finish(self):
        for half in range(2):
            for j in range(2):
                self.second_copy(half, j).wait_send()
            self.third_copy(half).wait_send()


class Given(Reduce):
    def __init__(self, given, mine, got, second, third, out, sems):
        super().__init__(0, None, None, None, None, mine, None, got, second, third, out, sems)
        self.given = given

    def rows_of(self, t, core):
        return pl.ds(pl.multiple_of((2 * t + core) * self.rows, self.rows), self.rows)

    def core_copy(self, t):
        return self.copy(self.given.at[self.rows_of(t, 1 - self.bit(1))], self.got.at[t], t, 1)

    def start(self):
        for t in range(4):
            self.core_copy(t).start()

    def finish(self):
        for t in range(4):
            self.core_copy(t).wait_send()
        super().finish()

    def keep(self, t):
        return self.given[self.rows_of(t, self.bit(1)), :]


def reduce_tasks(parts, given=()):
    tasks = [part.product(t) for part in parts for t in range(4)]

    def also(at, extra):
        while len(tasks) <= at:
            tasks.append(idle)
        before = tasks[at]

        def both():
            extra()
            before()

        tasks[at] = both

    for i, part in enumerate(parts):
        also(4 * i + 5, part.add_core)
        also(4 * i + 8, part.add_second)
        also(4 * i + 10, part.add_third)

    for part in given:
        also(0, part.start)
        also(2, part.add_core)
        also(4, part.add_second)
        also(6, part.add_third)

    def finish():
        for copy in parts[0].sent[-2:]:
            copy.wait_send()
        for part in [*parts, *given]:
            part.finish()

    return tasks, finish


def given_scratch(rows, width):
    sem = pltpu.SemaphoreType.DMA((1, 10))
    return [
        pltpu.VMEM((1, 4, rows, width), f32),
        pltpu.VMEM((1, 4, rows, width), f32),
        pltpu.VMEM((1, 2, 2, rows // 2, width), f32),
        pltpu.VMEM((1, 2, rows // 2, width), f32),
        sem,
        sem,
    ]


def reduce_scratch(arrays, rows, width):
    block = pltpu.VMEM((arrays, 4, rows, width), bf16)
    sem = pltpu.SemaphoreType.DMA((arrays, 10))
    return [
        block,
        pltpu.VMEM((2, rows, width), bf16),
        block,
        pltpu.VMEM((arrays, 2, 2, rows // 2, width), bf16),
        pltpu.VMEM((arrays, 2, rows // 2, width), bf16),
        sem,
        sem,
    ]


def gather_norm(n, x, gain, whole, send, recv):
    line = Line(n, x.shape[0], None, None, whole, None, (send, recv))
    line.greet()

    def point(k):
        def one(_, own, at):
            v = x[own, :].astype(f32)
            whole[at, :] = (v * rms_scale(v) * gain[...]).astype(bf16)

        line.tiles(k, one)

    line.run(point)


def row_view(array, rows):
    def view(owner, half):
        first = owner * rows + half * (rows // 2)
        return array.at[pl.ds(pl.multiple_of(first, TILE), rows // 2)]

    return view


def gather_tasks(plane, items, sems):
    def copies(stage):
        return [
            copy
            for item, (view, halves) in enumerate(items)
            for copy in plane.gather_copies(item, view, halves, stage, sems)
        ]

    def stage_task(stage):
        def task():
            if stage:
                for copy in copies(stage - 1):
                    copy.wait_recv()
            for copy in copies(stage):
                copy.start()

        return task

    def last():
        for copy in copies(2):
            copy.wait_recv()
        for stage in range(3):
            for copy in copies(stage):
                copy.wait_send()

    return stage_task(0), stage_task(1), stage_task(2), last


def gather_weights(
    n,
    x,
    gain,
    w_in,
    w_gate,
    w_out,
    blocks,
    chan,
    whole,
    all_in,
    all_gate,
    all_out,
    all_blocks,
    all_chan,
    send,
    recv,
    raw,
    plane_send,
    plane_recv,
):
    line = Line(n, x.shape[0], None, None, whole, None, (send, recv))
    plane = Plane()
    line.greet(plane)
    sems = plane_send, plane_recv
    rows, piece = w_in.shape[0], blocks.shape[1]
    lines = chan.shape[0]

    def blocks_view(owner, half):
        return all_blocks.at[:, pl.ds(pl.multiple_of(owner * piece, TILE), piece)]

    def chan_view(owner, half):
        return raw.at[pl.ds(pl.multiple_of(owner * lines, TILE), lines)]

    items = [(row_view(array, rows), (0, 1)) for array in (all_in, all_gate, all_out)]
    items += [(blocks_view, (0,)), (chan_view, (1,))]

    first, second, third, finish = gather_tasks(plane, items, sems)

    def last():
        finish()
        lane = lax.broadcasted_iota(jnp.int32, (LANE, LANE), 1)
        row = lax.broadcasted_iota(jnp.int32, (LANE, LANE), 0)
        total = jnp.zeros((lines, LANE), f32)
        for owner in range(LANE // piece):
            moved = ((row < piece) & (row + owner * piece == lane)).astype(f32).astype(bf16)
            total = total + dot(raw[pl.ds(owner * lines, lines), :], moved)
        for h in range(lines // SUB):
            par = total[h * SUB : (h + 1) * SUB]
            lanes = pl.ds(h * LANE, LANE)
            all_chan[0:SUB, lanes] = par
            decay = par[SUB - 1 : SUB]
            small = jnp.exp(-jnp.abs(decay))
            one_more = 1.0 + small
            rest = jnp.where(one_more == 1.0, 1.0, one_more - 1.0)
            log_one_more = jnp.where(one_more == 1.0, small, jnp.log(one_more) * (small / rest))
            all_chan[SUB - 1 : SUB, lanes] = jnp.maximum(decay, 0.0) + log_one_more
            all_chan[SUB : 2 * SUB, lanes] = jnp.broadcast_to(sigmoid(decay), (SUB, LANE))

    own = pl.ds(pl.multiple_of(plane.me * rows, TILE), rows)
    all_in[own, :] = w_in[...]
    all_gate[own, :] = w_gate[...]
    all_out[own, :] = w_out[...]
    all_blocks[:, pl.ds(pl.multiple_of(plane.me * piece, TILE), piece), :] = blocks[...]
    raw[pl.ds(pl.multiple_of(plane.me * lines, TILE), lines), :] = chan[...]

    def point(k):
        def one(_, own, at):
            v = x[own, :].astype(f32)
            whole[at, :] = (v * rms_scale(v) * gain[...]).astype(bf16)

        line.tiles(k, one)

    first()
    line.run(point, [idle] * 4 + [second] + [idle] * 3 + [third] + [idle] * 3 + [last])


def sum_norm_gather(n, x, gain, part, *rest):
    if len(rest) > 9:
        shares, rest = rest[:3], rest[3:]
        resid, whole, *alls = rest[:5]
        left, right, total, ss, sr, send, recv, plane_send, plane_recv = rest[5:]
        plane = Plane()
    else:
        resid, whole, left, right, total, ss, sr, send, recv = rest
        plane = None
    line = Line(n, x.shape[0], part, (left, right), whole, (ss, sr), (send, recv))
    line.greet(plane)
    tasks = []
    if plane is not None:
        rows = shares[0].shape[0]
        own = pl.ds(pl.multiple_of(plane.me * rows, TILE), rows)
        for share, array in zip(shares, alls):
            array[own, :] = share[...]
        items = [(row_view(array, rows), (0, 1)) for array in alls]
        first, second, third, last = gather_tasks(plane, items, (plane_send, plane_recv))
        tasks = [first] + [idle] * 5 + [second] + [idle] * 9 + [third] + [idle] * 6 + [last]

    def point(k):
        line.total(k, total)

        def one(here, own, at):
            v = x[own, :].astype(f32) + total[here, :]
            resid[own, :] = v
            whole[at, :] = (v * rms_scale(v) * gain[...]).astype(bf16)

        line.tiles(k, one)

    line.run(point, tasks)


def norm_back(value, gain, grad):
    scale = rms_scale(value)
    e = gain * grad
    slope = scale * scale * scale * jnp.mean(value * e, axis=-1, keepdims=True)
    return scale * e - value * slope, grad * value * scale


def sum_back_gather(n, resid, cot, gain, part, *rest):
    if len(rest) > 10:
        sources, rest = rest[:6], rest[6:]
        d_resid, gain_grad, whole, low_part, high_part, *outs = rest[:8]
        left, right, total, ss, sr, send, recv, *reduce = rest[8:]
        reduce, refs, late_sems = reduce[:7], reduce[7:13], reduce[13]
    else:
        d_resid, gain_grad, whole, left, right, total, ss, sr, send, recv = rest
        sources = ()
    line = Line(n, resid.shape[0], part, (left, right), whole, (ss, sr), (send, recv))
    line.greet(Plane() if sources else None)
    gain_grad[...] = jnp.zeros_like(gain_grad)

    def point(k):
        line.total(k, total)

        def one(here, own, at):
            back, terms = norm_back(resid[own, :], gain[...], total[here, :])
            gain_grad[...] += jnp.sum(terms, axis=0, keepdims=True)
            value = cot[own, :].astype(f32) + back
            d_resid[own, :] = value
            whole[at, :] = value.astype(bf16)

        line.tiles(k, one)

    if not sources:
        line.run(point)
        return
    norm, cots, d_up, d_gate, hidden, w_down = late_all(sources, refs, late_sems)
    sent = []
    tasks, finish = reduce_tasks(
        [
            Reduce(i, *side, slice(None), sent, *reduce[:5], out, reduce[5:])
            for i, (side, out) in enumerate(
                zip(((norm, d_up), (norm, d_gate), (cots, hidden)), outs)
            )
        ]
    )

    def project(b):
        w_down.ready()
        at = pl.ds(b * ROWS, ROWS)
        value = dot_last(hidden.ref[at, :], w_down.ref[...]).astype(bf16)
        low_part[at, :] = value[:, : value.shape[1] // 2]
        high_part[at, :] = value[:, value.shape[1] // 2 :]

    for b in range(part.shape[0] // ROWS):
        tasks.insert(12 + b, functools.partial(project, b))
    line.run(point, tasks)
    finish()


def sum_back(n, x, d_resid, gain, part, *rest):
    if len(rest) > 6:
        little, gains, *rest = rest
        sources, rest = rest[:4], rest[4:]
        grad_x, *outs, little_out, gains_out = rest[:6]
        left, right, total, ss, sr, *reduce = rest[6:]
        refs, late_sems = reduce[22:26], reduce[26]
        given = [
            Given(little, *reduce[7:11], little_out, reduce[11:13]),
            Given(gains, *reduce[13:17], gains_out, reduce[17:19]),
        ]
        met, met_send, met_recv = reduce[19:22]
    else:
        grad_x, left, right, total, ss, sr = rest
        sources = ()
    line = Line(n, x.shape[0], part, (left, right), None, (ss, sr), None)
    line.greet(Plane() if sources else None)

    def point(k):
        line.total(k, total)

        def one(here, own, at):
            back, _ = norm_back(x[own, :].astype(f32), gain[...], total[here, :])
            grad_x[own, :] = (d_resid[own, :] + back).astype(bf16)

        line.tiles(k, one)

    if not sources:
        line.run(point)
        return
    norm, back_all, cat, mixed = late_all(sources, refs, late_sems)
    width = mixed.ref.shape[1]
    sent = []
    sides = (
        (norm, cat, slice(0, width)),
        (norm, cat, slice(width, 2 * width)),
        (back_all, mixed, slice(None)),
    )
    tasks, finish = reduce_tasks(
        [
            Reduce(i, *side, sent, *reduce[:5], out, reduce[5:7])
            for i, (side, out) in enumerate(zip(sides, outs))
        ],
        given,
    )
    me = lax.axis_index("mp")

    def meet(away):
        return pltpu.make_async_remote_copy(
            src_ref=gains_out,
            dst_ref=met.at[away - 1],
            send_sem=met_send.at[away - 1],
            recv_sem=met_recv.at[away - 1],
            device_id={"mp": lax.rem(me + away, n)},
            device_id_type=MESH,
        )

    def send_gains():
        for away in range(1, n):
            meet(away).start()

    def add_gains():
        for away in range(1, n):
            meet(away).wait()
        gains_out[...] += sum(met[away] for away in range(n - 1))

    tasks[7:7] = [send_gains]
    line.run(point, tasks)
    finish()
    add_gains()


def line_call(body, n, identity, outs, sums, alls, args, more=(), late=0):
    whole = pl.BlockSpec(memory_space=pltpu.VMEM)
    local, model = args[0].shape
    sem = pltpu.SemaphoreType.DMA((2, n, PIECES))
    scratch = []
    if sums:
        scratch += [pltpu.VMEM((n * local, model), bf16)] * 2
        scratch += [pltpu.VMEM((max(rows for _, rows in cut_rows(local, PIECES)), model), f32)]
        scratch += [sem, sem]
    if alls:
        scratch += [sem, sem]
    scratch += more
    if late:
        scratch += [pltpu.VMEM(a.shape, a.dtype) for a in args[-late:]]
        scratch += [pltpu.SemaphoreType.DMA((late,))]
    moved = sum(a.size * a.dtype.itemsize for a in args)
    return pl.pallas_call(
        functools.partial(body, n),
        out_shape=outs,
        in_specs=[whole] * (len(args) - late) + [pl.BlockSpec(memory_space=pl.ANY)] * late,
        out_specs=[whole] * len(outs),
        scratch_shapes=scratch,
        compiler_params=pltpu.CompilerParams(
            vmem_limit_bytes=VMEM_MB << 20, collective_id=identity, has_side_effects=True
        ),
        cost_estimate=pl.CostEstimate(flops=0, bytes_accessed=100 * moved, transcendentals=0),
    )(*args)


def finish(heads, piece, share, resid, low, high, gains, little, *rest):
    count = (len(rest) - 6) // 2
    sources, rest = rest[:count], rest[count:]
    output, grad_gains, grad_conv, grad_bias, grad_decay, grad_blocks, *rest = rest
    targets, sems = rest[:count], rest[count:]
    copies = [
        pltpu.make_async_copy(source, target, sems[0].at[i])
        for i, (source, target) in enumerate(zip(sources, targets))
    ]
    for copy in copies:
        copy.start()
    half = low.shape[1]
    output[:, :half] = (resid[:, :half] + low[...].astype(f32)).astype(bf16)
    output[:, half:] = (resid[:, half:] + high[...].astype(f32)).astype(bf16)
    for position in range(gains.shape[0] // 2):

        @pl.when(lax.axis_index("mp") == position)
        def _():
            grad_gains[...] = gains[2 * position : 2 * position + 2, :share]

    for h in range(heads):
        for gate in range(2):
            first = (2 * h + gate) * LANE
            grad_blocks[gate, h] = little[:, first : first + LANE]
    first = 2 * heads * LANE
    lines = little[:, first : first + LANE]
    lines = jnp.concatenate([lines, jnp.zeros((LANE - piece, LANE), f32)], axis=0).T
    for h in range(heads):
        for k in range(SUB):
            row = lines[h * SUB + k : h * SUB + k + 1, :piece]
            if k < 4:
                grad_conv[k, h : h + 1, :] = row
            elif k < SUB - 1:
                grad_bias[k - 4, h : h + 1, :] = row
            else:
                grad_decay[h : h + 1, :] = row
    for copy in copies:
        copy.wait()


def local_call(body, outs, scratch, flops, args, late=0, held=0, far=0):
    whole, away = pl.BlockSpec(memory_space=pltpu.VMEM), pl.BlockSpec(memory_space=pl.ANY)
    twins = list(args[len(args) - late :]) + list(outs[len(outs) - held :])
    scratch = scratch + [pltpu.VMEM(a.shape, a.dtype) for a in twins]
    if late:
        scratch.append(pltpu.SemaphoreType.DMA((late,)))
    if held:
        scratch.append(pltpu.SemaphoreType.DMA((held, 4)))
    moved = sum(a.size * a.dtype.itemsize for a in args)
    moved += sum(o.size * o.dtype.itemsize for o in outs)
    return pl.pallas_call(
        body,
        out_shape=outs,
        in_specs=[whole] * (len(args) - late - far) + [away] * (late + far),
        out_specs=[whole] * (len(outs) - held - far) + [away] * (held + far),
        scratch_shapes=scratch,
        compiler_params=pltpu.CompilerParams(vmem_limit_bytes=VMEM_MB << 20),
        cost_estimate=pl.CostEstimate(flops=flops, bytes_accessed=moved, transcendentals=0),
    )(*args)


def shape_of(dtype, *shape):
    return jax.ShapeDtypeStruct(shape, dtype)


def shards(
    inputs,
    cotangent,
    token_mask,
    order,
    lengths,
    gains,
    w_in,
    w_gate,
    w_out,
    conv_weight,
    chan_bias,
    decay,
    gate_blocks,
    w_up,
    w_gate_ff,
    w_down,
):
    n_dp = lax.axis_size("dp")
    local_rows, model = inputs.shape
    count = local_rows * lax.axis_size("mp")
    heads, piece = decay.shape
    width = heads * piece * n_dp
    hidden_width = w_up.shape[1]

    fused = n_dp == 8
    rows = model // n_dp
    out_rows, down_rows = w_out.T, w_down.T
    lines = jnp.concatenate([conv_weight, chan_bias, decay[None]], axis=0).transpose(1, 0, 2)
    lines = lines.reshape(SUB * heads, piece)

    steps = count // SUB
    ends = jnp.cumsum(lengths[0], dtype=jnp.int32)
    starts = ends - lengths[0]
    places = jnp.arange(count, dtype=jnp.int32)
    own_start = jnp.max(
        jnp.where(places[:, None] >= starts[None, :], starts[None, :], 0), axis=1
    )
    pos = (places - own_start).reshape(SUB, steps).T
    wrap = jnp.concatenate([pos[: TAIL // SUB, 1:], jnp.full((TAIL // SUB, 1), -1, jnp.int32)], axis=1)
    pos_col = jnp.concatenate([pos, wrap], axis=0).reshape(count + TAIL, 1)
    order_int = order[0].reshape(SUB, steps).T.reshape(count)
    ocol, orow = order_int.reshape(count, 1), order_int.reshape(1, count)

    gain_f = gains.astype(f32)
    n_mp = lax.axis_size("mp")
    tok = shape_of(bf16, count, model)
    own = shape_of(f32, local_rows, model)
    if fused:
        grown = shape_of(bf16, model, width)
        norm_group, full_in, full_gate, full_out, blocks, chan = line_call(
            gather_weights,
            n_mp,
            0,
            [tok, grown, grown, grown, shape_of(bf16, 2 * heads, LANE, LANE), shape_of(f32, 16, width)],
            False,
            True,
            (
                inputs,
                gain_f[0:1],
                w_in,
                w_gate,
                out_rows,
                gate_blocks.reshape(2 * heads, piece, LANE),
                jnp.pad(lines, ((0, 0), (0, LANE - piece))),
            ),
            [pltpu.VMEM((n_dp * SUB * heads, LANE), bf16)] + [pltpu.SemaphoreType.DMA((5, 2, 7))] * 2,
        )
    else:
        (norm_group,) = line_call(gather_norm, n_mp, 0, [tok], False, True, (inputs, gain_f[0:1]))
        full_in = lax.all_gather(w_in, "dp", axis=0, tiled=True)
        full_gate = lax.all_gather(w_gate, "dp", axis=0, tiled=True)
        full_out = lax.all_gather(out_rows, "dp", axis=0, tiled=True)
        blocks = lax.all_gather(gate_blocks, "dp", axis=2, tiled=True).reshape(2 * heads, LANE, LANE)
        params = lax.all_gather(lines, "dp", axis=1, tiled=True).astype(f32)
        params = params.reshape(heads, SUB, LANE).transpose(1, 0, 2).reshape(SUB, width)
        decay_row = params[7:8]
        chan = jnp.concatenate(
            [params[:7], jax.nn.softplus(decay_row)] + [jax.nn.sigmoid(decay_row)] * SUB, axis=0
        )
    cot = cotangent * token_mask.astype(bf16)[:, None]

    cot_late, norm_group = lax.optimization_barrier((cot, norm_group))
    cot_group = lax.all_gather(cot_late, "mp", axis=0, tiled=True)

    wide = pltpu.VMEM((count, width), f32)
    saved = [shape_of(f32, count, width)] * 6
    gate_pre, branch, conv, gate_in, gate_rec, state, mixed, back_part = local_call(
        mixer_forward,
        saved + [shape_of(bf16, count, width), shape_of(bf16, count, model)],
        [
            pltpu.VMEM((ROWS, model), bf16),
            wide,
            wide,
            pltpu.VMEM((ROWS + TAIL, width), f32),
            pltpu.VMEM((count, width), bf16),
        ],
        2 * count * (count * model + 3 * model * width),
        (norm_group, ocol, orow, pos_col, full_in, full_gate, chan, blocks, full_out),
        1,
        8,
    )
    shares = (w_up, w_gate_ff, down_rows)
    resid, norm_mid_group, *ffn_weights = line_call(
        sum_norm_gather,
        n_mp,
        1,
        [own, tok] + [shape_of(bf16, model, hidden_width)] * (3 * fused),
        True,
        True,
        (inputs, gain_f[1:2], back_part) + (shares if fused else ()),
        [pltpu.SemaphoreType.DMA((3, 2, 7))] * (2 * fused),
    )
    if not fused:
        ffn_weights = [lax.all_gather(share, "dp", axis=0, tiled=True) for share in shares]
    full_up, full_gate_ff, full_down = ffn_weights

    hid = shape_of(bf16, count, hidden_width)
    d_norm_part, hidden, d_up, d_gate_ff = local_call(
        ffn,
        [tok, hid, hid, hid],
        [],
        10 * count * model * hidden_width,
        (norm_mid_group, full_up, full_gate_ff, cot_group, full_down),
        3,
        4,
    )
    d_resid, gain_mid, back_group, *ffn_grads = line_call(
        sum_back_gather,
        n_mp,
        2,
        [own, shape_of(f32, 1, model), tok]
        + ([shape_of(bf16, count, model // 2)] * 2 + [shape_of(f32, rows, hidden_width)] * 3) * fused,
        True,
        True,
        (resid, cot, gain_f[1:2], d_norm_part)
        + ((norm_mid_group, cot_group, d_up, d_gate_ff, hidden, full_down) if fused else ()),
        reduce_scratch(3, rows, hidden_width) if fused else (),
        6 * fused,
    )
    def reduced(left, right):
        grad = dot_first(left, right).astype(bf16)
        return lax.psum_scatter(grad, "dp", scatter_dimension=0, tiled=True).astype(f32)

    if fused:
        *ffn_parts, up_grad, gate_ff_grad, down_grad = ffn_grads
    else:
        ffn_parts = jnp.split(dot_last(hidden, full_down).astype(bf16), 2, axis=1)
        up_grad = reduced(norm_mid_group, d_up)
        gate_ff_grad = reduced(norm_mid_group, d_gate_ff)
        down_grad = reduced(cot_group, hidden)

    d_cat, d_norm_back, little, gain_in = local_call(
        mixer_backward,
        [
            shape_of(bf16, count, 2 * width),
            tok,
            shape_of(f32, LANE, 2 * width + LANE),
            shape_of(f32, 1, model),
        ],
        [
            pltpu.VMEM((count, width), bf16),
            wide,
            wide,
            wide,
            pltpu.VMEM((count + TAIL, width), f32),
            pltpu.VMEM((ROWS + TAIL, width), f32),
            pltpu.VMEM((count, 2 * width), bf16),
            pltpu.VMEM((SUB, width), f32),
            pltpu.VMEM((heads, LANE, 2 * LANE), f32),
        ],
        2 * count * (3 * count * width + 3 * model * width),
        (
            back_group,
            full_out,
            ocol,
            orow,
            pos_col,
            gain_f[0:1],
            chan,
            blocks,
            gate_pre,
            gate_rec,
            state,
            conv,
            gate_in,
            branch,
            norm_group,
            full_in,
            full_gate,
        ),
        9,
    )
    share = model // (n_dp * n_mp)
    gain_parts = jnp.concatenate([gain_in, gain_mid], axis=0).reshape(2, n_dp, n_mp, share)
    gain_parts = gain_parts.transpose(1, 2, 0, 3).reshape(n_dp, 2 * n_mp, share)
    gain_parts = jnp.pad(gain_parts, ((0, 0), (0, 2 * SUB - 2 * n_mp), (0, LANE - share)))
    gain_parts = gain_parts.reshape(2 * SUB * n_dp, LANE)
    ffn_low, ffn_high = (
        lax.psum_scatter(part, "mp", scatter_dimension=0, tiled=True) for part in ffn_parts
    )
    ffn_low, d_norm_back = lax.optimization_barrier((ffn_low, d_norm_back))
    grad_inputs, *mix_grads = line_call(
        sum_back,
        n_mp,
        3,
        [shape_of(bf16, local_rows, model)]
        + (
            [shape_of(f32, rows, width)] * 3
            + [shape_of(f32, piece, little.shape[1]), shape_of(f32, 2 * SUB, LANE)]
        )
        * fused,
        True,
        False,
        (inputs, d_resid, gain_f[0:1], d_norm_back)
        + ((little, gain_parts, norm_group, back_group, d_cat, mixed) if fused else ()),
        reduce_scratch(3, rows, width)
        + given_scratch(piece, little.shape[1])
        + given_scratch(2 * SUB, LANE)
        + [pltpu.VMEM((n_mp - 1, 2 * SUB, LANE), f32)]
        + [pltpu.SemaphoreType.DMA((n_mp - 1,))] * 2
        if fused
        else (),
        4 * fused,
    )
    if fused:
        *mix_grads, little_own, gain_own = mix_grads
    else:
        mix_grads = [
            reduced(norm_group, d_cat[:, :width]),
            reduced(norm_group, d_cat[:, width:]),
            reduced(back_group, mixed),
        ]
        little_own = lax.psum_scatter(little, "dp", scatter_dimension=0, tiled=True)
        gain_own = lax.psum(lax.psum_scatter(gain_parts, "dp", scatter_dimension=0, tiled=True), "mp")
    outs = [
        shape_of(bf16, local_rows, model),
        shape_of(f32, 2, share),
        shape_of(f32, 4, heads, piece),
        shape_of(f32, 3, heads, piece),
        shape_of(f32, heads, piece),
        shape_of(f32, 2, heads, piece, LANE),
    ]
    copied = [grad_inputs, mix_grads[0], mix_grads[1], up_grad, gate_ff_grad] if fused else []
    output, grad_gains, grad_conv, grad_bias, grad_decay, grad_blocks, *copied = local_call(
        functools.partial(finish, heads, piece, share),
        outs + [shape_of(a.dtype, *a.shape) for a in copied],
        [pltpu.SemaphoreType.DMA((5,))] if fused else [],
        0,
        (resid, ffn_low, ffn_high, gain_own, little_own, *copied),
        far=len(copied),
    )
    if fused:
        grad_inputs, grad_in, grad_gate, up_grad, gate_ff_grad = copied
    else:
        grad_in, grad_gate, _ = mix_grads
    return (
        output,
        grad_inputs,
        grad_gains,
        grad_in,
        grad_gate,
        mix_grads[2].T,
        grad_conv,
        grad_bias,
        grad_decay,
        grad_blocks,
        up_grad,
        gate_ff_grad,
        down_grad.T,
    )


def solution(mesh):
    row, col = P("dp", "mp"), P("mp", "dp")
    tok = P(("dp", "mp"), None)
    chan = P(None, "mp", "dp")
    gate = P(None, "mp", "dp", None)
    return jax.shard_map(
        shards,
        mesh=mesh,
        in_specs=(
            tok, tok, P(("dp", "mp")), P("dp", None), P("dp", None), P(),
            row, row, col, chan, chan, col, gate, row, row, col,
        ),
        out_specs=(
            tok, tok, P(None, ("dp", "mp")), row, row, col, chan, chan, col, gate, row, row, col,
        ),
        check_vma=False,
    )
```

```python
import functools

import jax
import jax.numpy as jnp
from jax import lax
from jax.experimental import pallas as pl
from jax.experimental.pallas import tpu as pltpu
from jax.sharding import PartitionSpec as P

epsilon = 1e-06
LANE = 128
SUB = 8
TAIL = 24
ROWS = 272
VMEM_MB = 62
f32 = jnp.float32
bf16 = jnp.bfloat16
GELU_C = 0.7978845608028654
GELU_A = 0.044715


def rms_scale(values):
    return lax.rsqrt(jnp.mean(values * values, axis=-1, keepdims=True) + epsilon)


def dot(left, right):
    return lax.dot_general(left, right, (((1,), (0,)), ((), ())), preferred_element_type=f32)


def dot_last(left, right):
    return lax.dot_general(left, right, (((1,), (1,)), ((), ())), preferred_element_type=f32)


def dot_first(left, right):
    return lax.dot_general(left, right, (((0,), (0,)), ((), ())), preferred_element_type=f32)


def gelu_of(v):
    return 0.5 * v * (1.0 + jnp.tanh(GELU_C * (v + GELU_A * v * v * v)))


def gelu_both(v):
    square = v * v
    th = jnp.tanh(GELU_C * (v + GELU_A * v * square))
    half = 0.5 * (1.0 + th)
    slope = half + 0.5 * v * (1.0 - th * th) * (GELU_C * (1.0 + 3.0 * GELU_A * square))
    return v * half, slope


def sigmoid(v):
    return 0.5 * jnp.tanh(0.5 * v) + 0.5


def split(values):
    high = values.astype(bf16)
    return high, (values - high.astype(f32)).astype(bf16)


def rows_of(index, rows):
    return pl.ds(pl.multiple_of(index * rows, rows), rows)


def pick_rows(order_col, count):
    places = lax.broadcasted_iota(jnp.int32, (order_col.shape[0], count), 1)
    return (places == order_col).astype(f32).astype(bf16)


def put_rows(order_row, first, rows):
    places = lax.broadcasted_iota(jnp.int32, (rows, order_row.shape[1]), 0) + first
    return (places == order_row).astype(f32).astype(bf16)


def mixer_forward(tokens, ocol, orow, pos, w_in, w_gate, chan, blocks, w_out_far, *rest):
    far, rest = rest[:8], rest[8:]
    packed, rate, prod, before, low, w_out, *near, late_sem, held_sem = rest
    gate_ref, branch_ref, conv_ref, gin_ref, grec_ref, state_ref, mixed_ref, out_ref = near
    (late_out,) = late_all([w_out_far], [w_out], late_sem)
    leaving = [
        pltpu.make_async_copy(source, target, held_sem.at[i, 0])
        for i, (source, target) in enumerate(zip(near, far))
    ]
    count, _ = tokens.shape
    width = w_in.shape[1]
    steps = count // SUB
    heads = width // LANE

    def project(b, carry):
        at = rows_of(b, ROWS)
        packed[...] = dot(pick_rows(ocol[at, :], count), tokens[...]).astype(bf16)
        branch_ref[at, :] = dot(packed[...], w_in[...])
        gate_ref[at, :] = dot(packed[...], w_gate[...])
        return carry

    lax.fori_loop(0, count // ROWS, project, 0)
    leaving[0].start()
    leaving[1].start()

    for k in range(TAIL // SUB):
        last = branch_ref[pl.ds(count - TAIL + k * SUB, SUB), :]
        before[pl.ds(k * SUB, SUB), :] = pltpu.roll(last, 1, 0)
    before[pl.ds(TAIL, ROWS), :] = branch_ref[pl.ds(0, ROWS), :]

    def gates(b, carry):
        at = rows_of(b, ROWS)

        @pl.when(b > 0)
        def _():
            before[...] = branch_ref[pl.ds(pl.multiple_of(b * ROWS - TAIL, SUB), ROWS + TAIL), :]

        place = pos[at, :]
        for h in range(heads):
            lanes = pl.ds(h * LANE, LANE)
            par = chan[:, lanes]
            conv = par[4:5] + par[0:1] * before[pl.ds(TAIL, ROWS), lanes]
            for k in range(1, 4):
                earlier = before[pl.ds(TAIL - SUB * k, ROWS), lanes]
                conv = conv + par[k : k + 1] * jnp.where(place >= k, earlier, 0.0)
            high, rest = split(conv)
            pair = jnp.concatenate([blocks[h], blocks[heads + h]], axis=1)
            pre = dot(
                jnp.concatenate([high, rest], axis=1), jnp.concatenate([pair, pair], axis=0)
            )
            gate_in = sigmoid(pre[:, :LANE] + par[5:6])
            gate_rec = sigmoid(pre[:, LANE:] + par[6:7])
            kept = jnp.exp(-8.0 * gate_rec * par[7:8])
            drive = jnp.sqrt(1.0 - kept * kept + 0.01) * gate_in * conv
            conv_ref[at, lanes] = conv
            gin_ref[at, lanes] = gate_in
            grec_ref[at, lanes] = gate_rec
            rate[at, lanes] = jnp.where(place >= 1, kept, 0.0)
            state_ref[at, lanes] = drive
        return carry

    lax.fori_loop(0, count // ROWS, gates, 0)
    for copy in leaving[2:5]:
        copy.start()

    def scan(i, carry):
        held, passed = carry
        at = rows_of(i, SUB)
        a = rate[at, :]
        held = a * held + state_ref[at, :]
        passed = a * passed
        state_ref[at, :] = held
        prod[at, :] = passed
        return held, passed

    ends = lax.fori_loop(
        0, steps, scan, (jnp.zeros((SUB, width), f32), jnp.ones((SUB, width), f32)), unroll=8
    )
    first = lax.broadcasted_iota(jnp.int32, (SUB, width), 0) == 0
    carry_in = jnp.zeros((SUB, width), f32)
    for _ in range(SUB - 1):
        carry_in = jnp.where(first, 0.0, pltpu.roll(ends[0] + ends[1] * carry_in, 1, 0))

    def finish(i, carry):
        at = rows_of(i, 2 * SUB)
        twice = jnp.concatenate([carry_in, carry_in], axis=0)
        value = state_ref[at, :] + prod[at, :] * twice
        state_ref[at, :] = value
        low[at, :] = (gelu_of(gate_ref[at, :]) * value).astype(bf16)
        return carry

    lax.fori_loop(0, steps // 2, finish, 0, unroll=2)
    leaving[5].start()
    late_out.ready()

    def leave(b, carry):
        at = rows_of(b, ROWS)
        mixed = dot(put_rows(orow[...], b * ROWS, ROWS), low[...]).astype(bf16)
        mixed_ref[at, :] = mixed
        out_ref[at, :] = dot_last(mixed, w_out[...]).astype(bf16)
        return carry

    lax.fori_loop(0, count // ROWS, leave, 0)
    for copy in leaving[6:]:
        copy.start()
    for copy in leaving:
        copy.wait()


def ffn(tokens, w_up, w_gate_far, cot_far, w_down_far, *rest):
    far, rest = rest[:4], rest[4:]
    w_gate, cot, w_down, *near, late_sem, held_sem = rest
    dnorm_ref, hidden_ref, dup_ref, dgate_ref = near
    late = late_all([w_gate_far, cot_far, w_down_far], [w_gate, cot, w_down], late_sem)
    blocks_of = tokens.shape[0] // ROWS

    def leaving(b):
        at = rows_of(b, ROWS)
        return [
            pltpu.make_async_copy(source.at[at], target.at[at], held_sem.at[i, b])
            for i, (source, target) in enumerate(zip(near, far))
        ]

    def block(b, carry):
        at = rows_of(b, ROWS)
        up = dot(tokens[at, :], w_up[...])

        @pl.when(b == 0)
        def _():
            for array in late:
                array.copy.wait()

        value, slope = gelu_both(dot(tokens[at, :], w_gate[...]))
        hidden_ref[at, :] = (value * up).astype(bf16)
        d_hidden = dot(cot[at, :], w_down[...])
        d_up = (d_hidden * value).astype(bf16)
        d_gate = (d_hidden * up * slope).astype(bf16)
        dup_ref[at, :] = d_up
        dgate_ref[at, :] = d_gate
        dnorm_ref[at, :] = (dot_last(d_up, w_up[...]) + dot_last(d_gate, w_gate[...])).astype(bf16)
        for copy in leaving(b):
            copy.start()
        return carry

    lax.fori_loop(0, blocks_of, block, 0)
    for b in range(blocks_of):
        for copy in leaving(b):
            copy.wait()


def mixer_backward(back, w_out, ocol, orow, pos, gain, chan, blocks, *rest):
    far, (dcat_ref, dnorm_ref, little_ref, dgain_ref), rest = rest[:9], rest[9:13], rest[13:]
    dmix_arr, dmix, adj, prod, after, before, low, small_ref, dblocks_ref, *rest = rest
    gate_ref, grec_ref, state_ref, conv_ref, gin_ref, branch_ref, norm, w_in, w_gate, late_sem = rest
    late = late_all(far, rest[:9], late_sem)
    count, _ = back.shape
    width = w_in.shape[1]
    steps = count // SUB
    heads = width // LANE
    blocks_of = count // ROWS

    def enter(b, carry):
        at = rows_of(b, ROWS)
        dmix_arr[at, :] = dot(back[at, :], w_out[...]).astype(bf16)
        return carry

    lax.fori_loop(0, blocks_of, enter, 0)
    for array in late[:3]:
        array.ready()

    def pack(b, carry):
        at = rows_of(b, ROWS)
        d_mixed = dot(pick_rows(ocol[at, :], count), dmix_arr[...])
        value, slope = gelu_both(gate_ref[at, :])
        adj[at, :] = d_mixed * value
        low[at, pl.ds(width, width)] = (d_mixed * state_ref[at, :] * slope).astype(bf16)
        kept = jnp.exp(-8.0 * grec_ref[at, :] * chan[7:8, :])
        dmix[at, :] = jnp.where(pos[at, :] >= 1, kept, 0.0)
        return carry

    lax.fori_loop(0, blocks_of, pack, 0)
    for array in late:
        array.ready()

    def scan(i, carry):
        held, passed, following = carry
        at = rows_of(steps - 1 - i, SUB)
        held = following * held + adj[at, :]
        passed = following * passed
        adj[at, :] = held
        prod[at, :] = passed
        return held, passed, dmix[at, :]

    last = lax.broadcasted_iota(jnp.int32, (SUB, width), 0) == SUB - 1
    wrapped = jnp.where(last, 0.0, pltpu.roll(dmix[pl.ds(0, SUB), :], SUB - 1, 0))
    ends = lax.fori_loop(
        0,
        steps,
        scan,
        (jnp.zeros((SUB, width), f32), jnp.ones((SUB, width), f32), wrapped),
        unroll=8,
    )
    carry_in = jnp.zeros((SUB, width), f32)
    for _ in range(SUB - 1):
        carry_in = jnp.where(last, 0.0, pltpu.roll(ends[0] + ends[1] * carry_in, SUB - 1, 0))

    small_ref[...] = jnp.zeros_like(small_ref)
    dblocks_ref[...] = jnp.zeros_like(dblocks_ref)
    first = lax.broadcasted_iota(jnp.int32, (SUB, width), 0) == 0
    state_last = state_ref[pl.ds(count - SUB, SUB), :]
    before[pl.ds(TAIL - SUB, SUB), :] = jnp.where(first, 0.0, pltpu.roll(state_last, 1, 0))
    before[pl.ds(TAIL, ROWS), :] = state_ref[pl.ds(0, ROWS), :]
    wide_carry = jnp.concatenate([carry_in] * (ROWS // SUB), axis=0)

    def point(b, carry):
        at = rows_of(b, ROWS)

        @pl.when(b > 0)
        def _():
            before[...] = state_ref[pl.ds(pl.multiple_of(b * ROWS - TAIL, SUB), ROWS + TAIL), :]

        place = pos[at, :]
        for h in range(heads):
            lanes = pl.ds(h * LANE, LANE)
            par = chan[:, lanes]
            adjoint = adj[at, lanes] + prod[at, lanes] * wide_carry[:, h * LANE : (h + 1) * LANE]
            conv = conv_ref[at, lanes]
            gate_in = gin_ref[at, lanes]
            gate_rec = grec_ref[at, lanes]
            kept = jnp.exp(-8.0 * gate_rec * par[7:8])
            square = kept * kept
            inside = 1.0 - square + 0.01
            inverse = lax.rsqrt(inside)
            root = inside * inverse
            previous = before[pl.ds(TAIL - SUB, ROWS), lanes]
            d_log = adjoint * previous * dmix[at, lanes]
            scaled = adjoint * gate_in
            d_log = d_log - scaled * conv * square * inverse
            d_in = adjoint * root * conv * gate_in * (1.0 - gate_in)
            d_rec = d_log * (-8.0 * par[7:8]) * gate_rec * (1.0 - gate_rec)
            both = jnp.concatenate([d_in, d_rec], axis=1)
            high, rest = split(both)
            pair = jnp.concatenate([blocks[h], blocks[heads + h]], axis=1)
            d_conv = scaled * root + dot_last(high, pair) + dot_last(rest, pair)
            dblocks_ref[h] += dot_first(conv.astype(bf16), high)
            after[at, lanes] = d_conv
            small_ref[4:5, lanes] += jnp.sum(d_conv, axis=0, keepdims=True)
            small_ref[5:6, lanes] += jnp.sum(d_in, axis=0, keepdims=True)
            small_ref[6:7, lanes] += jnp.sum(d_rec, axis=0, keepdims=True)
            small_ref[7:8, lanes] += (
                jnp.sum(d_log * gate_rec, axis=0, keepdims=True) * (-8.0) * par[8:9]
            )
        return carry

    lax.fori_loop(0, blocks_of, point, 0)

    for k in range(TAIL // SUB):
        head = after[pl.ds(k * SUB, SUB), :]
        after[pl.ds(count + k * SUB, SUB), :] = pltpu.roll(head, SUB - 1, 0)
        tail = branch_ref[pl.ds(count - TAIL + k * SUB, SUB), :]
        before[pl.ds(k * SUB, SUB), :] = pltpu.roll(tail, 1, 0)
    before[pl.ds(TAIL, ROWS), :] = branch_ref[pl.ds(0, ROWS), :]

    def unmix(b, carry):
        at = rows_of(b, ROWS)

        @pl.when(b > 0)
        def _():
            before[...] = branch_ref[pl.ds(pl.multiple_of(b * ROWS - TAIL, SUB), ROWS + TAIL), :]

        place = pos[at, :]
        for h in range(heads):
            lanes = pl.ds(h * LANE, LANE)
            par = chan[:, lanes]
            d_conv = after[at, lanes]
            d_branch = par[0:1] * d_conv
            small_ref[0:1, lanes] += jnp.sum(
                d_conv * before[pl.ds(TAIL, ROWS), lanes], axis=0, keepdims=True
            )
            for k in range(1, 4):
                later = pl.ds(pl.multiple_of(b * ROWS + SUB * k, SUB), ROWS)
                d_branch = d_branch + par[k : k + 1] * jnp.where(
                    pos[later, :] >= k, after[later, lanes], 0.0
                )
                earlier = before[pl.ds(TAIL - SUB * k, ROWS), lanes]
                small_ref[k : k + 1, lanes] += jnp.sum(
                    jnp.where(place >= k, d_conv * earlier, 0.0), axis=0, keepdims=True
                )
            low[at, lanes] = d_branch.astype(bf16)
        return carry

    lax.fori_loop(0, blocks_of, unmix, 0)
    lines = [small_ref[0:SUB, h * LANE : (h + 1) * LANE] for h in range(heads)]
    lines.append(jnp.zeros((LANE - SUB * heads, LANE), f32))
    little_ref[:, pl.ds(2 * width, LANE)] = jnp.concatenate(lines, axis=0).T
    for h in range(heads):
        little_ref[:, pl.ds(2 * h * LANE, 2 * LANE)] = dblocks_ref[h]
    dgain_ref[...] = jnp.zeros_like(dgain_ref)

    def leave(b, carry):
        at = rows_of(b, ROWS)
        cat = dot(put_rows(orow[...], b * ROWS, ROWS), low[...]).astype(bf16)
        dcat_ref[at, :] = cat
        d_norm = dot_last(cat[:, :width], w_in[...]) + dot_last(cat[:, width:], w_gate[...])
        dgain_ref[...] += jnp.sum(d_norm * norm[at, :].astype(f32), axis=0, keepdims=True)
        dnorm_ref[at, :] = d_norm.astype(bf16)
        return carry

    lax.fori_loop(0, blocks_of, leave, 0)
    dgain_ref[...] = dgain_ref[...] / gain[...]


MESH = pl.DeviceIdType.MESH
TILE = 16
PIECES = 8
HOP = 1
AFTER = 1


def cut_rows(rows, parts):
    tiles = rows // TILE
    ends = [tiles * (k + 1) // parts for k in range(parts)]
    return [(TILE * a, TILE * (b - a)) for a, b in zip([0] + ends[:-1], ends)]


class Line:
    def __init__(self, n, local, part, arrived, whole, sums, alls):
        self.n, self.local, self.part, self.arrived, self.whole = n, local, part, arrived, whole
        self.sums, self.alls = sums, alls
        self.me = lax.axis_index("mp")
        self.pieces = cut_rows(local, PIECES)
        self.has = (self.me > 0, self.me < n - 1)

    def greet(self, plane=None):
        barrier = pltpu.get_barrier_semaphore()
        more = 0
        if plane is not None:
            for bit in plane.bits:
                more += 1
                pl.semaphore_signal(
                    barrier, inc=1, device_id={"dp": plane.other(bit)}, device_id_type=MESH
                )
        for away in range(1, self.n):
            more += 1
            pl.semaphore_signal(
                barrier,
                inc=1,
                device_id={"mp": lax.rem(self.me + away, self.n)},
                device_id_type=MESH,
            )
        pl.semaphore_wait(barrier, more)

    def rows_at(self, owner, k):
        first, rows = self.pieces[k]
        return pl.ds(pl.multiple_of(owner * self.local + first, TILE), rows)

    def copy(self, source, target, sems, way, owner, k):
        return pltpu.make_async_remote_copy(
            src_ref=source,
            dst_ref=target,
            send_sem=sems[0].at[way, owner, k],
            recv_sem=sems[1].at[way, owner, k],
            device_id={"mp": self.me + 1 - 2 * way},
            device_id_type=MESH,
        )

    def sum_copy(self, way, owner, k, first=False):
        at = self.rows_at(owner, k)
        landed = self.arrived[way].at[at]
        return self.copy(self.part.at[at] if first else landed, landed, self.sums, way, owner, k)

    def all_copy(self, way, owner, k):
        block = self.whole.at[self.rows_at(owner, k)]
        return self.copy(block, block, self.alls, way, owner, k)

    def first(self, k):
        for away in range(self.n - 1):
            for way in range(2):
                owner = away if way else self.n - 1 - away

                @pl.when(jnp.logical_not(self.has[way]))
                def _():
                    self.sum_copy(way, owner, k, True).start()

    def relay(self, k, stage):
        for way in range(2):
            late = stage - (self.n - 1 - self.me if way else self.me)
            owner = late if way else self.n - 1 - late

            @pl.when(self.has[way] & (late >= 0))
            def _():
                self.sum_copy(way, owner, k).wait_recv()
                at = self.rows_at(owner, k)
                landed = self.arrived[way]
                landed[at, :] = (landed[at, :].astype(f32) + self.part[at, :].astype(f32)).astype(bf16)
                self.sum_copy(way, owner, k).start()

    def total(self, k, into):
        at = self.rows_at(self.me, k)
        rows = pl.ds(0, self.pieces[k][1])
        into[rows, :] = self.part[at, :].astype(f32)
        for way in range(2):

            @pl.when(self.has[way])
            def _():
                self.sum_copy(way, self.me, k).wait_recv()
                into[rows, :] += self.arrived[way][at, :].astype(f32)

    def spread(self, k):
        for way in range(2):

            @pl.when(self.has[1 - way])
            def _():
                self.all_copy(way, self.me, k).start()

    def forward(self, k, stage):
        for way in range(2):
            owner = self.me + stage if way else self.me - stage
            there = owner < self.n if way else owner >= 0

            @pl.when(there)
            def _():
                self.all_copy(way, owner, k).wait_recv()

            @pl.when(there & self.has[1 - way])
            def _():
                self.all_copy(way, owner, k).start()

    def finish(self):
        for k in range(PIECES):
            for owner in range(self.n):
                for way in range(2):
                    if self.part is not None:

                        @pl.when(self.me > owner if way else self.me < owner)
                        def _():
                            self.sum_copy(way, owner, k).wait_send()

                    if self.whole is not None:
                        reached = self.me <= owner if way else self.me >= owner

                        @pl.when(reached & self.has[1 - way])
                        def _():
                            self.all_copy(way, owner, k).wait_send()

    def run(self, point, tasks=()):
        sums, alls = self.part is not None, self.whole is not None
        slots = [[] for _ in range(PIECES + (HOP + AFTER) * (self.n - 1) + 1)]
        for k in range(PIECES):
            done = k + HOP * (self.n - 1) if sums else 0
            if sums:
                slots[k].append((0, functools.partial(self.first, k)))
                for stage in range(1, self.n - 1):
                    slots[k + HOP * stage].append((2, functools.partial(self.relay, k, stage)))
            slots[done].append((3, functools.partial(point, k)))
            if alls:
                slots[done].append((4, functools.partial(self.spread, k)))
                for stage in range(1, self.n):
                    at = (done if sums else k) + AFTER * stage
                    slots[at].append((1, functools.partial(self.forward, k, stage)))
        tasks = iter(tasks)
        for slot in slots:
            for step, (_, work) in enumerate(sorted(slot, key=lambda entry: entry[0])):
                if step in (0, 3):
                    next(tasks, idle)()
                work()
        for task in tasks:
            task()
        self.finish()

    def tiles(self, k, body):
        first, rows = self.pieces[k]

        def one(i, carry):
            body(
                pl.ds(pl.multiple_of(i * TILE, TILE), TILE),
                pl.ds(pl.multiple_of(first + i * TILE, TILE), TILE),
                pl.ds(pl.multiple_of(self.me * self.local + first + i * TILE, TILE), TILE),
            )
            return carry

        lax.fori_loop(0, rows // TILE, one, 0)


def idle():
    pass


class Late:
    def __init__(self, source, ref, sem):
        self.ref = ref
        self.copy = pltpu.make_async_copy(source, ref, sem)
        self.pending = True
        self.copy.start()

    def ready(self):
        if self.pending:
            self.copy.wait()
        self.pending = False


def late_all(sources, refs, sems):
    return [Late(source, ref, sems.at[i]) for i, (source, ref) in enumerate(zip(sources, refs))]


class Plane:
    bits = (1, 2, 4)
    orders = ((4, 2, 1), (2, 4, 1))

    def __init__(self):
        self.me = lax.axis_index("dp")

    def bit(self, bit):
        return lax.rem(self.me // bit, 2)

    def other(self, *bits):
        return self.me + sum(bit * (1 - 2 * self.bit(bit)) for bit in bits)

    def gather_copies(self, item, view, halves, stage, sems):
        copies = []
        for half in halves:
            order = self.orders[half]
            for combo in range(1 << stage):
                flipped = [bit for i, bit in enumerate(order[:stage]) if combo >> i & 1]
                block = view(self.other(*flipped), half)
                slot = (1 << stage) - 1 + combo
                copies.append(
                    pltpu.make_async_remote_copy(
                        src_ref=block,
                        dst_ref=block,
                        send_sem=sems[0].at[item, half, slot],
                        recv_sem=sems[1].at[item, half, slot],
                        device_id={"dp": self.other(order[stage])},
                        device_id_type=MESH,
                    )
                )
        return copies


class Reduce(Plane):
    def __init__(self, index, left, right, lanes, sent, mine, theirs, got, second, third, out, sems):
        super().__init__()
        self.sent, self.theirs = sent, theirs
        self.index, self.left, self.right, self.lanes = index, left, right, lanes
        self.mine, self.got = mine.at[index], got.at[index]
        self.second, self.third, self.out = second.at[index], third.at[index], out
        self.sems = sems
        self.rows = out.shape[0]
        self.half = self.rows // 2

    def copy(self, source, target, slot, bit):
        return pltpu.make_async_remote_copy(
            src_ref=source,
            dst_ref=target,
            send_sem=self.sems[0].at[self.index, slot],
            recv_sem=self.sems[1].at[self.index, slot],
            device_id={"dp": self.other(bit)},
            device_id_type=MESH,
        )

    def core_copy(self, t):
        return self.copy(self.theirs.at[(4 * self.index + t) % 2], self.got.at[t], t, 1)

    def second_copy(self, half, j):
        x, y = self.bit(2), self.bit(4)
        block = (1 - y) * 2 + j if half else j * 2 + 1 - x
        rows = self.mine.at[block, pl.ds(half * self.half, self.half)]
        return self.copy(rows, self.second.at[half, j], 4 + 2 * half + j, 4 if half else 2)

    def third_block(self, half):
        x, y = self.bit(2), self.bit(4)
        return y * 2 + 1 - x if half else (1 - y) * 2 + x

    def third_copy(self, half):
        rows = self.mine.at[self.third_block(half), pl.ds(half * self.half, self.half)]
        return self.copy(rows, self.third.at[half], 8 + half, 2 if half else 4)

    def product(self, t):
        def task():
            core = self.bit(1)
            pair = pl.ds(t * 2 * self.rows, 2 * self.rows)
            if t == 0:
                self.left.ready()
                self.right.ready()
            if len(self.sent) > 1:
                self.sent[-2].wait_send()
            both = dot_first(self.left.ref[:, pair], self.right.ref[:, self.lanes])
            low, high = both[: self.rows], both[self.rows :]
            self.mine[t] = jnp.where(core == 0, low, high).astype(bf16)
            self.theirs[(4 * self.index + t) % 2] = jnp.where(core == 0, high, low).astype(bf16)
            self.sent.append(self.core_copy(t))
            self.sent[-1].start()

        return task

    def keep(self, t):
        return self.mine[t]

    def add_core(self):
        for t in range(4):
            self.core_copy(t).wait_recv()
            self.mine[t] = (self.keep(t).astype(f32) + self.got[t].astype(f32)).astype(self.mine.dtype)
        for half in range(2):
            for j in range(2):
                self.second_copy(half, j).start()

    def add_second(self):
        for half in range(2):
            for j in range(2):
                self.second_copy(half, j).wait_recv()
        for half in range(2):
            block, at = self.third_block(half), pl.ds(half * self.half, self.half)
            far = 1 - self.bit(2 if half else 4)
            self.mine[block, at] = (
                self.mine[block, at].astype(f32) + self.second[half, far].astype(f32)
            ).astype(self.mine.dtype)
            self.third_copy(half).start()

    def add_third(self):
        own = self.bit(4) * 2 + self.bit(2)
        for half in range(2):
            self.third_copy(half).wait_recv()
            at = pl.ds(half * self.half, self.half)
            near = self.bit(2 if half else 4)
            self.out[at, :] = (
                self.mine[own, at].astype(f32)
                + self.second[half, near].astype(f32)
                + self.third[half].astype(f32)
            )

    def finish(self):
        for half in range(2):
            for j in range(2):
                self.second_copy(half, j).wait_send()
            self.third_copy(half).wait_send()


class Given(Reduce):
    def __init__(self, given, mine, got, second, third, out, sems):
        super().__init__(0, None, None, None, None, mine, None, got, second, third, out, sems)
        self.given = given

    def rows_of(self, t, core):
        return pl.ds(pl.multiple_of((2 * t + core) * self.rows, self.rows), self.rows)

    def core_copy(self, t):
        return self.copy(self.given.at[self.rows_of(t, 1 - self.bit(1))], self.got.at[t], t, 1)

    def start(self):
        for t in range(4):
            self.core_copy(t).start()

    def finish(self):
        for t in range(4):
            self.core_copy(t).wait_send()
        super().finish()

    def keep(self, t):
        return self.given[self.rows_of(t, self.bit(1)), :]


def reduce_tasks(parts, given=()):
    tasks = [part.product(t) for part in parts for t in range(4)]

    def also(at, extra):
        while len(tasks) <= at:
            tasks.append(idle)
        before = tasks[at]

        def both():
            extra()
            before()

        tasks[at] = both

    for i, part in enumerate(parts):
        also(4 * i + 5, part.add_core)
        also(4 * i + 8, part.add_second)
        also(4 * i + 10, part.add_third)

    for part in given:
        also(0, part.start)
        also(2, part.add_core)
        also(4, part.add_second)
        also(6, part.add_third)

    def finish():
        for copy in parts[0].sent[-2:]:
            copy.wait_send()
        for part in [*parts, *given]:
            part.finish()

    return tasks, finish


def given_scratch(rows, width):
    sem = pltpu.SemaphoreType.DMA((1, 10))
    return [
        pltpu.VMEM((1, 4, rows, width), f32),
        pltpu.VMEM((1, 4, rows, width), f32),
        pltpu.VMEM((1, 2, 2, rows // 2, width), f32),
        pltpu.VMEM((1, 2, rows // 2, width), f32),
        sem,
        sem,
    ]


def reduce_scratch(arrays, rows, width):
    block = pltpu.VMEM((arrays, 4, rows, width), bf16)
    sem = pltpu.SemaphoreType.DMA((arrays, 10))
    return [
        block,
        pltpu.VMEM((2, rows, width), bf16),
        block,
        pltpu.VMEM((arrays, 2, 2, rows // 2, width), bf16),
        pltpu.VMEM((arrays, 2, rows // 2, width), bf16),
        sem,
        sem,
    ]


def gather_norm(n, x, gain, whole, send, recv):
    line = Line(n, x.shape[0], None, None, whole, None, (send, recv))
    line.greet()

    def point(k):
        def one(_, own, at):
            v = x[own, :].astype(f32)
            whole[at, :] = (v * rms_scale(v) * gain[...]).astype(bf16)

        line.tiles(k, one)

    line.run(point)


def row_view(array, rows):
    def view(owner, half):
        first = owner * rows + half * (rows // 2)
        return array.at[pl.ds(pl.multiple_of(first, TILE), rows // 2)]

    return view


def gather_tasks(plane, items, sems):
    def copies(stage):
        return [
            copy
            for item, (view, halves) in enumerate(items)
            for copy in plane.gather_copies(item, view, halves, stage, sems)
        ]

    def stage_task(stage):
        def task():
            if stage:
                for copy in copies(stage - 1):
                    copy.wait_recv()
            for copy in copies(stage):
                copy.start()

        return task

    def last():
        for copy in copies(2):
            copy.wait_recv()
        for stage in range(3):
            for copy in copies(stage):
                copy.wait_send()

    return stage_task(0), stage_task(1), stage_task(2), last


def gather_weights(
    n,
    x,
    gain,
    w_in,
    w_gate,
    w_out,
    blocks,
    chan,
    whole,
    all_in,
    all_gate,
    all_out,
    all_blocks,
    all_chan,
    send,
    recv,
    raw,
    plane_send,
    plane_recv,
):
    line = Line(n, x.shape[0], None, None, whole, None, (send, recv))
    plane = Plane()
    line.greet(plane)
    sems = plane_send, plane_recv
    rows, piece = w_in.shape[0], blocks.shape[1]
    lines = chan.shape[0]

    def blocks_view(owner, half):
        return all_blocks.at[:, pl.ds(pl.multiple_of(owner * piece, TILE), piece)]

    def chan_view(owner, half):
        return raw.at[pl.ds(pl.multiple_of(owner * lines, TILE), lines)]

    items = [(row_view(array, rows), (0, 1)) for array in (all_in, all_gate, all_out)]
    items += [(blocks_view, (0,)), (chan_view, (1,))]

    first, second, third, finish = gather_tasks(plane, items, sems)

    def last():
        finish()
        lane = lax.broadcasted_iota(jnp.int32, (LANE, LANE), 1)
        row = lax.broadcasted_iota(jnp.int32, (LANE, LANE), 0)
        total = jnp.zeros((lines, LANE), f32)
        for owner in range(LANE // piece):
            moved = ((row < piece) & (row + owner * piece == lane)).astype(f32).astype(bf16)
            total = total + dot(raw[pl.ds(owner * lines, lines), :], moved)
        for h in range(lines // SUB):
            par = total[h * SUB : (h + 1) * SUB]
            lanes = pl.ds(h * LANE, LANE)
            all_chan[0:SUB, lanes] = par
            decay = par[SUB - 1 : SUB]
            small = jnp.exp(-jnp.abs(decay))
            one_more = 1.0 + small
            rest = jnp.where(one_more == 1.0, 1.0, one_more - 1.0)
            log_one_more = jnp.where(one_more == 1.0, small, jnp.log(one_more) * (small / rest))
            all_chan[SUB - 1 : SUB, lanes] = jnp.maximum(decay, 0.0) + log_one_more
            all_chan[SUB : 2 * SUB, lanes] = jnp.broadcast_to(sigmoid(decay), (SUB, LANE))

    own = pl.ds(pl.multiple_of(plane.me * rows, TILE), rows)
    all_in[own, :] = w_in[...]
    all_gate[own, :] = w_gate[...]
    all_out[own, :] = w_out[...]
    all_blocks[:, pl.ds(pl.multiple_of(plane.me * piece, TILE), piece), :] = blocks[...]
    raw[pl.ds(pl.multiple_of(plane.me * lines, TILE), lines), :] = chan[...]

    def point(k):
        def one(_, own, at):
            v = x[own, :].astype(f32)
            whole[at, :] = (v * rms_scale(v) * gain[...]).astype(bf16)

        line.tiles(k, one)

    first()
    line.run(point, [idle] * 4 + [second] + [idle] * 3 + [third] + [idle] * 3 + [last])


def sum_norm_gather(n, x, gain, part, *rest):
    if len(rest) > 9:
        shares, rest = rest[:3], rest[3:]
        resid, whole, *alls = rest[:5]
        left, right, total, ss, sr, send, recv, plane_send, plane_recv = rest[5:]
        plane = Plane()
    else:
        resid, whole, left, right, total, ss, sr, send, recv = rest
        plane = None
    line = Line(n, x.shape[0], part, (left, right), whole, (ss, sr), (send, recv))
    line.greet(plane)
    tasks = []
    if plane is not None:
        rows = shares[0].shape[0]
        own = pl.ds(pl.multiple_of(plane.me * rows, TILE), rows)
        for share, array in zip(shares, alls):
            array[own, :] = share[...]
        items = [(row_view(array, rows), (0, 1)) for array in alls]
        first, second, third, last = gather_tasks(plane, items, (plane_send, plane_recv))
        tasks = [first] + [idle] * 5 + [second] + [idle] * 9 + [third] + [idle] * 6 + [last]

    def point(k):
        line.total(k, total)

        def one(here, own, at):
            v = x[own, :].astype(f32) + total[here, :]
            resid[own, :] = v
            whole[at, :] = (v * rms_scale(v) * gain[...]).astype(bf16)

        line.tiles(k, one)

    line.run(point, tasks)


def norm_back(value, gain, grad):
    scale = rms_scale(value)
    e = gain * grad
    slope = scale * scale * scale * jnp.mean(value * e, axis=-1, keepdims=True)
    return scale * e - value * slope, grad * value * scale


def sum_back_gather(n, resid, cot, gain, part, *rest):
    if len(rest) > 10:
        sources, rest = rest[:6], rest[6:]
        d_resid, gain_grad, whole, low_part, high_part, *outs = rest[:8]
        left, right, total, ss, sr, send, recv, *reduce = rest[8:]
        reduce, refs, late_sems = reduce[:7], reduce[7:13], reduce[13]
    else:
        d_resid, gain_grad, whole, left, right, total, ss, sr, send, recv = rest
        sources = ()
    line = Line(n, resid.shape[0], part, (left, right), whole, (ss, sr), (send, recv))
    line.greet(Plane() if sources else None)
    gain_grad[...] = jnp.zeros_like(gain_grad)

    def point(k):
        line.total(k, total)

        def one(here, own, at):
            back, terms = norm_back(resid[own, :], gain[...], total[here, :])
            gain_grad[...] += jnp.sum(terms, axis=0, keepdims=True)
            value = cot[own, :].astype(f32) + back
            d_resid[own, :] = value
            whole[at, :] = value.astype(bf16)

        line.tiles(k, one)

    if not sources:
        line.run(point)
        return
    norm, cots, d_up, d_gate, hidden, w_down = late_all(sources, refs, late_sems)
    sent = []
    tasks, finish = reduce_tasks(
        [
            Reduce(i, *side, slice(None), sent, *reduce[:5], out, reduce[5:])
            for i, (side, out) in enumerate(
                zip(((norm, d_up), (norm, d_gate), (cots, hidden)), outs)
            )
        ]
    )

    def project(b):
        w_down.ready()
        at = pl.ds(b * ROWS, ROWS)
        value = dot_last(hidden.ref[at, :], w_down.ref[...]).astype(bf16)
        low_part[at, :] = value[:, : value.shape[1] // 2]
        high_part[at, :] = value[:, value.shape[1] // 2 :]

    for b in range(part.shape[0] // ROWS):
        tasks.insert(12 + b, functools.partial(project, b))
    line.run(point, tasks)
    finish()


def sum_back(n, x, d_resid, gain, part, *rest):
    if len(rest) > 6:
        little, gains, *rest = rest
        sources, rest = rest[:4], rest[4:]
        grad_x, *outs, little_out, gains_out = rest[:6]
        left, right, total, ss, sr, *reduce = rest[6:]
        refs, late_sems = reduce[22:26], reduce[26]
        given = [
            Given(little, *reduce[7:11], little_out, reduce[11:13]),
            Given(gains, *reduce[13:17], gains_out, reduce[17:19]),
        ]
        met, met_send, met_recv = reduce[19:22]
    else:
        grad_x, left, right, total, ss, sr = rest
        sources = ()
    line = Line(n, x.shape[0], part, (left, right), None, (ss, sr), None)
    line.greet(Plane() if sources else None)

    def point(k):
        line.total(k, total)

        def one(here, own, at):
            back, _ = norm_back(x[own, :].astype(f32), gain[...], total[here, :])
            grad_x[own, :] = (d_resid[own, :] + back).astype(bf16)

        line.tiles(k, one)

    if not sources:
        line.run(point)
        return
    norm, back_all, cat, mixed = late_all(sources, refs, late_sems)
    width = mixed.ref.shape[1]
    sent = []
    sides = (
        (norm, cat, slice(0, width)),
        (norm, cat, slice(width, 2 * width)),
        (back_all, mixed, slice(None)),
    )
    tasks, finish = reduce_tasks(
        [
            Reduce(i, *side, sent, *reduce[:5], out, reduce[5:7])
            for i, (side, out) in enumerate(zip(sides, outs))
        ],
        given,
    )
    me = lax.axis_index("mp")

    def meet(away):
        return pltpu.make_async_remote_copy(
            src_ref=gains_out,
            dst_ref=met.at[away - 1],
            send_sem=met_send.at[away - 1],
            recv_sem=met_recv.at[away - 1],
            device_id={"mp": lax.rem(me + away, n)},
            device_id_type=MESH,
        )

    def send_gains():
        for away in range(1, n):
            meet(away).start()

    def add_gains():
        for away in range(1, n):
            meet(away).wait()
        gains_out[...] += sum(met[away] for away in range(n - 1))

    tasks[7:7] = [send_gains]
    line.run(point, tasks)
    finish()
    add_gains()


def line_call(body, n, identity, outs, sums, alls, args, more=(), late=0):
    whole = pl.BlockSpec(memory_space=pltpu.VMEM)
    local, model = args[0].shape
    sem = pltpu.SemaphoreType.DMA((2, n, PIECES))
    scratch = []
    if sums:
        scratch += [pltpu.VMEM((n * local, model), bf16)] * 2
        scratch += [pltpu.VMEM((max(rows for _, rows in cut_rows(local, PIECES)), model), f32)]
        scratch += [sem, sem]
    if alls:
        scratch += [sem, sem]
    scratch += more
    if late:
        scratch += [pltpu.VMEM(a.shape, a.dtype) for a in args[-late:]]
        scratch += [pltpu.SemaphoreType.DMA((late,))]
    moved = sum(a.size * a.dtype.itemsize for a in args)
    return pl.pallas_call(
        functools.partial(body, n),
        out_shape=outs,
        in_specs=[whole] * (len(args) - late) + [pl.BlockSpec(memory_space=pl.ANY)] * late,
        out_specs=[whole] * len(outs),
        scratch_shapes=scratch,
        compiler_params=pltpu.CompilerParams(
            vmem_limit_bytes=VMEM_MB << 20, collective_id=identity, has_side_effects=True
        ),
        cost_estimate=pl.CostEstimate(flops=0, bytes_accessed=100 * moved, transcendentals=0),
    )(*args)


def finish(heads, piece, share, resid, low, high, gains, little, *rest):
    count = (len(rest) - 6) // 2
    sources, rest = rest[:count], rest[count:]
    output, grad_gains, grad_conv, grad_bias, grad_decay, grad_blocks, *targets = rest
    for source, target in zip(sources, targets):
        target[...] = source[...]
    half = low.shape[1]
    output[:, :half] = (resid[:, :half] + low[...].astype(f32)).astype(bf16)
    output[:, half:] = (resid[:, half:] + high[...].astype(f32)).astype(bf16)
    for position in range(gains.shape[0] // 2):

        @pl.when(lax.axis_index("mp") == position)
        def _():
            grad_gains[...] = gains[2 * position : 2 * position + 2, :share]

    for h in range(heads):
        for gate in range(2):
            first = (2 * h + gate) * LANE
            grad_blocks[gate, h] = little[:, first : first + LANE]
    first = 2 * heads * LANE
    lines = little[:, first : first + LANE]
    lines = jnp.concatenate([lines, jnp.zeros((LANE - piece, LANE), f32)], axis=0).T
    for h in range(heads):
        for k in range(SUB):
            row = lines[h * SUB + k : h * SUB + k + 1, :piece]
            if k < 4:
                grad_conv[k, h : h + 1, :] = row
            elif k < SUB - 1:
                grad_bias[k - 4, h : h + 1, :] = row
            else:
                grad_decay[h : h + 1, :] = row


def local_call(body, outs, scratch, flops, args, late=0, held=0):
    whole, away = pl.BlockSpec(memory_space=pltpu.VMEM), pl.BlockSpec(memory_space=pl.ANY)
    twins = list(args[len(args) - late :]) + list(outs[len(outs) - held :])
    scratch = scratch + [pltpu.VMEM(a.shape, a.dtype) for a in twins]
    if late:
        scratch.append(pltpu.SemaphoreType.DMA((late,)))
    if held:
        scratch.append(pltpu.SemaphoreType.DMA((held, 4)))
    moved = sum(a.size * a.dtype.itemsize for a in args)
    moved += sum(o.size * o.dtype.itemsize for o in outs)
    return pl.pallas_call(
        body,
        out_shape=outs,
        in_specs=[whole] * (len(args) - late) + [away] * late,
        out_specs=[whole] * (len(outs) - held) + [away] * held,
        scratch_shapes=scratch,
        compiler_params=pltpu.CompilerParams(vmem_limit_bytes=VMEM_MB << 20),
        cost_estimate=pl.CostEstimate(flops=flops, bytes_accessed=moved, transcendentals=0),
    )(*args)


def shape_of(dtype, *shape):
    return jax.ShapeDtypeStruct(shape, dtype)


def shards(
    inputs,
    cotangent,
    token_mask,
    order,
    lengths,
    gains,
    w_in,
    w_gate,
    w_out,
    conv_weight,
    chan_bias,
    decay,
    gate_blocks,
    w_up,
    w_gate_ff,
    w_down,
):
    n_dp = lax.axis_size("dp")
    local_rows, model = inputs.shape
    count = local_rows * lax.axis_size("mp")
    heads, piece = decay.shape
    width = heads * piece * n_dp
    hidden_width = w_up.shape[1]

    fused = n_dp == 8
    rows = model // n_dp
    out_rows, down_rows = w_out.T, w_down.T
    lines = jnp.concatenate([conv_weight, chan_bias, decay[None]], axis=0).transpose(1, 0, 2)
    lines = lines.reshape(SUB * heads, piece)

    steps = count // SUB
    ends = jnp.cumsum(lengths[0], dtype=jnp.int32)
    starts = ends - lengths[0]
    places = jnp.arange(count, dtype=jnp.int32)
    own_start = jnp.max(
        jnp.where(places[:, None] >= starts[None, :], starts[None, :], 0), axis=1
    )
    pos = (places - own_start).reshape(SUB, steps).T
    wrap = jnp.concatenate([pos[: TAIL // SUB, 1:], jnp.full((TAIL // SUB, 1), -1, jnp.int32)], axis=1)
    pos_col = jnp.concatenate([pos, wrap], axis=0).reshape(count + TAIL, 1)
    order_int = order[0].reshape(SUB, steps).T.reshape(count)
    ocol, orow = order_int.reshape(count, 1), order_int.reshape(1, count)

    gain_f = gains.astype(f32)
    n_mp = lax.axis_size("mp")
    tok = shape_of(bf16, count, model)
    own = shape_of(f32, local_rows, model)
    if fused:
        grown = shape_of(bf16, model, width)
        norm_group, full_in, full_gate, full_out, blocks, chan = line_call(
            gather_weights,
            n_mp,
            0,
            [tok, grown, grown, grown, shape_of(bf16, 2 * heads, LANE, LANE), shape_of(f32, 16, width)],
            False,
            True,
            (
                inputs,
                gain_f[0:1],
                w_in,
                w_gate,
                out_rows,
                gate_blocks.reshape(2 * heads, piece, LANE),
                jnp.pad(lines, ((0, 0), (0, LANE - piece))),
            ),
            [pltpu.VMEM((n_dp * SUB * heads, LANE), bf16)] + [pltpu.SemaphoreType.DMA((5, 2, 7))] * 2,
        )
    else:
        (norm_group,) = line_call(gather_norm, n_mp, 0, [tok], False, True, (inputs, gain_f[0:1]))
        full_in = lax.all_gather(w_in, "dp", axis=0, tiled=True)
        full_gate = lax.all_gather(w_gate, "dp", axis=0, tiled=True)
        full_out = lax.all_gather(out_rows, "dp", axis=0, tiled=True)
        blocks = lax.all_gather(gate_blocks, "dp", axis=2, tiled=True).reshape(2 * heads, LANE, LANE)
        params = lax.all_gather(lines, "dp", axis=1, tiled=True).astype(f32)
        params = params.reshape(heads, SUB, LANE).transpose(1, 0, 2).reshape(SUB, width)
        decay_row = params[7:8]
        chan = jnp.concatenate(
            [params[:7], jax.nn.softplus(decay_row)] + [jax.nn.sigmoid(decay_row)] * SUB, axis=0
        )
    cot = cotangent * token_mask.astype(bf16)[:, None]

    cot_late, norm_group = lax.optimization_barrier((cot, norm_group))
    cot_group = lax.all_gather(cot_late, "mp", axis=0, tiled=True)

    wide = pltpu.VMEM((count, width), f32)
    saved = [shape_of(f32, count, width)] * 6
    gate_pre, branch, conv, gate_in, gate_rec, state, mixed, back_part = local_call(
        mixer_forward,
        saved + [shape_of(bf16, count, width), shape_of(bf16, count, model)],
        [
            pltpu.VMEM((ROWS, model), bf16),
            wide,
            wide,
            pltpu.VMEM((ROWS + TAIL, width), f32),
            pltpu.VMEM((count, width), bf16),
        ],
        2 * count * (count * model + 3 * model * width),
        (norm_group, ocol, orow, pos_col, full_in, full_gate, chan, blocks, full_out),
        1,
        8,
    )
    shares = (w_up, w_gate_ff, down_rows)
    resid, norm_mid_group, *ffn_weights = line_call(
        sum_norm_gather,
        n_mp,
        1,
        [own, tok] + [shape_of(bf16, model, hidden_width)] * (3 * fused),
        True,
        True,
        (inputs, gain_f[1:2], back_part) + (shares if fused else ()),
        [pltpu.SemaphoreType.DMA((3, 2, 7))] * (2 * fused),
    )
    if not fused:
        ffn_weights = [lax.all_gather(share, "dp", axis=0, tiled=True) for share in shares]
    full_up, full_gate_ff, full_down = ffn_weights

    hid = shape_of(bf16, count, hidden_width)
    d_norm_part, hidden, d_up, d_gate_ff = local_call(
        ffn,
        [tok, hid, hid, hid],
        [],
        10 * count * model * hidden_width,
        (norm_mid_group, full_up, full_gate_ff, cot_group, full_down),
        3,
        4,
    )
    d_resid, gain_mid, back_group, *ffn_grads = line_call(
        sum_back_gather,
        n_mp,
        2,
        [own, shape_of(f32, 1, model), tok]
        + ([shape_of(bf16, count, model // 2)] * 2 + [shape_of(f32, rows, hidden_width)] * 3) * fused,
        True,
        True,
        (resid, cot, gain_f[1:2], d_norm_part)
        + ((norm_mid_group, cot_group, d_up, d_gate_ff, hidden, full_down) if fused else ()),
        reduce_scratch(3, rows, hidden_width) if fused else (),
        6 * fused,
    )
    def reduced(left, right):
        grad = dot_first(left, right).astype(bf16)
        return lax.psum_scatter(grad, "dp", scatter_dimension=0, tiled=True).astype(f32)

    if fused:
        *ffn_parts, up_grad, gate_ff_grad, down_grad = ffn_grads
    else:
        ffn_parts = jnp.split(dot_last(hidden, full_down).astype(bf16), 2, axis=1)
        up_grad = reduced(norm_mid_group, d_up)
        gate_ff_grad = reduced(norm_mid_group, d_gate_ff)
        down_grad = reduced(cot_group, hidden)

    d_cat, d_norm_back, little, gain_in = local_call(
        mixer_backward,
        [
            shape_of(bf16, count, 2 * width),
            tok,
            shape_of(f32, LANE, 2 * width + LANE),
            shape_of(f32, 1, model),
        ],
        [
            pltpu.VMEM((count, width), bf16),
            wide,
            wide,
            wide,
            pltpu.VMEM((count + TAIL, width), f32),
            pltpu.VMEM((ROWS + TAIL, width), f32),
            pltpu.VMEM((count, 2 * width), bf16),
            pltpu.VMEM((SUB, width), f32),
            pltpu.VMEM((heads, LANE, 2 * LANE), f32),
        ],
        2 * count * (3 * count * width + 3 * model * width),
        (
            back_group,
            full_out,
            ocol,
            orow,
            pos_col,
            gain_f[0:1],
            chan,
            blocks,
            gate_pre,
            gate_rec,
            state,
            conv,
            gate_in,
            branch,
            norm_group,
            full_in,
            full_gate,
        ),
        9,
    )
    share = model // (n_dp * n_mp)
    gain_parts = jnp.concatenate([gain_in, gain_mid], axis=0).reshape(2, n_dp, n_mp, share)
    gain_parts = gain_parts.transpose(1, 2, 0, 3).reshape(n_dp, 2 * n_mp, share)
    gain_parts = jnp.pad(gain_parts, ((0, 0), (0, 2 * SUB - 2 * n_mp), (0, LANE - share)))
    gain_parts = gain_parts.reshape(2 * SUB * n_dp, LANE)
    ffn_low, ffn_high = (
        lax.psum_scatter(part, "mp", scatter_dimension=0, tiled=True) for part in ffn_parts
    )
    ffn_low, d_norm_back = lax.optimization_barrier((ffn_low, d_norm_back))
    grad_inputs, *mix_grads = line_call(
        sum_back,
        n_mp,
        3,
        [shape_of(bf16, local_rows, model)]
        + (
            [shape_of(f32, rows, width)] * 3
            + [shape_of(f32, piece, little.shape[1]), shape_of(f32, 2 * SUB, LANE)]
        )
        * fused,
        True,
        False,
        (inputs, d_resid, gain_f[0:1], d_norm_back)
        + ((little, gain_parts, norm_group, back_group, d_cat, mixed) if fused else ()),
        reduce_scratch(3, rows, width)
        + given_scratch(piece, little.shape[1])
        + given_scratch(2 * SUB, LANE)
        + [pltpu.VMEM((n_mp - 1, 2 * SUB, LANE), f32)]
        + [pltpu.SemaphoreType.DMA((n_mp - 1,))] * 2
        if fused
        else (),
        4 * fused,
    )
    if fused:
        *mix_grads, little_own, gain_own = mix_grads
    else:
        mix_grads = [
            reduced(norm_group, d_cat[:, :width]),
            reduced(norm_group, d_cat[:, width:]),
            reduced(back_group, mixed),
        ]
        little_own = lax.psum_scatter(little, "dp", scatter_dimension=0, tiled=True)
        gain_own = lax.psum(lax.psum_scatter(gain_parts, "dp", scatter_dimension=0, tiled=True), "mp")
    outs = [
        shape_of(bf16, local_rows, model),
        shape_of(f32, 2, share),
        shape_of(f32, 4, heads, piece),
        shape_of(f32, 3, heads, piece),
        shape_of(f32, heads, piece),
        shape_of(f32, 2, heads, piece, LANE),
    ]
    copied = [grad_inputs, mix_grads[0], mix_grads[1], up_grad, gate_ff_grad] if fused else []
    output, grad_gains, grad_conv, grad_bias, grad_decay, grad_blocks, *copied = local_call(
        functools.partial(finish, heads, piece, share),
        outs + [shape_of(a.dtype, *a.shape) for a in copied],
        [],
        0,
        (resid, ffn_low, ffn_high, gain_own, little_own, *copied),
    )
    if fused:
        grad_inputs, grad_in, grad_gate, up_grad, gate_ff_grad = copied
    else:
        grad_in, grad_gate, _ = mix_grads
    return (
        output,
        grad_inputs,
        grad_gains,
        grad_in,
        grad_gate,
        mix_grads[2].T,
        grad_conv,
        grad_bias,
        grad_decay,
        grad_blocks,
        up_grad,
        gate_ff_grad,
        down_grad.T,
    )


def solution(mesh):
    row, col = P("dp", "mp"), P("mp", "dp")
    tok = P(("dp", "mp"), None)
    chan = P(None, "mp", "dp")
    gate = P(None, "mp", "dp", None)
    return jax.shard_map(
        shards,
        mesh=mesh,
        in_specs=(
            tok, tok, P(("dp", "mp")), P("dp", None), P("dp", None), P(),
            row, row, col, chan, chan, col, gate, row, row, col,
        ),
        out_specs=(
            tok, tok, P(None, ("dp", "mp")), row, row, col, chan, chan, col, gate, row, row, col,
        ),
        check_vma=False,
    )
```

```python
import functools

import jax
import jax.numpy as jnp
from jax import lax
from jax.experimental import pallas as pl
from jax.experimental.pallas import tpu as pltpu
from jax.sharding import PartitionSpec as P

epsilon = 1e-06
LANE = 128
SUB = 8
TAIL = 24
ROWS = 272
VMEM_MB = 62
f32 = jnp.float32
bf16 = jnp.bfloat16
GELU_C = 0.7978845608028654
GELU_A = 0.044715


def rms_scale(values):
    return lax.rsqrt(jnp.mean(values * values, axis=-1, keepdims=True) + epsilon)


def dot(left, right):
    return lax.dot_general(left, right, (((1,), (0,)), ((), ())), preferred_element_type=f32)


def dot_last(left, right):
    return lax.dot_general(left, right, (((1,), (1,)), ((), ())), preferred_element_type=f32)


def dot_first(left, right):
    return lax.dot_general(left, right, (((0,), (0,)), ((), ())), preferred_element_type=f32)


def gelu_of(v):
    return 0.5 * v * (1.0 + jnp.tanh(GELU_C * (v + GELU_A * v * v * v)))


def gelu_both(v):
    square = v * v
    th = jnp.tanh(GELU_C * (v + GELU_A * v * square))
    half = 0.5 * (1.0 + th)
    slope = half + 0.5 * v * (1.0 - th * th) * (GELU_C * (1.0 + 3.0 * GELU_A * square))
    return v * half, slope


def sigmoid(v):
    return 0.5 * jnp.tanh(0.5 * v) + 0.5


def split(values):
    high = values.astype(bf16)
    return high, (values - high.astype(f32)).astype(bf16)


def rows_of(index, rows):
    return pl.ds(pl.multiple_of(index * rows, rows), rows)


def pick_rows(order_col, count):
    places = lax.broadcasted_iota(jnp.int32, (order_col.shape[0], count), 1)
    return (places == order_col).astype(f32).astype(bf16)


def put_rows(order_row, first, rows):
    places = lax.broadcasted_iota(jnp.int32, (rows, order_row.shape[1]), 0) + first
    return (places == order_row).astype(f32).astype(bf16)


def mixer_forward(tokens, ocol, orow, pos, w_in, w_gate, chan, blocks, w_out_far, *rest):
    far, rest = rest[:8], rest[8:]
    packed, rate, prod, before, low, w_out, *near, late_sem, held_sem = rest
    gate_ref, branch_ref, conv_ref, gin_ref, grec_ref, state_ref, mixed_ref, out_ref = near
    (late_out,) = late_all([w_out_far], [w_out], late_sem)
    leaving = [
        pltpu.make_async_copy(source, target, held_sem.at[i, 0])
        for i, (source, target) in enumerate(zip(near, far))
    ]
    count, _ = tokens.shape
    width = w_in.shape[1]
    steps = count // SUB
    heads = width // LANE

    def project(b, carry):
        at = rows_of(b, ROWS)
        packed[...] = dot(pick_rows(ocol[at, :], count), tokens[...]).astype(bf16)
        branch_ref[at, :] = dot(packed[...], w_in[...])
        gate_ref[at, :] = dot(packed[...], w_gate[...])
        return carry

    lax.fori_loop(0, count // ROWS, project, 0)
    leaving[0].start()
    leaving[1].start()

    for k in range(TAIL // SUB):
        last = branch_ref[pl.ds(count - TAIL + k * SUB, SUB), :]
        before[pl.ds(k * SUB, SUB), :] = pltpu.roll(last, 1, 0)
    before[pl.ds(TAIL, ROWS), :] = branch_ref[pl.ds(0, ROWS), :]

    def gates(b, carry):
        at = rows_of(b, ROWS)

        @pl.when(b > 0)
        def _():
            before[...] = branch_ref[pl.ds(pl.multiple_of(b * ROWS - TAIL, SUB), ROWS + TAIL), :]

        place = pos[at, :]
        for h in range(heads):
            lanes = pl.ds(h * LANE, LANE)
            par = chan[:, lanes]
            conv = par[4:5] + par[0:1] * before[pl.ds(TAIL, ROWS), lanes]
            for k in range(1, 4):
                earlier = before[pl.ds(TAIL - SUB * k, ROWS), lanes]
                conv = conv + par[k : k + 1] * jnp.where(place >= k, earlier, 0.0)
            high, rest = split(conv)
            pair = jnp.concatenate([blocks[h], blocks[heads + h]], axis=1)
            pre = dot(
                jnp.concatenate([high, rest], axis=1), jnp.concatenate([pair, pair], axis=0)
            )
            gate_in = sigmoid(pre[:, :LANE] + par[5:6])
            gate_rec = sigmoid(pre[:, LANE:] + par[6:7])
            kept = jnp.exp(-8.0 * gate_rec * par[7:8])
            drive = jnp.sqrt(1.0 - kept * kept + 0.01) * gate_in * conv
            conv_ref[at, lanes] = conv
            gin_ref[at, lanes] = gate_in
            grec_ref[at, lanes] = gate_rec
            rate[at, lanes] = jnp.where(place >= 1, kept, 0.0)
            state_ref[at, lanes] = drive
        return carry

    lax.fori_loop(0, count // ROWS, gates, 0)
    for copy in leaving[2:5]:
        copy.start()

    def scan(i, carry):
        held, passed = carry
        at = rows_of(i, SUB)
        a = rate[at, :]
        held = a * held + state_ref[at, :]
        passed = a * passed
        state_ref[at, :] = held
        prod[at, :] = passed
        return held, passed

    ends = lax.fori_loop(
        0, steps, scan, (jnp.zeros((SUB, width), f32), jnp.ones((SUB, width), f32)), unroll=8
    )
    first = lax.broadcasted_iota(jnp.int32, (SUB, width), 0) == 0
    carry_in = jnp.zeros((SUB, width), f32)
    for _ in range(SUB - 1):
        carry_in = jnp.where(first, 0.0, pltpu.roll(ends[0] + ends[1] * carry_in, 1, 0))

    def finish(i, carry):
        at = rows_of(i, 2 * SUB)
        twice = jnp.concatenate([carry_in, carry_in], axis=0)
        value = state_ref[at, :] + prod[at, :] * twice
        state_ref[at, :] = value
        low[at, :] = (gelu_of(gate_ref[at, :]) * value).astype(bf16)
        return carry

    lax.fori_loop(0, steps // 2, finish, 0, unroll=2)
    leaving[5].start()
    late_out.ready()

    def leave(b, carry):
        at = rows_of(b, ROWS)
        mixed = dot(put_rows(orow[...], b * ROWS, ROWS), low[...]).astype(bf16)
        mixed_ref[at, :] = mixed
        out_ref[at, :] = dot_last(mixed, w_out[...]).astype(bf16)
        return carry

    lax.fori_loop(0, count // ROWS, leave, 0)
    for copy in leaving[6:]:
        copy.start()
    for copy in leaving:
        copy.wait()


def mixer_backward(back, w_out, ocol, orow, pos, gain, chan, blocks, *rest):
    far, (dcat_ref, dnorm_ref, little_ref, dgain_ref), rest = rest[:9], rest[9:13], rest[13:]
    dmix_arr, dmix, adj, prod, after, before, low, small_ref, dblocks_ref, *rest = rest
    gate_ref, grec_ref, state_ref, conv_ref, gin_ref, branch_ref, norm, w_in, w_gate, late_sem = rest
    late = late_all(far, rest[:9], late_sem)
    count, _ = back.shape
    width = w_in.shape[1]
    steps = count // SUB
    heads = width // LANE
    blocks_of = count // ROWS

    def enter(b, carry):
        at = rows_of(b, ROWS)
        dmix_arr[at, :] = dot(back[at, :], w_out[...]).astype(bf16)
        return carry

    lax.fori_loop(0, blocks_of, enter, 0)
    for array in late[:3]:
        array.ready()

    def pack(b, carry):
        at = rows_of(b, ROWS)
        d_mixed = dot(pick_rows(ocol[at, :], count), dmix_arr[...])
        value, slope = gelu_both(gate_ref[at, :])
        adj[at, :] = d_mixed * value
        low[at, pl.ds(width, width)] = (d_mixed * state_ref[at, :] * slope).astype(bf16)
        kept = jnp.exp(-8.0 * grec_ref[at, :] * chan[7:8, :])
        dmix[at, :] = jnp.where(pos[at, :] >= 1, kept, 0.0)
        return carry

    lax.fori_loop(0, blocks_of, pack, 0)
    for array in late:
        array.ready()

    def scan(i, carry):
        held, passed, following = carry
        at = rows_of(steps - 1 - i, SUB)
        held = following * held + adj[at, :]
        passed = following * passed
        adj[at, :] = held
        prod[at, :] = passed
        return held, passed, dmix[at, :]

    last = lax.broadcasted_iota(jnp.int32, (SUB, width), 0) == SUB - 1
    wrapped = jnp.where(last, 0.0, pltpu.roll(dmix[pl.ds(0, SUB), :], SUB - 1, 0))
    ends = lax.fori_loop(
        0,
        steps,
        scan,
        (jnp.zeros((SUB, width), f32), jnp.ones((SUB, width), f32), wrapped),
        unroll=8,
    )
    carry_in = jnp.zeros((SUB, width), f32)
    for _ in range(SUB - 1):
        carry_in = jnp.where(last, 0.0, pltpu.roll(ends[0] + ends[1] * carry_in, SUB - 1, 0))

    small_ref[...] = jnp.zeros_like(small_ref)
    dblocks_ref[...] = jnp.zeros_like(dblocks_ref)
    first = lax.broadcasted_iota(jnp.int32, (SUB, width), 0) == 0
    state_last = state_ref[pl.ds(count - SUB, SUB), :]
    before[pl.ds(TAIL - SUB, SUB), :] = jnp.where(first, 0.0, pltpu.roll(state_last, 1, 0))
    before[pl.ds(TAIL, ROWS), :] = state_ref[pl.ds(0, ROWS), :]
    wide_carry = jnp.concatenate([carry_in] * (ROWS // SUB), axis=0)

    def point(b, carry):
        at = rows_of(b, ROWS)

        @pl.when(b > 0)
        def _():
            before[...] = state_ref[pl.ds(pl.multiple_of(b * ROWS - TAIL, SUB), ROWS + TAIL), :]

        place = pos[at, :]
        for h in range(heads):
            lanes = pl.ds(h * LANE, LANE)
            par = chan[:, lanes]
            adjoint = adj[at, lanes] + prod[at, lanes] * wide_carry[:, h * LANE : (h + 1) * LANE]
            conv = conv_ref[at, lanes]
            gate_in = gin_ref[at, lanes]
            gate_rec = grec_ref[at, lanes]
            kept = jnp.exp(-8.0 * gate_rec * par[7:8])
            square = kept * kept
            inside = 1.0 - square + 0.01
            inverse = lax.rsqrt(inside)
            root = inside * inverse
            previous = before[pl.ds(TAIL - SUB, ROWS), lanes]
            d_log = adjoint * previous * dmix[at, lanes]
            scaled = adjoint * gate_in
            d_log = d_log - scaled * conv * square * inverse
            d_in = adjoint * root * conv * gate_in * (1.0 - gate_in)
            d_rec = d_log * (-8.0 * par[7:8]) * gate_rec * (1.0 - gate_rec)
            both = jnp.concatenate([d_in, d_rec], axis=1)
            high, rest = split(both)
            pair = jnp.concatenate([blocks[h], blocks[heads + h]], axis=1)
            d_conv = scaled * root + dot_last(high, pair) + dot_last(rest, pair)
            dblocks_ref[h] += dot_first(conv.astype(bf16), high)
            after[at, lanes] = d_conv
            small_ref[4:5, lanes] += jnp.sum(d_conv, axis=0, keepdims=True)
            small_ref[5:6, lanes] += jnp.sum(d_in, axis=0, keepdims=True)
            small_ref[6:7, lanes] += jnp.sum(d_rec, axis=0, keepdims=True)
            small_ref[7:8, lanes] += (
                jnp.sum(d_log * gate_rec, axis=0, keepdims=True) * (-8.0) * par[8:9]
            )
        return carry

    lax.fori_loop(0, blocks_of, point, 0)

    for k in range(TAIL // SUB):
        head = after[pl.ds(k * SUB, SUB), :]
        after[pl.ds(count + k * SUB, SUB), :] = pltpu.roll(head, SUB - 1, 0)
        tail = branch_ref[pl.ds(count - TAIL + k * SUB, SUB), :]
        before[pl.ds(k * SUB, SUB), :] = pltpu.roll(tail, 1, 0)
    before[pl.ds(TAIL, ROWS), :] = branch_ref[pl.ds(0, ROWS), :]

    def unmix(b, carry):
        at = rows_of(b, ROWS)

        @pl.when(b > 0)
        def _():
            before[...] = branch_ref[pl.ds(pl.multiple_of(b * ROWS - TAIL, SUB), ROWS + TAIL), :]

        place = pos[at, :]
        for h in range(heads):
            lanes = pl.ds(h * LANE, LANE)
            par = chan[:, lanes]
            d_conv = after[at, lanes]
            d_branch = par[0:1] * d_conv
            small_ref[0:1, lanes] += jnp.sum(
                d_conv * before[pl.ds(TAIL, ROWS), lanes], axis=0, keepdims=True
            )
            for k in range(1, 4):
                later = pl.ds(pl.multiple_of(b * ROWS + SUB * k, SUB), ROWS)
                d_branch = d_branch + par[k : k + 1] * jnp.where(
                    pos[later, :] >= k, after[later, lanes], 0.0
                )
                earlier = before[pl.ds(TAIL - SUB * k, ROWS), lanes]
                small_ref[k : k + 1, lanes] += jnp.sum(
                    jnp.where(place >= k, d_conv * earlier, 0.0), axis=0, keepdims=True
                )
            low[at, lanes] = d_branch.astype(bf16)
        return carry

    lax.fori_loop(0, blocks_of, unmix, 0)
    lines = [small_ref[0:SUB, h * LANE : (h + 1) * LANE] for h in range(heads)]
    lines.append(jnp.zeros((LANE - SUB * heads, LANE), f32))
    little_ref[:, pl.ds(2 * width, LANE)] = jnp.concatenate(lines, axis=0).T
    for h in range(heads):
        little_ref[:, pl.ds(2 * h * LANE, 2 * LANE)] = dblocks_ref[h]
    dgain_ref[...] = jnp.zeros_like(dgain_ref)

    def leave(b, carry):
        at = rows_of(b, ROWS)
        cat = dot(put_rows(orow[...], b * ROWS, ROWS), low[...]).astype(bf16)
        dcat_ref[at, :] = cat
        d_norm = dot_last(cat[:, :width], w_in[...]) + dot_last(cat[:, width:], w_gate[...])
        dgain_ref[...] += jnp.sum(d_norm * norm[at, :].astype(f32), axis=0, keepdims=True)
        dnorm_ref[at, :] = d_norm.astype(bf16)
        return carry

    lax.fori_loop(0, blocks_of, leave, 0)
    dgain_ref[...] = dgain_ref[...] / gain[...]


MESH = pl.DeviceIdType.MESH
TILE = 16
PIECES = 8
HOP = 1
AFTER = 1


def cut_rows(rows, parts):
    tiles = rows // TILE
    ends = [tiles * (k + 1) // parts for k in range(parts)]
    return [(TILE * a, TILE * (b - a)) for a, b in zip([0] + ends[:-1], ends)]


class Line:
    def __init__(self, n, local, part, arrived, whole, sums, alls):
        self.n, self.local, self.part, self.arrived, self.whole = n, local, part, arrived, whole
        self.sums, self.alls = sums, alls
        self.me = lax.axis_index("mp")
        self.pieces = cut_rows(local, PIECES)
        self.has = (self.me > 0, self.me < n - 1)

    def greet(self, plane=None):
        barrier = pltpu.get_barrier_semaphore()
        more = 0
        if plane is not None:
            for bit in plane.bits:
                more += 1
                pl.semaphore_signal(
                    barrier, inc=1, device_id={"dp": plane.other(bit)}, device_id_type=MESH
                )
        for away in range(1, self.n):
            more += 1
            pl.semaphore_signal(
                barrier,
                inc=1,
                device_id={"mp": lax.rem(self.me + away, self.n)},
                device_id_type=MESH,
            )
        pl.semaphore_wait(barrier, more)

    def rows_at(self, owner, k):
        first, rows = self.pieces[k]
        return pl.ds(pl.multiple_of(owner * self.local + first, TILE), rows)

    def copy(self, source, target, sems, way, owner, k):
        return pltpu.make_async_remote_copy(
            src_ref=source,
            dst_ref=target,
            send_sem=sems[0].at[way, owner, k],
            recv_sem=sems[1].at[way, owner, k],
            device_id={"mp": self.me + 1 - 2 * way},
            device_id_type=MESH,
        )

    def sum_copy(self, way, owner, k, first=False):
        at = self.rows_at(owner, k)
        landed = self.arrived[way].at[at]
        return self.copy(self.part.at[at] if first else landed, landed, self.sums, way, owner, k)

    def all_copy(self, way, owner, k):
        block = self.whole.at[self.rows_at(owner, k)]
        return self.copy(block, block, self.alls, way, owner, k)

    def first(self, k):
        for away in range(self.n - 1):
            for way in range(2):
                owner = away if way else self.n - 1 - away

                @pl.when(jnp.logical_not(self.has[way]))
                def _():
                    self.sum_copy(way, owner, k, True).start()

    def relay(self, k, stage):
        for way in range(2):
            late = stage - (self.n - 1 - self.me if way else self.me)
            owner = late if way else self.n - 1 - late

            @pl.when(self.has[way] & (late >= 0))
            def _():
                self.sum_copy(way, owner, k).wait_recv()
                at = self.rows_at(owner, k)
                landed = self.arrived[way]
                landed[at, :] = (landed[at, :].astype(f32) + self.part[at, :].astype(f32)).astype(bf16)
                self.sum_copy(way, owner, k).start()

    def total(self, k, into):
        at = self.rows_at(self.me, k)
        rows = pl.ds(0, self.pieces[k][1])
        into[rows, :] = self.part[at, :].astype(f32)
        for way in range(2):

            @pl.when(self.has[way])
            def _():
                self.sum_copy(way, self.me, k).wait_recv()
                into[rows, :] += self.arrived[way][at, :].astype(f32)

    def spread(self, k):
        for way in range(2):

            @pl.when(self.has[1 - way])
            def _():
                self.all_copy(way, self.me, k).start()

    def forward(self, k, stage):
        for way in range(2):
            owner = self.me + stage if way else self.me - stage
            there = owner < self.n if way else owner >= 0

            @pl.when(there)
            def _():
                self.all_copy(way, owner, k).wait_recv()

            @pl.when(there & self.has[1 - way])
            def _():
                self.all_copy(way, owner, k).start()

    def sent(self, k):
        for owner in range(self.n):
            for way in range(2):

                @pl.when(self.me > owner if way else self.me < owner)
                def _():
                    self.sum_copy(way, owner, k).wait_send()

    def finish(self):
        for k in range(PIECES):
            for owner in range(self.n):
                for way in range(2):
                    if self.whole is not None:
                        reached = self.me <= owner if way else self.me >= owner

                        @pl.when(reached & self.has[1 - way])
                        def _():
                            self.all_copy(way, owner, k).wait_send()

    def run(self, point, tasks=()):
        sums, alls = self.part is not None, self.whole is not None
        slots = [[] for _ in range(PIECES + (HOP + AFTER) * (self.n - 1) + 1)]
        for k in range(PIECES):
            done = k + HOP * (self.n - 1) if sums else 0
            if sums:
                slots[k].append((0, functools.partial(self.first, k)))
                for stage in range(1, self.n - 1):
                    slots[k + HOP * stage].append((2, functools.partial(self.relay, k, stage)))
                slots[done].append((3, functools.partial(self.sent, k)))
            slots[done].append((3, functools.partial(point, k)))
            if alls:
                slots[done].append((4, functools.partial(self.spread, k)))
                for stage in range(1, self.n):
                    at = (done if sums else k) + AFTER * stage
                    slots[at].append((1, functools.partial(self.forward, k, stage)))
        tasks = iter(tasks)
        for slot in slots:
            for step, (_, work) in enumerate(sorted(slot, key=lambda entry: entry[0])):
                if step in (0, 3):
                    next(tasks, idle)()
                work()
        for task in tasks:
            task()
        self.finish()

    def tiles(self, k, body):
        first, rows = self.pieces[k]

        def one(i, carry):
            body(
                pl.ds(pl.multiple_of(i * TILE, TILE), TILE),
                pl.ds(pl.multiple_of(first + i * TILE, TILE), TILE),
                pl.ds(pl.multiple_of(self.me * self.local + first + i * TILE, TILE), TILE),
            )
            return carry

        lax.fori_loop(0, rows // TILE, one, 0)


def idle():
    pass


class Late:
    def __init__(self, source, ref, sem):
        self.ref = ref
        self.copy = pltpu.make_async_copy(source, ref, sem)
        self.pending = True

    def begin(self):
        self.copy.start()

    def ready(self):
        if self.pending:
            self.copy.wait()
        self.pending = False


def late_all(sources, refs, sems):
    arrays = [Late(source, ref, sems.at[i]) for i, (source, ref) in enumerate(zip(sources, refs))]
    for array in arrays:
        array.begin()
    return arrays


class Plane:
    bits = (1, 2, 4)
    orders = ((4, 2, 1), (2, 4, 1))

    def __init__(self):
        self.me = lax.axis_index("dp")

    def bit(self, bit):
        return lax.rem(self.me // bit, 2)

    def other(self, *bits):
        return self.me + sum(bit * (1 - 2 * self.bit(bit)) for bit in bits)

    def gather_copies(self, item, view, halves, stage, sems):
        copies = []
        for half in halves:
            order = self.orders[half]
            for combo in range(1 << stage):
                flipped = [bit for i, bit in enumerate(order[:stage]) if combo >> i & 1]
                block = view(self.other(*flipped), half)
                slot = (1 << stage) - 1 + combo
                copies.append(
                    pltpu.make_async_remote_copy(
                        src_ref=block,
                        dst_ref=block,
                        send_sem=sems[0].at[item, half, slot],
                        recv_sem=sems[1].at[item, half, slot],
                        device_id={"dp": self.other(order[stage])},
                        device_id_type=MESH,
                    )
                )
        return copies


class Reduce(Plane):
    def __init__(self, index, left, right, lanes, sent, mine, theirs, got, second, third, out, sems):
        super().__init__()
        self.sent, self.theirs = sent, theirs
        self.index, self.left, self.right, self.lanes = index, left, right, lanes
        self.mine, self.got = mine.at[index], got.at[index]
        self.second, self.third, self.out = second.at[index], third.at[index], out
        self.sems = sems
        self.rows = out.shape[0]
        self.half = self.rows // 2

    def copy(self, source, target, slot, bit):
        return pltpu.make_async_remote_copy(
            src_ref=source,
            dst_ref=target,
            send_sem=self.sems[0].at[self.index, slot],
            recv_sem=self.sems[1].at[self.index, slot],
            device_id={"dp": self.other(bit)},
            device_id_type=MESH,
        )

    def core_copy(self, t):
        return self.copy(self.theirs.at[(4 * self.index + t) % 2], self.got.at[t], t, 1)

    def second_copy(self, half, j):
        x, y = self.bit(2), self.bit(4)
        block = (1 - y) * 2 + j if half else j * 2 + 1 - x
        rows = self.mine.at[block, pl.ds(half * self.half, self.half)]
        return self.copy(rows, self.second.at[half, j], 4 + 2 * half + j, 4 if half else 2)

    def third_block(self, half):
        x, y = self.bit(2), self.bit(4)
        return y * 2 + 1 - x if half else (1 - y) * 2 + x

    def third_copy(self, half):
        rows = self.mine.at[self.third_block(half), pl.ds(half * self.half, self.half)]
        return self.copy(rows, self.third.at[half], 8 + half, 2 if half else 4)

    def product(self, t):
        def task():
            core = self.bit(1)
            pair = pl.ds(t * 2 * self.rows, 2 * self.rows)
            if t == 0:
                self.left.ready()
                self.right.ready()
            if len(self.sent) > 1:
                self.sent[-2].wait_send()
            both = dot_first(self.left.ref[:, pair], self.right.ref[:, self.lanes])
            low, high = both[: self.rows], both[self.rows :]
            self.mine[t] = jnp.where(core == 0, low, high).astype(bf16)
            self.theirs[(4 * self.index + t) % 2] = jnp.where(core == 0, high, low).astype(bf16)
            self.sent.append(self.core_copy(t))
            self.sent[-1].start()

        return task

    def keep(self, t):
        return self.mine[t]

    def add_core(self):
        for t in range(4):
            self.core_copy(t).wait_recv()
            self.mine[t] = (self.keep(t).astype(f32) + self.got[t].astype(f32)).astype(self.mine.dtype)
        for half in range(2):
            for j in range(2):
                self.second_copy(half, j).start()

    def add_second(self):
        for half in range(2):
            for j in range(2):
                self.second_copy(half, j).wait_recv()
        for half in range(2):
            block, at = self.third_block(half), pl.ds(half * self.half, self.half)
            far = 1 - self.bit(2 if half else 4)
            self.mine[block, at] = (
                self.mine[block, at].astype(f32) + self.second[half, far].astype(f32)
            ).astype(self.mine.dtype)
            self.third_copy(half).start()

    def add_third(self):
        own = self.bit(4) * 2 + self.bit(2)
        for half in range(2):
            self.third_copy(half).wait_recv()
            at = pl.ds(half * self.half, self.half)
            near = self.bit(2 if half else 4)
            self.out[at, :] = (
                self.mine[own, at].astype(f32)
                + self.second[half, near].astype(f32)
                + self.third[half].astype(f32)
            )

    def finish(self):
        for half in range(2):
            for j in range(2):
                self.second_copy(half, j).wait_send()
            self.third_copy(half).wait_send()


class Given(Reduce):
    def __init__(self, given, mine, got, second, third, out, sems):
        super().__init__(0, None, None, None, None, mine, None, got, second, third, out, sems)
        self.given = given

    def rows_of(self, t, core):
        return pl.ds(pl.multiple_of((2 * t + core) * self.rows, self.rows), self.rows)

    def core_copy(self, t):
        return self.copy(self.given.at[self.rows_of(t, 1 - self.bit(1))], self.got.at[t], t, 1)

    def start(self):
        for t in range(4):
            self.core_copy(t).start()

    def finish(self):
        for t in range(4):
            self.core_copy(t).wait_send()
        super().finish()

    def keep(self, t):
        return self.given[self.rows_of(t, self.bit(1)), :]


def reduce_tasks(parts, given=()):
    tasks = [part.product(t) for part in parts for t in range(4)]

    def also(at, extra):
        while len(tasks) <= at:
            tasks.append(idle)
        before = tasks[at]

        def both():
            extra()
            before()

        tasks[at] = both

    for i, part in enumerate(parts):
        also(4 * i + 5, part.add_core)
        also(4 * i + 8, part.add_second)
        also(4 * i + 10, part.add_third)

    for part in given:
        also(0, part.start)
        also(2, part.add_core)
        also(4, part.add_second)
        also(6, part.add_third)

    def finish():
        for ring in {id(part.sent): part.sent for part in parts}.values():
            for copy in ring[-2:]:
                copy.wait_send()
        for part in [*parts, *given]:
            part.finish()

    return tasks, finish


def given_scratch(rows, width):
    sem = pltpu.SemaphoreType.DMA((1, 10))
    return [
        pltpu.VMEM((1, 4, rows, width), f32),
        pltpu.VMEM((1, 4, rows, width), f32),
        pltpu.VMEM((1, 2, 2, rows // 2, width), f32),
        pltpu.VMEM((1, 2, rows // 2, width), f32),
        sem,
        sem,
    ]


def reduce_scratch(arrays, rows, width):
    block = pltpu.VMEM((arrays, 4, rows, width), bf16)
    sem = pltpu.SemaphoreType.DMA((arrays, 10))
    return [
        block,
        pltpu.VMEM((2, rows, width), bf16),
        block,
        pltpu.VMEM((arrays, 2, 2, rows // 2, width), bf16),
        pltpu.VMEM((arrays, 2, rows // 2, width), bf16),
        sem,
        sem,
    ]


def gather_norm(n, x, gain, whole, send, recv):
    line = Line(n, x.shape[0], None, None, whole, None, (send, recv))
    line.greet()

    def point(k):
        def one(_, own, at):
            v = x[own, :].astype(f32)
            whole[at, :] = (v * rms_scale(v) * gain[...]).astype(bf16)

        line.tiles(k, one)

    line.run(point)


def row_view(array, rows):
    def view(owner, half):
        first = owner * rows + half * (rows // 2)
        return array.at[pl.ds(pl.multiple_of(first, TILE), rows // 2)]

    return view


def gather_tasks(plane, items, sems):
    def copies(stage):
        return [
            copy
            for item, (view, halves) in enumerate(items)
            for copy in plane.gather_copies(item, view, halves, stage, sems)
        ]

    def stage_task(stage):
        def task():
            if stage:
                for copy in copies(stage - 1):
                    copy.wait_recv()
            for copy in copies(stage):
                copy.start()

        return task

    def last():
        for copy in copies(2):
            copy.wait_recv()
        for stage in range(3):
            for copy in copies(stage):
                copy.wait_send()

    return stage_task(0), stage_task(1), stage_task(2), last


def gather_weights(
    n,
    x,
    gain,
    w_in,
    w_gate,
    w_out,
    blocks,
    chan,
    whole,
    all_in,
    all_gate,
    all_out,
    all_blocks,
    all_chan,
    send,
    recv,
    raw,
    plane_send,
    plane_recv,
):
    line = Line(n, x.shape[0], None, None, whole, None, (send, recv))
    plane = Plane()
    line.greet(plane)
    sems = plane_send, plane_recv
    rows, piece = w_in.shape[0], blocks.shape[1]
    lines = chan.shape[0]

    def blocks_view(owner, half):
        return all_blocks.at[:, pl.ds(pl.multiple_of(owner * piece, TILE), piece)]

    def chan_view(owner, half):
        return raw.at[pl.ds(pl.multiple_of(owner * lines, TILE), lines)]

    items = [(row_view(array, rows), (0, 1)) for array in (all_in, all_gate, all_out)]
    items += [(blocks_view, (0,)), (chan_view, (1,))]

    first, second, third, finish = gather_tasks(plane, items, sems)

    def last():
        finish()
        lane = lax.broadcasted_iota(jnp.int32, (LANE, LANE), 1)
        row = lax.broadcasted_iota(jnp.int32, (LANE, LANE), 0)
        total = jnp.zeros((lines, LANE), f32)
        for owner in range(LANE // piece):
            moved = ((row < piece) & (row + owner * piece == lane)).astype(f32).astype(bf16)
            total = total + dot(raw[pl.ds(owner * lines, lines), :], moved)
        for h in range(lines // SUB):
            par = total[h * SUB : (h + 1) * SUB]
            lanes = pl.ds(h * LANE, LANE)
            all_chan[0:SUB, lanes] = par
            decay = par[SUB - 1 : SUB]
            small = jnp.exp(-jnp.abs(decay))
            one_more = 1.0 + small
            rest = jnp.where(one_more == 1.0, 1.0, one_more - 1.0)
            log_one_more = jnp.where(one_more == 1.0, small, jnp.log(one_more) * (small / rest))
            all_chan[SUB - 1 : SUB, lanes] = jnp.maximum(decay, 0.0) + log_one_more
            all_chan[SUB : 2 * SUB, lanes] = jnp.broadcast_to(sigmoid(decay), (SUB, LANE))

    own = pl.ds(pl.multiple_of(plane.me * rows, TILE), rows)
    all_in[own, :] = w_in[...]
    all_gate[own, :] = w_gate[...]
    all_out[own, :] = w_out[...]
    all_blocks[:, pl.ds(pl.multiple_of(plane.me * piece, TILE), piece), :] = blocks[...]
    raw[pl.ds(pl.multiple_of(plane.me * lines, TILE), lines), :] = chan[...]

    def point(k):
        def one(_, own, at):
            v = x[own, :].astype(f32)
            whole[at, :] = (v * rms_scale(v) * gain[...]).astype(bf16)

        line.tiles(k, one)

    first()
    line.run(point, [idle] * 4 + [second] + [idle] * 3 + [third] + [idle] * 3 + [last])


def norm_back(value, gain, grad):
    scale = rms_scale(value)
    e = gain * grad
    slope = scale * scale * scale * jnp.mean(value * e, axis=-1, keepdims=True)
    return scale * e - value * slope, grad * value * scale


def middle(n, x, gain, cot, part, *rest):
    shares, (d_resid, gain_grad, back), far, rest = rest[:3], rest[3:6], rest[6:14], rest[14:]
    left, right, total, ss, sr, send, recv, part2, ss2, sr2, send2, recv2, csend, crecv, *rest = rest
    up_s, value_s, grad_s, *rest = rest
    *rest, held_sem = rest
    near, rest = rest[-8:], rest[:-8]
    whole, cots, resid, hidden, d_up, d_gate, low_part, high_part = near
    plane = Plane() if rest else None
    w_up, w_gate, w_down = weights = rest[:3] if rest else shares
    local = x.shape[0]
    line = Line(n, local, part, (left, right), whole, (ss, sr), (send, recv))
    back_line = Line(n, local, part2, (left, right), back, (ss2, sr2), (send2, recv2))
    cot_line = Line(n, local, None, None, cots, None, (csend, crecv))
    line.greet(plane)
    gain_grad[...] = jnp.zeros_like(gain_grad)
    leaving = [
        pltpu.make_async_copy(source, target, held_sem.at[i])
        for i, (source, target) in enumerate(zip(near, far))
    ]

    def keep_cot(_, own, at):
        cots[at, :] = cot[own, :]

    def point(k):
        line.total(k, total)

        def one(here, own, at):
            v = x[own, :].astype(f32) + total[here, :]
            resid[own, :] = v
            whole[at, :] = (v * rms_scale(v) * gain[...]).astype(bf16)

        line.tiles(k, one)

    def back_point(k):
        back_line.total(k, total)

        def one(here, own, at):
            grad, terms = norm_back(resid[own, :], gain[...], total[here, :])
            gain_grad[...] += jnp.sum(terms, axis=0, keepdims=True)
            value = cot[own, :].astype(f32) + grad
            d_resid[own, :] = value
            back[at, :] = value.astype(bf16)

        line.tiles(k, one)

    def pair_steps(j):
        first = line.pieces[2 * j][0]
        rows = line.pieces[2 * j][1] + line.pieces[2 * j + 1][1]
        at = [pl.ds(owner * local + first, rows) for owner in range(n)]
        here = pl.ds(0, n * rows)

        def read(array):
            return jnp.concatenate([array[rows_at, :] for rows_at in at], axis=0)

        def write(array, value):
            for owner, rows_at in enumerate(at):
                array[rows_at, :] = value[owner * rows : (owner + 1) * rows]

        def up():
            up_s[here, :] = dot(read(whole), w_up[...])

        def gate():
            value, slope = gelu_both(dot(read(whole), w_gate[...]))
            write(hidden, (value * up_s[here, :]).astype(bf16))
            value_s[here, :] = value
            up_s[here, :] = up_s[here, :] * slope

        def into_hidden():
            d_hidden = dot(read(cots), w_down[...])
            write(d_up, (d_hidden * value_s[here, :]).astype(bf16))
            write(d_gate, (d_hidden * up_s[here, :]).astype(bf16))

        def through_up():
            grad_s[here, :] = dot_last(read(d_up), w_up[...])

        def through_gate():
            write(part2, (grad_s[here, :] + dot_last(read(d_gate), w_gate[...])).astype(bf16))

        def project():
            value = dot_last(read(hidden), w_down[...]).astype(bf16)
            write(low_part, value[:, : value.shape[1] // 2])
            write(high_part, value[:, value.shape[1] // 2 :])

        return up, gate, into_hidden, through_up, through_gate, project

    hops = n - 1
    slots = [[] for _ in range(PIECES + 5 * hops)]

    def put(slot, order, work, *args):
        slots[slot].append((order, functools.partial(work, *args)))

    for k in range(PIECES):
        put(k, 0, line.first, k)
        for stage in range(1, hops):
            put(k + stage, 2, line.relay, k, stage)
        met = k + hops
        put(met, 3, line.sent, k)
        put(met, 3, point, k)
        put(met, 3, line.spread, k)
        given = k if 2 * k < PIECES else min(2 * k - PIECES // 2 + 1, PIECES + 2)
        put(given, 0, cot_line.tiles, k, keep_cot)
        put(given, 0, cot_line.spread, k)
        for stage in range(1, n):
            put(met + stage, 1, line.forward, k, stage)
            put(given + stage, 1, cot_line.forward, k, stage)
    for j in range(PIECES // 2):
        slot = 2 * j + 2 + 2 * hops
        steps = pair_steps(j)
        for at, order, step in zip((0, 0, 0, 1, 1, 1), (0.5, 1.5, 2.5, 0.5, 1.5, 3.5), steps):
            put(slot + at, order, step)
        for k in (2 * j, 2 * j + 1):
            begun = slot + 1 + k % 2
            put(begun, 2 if begun == slot + 1 else 0, back_line.first, k)
            for stage in range(1, hops):
                put(begun + stage, 2, back_line.relay, k, stage)
            put(begun + hops, 3, back_line.sent, k)
            put(begun + hops, 3, back_point, k)
            put(begun + hops, 3, back_line.spread, k)
            for stage in range(1, n):
                put(begun + hops + stage, 1, back_line.forward, k, stage)
    done = PIECES + 2 * hops + 2
    for copy in leaving:
        put(done, 0, copy.start)
    if plane is not None:
        rows = shares[0].shape[0]
        own = pl.ds(pl.multiple_of(plane.me * rows, TILE), rows)
        for share, array in zip(shares, weights):
            array[own, :] = share[...]
        items = [(row_view(array, rows), (0, 1)) for array in weights]
        stages = gather_tasks(plane, items, rest[3:])
        for slot, stage in zip((0, 3, 6, 2 * hops + 2), stages):
            put(slot, 0, stage)
    for slot in slots:
        for _, work in sorted(slot, key=lambda entry: entry[0]):
            work()
    for each in (line, back_line, cot_line):
        each.finish()
    for copy in leaving:
        copy.wait()


def sum_back(n, x, d_resid, gain, part, *rest):
    if len(rest) > 6:
        little, gains, *rest = rest
        sources, rest = rest[:9], rest[9:]
        grad_x, *outs, little_out, gains_out = rest[:9]
        left, right, total, ss, sr, *reduce = rest[9:]
        wide, late_refs, late_sems = reduce[22:29], reduce[29:34], reduce[34]
        given = [
            Given(little, *reduce[7:11], little_out, reduce[11:13]),
            Given(gains, *reduce[13:17], gains_out, reduce[17:19]),
        ]
        met, met_send, met_recv = reduce[19:22]
    else:
        grad_x, left, right, total, ss, sr = rest
        sources = ()
    line = Line(n, x.shape[0], part, (left, right), None, (ss, sr), None)
    line.greet(Plane() if sources else None)

    def point(k):
        line.total(k, total)

        def one(here, own, at):
            back, _ = norm_back(x[own, :].astype(f32), gain[...], total[here, :])
            grad_x[own, :] = (d_resid[own, :] + back).astype(bf16)

        line.tiles(k, one)

    if not sources:
        line.run(point)
        return
    left_a, left_b, right_a, right_b, right_c = late_refs
    across, width = sources[7].shape[1], sources[8].shape[1]
    places = (left_a, left_b, right_a, right_b, right_c)
    places += (left_a, left_b, right_a.at[:, pl.ds(0, across)], right_c.at[:, pl.ds(0, width)])
    mid, cots, d_up, d_gate, hidden, norm, back_all, cat, mixed = (
        Late(source, ref, late_sems.at[i]) for i, (source, ref) in enumerate(zip(sources, places))
    )
    for array in (mid, d_up, d_gate, cots, hidden):
        array.begin()
    every, sent, sent_wide = slice(None), [], []
    wide_sides = ((mid, d_up, every), (mid, d_gate, every), (cots, hidden, every))
    sides = (
        (norm, cat, slice(0, width)),
        (norm, cat, slice(width, 2 * width)),
        (back_all, mixed, every),
    )
    parts = [
        Reduce(i, *side, sent_wide, *wide[:5], out, wide[5:7])
        for i, (side, out) in enumerate(zip(wide_sides, outs))
    ]
    parts += [
        Reduce(i, *side, sent, *reduce[:5], out, reduce[5:7])
        for i, (side, out) in enumerate(zip(sides, outs[3:]))
    ]
    tasks, finish = reduce_tasks(parts, given)

    def then(task, *arrays):
        def both():
            task()
            for array in arrays:
                array.begin()

        return both

    tasks[7] = then(tasks[7], norm, cat)
    tasks[11] = then(tasks[11], back_all, mixed)
    me = lax.axis_index("mp")

    def meet(away):
        return pltpu.make_async_remote_copy(
            src_ref=gains_out,
            dst_ref=met.at[away - 1],
            send_sem=met_send.at[away - 1],
            recv_sem=met_recv.at[away - 1],
            device_id={"mp": lax.rem(me + away, n)},
            device_id_type=MESH,
        )

    def send_gains():
        for away in range(1, n):
            meet(away).start()

    def add_gains():
        for away in range(1, n):
            meet(away).wait()
        gains_out[...] += sum(met[away] for away in range(n - 1))

    tasks[7:7] = [send_gains]
    line.run(point, tasks)
    finish()
    add_gains()


def line_call(body, n, identity, outs, sums, alls, args, more=(), late=0, held=0):
    whole = pl.BlockSpec(memory_space=pltpu.VMEM)
    local, model = args[0].shape
    sem = pltpu.SemaphoreType.DMA((2, n, PIECES))
    scratch = []
    if sums:
        scratch += [pltpu.VMEM((n * local, model), bf16)] * 2
        scratch += [pltpu.VMEM((max(rows for _, rows in cut_rows(local, PIECES)), model), f32)]
        scratch += [sem, sem]
    if alls:
        scratch += [sem, sem]
    scratch += more
    if held:
        scratch += [pltpu.VMEM(o.shape, o.dtype) for o in outs[len(outs) - held :]]
        scratch += [pltpu.SemaphoreType.DMA((held,))]
    away = pl.BlockSpec(memory_space=pl.ANY)
    moved = sum(a.size * a.dtype.itemsize for a in args)
    return pl.pallas_call(
        functools.partial(body, n),
        out_shape=outs,
        in_specs=[whole] * (len(args) - late) + [away] * late,
        out_specs=[whole] * (len(outs) - held) + [away] * held,
        scratch_shapes=scratch,
        compiler_params=pltpu.CompilerParams(
            vmem_limit_bytes=VMEM_MB << 20, collective_id=identity, has_side_effects=True
        ),
        cost_estimate=pl.CostEstimate(flops=0, bytes_accessed=100 * moved, transcendentals=0),
    )(*args)


def finish(heads, piece, share, resid, low, high, gains, little, *rest):
    count = (len(rest) - 6) // 2
    sources, rest = rest[:count], rest[count:]
    output, grad_gains, grad_conv, grad_bias, grad_decay, grad_blocks, *targets = rest
    for source, target in zip(sources, targets):
        target[...] = source[...]
    half = low.shape[1]
    output[:, :half] = (resid[:, :half] + low[...].astype(f32)).astype(bf16)
    output[:, half:] = (resid[:, half:] + high[...].astype(f32)).astype(bf16)
    for position in range(gains.shape[0] // 2):

        @pl.when(lax.axis_index("mp") == position)
        def _():
            grad_gains[...] = gains[2 * position : 2 * position + 2, :share]

    for h in range(heads):
        for gate in range(2):
            first = (2 * h + gate) * LANE
            grad_blocks[gate, h] = little[:, first : first + LANE]
    first = 2 * heads * LANE
    lines = little[:, first : first + LANE]
    lines = jnp.concatenate([lines, jnp.zeros((LANE - piece, LANE), f32)], axis=0).T
    for h in range(heads):
        for k in range(SUB):
            row = lines[h * SUB + k : h * SUB + k + 1, :piece]
            if k < 4:
                grad_conv[k, h : h + 1, :] = row
            elif k < SUB - 1:
                grad_bias[k - 4, h : h + 1, :] = row
            else:
                grad_decay[h : h + 1, :] = row


def local_call(body, outs, scratch, flops, args, late=0, held=0):
    whole, away = pl.BlockSpec(memory_space=pltpu.VMEM), pl.BlockSpec(memory_space=pl.ANY)
    twins = list(args[len(args) - late :]) + list(outs[len(outs) - held :])
    scratch = scratch + [pltpu.VMEM(a.shape, a.dtype) for a in twins]
    if late:
        scratch.append(pltpu.SemaphoreType.DMA((late,)))
    if held:
        scratch.append(pltpu.SemaphoreType.DMA((held, 4)))
    moved = sum(a.size * a.dtype.itemsize for a in args)
    moved += sum(o.size * o.dtype.itemsize for o in outs)
    return pl.pallas_call(
        body,
        out_shape=outs,
        in_specs=[whole] * (len(args) - late) + [away] * late,
        out_specs=[whole] * (len(outs) - held) + [away] * held,
        scratch_shapes=scratch,
        compiler_params=pltpu.CompilerParams(vmem_limit_bytes=VMEM_MB << 20),
        cost_estimate=pl.CostEstimate(flops=flops, bytes_accessed=moved, transcendentals=0),
    )(*args)


def shape_of(dtype, *shape):
    return jax.ShapeDtypeStruct(shape, dtype)


def shards(
    inputs,
    cotangent,
    token_mask,
    order,
    lengths,
    gains,
    w_in,
    w_gate,
    w_out,
    conv_weight,
    chan_bias,
    decay,
    gate_blocks,
    w_up,
    w_gate_ff,
    w_down,
):
    n_dp = lax.axis_size("dp")
    local_rows, model = inputs.shape
    count = local_rows * lax.axis_size("mp")
    heads, piece = decay.shape
    width = heads * piece * n_dp
    hidden_width = w_up.shape[1]

    fused = n_dp == 8
    rows = model // n_dp
    out_rows, down_rows = w_out.T, w_down.T
    lines = jnp.concatenate([conv_weight, chan_bias, decay[None]], axis=0).transpose(1, 0, 2)
    lines = lines.reshape(SUB * heads, piece)

    steps = count // SUB
    ends = jnp.cumsum(lengths[0], dtype=jnp.int32)
    starts = ends - lengths[0]
    places = jnp.arange(count, dtype=jnp.int32)
    own_start = jnp.max(
        jnp.where(places[:, None] >= starts[None, :], starts[None, :], 0), axis=1
    )
    pos = (places - own_start).reshape(SUB, steps).T
    wrap = jnp.concatenate([pos[: TAIL // SUB, 1:], jnp.full((TAIL // SUB, 1), -1, jnp.int32)], axis=1)
    pos_col = jnp.concatenate([pos, wrap], axis=0).reshape(count + TAIL, 1)
    order_int = order[0].reshape(SUB, steps).T.reshape(count)
    ocol, orow = order_int.reshape(count, 1), order_int.reshape(1, count)

    gain_f = gains.astype(f32)
    n_mp = lax.axis_size("mp")
    tok = shape_of(bf16, count, model)
    own = shape_of(f32, local_rows, model)
    if fused:
        grown = shape_of(bf16, model, width)
        norm_group, full_in, full_gate, full_out, blocks, chan = line_call(
            gather_weights,
            n_mp,
            0,
            [tok, grown, grown, grown, shape_of(bf16, 2 * heads, LANE, LANE), shape_of(f32, 16, width)],
            False,
            True,
            (
                inputs,
                gain_f[0:1],
                w_in,
                w_gate,
                out_rows,
                gate_blocks.reshape(2 * heads, piece, LANE),
                jnp.pad(lines, ((0, 0), (0, LANE - piece))),
            ),
            [pltpu.VMEM((n_dp * SUB * heads, LANE), bf16)] + [pltpu.SemaphoreType.DMA((5, 2, 7))] * 2,
        )
    else:
        (norm_group,) = line_call(gather_norm, n_mp, 0, [tok], False, True, (inputs, gain_f[0:1]))
        full_in = lax.all_gather(w_in, "dp", axis=0, tiled=True)
        full_gate = lax.all_gather(w_gate, "dp", axis=0, tiled=True)
        full_out = lax.all_gather(out_rows, "dp", axis=0, tiled=True)
        blocks = lax.all_gather(gate_blocks, "dp", axis=2, tiled=True).reshape(2 * heads, LANE, LANE)
        params = lax.all_gather(lines, "dp", axis=1, tiled=True).astype(f32)
        params = params.reshape(heads, SUB, LANE).transpose(1, 0, 2).reshape(SUB, width)
        decay_row = params[7:8]
        chan = jnp.concatenate(
            [params[:7], jax.nn.softplus(decay_row)] + [jax.nn.sigmoid(decay_row)] * SUB, axis=0
        )
    cot = cotangent * token_mask.astype(bf16)[:, None]

    wide = pltpu.VMEM((count, width), f32)
    saved = [shape_of(f32, count, width)] * 6
    gate_pre, branch, conv, gate_in, gate_rec, state, mixed, back_part = local_call(
        mixer_forward,
        saved + [shape_of(bf16, count, width), shape_of(bf16, count, model)],
        [
            pltpu.VMEM((ROWS, model), bf16),
            wide,
            wide,
            pltpu.VMEM((ROWS + TAIL, width), f32),
            pltpu.VMEM((count, width), bf16),
        ],
        2 * count * (count * model + 3 * model * width),
        (norm_group, ocol, orow, pos_col, full_in, full_gate, chan, blocks, full_out),
        1,
        8,
    )
    shares = (w_up, w_gate_ff, down_rows)
    if not fused:
        shares = [lax.all_gather(share, "dp", axis=0, tiled=True) for share in shares]
    hid = shape_of(bf16, count, hidden_width)
    half = shape_of(bf16, count, model // 2)
    pieces = cut_rows(local_rows, PIECES)
    most = n_mp * max(pieces[k][1] + pieces[k + 1][1] for k in range(0, PIECES, 2))
    pair = pltpu.VMEM((most, hidden_width), f32)
    flow = pltpu.SemaphoreType.DMA((2, n_mp, PIECES))
    plane_scratch = [pltpu.VMEM((model, hidden_width), bf16)] * 3 + [pltpu.SemaphoreType.DMA((3, 2, 7))] * 2
    (
        d_resid,
        gain_mid,
        back_group,
        norm_mid_group,
        cot_group,
        resid,
        hidden,
        d_up,
        d_gate_ff,
        *ffn_parts,
    ) = line_call(
        middle,
        n_mp,
        1,
        [own, shape_of(f32, 1, model), tok, tok, tok, own, hid, hid, hid, half, half],
        True,
        True,
        (inputs, gain_f[1:2], cot, back_part, *shares),
        [pltpu.VMEM((count, model), bf16)]
        + [flow] * 6
        + [pair, pair, pltpu.VMEM((most, model), f32)]
        + plane_scratch * fused,
        held=8,
    )

    def reduced(left, right):
        grad = dot_first(left, right).astype(bf16)
        return lax.psum_scatter(grad, "dp", scatter_dimension=0, tiled=True).astype(f32)

    d_cat, d_norm_back, little, gain_in = local_call(
        mixer_backward,
        [
            shape_of(bf16, count, 2 * width),
            tok,
            shape_of(f32, LANE, 2 * width + LANE),
            shape_of(f32, 1, model),
        ],
        [
            pltpu.VMEM((count, width), bf16),
            wide,
            wide,
            wide,
            pltpu.VMEM((count + TAIL, width), f32),
            pltpu.VMEM((ROWS + TAIL, width), f32),
            pltpu.VMEM((count, 2 * width), bf16),
            pltpu.VMEM((SUB, width), f32),
            pltpu.VMEM((heads, LANE, 2 * LANE), f32),
        ],
        2 * count * (3 * count * width + 3 * model * width),
        (
            back_group,
            full_out,
            ocol,
            orow,
            pos_col,
            gain_f[0:1],
            chan,
            blocks,
            gate_pre,
            gate_rec,
            state,
            conv,
            gate_in,
            branch,
            norm_group,
            full_in,
            full_gate,
        ),
        9,
    )
    share = model // (n_dp * n_mp)
    gain_parts = jnp.concatenate([gain_in, gain_mid], axis=0).reshape(2, n_dp, n_mp, share)
    gain_parts = gain_parts.transpose(1, 2, 0, 3).reshape(n_dp, 2 * n_mp, share)
    gain_parts = jnp.pad(gain_parts, ((0, 0), (0, 2 * SUB - 2 * n_mp), (0, LANE - share)))
    gain_parts = gain_parts.reshape(2 * SUB * n_dp, LANE)
    ffn_low, ffn_high = (
        lax.psum_scatter(part, "mp", scatter_dimension=0, tiled=True) for part in ffn_parts
    )
    ffn_low, d_norm_back = lax.optimization_barrier((ffn_low, d_norm_back))
    grad_inputs, *mix_grads = line_call(
        sum_back,
        n_mp,
        3,
        [shape_of(bf16, local_rows, model)]
        + (
            [shape_of(f32, rows, hidden_width)] * 3
            + [shape_of(f32, rows, width)] * 3
            + [shape_of(f32, piece, little.shape[1]), shape_of(f32, 2 * SUB, LANE)]
        )
        * fused,
        True,
        False,
        (inputs, d_resid, gain_f[0:1], d_norm_back)
        + (
            (
                little,
                gain_parts,
                norm_mid_group,
                cot_group,
                d_up,
                d_gate_ff,
                hidden,
                norm_group,
                back_group,
                d_cat,
                mixed,
            )
            if fused
            else ()
        ),
        reduce_scratch(3, rows, width)
        + given_scratch(piece, little.shape[1])
        + given_scratch(2 * SUB, LANE)
        + [pltpu.VMEM((n_mp - 1, 2 * SUB, LANE), f32)]
        + [pltpu.SemaphoreType.DMA((n_mp - 1,))] * 2
        + reduce_scratch(3, rows, hidden_width)
        + [pltpu.VMEM((count, model), bf16)] * 2
        + [pltpu.VMEM((count, hidden_width), bf16)] * 3
        + [pltpu.SemaphoreType.DMA((9,))]
        if fused
        else (),
        9 * fused,
    )
    if fused:
        up_grad, gate_ff_grad, down_grad, *mix_grads, little_own, gain_own = mix_grads
    else:
        up_grad = reduced(norm_mid_group, d_up)
        gate_ff_grad = reduced(norm_mid_group, d_gate_ff)
        down_grad = reduced(cot_group, hidden)
        mix_grads = [
            reduced(norm_group, d_cat[:, :width]),
            reduced(norm_group, d_cat[:, width:]),
            reduced(back_group, mixed),
        ]
        little_own = lax.psum_scatter(little, "dp", scatter_dimension=0, tiled=True)
        gain_own = lax.psum(lax.psum_scatter(gain_parts, "dp", scatter_dimension=0, tiled=True), "mp")
    outs = [
        shape_of(bf16, local_rows, model),
        shape_of(f32, 2, share),
        shape_of(f32, 4, heads, piece),
        shape_of(f32, 3, heads, piece),
        shape_of(f32, heads, piece),
        shape_of(f32, 2, heads, piece, LANE),
    ]
    copied = [grad_inputs, mix_grads[0], mix_grads[1], up_grad, gate_ff_grad] if fused else []
    output, grad_gains, grad_conv, grad_bias, grad_decay, grad_blocks, *copied = local_call(
        functools.partial(finish, heads, piece, share),
        outs + [shape_of(a.dtype, *a.shape) for a in copied],
        [],
        0,
        (resid, ffn_low, ffn_high, gain_own, little_own, *copied),
    )
    if fused:
        grad_inputs, grad_in, grad_gate, up_grad, gate_ff_grad = copied
    else:
        grad_in, grad_gate, _ = mix_grads
    return (
        output,
        grad_inputs,
        grad_gains,
        grad_in,
        grad_gate,
        mix_grads[2].T,
        grad_conv,
        grad_bias,
        grad_decay,
        grad_blocks,
        up_grad,
        gate_ff_grad,
        down_grad.T,
    )


def solution(mesh):
    row, col = P("dp", "mp"), P("mp", "dp")
    tok = P(("dp", "mp"), None)
    chan = P(None, "mp", "dp")
    gate = P(None, "mp", "dp", None)
    return jax.shard_map(
        shards,
        mesh=mesh,
        in_specs=(
            tok, tok, P(("dp", "mp")), P("dp", None), P("dp", None), P(),
            row, row, col, chan, chan, col, gate, row, row, col,
        ),
        out_specs=(
            tok, tok, P(None, ("dp", "mp")), row, row, col, chan, chan, col, gate, row, row, col,
        ),
        check_vma=False,
    )
```

```python
import functools

import jax
import jax.numpy as jnp
from jax import lax
from jax.experimental import pallas as pl
from jax.experimental.pallas import tpu as pltpu
from jax.sharding import PartitionSpec as P

epsilon = 1e-06
LANE = 128
SUB = 8
TAIL = 24
ROWS = 272
VMEM_MB = 62
f32 = jnp.float32
bf16 = jnp.bfloat16
GELU_C = 0.7978845608028654
GELU_A = 0.044715


def rms_scale(values):
    return lax.rsqrt(jnp.mean(values * values, axis=-1, keepdims=True) + epsilon)


def dot(left, right):
    return lax.dot_general(left, right, (((1,), (0,)), ((), ())), preferred_element_type=f32)


def dot_last(left, right):
    return lax.dot_general(left, right, (((1,), (1,)), ((), ())), preferred_element_type=f32)


def dot_first(left, right):
    return lax.dot_general(left, right, (((0,), (0,)), ((), ())), preferred_element_type=f32)


def gelu_of(v):
    return 0.5 * v * (1.0 + jnp.tanh(GELU_C * (v + GELU_A * v * v * v)))


def gelu_both(v):
    square = v * v
    th = jnp.tanh(GELU_C * (v + GELU_A * v * square))
    half = 0.5 * (1.0 + th)
    slope = half + 0.5 * v * (1.0 - th * th) * (GELU_C * (1.0 + 3.0 * GELU_A * square))
    return v * half, slope


def sigmoid(v):
    return 0.5 * jnp.tanh(0.5 * v) + 0.5


def split(values):
    high = values.astype(bf16)
    return high, (values - high.astype(f32)).astype(bf16)


def rows_of(index, rows):
    return pl.ds(pl.multiple_of(index * rows, rows), rows)


def pick_rows(order_col, count):
    places = lax.broadcasted_iota(jnp.int32, (order_col.shape[0], count), 1)
    return (places == order_col).astype(f32).astype(bf16)


def put_rows(order_row, first, rows):
    places = lax.broadcasted_iota(jnp.int32, (rows, order_row.shape[1]), 0) + first
    return (places == order_row).astype(f32).astype(bf16)


def mixer_forward(tokens, ocol, orow, pos, w_in, w_gate, chan, blocks, w_out_far, *rest):
    far, rest = rest[:8], rest[8:]
    packed, rate, prod, before, low, w_out, *near, late_sem, held_sem = rest
    gate_ref, branch_ref, conv_ref, gin_ref, grec_ref, state_ref, mixed_ref, out_ref = near
    (late_out,) = late_all([w_out_far], [w_out], late_sem)
    leaving = [
        pltpu.make_async_copy(source, target, held_sem.at[i, 0])
        for i, (source, target) in enumerate(zip(near, far))
    ]
    count, _ = tokens.shape
    width = w_in.shape[1]
    steps = count // SUB
    heads = width // LANE

    def project(b, carry):
        at = rows_of(b, ROWS)
        packed[...] = dot(pick_rows(ocol[at, :], count), tokens[...]).astype(bf16)
        branch_ref[at, :] = dot(packed[...], w_in[...])
        gate_ref[at, :] = dot(packed[...], w_gate[...])
        return carry

    lax.fori_loop(0, count // ROWS, project, 0)
    leaving[0].start()
    leaving[1].start()

    for k in range(TAIL // SUB):
        last = branch_ref[pl.ds(count - TAIL + k * SUB, SUB), :]
        before[pl.ds(k * SUB, SUB), :] = pltpu.roll(last, 1, 0)
    before[pl.ds(TAIL, ROWS), :] = branch_ref[pl.ds(0, ROWS), :]

    def gates(b, carry):
        at = rows_of(b, ROWS)

        @pl.when(b > 0)
        def _():
            before[...] = branch_ref[pl.ds(pl.multiple_of(b * ROWS - TAIL, SUB), ROWS + TAIL), :]

        place = pos[at, :]
        for h in range(heads):
            lanes = pl.ds(h * LANE, LANE)
            par = chan[:, lanes]
            conv = par[4:5] + par[0:1] * before[pl.ds(TAIL, ROWS), lanes]
            for k in range(1, 4):
                earlier = before[pl.ds(TAIL - SUB * k, ROWS), lanes]
                conv = conv + par[k : k + 1] * jnp.where(place >= k, earlier, 0.0)
            high, rest = split(conv)
            pair = jnp.concatenate([blocks[h], blocks[heads + h]], axis=1)
            pre = dot(
                jnp.concatenate([high, rest], axis=1), jnp.concatenate([pair, pair], axis=0)
            )
            gate_in = sigmoid(pre[:, :LANE] + par[5:6])
            gate_rec = sigmoid(pre[:, LANE:] + par[6:7])
            kept = jnp.exp(-8.0 * gate_rec * par[7:8])
            drive = jnp.sqrt(1.0 - kept * kept + 0.01) * gate_in * conv
            conv_ref[at, lanes] = conv
            gin_ref[at, lanes] = gate_in
            grec_ref[at, lanes] = gate_rec
            rate[at, lanes] = jnp.where(place >= 1, kept, 0.0)
            state_ref[at, lanes] = drive
        return carry

    lax.fori_loop(0, count // ROWS, gates, 0)
    for copy in leaving[2:5]:
        copy.start()

    def scan(i, carry):
        held, passed = carry
        at = rows_of(i, SUB)
        a = rate[at, :]
        held = a * held + state_ref[at, :]
        passed = a * passed
        state_ref[at, :] = held
        prod[at, :] = passed
        return held, passed

    ends = lax.fori_loop(
        0, steps, scan, (jnp.zeros((SUB, width), f32), jnp.ones((SUB, width), f32)), unroll=8
    )
    first = lax.broadcasted_iota(jnp.int32, (SUB, width), 0) == 0
    carry_in = jnp.zeros((SUB, width), f32)
    for _ in range(SUB - 1):
        carry_in = jnp.where(first, 0.0, pltpu.roll(ends[0] + ends[1] * carry_in, 1, 0))

    def finish(i, carry):
        at = rows_of(i, 2 * SUB)
        twice = jnp.concatenate([carry_in, carry_in], axis=0)
        value = state_ref[at, :] + prod[at, :] * twice
        state_ref[at, :] = value
        low[at, :] = (gelu_of(gate_ref[at, :]) * value).astype(bf16)
        return carry

    lax.fori_loop(0, steps // 2, finish, 0, unroll=2)
    leaving[5].start()
    late_out.ready()

    def leave(b, carry):
        at = rows_of(b, ROWS)
        mixed = dot(put_rows(orow[...], b * ROWS, ROWS), low[...]).astype(bf16)
        mixed_ref[at, :] = mixed
        out_ref[at, :] = dot_last(mixed, w_out[...]).astype(bf16)
        return carry

    lax.fori_loop(0, count // ROWS, leave, 0)
    for copy in leaving[6:]:
        copy.start()
    for copy in leaving:
        copy.wait()


def mixer_backward(back, w_out, ocol, orow, pos, gain, chan, blocks, *rest):
    far, (dcat_ref, dnorm_ref, little_ref, dgain_ref), rest = rest[:9], rest[9:13], rest[13:]
    dmix_arr, dmix, adj, prod, after, before, low, small_ref, dblocks_ref, *rest = rest
    gate_ref, grec_ref, state_ref, conv_ref, gin_ref, branch_ref, norm, w_in, w_gate, late_sem = rest
    late = late_all(far, rest[:9], late_sem)
    count, _ = back.shape
    width = w_in.shape[1]
    steps = count // SUB
    heads = width // LANE
    blocks_of = count // ROWS

    def enter(b, carry):
        at = rows_of(b, ROWS)
        dmix_arr[at, :] = dot(back[at, :], w_out[...]).astype(bf16)
        return carry

    lax.fori_loop(0, blocks_of, enter, 0)
    for array in late[:3]:
        array.ready()

    def pack(b, carry):
        at = rows_of(b, ROWS)
        d_mixed = dot(pick_rows(ocol[at, :], count), dmix_arr[...])
        value, slope = gelu_both(gate_ref[at, :])
        adj[at, :] = d_mixed * value
        low[at, pl.ds(width, width)] = (d_mixed * state_ref[at, :] * slope).astype(bf16)
        kept = jnp.exp(-8.0 * grec_ref[at, :] * chan[7:8, :])
        dmix[at, :] = jnp.where(pos[at, :] >= 1, kept, 0.0)
        return carry

    lax.fori_loop(0, blocks_of, pack, 0)
    for array in late:
        array.ready()

    def scan(i, carry):
        held, passed, following = carry
        at = rows_of(steps - 1 - i, SUB)
        held = following * held + adj[at, :]
        passed = following * passed
        adj[at, :] = held
        prod[at, :] = passed
        return held, passed, dmix[at, :]

    last = lax.broadcasted_iota(jnp.int32, (SUB, width), 0) == SUB - 1
    wrapped = jnp.where(last, 0.0, pltpu.roll(dmix[pl.ds(0, SUB), :], SUB - 1, 0))
    ends = lax.fori_loop(
        0,
        steps,
        scan,
        (jnp.zeros((SUB, width), f32), jnp.ones((SUB, width), f32), wrapped),
        unroll=8,
    )
    carry_in = jnp.zeros((SUB, width), f32)
    for _ in range(SUB - 1):
        carry_in = jnp.where(last, 0.0, pltpu.roll(ends[0] + ends[1] * carry_in, SUB - 1, 0))

    small_ref[...] = jnp.zeros_like(small_ref)
    dblocks_ref[...] = jnp.zeros_like(dblocks_ref)
    first = lax.broadcasted_iota(jnp.int32, (SUB, width), 0) == 0
    state_last = state_ref[pl.ds(count - SUB, SUB), :]
    before[pl.ds(TAIL - SUB, SUB), :] = jnp.where(first, 0.0, pltpu.roll(state_last, 1, 0))
    before[pl.ds(TAIL, ROWS), :] = state_ref[pl.ds(0, ROWS), :]
    wide_carry = jnp.concatenate([carry_in] * (ROWS // SUB), axis=0)

    def point(b, carry):
        at = rows_of(b, ROWS)

        @pl.when(b > 0)
        def _():
            before[...] = state_ref[pl.ds(pl.multiple_of(b * ROWS - TAIL, SUB), ROWS + TAIL), :]

        place = pos[at, :]
        for h in range(heads):
            lanes = pl.ds(h * LANE, LANE)
            par = chan[:, lanes]
            adjoint = adj[at, lanes] + prod[at, lanes] * wide_carry[:, h * LANE : (h + 1) * LANE]
            conv = conv_ref[at, lanes]
            gate_in = gin_ref[at, lanes]
            gate_rec = grec_ref[at, lanes]
            kept = jnp.exp(-8.0 * gate_rec * par[7:8])
            square = kept * kept
            inside = 1.0 - square + 0.01
            inverse = lax.rsqrt(inside)
            root = inside * inverse
            previous = before[pl.ds(TAIL - SUB, ROWS), lanes]
            d_log = adjoint * previous * dmix[at, lanes]
            scaled = adjoint * gate_in
            d_log = d_log - scaled * conv * square * inverse
            d_in = adjoint * root * conv * gate_in * (1.0 - gate_in)
            d_rec = d_log * (-8.0 * par[7:8]) * gate_rec * (1.0 - gate_rec)
            both = jnp.concatenate([d_in, d_rec], axis=1)
            high, rest = split(both)
            pair = jnp.concatenate([blocks[h], blocks[heads + h]], axis=1)
            d_conv = scaled * root + dot_last(high, pair) + dot_last(rest, pair)
            dblocks_ref[h] += dot_first(conv.astype(bf16), high)
            after[at, lanes] = d_conv
            small_ref[4:5, lanes] += jnp.sum(d_conv, axis=0, keepdims=True)
            small_ref[5:6, lanes] += jnp.sum(d_in, axis=0, keepdims=True)
            small_ref[6:7, lanes] += jnp.sum(d_rec, axis=0, keepdims=True)
            small_ref[7:8, lanes] += (
                jnp.sum(d_log * gate_rec, axis=0, keepdims=True) * (-8.0) * par[8:9]
            )
        return carry

    lax.fori_loop(0, blocks_of, point, 0)

    for k in range(TAIL // SUB):
        head = after[pl.ds(k * SUB, SUB), :]
        after[pl.ds(count + k * SUB, SUB), :] = pltpu.roll(head, SUB - 1, 0)
        tail = branch_ref[pl.ds(count - TAIL + k * SUB, SUB), :]
        before[pl.ds(k * SUB, SUB), :] = pltpu.roll(tail, 1, 0)
    before[pl.ds(TAIL, ROWS), :] = branch_ref[pl.ds(0, ROWS), :]

    def unmix(b, carry):
        at = rows_of(b, ROWS)

        @pl.when(b > 0)
        def _():
            before[...] = branch_ref[pl.ds(pl.multiple_of(b * ROWS - TAIL, SUB), ROWS + TAIL), :]

        place = pos[at, :]
        for h in range(heads):
            lanes = pl.ds(h * LANE, LANE)
            par = chan[:, lanes]
            d_conv = after[at, lanes]
            d_branch = par[0:1] * d_conv
            small_ref[0:1, lanes] += jnp.sum(
                d_conv * before[pl.ds(TAIL, ROWS), lanes], axis=0, keepdims=True
            )
            for k in range(1, 4):
                later = pl.ds(pl.multiple_of(b * ROWS + SUB * k, SUB), ROWS)
                d_branch = d_branch + par[k : k + 1] * jnp.where(
                    pos[later, :] >= k, after[later, lanes], 0.0
                )
                earlier = before[pl.ds(TAIL - SUB * k, ROWS), lanes]
                small_ref[k : k + 1, lanes] += jnp.sum(
                    jnp.where(place >= k, d_conv * earlier, 0.0), axis=0, keepdims=True
                )
            low[at, lanes] = d_branch.astype(bf16)
        return carry

    lax.fori_loop(0, blocks_of, unmix, 0)
    lines = [small_ref[0:SUB, h * LANE : (h + 1) * LANE] for h in range(heads)]
    lines.append(jnp.zeros((LANE - SUB * heads, LANE), f32))
    little_ref[:, pl.ds(2 * width, LANE)] = jnp.concatenate(lines, axis=0).T
    for h in range(heads):
        little_ref[:, pl.ds(2 * h * LANE, 2 * LANE)] = dblocks_ref[h]
    dgain_ref[...] = jnp.zeros_like(dgain_ref)

    def leave(b, carry):
        at = rows_of(b, ROWS)
        cat = dot(put_rows(orow[...], b * ROWS, ROWS), low[...]).astype(bf16)
        dcat_ref[at, :] = cat
        d_norm = dot_last(cat[:, :width], w_in[...]) + dot_last(cat[:, width:], w_gate[...])
        dgain_ref[...] += jnp.sum(d_norm * norm[at, :].astype(f32), axis=0, keepdims=True)
        dnorm_ref[at, :] = d_norm.astype(bf16)
        return carry

    lax.fori_loop(0, blocks_of, leave, 0)
    dgain_ref[...] = dgain_ref[...] / gain[...]


MESH = pl.DeviceIdType.MESH
TILE = 16
PIECES = 8
HOP = 1
AFTER = 1


def cut_rows(rows, parts):
    tiles = rows // TILE
    ends = [tiles * (k + 1) // parts for k in range(parts)]
    return [(TILE * a, TILE * (b - a)) for a, b in zip([0] + ends[:-1], ends)]


class Line:
    def __init__(self, n, local, part, arrived, whole, sums, alls):
        self.n, self.local, self.part, self.arrived, self.whole = n, local, part, arrived, whole
        self.sums, self.alls = sums, alls
        self.me = lax.axis_index("mp")
        self.pieces = cut_rows(local, PIECES)
        self.has = (self.me > 0, self.me < n - 1)

    def greet(self, plane=None):
        barrier = pltpu.get_barrier_semaphore()
        more = 0
        if plane is not None:
            for bit in plane.bits:
                more += 1
                pl.semaphore_signal(
                    barrier, inc=1, device_id={"dp": plane.other(bit)}, device_id_type=MESH
                )
        for away in range(1, self.n):
            more += 1
            pl.semaphore_signal(
                barrier,
                inc=1,
                device_id={"mp": lax.rem(self.me + away, self.n)},
                device_id_type=MESH,
            )
        pl.semaphore_wait(barrier, more)

    def rows_at(self, owner, k):
        first, rows = self.pieces[k]
        return pl.ds(pl.multiple_of(owner * self.local + first, TILE), rows)

    def copy(self, source, target, sems, way, owner, k):
        return pltpu.make_async_remote_copy(
            src_ref=source,
            dst_ref=target,
            send_sem=sems[0].at[way, owner, k],
            recv_sem=sems[1].at[way, owner, k],
            device_id={"mp": self.me + 1 - 2 * way},
            device_id_type=MESH,
        )

    def sum_copy(self, way, owner, k, first=False):
        at = self.rows_at(owner, k)
        landed = self.arrived[way].at[at]
        return self.copy(self.part.at[at] if first else landed, landed, self.sums, way, owner, k)

    def all_copy(self, way, owner, k):
        block = self.whole.at[self.rows_at(owner, k)]
        return self.copy(block, block, self.alls, way, owner, k)

    def first(self, k):
        for away in range(self.n - 1):
            for way in range(2):
                owner = away if way else self.n - 1 - away

                @pl.when(jnp.logical_not(self.has[way]))
                def _():
                    self.sum_copy(way, owner, k, True).start()

    def relay(self, k, stage):
        for way in range(2):
            late = stage - (self.n - 1 - self.me if way else self.me)
            owner = late if way else self.n - 1 - late

            @pl.when(self.has[way] & (late >= 0))
            def _():
                self.sum_copy(way, owner, k).wait_recv()
                at = self.rows_at(owner, k)
                landed = self.arrived[way]
                landed[at, :] = (landed[at, :].astype(f32) + self.part[at, :].astype(f32)).astype(bf16)
                self.sum_copy(way, owner, k).start()

    def total(self, k, into):
        at = self.rows_at(self.me, k)
        rows = pl.ds(0, self.pieces[k][1])
        into[rows, :] = self.part[at, :].astype(f32)
        for way in range(2):

            @pl.when(self.has[way])
            def _():
                self.sum_copy(way, self.me, k).wait_recv()
                into[rows, :] += self.arrived[way][at, :].astype(f32)

    def spread(self, k):
        for way in range(2):

            @pl.when(self.has[1 - way])
            def _():
                self.all_copy(way, self.me, k).start()

    def forward(self, k, stage):
        for way in range(2):
            owner = self.me + stage if way else self.me - stage
            there = owner < self.n if way else owner >= 0

            @pl.when(there)
            def _():
                self.all_copy(way, owner, k).wait_recv()

            @pl.when(there & self.has[1 - way])
            def _():
                self.all_copy(way, owner, k).start()

    def sent(self, k):
        for owner in range(self.n):
            for way in range(2):

                @pl.when(self.me > owner if way else self.me < owner)
                def _():
                    self.sum_copy(way, owner, k).wait_send()

    def finish(self):
        for k in range(PIECES):
            for owner in range(self.n):
                for way in range(2):
                    if self.whole is not None:
                        reached = self.me <= owner if way else self.me >= owner

                        @pl.when(reached & self.has[1 - way])
                        def _():
                            self.all_copy(way, owner, k).wait_send()

    def run(self, point, tasks=()):
        sums, alls = self.part is not None, self.whole is not None
        slots = [[] for _ in range(PIECES + (HOP + AFTER) * (self.n - 1) + 1)]
        for k in range(PIECES):
            done = k + HOP * (self.n - 1) if sums else 0
            if sums:
                slots[k].append((0, functools.partial(self.first, k)))
                for stage in range(1, self.n - 1):
                    slots[k + HOP * stage].append((2, functools.partial(self.relay, k, stage)))
                slots[done].append((3, functools.partial(self.sent, k)))
            slots[done].append((3, functools.partial(point, k)))
            if alls:
                slots[done].append((4, functools.partial(self.spread, k)))
                for stage in range(1, self.n):
                    at = (done if sums else k) + AFTER * stage
                    slots[at].append((1, functools.partial(self.forward, k, stage)))
        tasks = iter(tasks)
        for slot in slots:
            for step, (_, work) in enumerate(sorted(slot, key=lambda entry: entry[0])):
                if step in (0, 1, 3):
                    next(tasks, idle)()
                work()
        for task in tasks:
            task()
        self.finish()

    def tiles(self, k, body):
        first, rows = self.pieces[k]

        def one(i, carry):
            body(
                pl.ds(pl.multiple_of(i * TILE, TILE), TILE),
                pl.ds(pl.multiple_of(first + i * TILE, TILE), TILE),
                pl.ds(pl.multiple_of(self.me * self.local + first + i * TILE, TILE), TILE),
            )
            return carry

        lax.fori_loop(0, rows // TILE, one, 0)


def idle():
    pass


class Late:
    def __init__(self, source, ref, sem):
        self.ref = ref
        self.copy = pltpu.make_async_copy(source, ref, sem)
        self.pending = True

    def begin(self):
        self.copy.start()

    def ready(self):
        if self.pending:
            self.copy.wait()
        self.pending = False


def late_all(sources, refs, sems):
    arrays = [Late(source, ref, sems.at[i]) for i, (source, ref) in enumerate(zip(sources, refs))]
    for array in arrays:
        array.begin()
    return arrays


class Plane:
    bits = (1, 2, 4)
    orders = ((4, 2, 1), (2, 4, 1))

    def __init__(self):
        self.me = lax.axis_index("dp")

    def bit(self, bit):
        return lax.rem(self.me // bit, 2)

    def other(self, *bits):
        return self.me + sum(bit * (1 - 2 * self.bit(bit)) for bit in bits)

    def gather_copies(self, item, view, halves, stage, sems):
        copies = []
        for half in halves:
            order = self.orders[half]
            for combo in range(1 << stage):
                flipped = [bit for i, bit in enumerate(order[:stage]) if combo >> i & 1]
                block = view(self.other(*flipped), half)
                slot = (1 << stage) - 1 + combo
                copies.append(
                    pltpu.make_async_remote_copy(
                        src_ref=block,
                        dst_ref=block,
                        send_sem=sems[0].at[item, half, slot],
                        recv_sem=sems[1].at[item, half, slot],
                        device_id={"dp": self.other(order[stage])},
                        device_id_type=MESH,
                    )
                )
        return copies


class Reduce(Plane):
    def __init__(self, index, left, right, lanes, sent, mine, theirs, got, second, third, out, sems):
        super().__init__()
        self.sent, self.theirs = sent, theirs
        self.index, self.left, self.right, self.lanes = index, left, right, lanes
        self.mine, self.got = mine.at[index], got.at[index]
        self.second, self.third, self.out = second.at[index], third.at[index], out
        self.sems = sems
        self.rows = out.shape[0]
        self.half = self.rows // 2

    def copy(self, source, target, slot, bit):
        return pltpu.make_async_remote_copy(
            src_ref=source,
            dst_ref=target,
            send_sem=self.sems[0].at[self.index, slot],
            recv_sem=self.sems[1].at[self.index, slot],
            device_id={"dp": self.other(bit)},
            device_id_type=MESH,
        )

    def core_copy(self, t):
        return self.copy(self.theirs.at[(4 * self.index + t) % 2], self.got.at[t], t, 1)

    def second_copy(self, half, j):
        x, y = self.bit(2), self.bit(4)
        block = (1 - y) * 2 + j if half else j * 2 + 1 - x
        rows = self.mine.at[block, pl.ds(half * self.half, self.half)]
        return self.copy(rows, self.second.at[half, j], 4 + 2 * half + j, 4 if half else 2)

    def third_block(self, half):
        x, y = self.bit(2), self.bit(4)
        return y * 2 + 1 - x if half else (1 - y) * 2 + x

    def third_copy(self, half):
        rows = self.mine.at[self.third_block(half), pl.ds(half * self.half, self.half)]
        return self.copy(rows, self.third.at[half], 8 + half, 2 if half else 4)

    def product(self, t):
        def task():
            core = self.bit(1)
            pair = pl.ds(t * 2 * self.rows, 2 * self.rows)
            if t == 0:
                self.left.ready()
                self.right.ready()
            if len(self.sent) > 1:
                self.sent[-2].wait_send()
            both = dot_first(self.left.ref[:, pair], self.right.ref[:, self.lanes])
            low, high = both[: self.rows], both[self.rows :]
            self.mine[t] = jnp.where(core == 0, low, high).astype(bf16)
            self.theirs[(4 * self.index + t) % 2] = jnp.where(core == 0, high, low).astype(bf16)
            self.sent.append(self.core_copy(t))
            self.sent[-1].start()

        return task

    def keep(self, t):
        return self.mine[t]

    def add_core(self):
        for t in range(4):
            self.core_copy(t).wait_recv()
            self.mine[t] = (self.keep(t).astype(f32) + self.got[t].astype(f32)).astype(self.mine.dtype)
        for half in range(2):
            for j in range(2):
                self.second_copy(half, j).start()

    def add_second(self):
        for half in range(2):
            for j in range(2):
                self.second_copy(half, j).wait_recv()
        for half in range(2):
            block, at = self.third_block(half), pl.ds(half * self.half, self.half)
            far = 1 - self.bit(2 if half else 4)
            self.mine[block, at] = (
                self.mine[block, at].astype(f32) + self.second[half, far].astype(f32)
            ).astype(self.mine.dtype)
            self.third_copy(half).start()

    def add_third(self):
        own = self.bit(4) * 2 + self.bit(2)
        for half in range(2):
            self.third_copy(half).wait_recv()
            at = pl.ds(half * self.half, self.half)
            near = self.bit(2 if half else 4)
            self.out[at, :] = (
                self.mine[own, at].astype(f32)
                + self.second[half, near].astype(f32)
                + self.third[half].astype(f32)
            )

    def finish(self):
        for half in range(2):
            for j in range(2):
                self.second_copy(half, j).wait_send()
            self.third_copy(half).wait_send()


class Given(Reduce):
    def __init__(self, given, mine, got, second, third, out, sems):
        super().__init__(0, None, None, None, None, mine, None, got, second, third, out, sems)
        self.given = given

    def rows_of(self, t, core):
        return pl.ds(pl.multiple_of((2 * t + core) * self.rows, self.rows), self.rows)

    def core_copy(self, t):
        return self.copy(self.given.at[self.rows_of(t, 1 - self.bit(1))], self.got.at[t], t, 1)

    def start(self):
        for t in range(4):
            self.core_copy(t).start()

    def finish(self):
        for t in range(4):
            self.core_copy(t).wait_send()
        super().finish()

    def keep(self, t):
        return self.given[self.rows_of(t, self.bit(1)), :]


def reduce_tasks(parts, given=()):
    tasks = [part.product(t) for part in parts for t in range(4)]

    def also(at, extra):
        while len(tasks) <= at:
            tasks.append(idle)
        before = tasks[at]

        def both():
            extra()
            before()

        tasks[at] = both

    for i, part in enumerate(parts):
        also(4 * i + 5, part.add_core)
        also(4 * i + 8, part.add_second)
        also(4 * i + 10, part.add_third)

    for part in given:
        also(0, part.start)
        also(2, part.add_core)
        also(4, part.add_second)
        also(6, part.add_third)

    def finish():
        for ring in {id(part.sent): part.sent for part in parts}.values():
            for copy in ring[-2:]:
                copy.wait_send()
        for part in [*parts, *given]:
            part.finish()

    return tasks, finish


def given_scratch(rows, width):
    sem = pltpu.SemaphoreType.DMA((1, 10))
    return [
        pltpu.VMEM((1, 4, rows, width), f32),
        pltpu.VMEM((1, 4, rows, width), f32),
        pltpu.VMEM((1, 2, 2, rows // 2, width), f32),
        pltpu.VMEM((1, 2, rows // 2, width), f32),
        sem,
        sem,
    ]


def reduce_scratch(arrays, rows, width):
    block = pltpu.VMEM((arrays, 4, rows, width), bf16)
    sem = pltpu.SemaphoreType.DMA((arrays, 10))
    return [
        block,
        pltpu.VMEM((2, rows, width), bf16),
        block,
        pltpu.VMEM((arrays, 2, 2, rows // 2, width), bf16),
        pltpu.VMEM((arrays, 2, rows // 2, width), bf16),
        sem,
        sem,
    ]


def gather_norm(n, x, gain, whole, send, recv):
    line = Line(n, x.shape[0], None, None, whole, None, (send, recv))
    line.greet()

    def point(k):
        def one(_, own, at):
            v = x[own, :].astype(f32)
            whole[at, :] = (v * rms_scale(v) * gain[...]).astype(bf16)

        line.tiles(k, one)

    line.run(point)


def row_view(array, rows):
    def view(owner, half):
        first = owner * rows + half * (rows // 2)
        return array.at[pl.ds(pl.multiple_of(first, TILE), rows // 2)]

    return view


def gather_tasks(plane, items, sems):
    def copies(stage):
        return [
            copy
            for item, (view, halves) in enumerate(items)
            for copy in plane.gather_copies(item, view, halves, stage, sems)
        ]

    def stage_task(stage):
        def task():
            if stage:
                for copy in copies(stage - 1):
                    copy.wait_recv()
            for copy in copies(stage):
                copy.start()

        return task

    def last():
        for copy in copies(2):
            copy.wait_recv()
        for stage in range(3):
            for copy in copies(stage):
                copy.wait_send()

    return stage_task(0), stage_task(1), stage_task(2), last


def gather_weights(
    n,
    x,
    gain,
    w_in,
    w_gate,
    w_out,
    blocks,
    chan,
    whole,
    all_in,
    all_gate,
    all_out,
    all_blocks,
    all_chan,
    send,
    recv,
    raw,
    plane_send,
    plane_recv,
):
    line = Line(n, x.shape[0], None, None, whole, None, (send, recv))
    plane = Plane()
    line.greet(plane)
    sems = plane_send, plane_recv
    rows, piece = w_in.shape[0], blocks.shape[1]
    lines = chan.shape[0]

    def blocks_view(owner, half):
        return all_blocks.at[:, pl.ds(pl.multiple_of(owner * piece, TILE), piece)]

    def chan_view(owner, half):
        return raw.at[pl.ds(pl.multiple_of(owner * lines, TILE), lines)]

    items = [(row_view(array, rows), (0, 1)) for array in (all_in, all_gate, all_out)]
    items += [(blocks_view, (0,)), (chan_view, (1,))]

    first, second, third, finish = gather_tasks(plane, items, sems)

    def last():
        finish()
        lane = lax.broadcasted_iota(jnp.int32, (LANE, LANE), 1)
        row = lax.broadcasted_iota(jnp.int32, (LANE, LANE), 0)
        total = jnp.zeros((lines, LANE), f32)
        for owner in range(LANE // piece):
            moved = ((row < piece) & (row + owner * piece == lane)).astype(f32).astype(bf16)
            total = total + dot(raw[pl.ds(owner * lines, lines), :], moved)
        for h in range(lines // SUB):
            par = total[h * SUB : (h + 1) * SUB]
            lanes = pl.ds(h * LANE, LANE)
            all_chan[0:SUB, lanes] = par
            decay = par[SUB - 1 : SUB]
            small = jnp.exp(-jnp.abs(decay))
            one_more = 1.0 + small
            rest = jnp.where(one_more == 1.0, 1.0, one_more - 1.0)
            log_one_more = jnp.where(one_more == 1.0, small, jnp.log(one_more) * (small / rest))
            all_chan[SUB - 1 : SUB, lanes] = jnp.maximum(decay, 0.0) + log_one_more
            all_chan[SUB : 2 * SUB, lanes] = jnp.broadcast_to(sigmoid(decay), (SUB, LANE))

    own = pl.ds(pl.multiple_of(plane.me * rows, TILE), rows)
    all_in[own, :] = w_in[...]
    all_gate[own, :] = w_gate[...]
    all_out[own, :] = w_out[...]
    all_blocks[:, pl.ds(pl.multiple_of(plane.me * piece, TILE), piece), :] = blocks[...]
    raw[pl.ds(pl.multiple_of(plane.me * lines, TILE), lines), :] = chan[...]

    def point(k):
        def one(_, own, at):
            v = x[own, :].astype(f32)
            whole[at, :] = (v * rms_scale(v) * gain[...]).astype(bf16)

        line.tiles(k, one)

    first()
    line.run(point, [idle] * 4 + [second] + [idle] * 3 + [third] + [idle] * 3 + [last])


def norm_back(value, gain, grad):
    scale = rms_scale(value)
    e = gain * grad
    slope = scale * scale * scale * jnp.mean(value * e, axis=-1, keepdims=True)
    return scale * e - value * slope, grad * value * scale


def middle(n, x, gain, cot, part, *rest):
    (*shares, cot_first), rest = rest[:4], rest[4:]
    (d_resid, gain_grad, back, high_sum), far, rest = rest[:4], rest[4:11], rest[11:]
    left, right, total, ss, sr, send, recv, part2, ss2, sr2, send2, recv2, csend, crecv, *rest = rest
    up_s, value_s, grad_s, high_part, left3, right3, total3, ss3, sr3, cot_sem, *rest = rest
    *rest, held_sem = rest
    near, rest = rest[-7:], rest[:-7]
    whole, cots, resid, hidden, d_up, d_gate, low_part = near
    plane = Plane() if rest else None
    w_up, w_gate, w_down = weights = rest[:3] if rest else shares
    local = x.shape[0]
    line = Line(n, local, part, (left, right), whole, (ss, sr), (send, recv))
    back_line = Line(n, local, part2, (left, right), back, (ss2, sr2), (send2, recv2))
    early = cot_first.shape[1]
    later = pl.ds(early, cot.shape[1] - early)
    cot_line = Line(n, local, None, None, cots.at[:, later], None, (csend, crecv))
    high_line = Line(n, local, high_part, (left3, right3), None, (ss3, sr3), None)
    line.greet(plane)
    arriving = pltpu.make_async_copy(cot_first, cots.at[:, pl.ds(0, early)], cot_sem)
    arriving.start()
    gain_grad[...] = jnp.zeros_like(gain_grad)
    leaving = [
        pltpu.make_async_copy(source, target, held_sem.at[i])
        for i, (source, target) in enumerate(zip(near, far))
    ]

    def keep_cot(_, own, at):
        cots[at, later] = cot[own, later]

    def point(k):
        line.total(k, total)

        def one(here, own, at):
            v = x[own, :].astype(f32) + total[here, :]
            resid[own, :] = v
            whole[at, :] = (v * rms_scale(v) * gain[...]).astype(bf16)

        line.tiles(k, one)

    def back_point(k):
        back_line.total(k, total)

        def one(here, own, at):
            grad, terms = norm_back(resid[own, :], gain[...], total[here, :])
            gain_grad[...] += jnp.sum(terms, axis=0, keepdims=True)
            value = cot[own, :].astype(f32) + grad
            d_resid[own, :] = value
            back[at, :] = value.astype(bf16)

        line.tiles(k, one)

    def high_point(k):
        high_line.total(k, total3)
        first, rows = line.pieces[k]
        high_sum[pl.ds(first, rows), :] = total3[pl.ds(0, rows), :].astype(bf16)

    def pair_steps(j):
        first = line.pieces[2 * j][0]
        rows = line.pieces[2 * j][1] + line.pieces[2 * j + 1][1]
        at = [pl.ds(owner * local + first, rows) for owner in range(n)]
        here = pl.ds(0, n * rows)

        def read(array):
            return jnp.concatenate([array[rows_at, :] for rows_at in at], axis=0)

        def write(array, value):
            for owner, rows_at in enumerate(at):
                array[rows_at, :] = value[owner * rows : (owner + 1) * rows]

        def up():
            up_s[here, :] = dot(read(whole), w_up[...])

        def gate():
            value, slope = gelu_both(dot(read(whole), w_gate[...]))
            write(hidden, (value * up_s[here, :]).astype(bf16))
            value_s[here, :] = value
            up_s[here, :] = up_s[here, :] * slope

        def into_hidden():
            d_hidden = dot(read(cots), w_down[...])
            write(d_up, (d_hidden * value_s[here, :]).astype(bf16))
            write(d_gate, (d_hidden * up_s[here, :]).astype(bf16))

        def through_up():
            grad_s[here, :] = dot_last(read(d_up), w_up[...])

        def through_gate():
            write(part2, (grad_s[here, :] + dot_last(read(d_gate), w_gate[...])).astype(bf16))

        def project():
            value = dot_last(read(hidden), w_down[...]).astype(bf16)
            write(low_part, value[:, : value.shape[1] // 2])
            write(high_part, value[:, value.shape[1] // 2 :])

        return up, gate, into_hidden, through_up, through_gate, project

    hops = n - 1
    slots = [[] for _ in range(PIECES + 5 * hops)]

    def put(slot, order, work, *args):
        slots[slot].append((order, functools.partial(work, *args)))

    for k in range(PIECES):
        put(k, 0, line.first, k)
        for stage in range(1, hops):
            put(k + stage, 2, line.relay, k, stage)
        met = k + hops
        put(met, 3, line.sent, k)
        put(met, 3, point, k)
        put(met, 3, line.spread, k)
        given = k if 2 * k < PIECES else min(2 * k - PIECES // 2 + 1, PIECES + 2)
        put(given, 0, cot_line.tiles, k, keep_cot)
        put(given, 0, cot_line.spread, k)
        for stage in range(1, n):
            put(met + stage, 5, line.forward, k, stage)
            put(given + stage, 5, cot_line.forward, k, stage)
    for j in range(PIECES // 2):
        slot = 2 * j + 2 + 2 * hops
        steps = pair_steps(j)
        for at, order, step in zip((0, 0, 0, 1, 1, 1), (0.5, 1.5, 2.5, 0.5, 1.5, 3.5), steps):
            put(slot + at, order, step)
        for k in (2 * j, 2 * j + 1):
            begun = slot + 1 + k % 2
            put(begun, 2 if begun == slot + 1 else 0, back_line.first, k)
            for stage in range(1, hops):
                put(begun + stage, 2, back_line.relay, k, stage)
            put(begun + hops, 3, back_line.sent, k)
            put(begun + hops, 3, back_point, k)
            put(begun + hops, 3, back_line.spread, k)
            for stage in range(1, n):
                put(begun + hops + stage, 5, back_line.forward, k, stage)
            begun += 1
            put(begun, 4, high_line.first, k)
            for stage in range(1, hops):
                put(begun + stage, 4, high_line.relay, k, stage)
            put(begun + hops, 4, high_line.sent, k)
            put(begun + hops, 4, high_point, k)
    put(2 * hops + 2, 0, arriving.wait)
    done = PIECES + 2 * hops + 2
    for copy in leaving:
        put(done, 0, copy.start)
    if plane is not None:
        rows = shares[0].shape[0]
        own = pl.ds(pl.multiple_of(plane.me * rows, TILE), rows)
        for share, array in zip(shares, weights):
            array[own, :] = share[...]
        items = [(row_view(array, rows), (0, 1)) for array in weights]
        stages = gather_tasks(plane, items, rest[3:])
        for slot, stage in zip((0, 3, 6, 2 * hops + 2), stages):
            put(slot, 0, stage)
    for slot in slots:
        for _, work in sorted(slot, key=lambda entry: entry[0]):
            work()
    for each in (line, back_line, cot_line):
        each.finish()
    for copy in leaving:
        copy.wait()


def sum_back(n, x, d_resid, gain, part, *rest):
    if len(rest) > 6:
        little, gains, *rest = rest
        sources, rest = rest[:9], rest[9:]
        grad_x, *outs, little_out, gains_out = rest[:9]
        left, right, total, ss, sr, *reduce = rest[9:]
        wide, late_refs, late_sems = reduce[22:29], reduce[29:34], reduce[34]
        given = [
            Given(little, *reduce[7:11], little_out, reduce[11:13]),
            Given(gains, *reduce[13:17], gains_out, reduce[17:19]),
        ]
        met, met_send, met_recv = reduce[19:22]
    else:
        grad_x, left, right, total, ss, sr = rest
        sources = ()
    line = Line(n, x.shape[0], part, (left, right), None, (ss, sr), None)
    line.greet(Plane() if sources else None)

    def point(k):
        line.total(k, total)

        def one(here, own, at):
            back, _ = norm_back(x[own, :].astype(f32), gain[...], total[here, :])
            grad_x[own, :] = (d_resid[own, :] + back).astype(bf16)

        line.tiles(k, one)

    if not sources:
        line.run(point)
        return
    left_a, left_b, right_a, right_b, right_c = late_refs
    across, width = sources[7].shape[1], sources[8].shape[1]
    places = (left_a, left_b, right_a, right_b, right_c)
    places += (left_a, left_b, right_a.at[:, pl.ds(0, across)], right_c.at[:, pl.ds(0, width)])
    mid, cots, d_up, d_gate, hidden, norm, back_all, cat, mixed = (
        Late(source, ref, late_sems.at[i]) for i, (source, ref) in enumerate(zip(sources, places))
    )
    for array in (mid, d_up, d_gate, cots, hidden):
        array.begin()
    every, sent, sent_wide = slice(None), [], []
    wide_sides = ((mid, d_up, every), (mid, d_gate, every), (cots, hidden, every))
    sides = (
        (norm, cat, slice(0, width)),
        (norm, cat, slice(width, 2 * width)),
        (back_all, mixed, every),
    )
    parts = [
        Reduce(i, *side, sent_wide, *wide[:5], out, wide[5:7])
        for i, (side, out) in enumerate(zip(wide_sides, outs))
    ]
    parts += [
        Reduce(i, *side, sent, *reduce[:5], out, reduce[5:7])
        for i, (side, out) in enumerate(zip(sides, outs[3:]))
    ]
    tasks, finish = reduce_tasks(parts, given)

    def then(task, *arrays):
        def both():
            task()
            for array in arrays:
                array.begin()

        return both

    tasks[7] = then(tasks[7], norm, cat)
    tasks[11] = then(tasks[11], back_all, mixed)
    me = lax.axis_index("mp")

    def meet(away):
        return pltpu.make_async_remote_copy(
            src_ref=gains_out,
            dst_ref=met.at[away - 1],
            send_sem=met_send.at[away - 1],
            recv_sem=met_recv.at[away - 1],
            device_id={"mp": lax.rem(me + away, n)},
            device_id_type=MESH,
        )

    def send_gains():
        for away in range(1, n):
            meet(away).start()

    def add_gains():
        for away in range(1, n):
            meet(away).wait()
        gains_out[...] += sum(met[away] for away in range(n - 1))

    tasks[7:7] = [send_gains]
    line.run(point, tasks)
    finish()
    add_gains()


def line_call(body, n, identity, outs, sums, alls, args, more=(), late=0, held=0):
    whole = pl.BlockSpec(memory_space=pltpu.VMEM)
    local, model = args[0].shape
    sem = pltpu.SemaphoreType.DMA((2, n, PIECES))
    scratch = []
    if sums:
        scratch += [pltpu.VMEM((n * local, model), bf16)] * 2
        scratch += [pltpu.VMEM((max(rows for _, rows in cut_rows(local, PIECES)), model), f32)]
        scratch += [sem, sem]
    if alls:
        scratch += [sem, sem]
    scratch += more
    if held:
        scratch += [pltpu.VMEM(o.shape, o.dtype) for o in outs[len(outs) - held :]]
        scratch += [pltpu.SemaphoreType.DMA((held,))]
    away = pl.BlockSpec(memory_space=pl.ANY)
    moved = sum(a.size * a.dtype.itemsize for a in args)
    return pl.pallas_call(
        functools.partial(body, n),
        out_shape=outs,
        in_specs=[whole] * (len(args) - late) + [away] * late,
        out_specs=[whole] * (len(outs) - held) + [away] * held,
        scratch_shapes=scratch,
        compiler_params=pltpu.CompilerParams(
            vmem_limit_bytes=VMEM_MB << 20, collective_id=identity, has_side_effects=True
        ),
        cost_estimate=pl.CostEstimate(flops=0, bytes_accessed=100 * moved, transcendentals=0),
    )(*args)


def finish(heads, piece, share, resid, low, high, gains, little, *rest):
    count = (len(rest) - 6) // 2
    sources, rest = rest[:count], rest[count:]
    output, grad_gains, grad_conv, grad_bias, grad_decay, grad_blocks, *targets = rest
    for source, target in zip(sources, targets):
        target[...] = source[...]
    half = low.shape[1]
    output[:, :half] = (resid[:, :half] + low[...].astype(f32)).astype(bf16)
    output[:, half:] = (resid[:, half:] + high[...].astype(f32)).astype(bf16)
    for position in range(gains.shape[0] // 2):

        @pl.when(lax.axis_index("mp") == position)
        def _():
            grad_gains[...] = gains[2 * position : 2 * position + 2, :share]

    for h in range(heads):
        for gate in range(2):
            first = (2 * h + gate) * LANE
            grad_blocks[gate, h] = little[:, first : first + LANE]
    first = 2 * heads * LANE
    lines = little[:, first : first + LANE]
    lines = jnp.concatenate([lines, jnp.zeros((LANE - piece, LANE), f32)], axis=0).T
    for h in range(heads):
        for k in range(SUB):
            row = lines[h * SUB + k : h * SUB + k + 1, :piece]
            if k < 4:
                grad_conv[k, h : h + 1, :] = row
            elif k < SUB - 1:
                grad_bias[k - 4, h : h + 1, :] = row
            else:
                grad_decay[h : h + 1, :] = row


def local_call(body, outs, scratch, flops, args, late=0, held=0):
    whole, away = pl.BlockSpec(memory_space=pltpu.VMEM), pl.BlockSpec(memory_space=pl.ANY)
    twins = list(args[len(args) - late :]) + list(outs[len(outs) - held :])
    scratch = scratch + [pltpu.VMEM(a.shape, a.dtype) for a in twins]
    if late:
        scratch.append(pltpu.SemaphoreType.DMA((late,)))
    if held:
        scratch.append(pltpu.SemaphoreType.DMA((held, 4)))
    moved = sum(a.size * a.dtype.itemsize for a in args)
    moved += sum(o.size * o.dtype.itemsize for o in outs)
    return pl.pallas_call(
        body,
        out_shape=outs,
        in_specs=[whole] * (len(args) - late) + [away] * late,
        out_specs=[whole] * (len(outs) - held) + [away] * held,
        scratch_shapes=scratch,
        compiler_params=pltpu.CompilerParams(vmem_limit_bytes=VMEM_MB << 20),
        cost_estimate=pl.CostEstimate(flops=flops, bytes_accessed=moved, transcendentals=0),
    )(*args)


def shape_of(dtype, *shape):
    return jax.ShapeDtypeStruct(shape, dtype)


def shards(
    inputs,
    cotangent,
    token_mask,
    order,
    lengths,
    gains,
    w_in,
    w_gate,
    w_out,
    conv_weight,
    chan_bias,
    decay,
    gate_blocks,
    w_up,
    w_gate_ff,
    w_down,
):
    n_dp = lax.axis_size("dp")
    local_rows, model = inputs.shape
    count = local_rows * lax.axis_size("mp")
    heads, piece = decay.shape
    width = heads * piece * n_dp
    hidden_width = w_up.shape[1]

    fused = n_dp == 8
    rows = model // n_dp
    out_rows, down_rows = w_out.T, w_down.T
    lines = jnp.concatenate([conv_weight, chan_bias, decay[None]], axis=0).transpose(1, 0, 2)
    lines = lines.reshape(SUB * heads, piece)

    steps = count // SUB
    ends = jnp.cumsum(lengths[0], dtype=jnp.int32)
    starts = ends - lengths[0]
    places = jnp.arange(count, dtype=jnp.int32)
    own_start = jnp.max(
        jnp.where(places[:, None] >= starts[None, :], starts[None, :], 0), axis=1
    )
    pos = (places - own_start).reshape(SUB, steps).T
    wrap = jnp.concatenate([pos[: TAIL // SUB, 1:], jnp.full((TAIL // SUB, 1), -1, jnp.int32)], axis=1)
    pos_col = jnp.concatenate([pos, wrap], axis=0).reshape(count + TAIL, 1)
    order_int = order[0].reshape(SUB, steps).T.reshape(count)
    ocol, orow = order_int.reshape(count, 1), order_int.reshape(1, count)

    gain_f = gains.astype(f32)
    n_mp = lax.axis_size("mp")
    tok = shape_of(bf16, count, model)
    own = shape_of(f32, local_rows, model)
    if fused:
        grown = shape_of(bf16, model, width)
        norm_group, full_in, full_gate, full_out, blocks, chan = line_call(
            gather_weights,
            n_mp,
            0,
            [tok, grown, grown, grown, shape_of(bf16, 2 * heads, LANE, LANE), shape_of(f32, 16, width)],
            False,
            True,
            (
                inputs,
                gain_f[0:1],
                w_in,
                w_gate,
                out_rows,
                gate_blocks.reshape(2 * heads, piece, LANE),
                jnp.pad(lines, ((0, 0), (0, LANE - piece))),
            ),
            [pltpu.VMEM((n_dp * SUB * heads, LANE), bf16)] + [pltpu.SemaphoreType.DMA((5, 2, 7))] * 2,
        )
    else:
        (norm_group,) = line_call(gather_norm, n_mp, 0, [tok], False, True, (inputs, gain_f[0:1]))
        full_in = lax.all_gather(w_in, "dp", axis=0, tiled=True)
        full_gate = lax.all_gather(w_gate, "dp", axis=0, tiled=True)
        full_out = lax.all_gather(out_rows, "dp", axis=0, tiled=True)
        blocks = lax.all_gather(gate_blocks, "dp", axis=2, tiled=True).reshape(2 * heads, LANE, LANE)
        params = lax.all_gather(lines, "dp", axis=1, tiled=True).astype(f32)
        params = params.reshape(heads, SUB, LANE).transpose(1, 0, 2).reshape(SUB, width)
        decay_row = params[7:8]
        chan = jnp.concatenate(
            [params[:7], jax.nn.softplus(decay_row)] + [jax.nn.sigmoid(decay_row)] * SUB, axis=0
        )
    cot = cotangent * token_mask.astype(bf16)[:, None]

    cot_first, norm_group = lax.optimization_barrier((cot[:, : model // 3], norm_group))
    cot_first = lax.all_gather(cot_first, "mp", axis=0, tiled=True)

    wide = pltpu.VMEM((count, width), f32)
    saved = [shape_of(f32, count, width)] * 6
    gate_pre, branch, conv, gate_in, gate_rec, state, mixed, back_part = local_call(
        mixer_forward,
        saved + [shape_of(bf16, count, width), shape_of(bf16, count, model)],
        [
            pltpu.VMEM((ROWS, model), bf16),
            wide,
            wide,
            pltpu.VMEM((ROWS + TAIL, width), f32),
            pltpu.VMEM((count, width), bf16),
        ],
        2 * count * (count * model + 3 * model * width),
        (norm_group, ocol, orow, pos_col, full_in, full_gate, chan, blocks, full_out),
        1,
        8,
    )
    shares = (w_up, w_gate_ff, down_rows)
    if not fused:
        shares = [lax.all_gather(share, "dp", axis=0, tiled=True) for share in shares]
    hid = shape_of(bf16, count, hidden_width)
    half = shape_of(bf16, count, model // 2)
    half_twin = pltpu.VMEM(half.shape, bf16)
    pieces = cut_rows(local_rows, PIECES)
    most = n_mp * max(pieces[k][1] + pieces[k + 1][1] for k in range(0, PIECES, 2))
    pair = pltpu.VMEM((most, hidden_width), f32)
    flow = pltpu.SemaphoreType.DMA((2, n_mp, PIECES))
    plane_scratch = [pltpu.VMEM((model, hidden_width), bf16)] * 3 + [pltpu.SemaphoreType.DMA((3, 2, 7))] * 2
    (
        d_resid,
        gain_mid,
        back_group,
        ffn_high,
        norm_mid_group,
        cot_group,
        resid,
        hidden,
        d_up,
        d_gate_ff,
        ffn_part,
    ) = line_call(
        middle,
        n_mp,
        1,
        [own, shape_of(f32, 1, model), tok, shape_of(bf16, local_rows, model // 2)]
        + [tok, tok, own, hid, hid, hid, half],
        True,
        True,
        (inputs, gain_f[1:2], cot, back_part, *shares, cot_first),
        [pltpu.VMEM((count, model), bf16)]
        + [flow] * 6
        + [pair, pair, pltpu.VMEM((most, model), f32)]
        + [half_twin] * 3
        + [pltpu.VMEM((max(rows for _, rows in pieces), model // 2), f32), flow, flow]
        + [pltpu.SemaphoreType.DMA(())]
        + plane_scratch * fused,
        late=1,
        held=7,
    )

    def reduced(left, right):
        grad = dot_first(left, right).astype(bf16)
        return lax.psum_scatter(grad, "dp", scatter_dimension=0, tiled=True).astype(f32)

    d_cat, d_norm_back, little, gain_in = local_call(
        mixer_backward,
        [
            shape_of(bf16, count, 2 * width),
            tok,
            shape_of(f32, LANE, 2 * width + LANE),
            shape_of(f32, 1, model),
        ],
        [
            pltpu.VMEM((count, width), bf16),
            wide,
            wide,
            wide,
            pltpu.VMEM((count + TAIL, width), f32),
            pltpu.VMEM((ROWS + TAIL, width), f32),
            pltpu.VMEM((count, 2 * width), bf16),
            pltpu.VMEM((SUB, width), f32),
            pltpu.VMEM((heads, LANE, 2 * LANE), f32),
        ],
        2 * count * (3 * count * width + 3 * model * width),
        (
            back_group,
            full_out,
            ocol,
            orow,
            pos_col,
            gain_f[0:1],
            chan,
            blocks,
            gate_pre,
            gate_rec,
            state,
            conv,
            gate_in,
            branch,
            norm_group,
            full_in,
            full_gate,
        ),
        9,
    )
    share = model // (n_dp * n_mp)
    gain_parts = jnp.concatenate([gain_in, gain_mid], axis=0).reshape(2, n_dp, n_mp, share)
    gain_parts = gain_parts.transpose(1, 2, 0, 3).reshape(n_dp, 2 * n_mp, share)
    gain_parts = jnp.pad(gain_parts, ((0, 0), (0, 2 * SUB - 2 * n_mp), (0, LANE - share)))
    gain_parts = gain_parts.reshape(2 * SUB * n_dp, LANE)
    ffn_low = lax.psum_scatter(ffn_part, "mp", scatter_dimension=0, tiled=True)
    ffn_low, d_norm_back = lax.optimization_barrier((ffn_low, d_norm_back))
    grad_inputs, *mix_grads = line_call(
        sum_back,
        n_mp,
        3,
        [shape_of(bf16, local_rows, model)]
        + (
            [shape_of(f32, rows, hidden_width)] * 3
            + [shape_of(f32, rows, width)] * 3
            + [shape_of(f32, piece, little.shape[1]), shape_of(f32, 2 * SUB, LANE)]
        )
        * fused,
        True,
        False,
        (inputs, d_resid, gain_f[0:1], d_norm_back)
        + (
            (
                little,
                gain_parts,
                norm_mid_group,
                cot_group,
                d_up,
                d_gate_ff,
                hidden,
                norm_group,
                back_group,
                d_cat,
                mixed,
            )
            if fused
            else ()
        ),
        reduce_scratch(3, rows, width)
        + given_scratch(piece, little.shape[1])
        + given_scratch(2 * SUB, LANE)
        + [pltpu.VMEM((n_mp - 1, 2 * SUB, LANE), f32)]
        + [pltpu.SemaphoreType.DMA((n_mp - 1,))] * 2
        + reduce_scratch(3, rows, hidden_width)
        + [pltpu.VMEM((count, model), bf16)] * 2
        + [pltpu.VMEM((count, hidden_width), bf16)] * 3
        + [pltpu.SemaphoreType.DMA((9,))]
        if fused
        else (),
        9 * fused,
    )
    if fused:
        up_grad, gate_ff_grad, down_grad, *mix_grads, little_own, gain_own = mix_grads
    else:
        up_grad = reduced(norm_mid_group, d_up)
        gate_ff_grad = reduced(norm_mid_group, d_gate_ff)
        down_grad = reduced(cot_group, hidden)
        mix_grads = [
            reduced(norm_group, d_cat[:, :width]),
            reduced(norm_group, d_cat[:, width:]),
            reduced(back_group, mixed),
        ]
        little_own = lax.psum_scatter(little, "dp", scatter_dimension=0, tiled=True)
        gain_own = lax.psum(lax.psum_scatter(gain_parts, "dp", scatter_dimension=0, tiled=True), "mp")
    outs = [
        shape_of(bf16, local_rows, model),
        shape_of(f32, 2, share),
        shape_of(f32, 4, heads, piece),
        shape_of(f32, 3, heads, piece),
        shape_of(f32, heads, piece),
        shape_of(f32, 2, heads, piece, LANE),
    ]
    copied = [grad_inputs, mix_grads[0], mix_grads[1], up_grad, gate_ff_grad] if fused else []
    output, grad_gains, grad_conv, grad_bias, grad_decay, grad_blocks, *copied = local_call(
        functools.partial(finish, heads, piece, share),
        outs + [shape_of(a.dtype, *a.shape) for a in copied],
        [],
        0,
        (resid, ffn_low, ffn_high, gain_own, little_own, *copied),
    )
    if fused:
        grad_inputs, grad_in, grad_gate, up_grad, gate_ff_grad = copied
    else:
        grad_in, grad_gate, _ = mix_grads
    return (
        output,
        grad_inputs,
        grad_gains,
        grad_in,
        grad_gate,
        mix_grads[2].T,
        grad_conv,
        grad_bias,
        grad_decay,
        grad_blocks,
        up_grad,
        gate_ff_grad,
        down_grad.T,
    )


def solution(mesh):
    row, col = P("dp", "mp"), P("mp", "dp")
    tok = P(("dp", "mp"), None)
    chan = P(None, "mp", "dp")
    gate = P(None, "mp", "dp", None)
    return jax.shard_map(
        shards,
        mesh=mesh,
        in_specs=(
            tok, tok, P(("dp", "mp")), P("dp", None), P("dp", None), P(),
            row, row, col, chan, chan, col, gate, row, row, col,
        ),
        out_specs=(
            tok, tok, P(None, ("dp", "mp")), row, row, col, chan, chan, col, gate, row, row, col,
        ),
        check_vma=False,
    )
```

```python
import functools

import jax
import jax.numpy as jnp
from jax import lax
from jax.experimental import pallas as pl
from jax.experimental.pallas import tpu as pltpu
from jax.sharding import PartitionSpec as P

epsilon = 1e-06
LANE = 128
SUB = 8
TAIL = 24
ROWS = 272
VMEM_MB = 62
f32 = jnp.float32
bf16 = jnp.bfloat16
GELU_C = 0.7978845608028654
GELU_A = 0.044715


def rms_scale(values):
    return lax.rsqrt(jnp.mean(values * values, axis=-1, keepdims=True) + epsilon)


def dot(left, right):
    return lax.dot_general(left, right, (((1,), (0,)), ((), ())), preferred_element_type=f32)


def dot_last(left, right):
    return lax.dot_general(left, right, (((1,), (1,)), ((), ())), preferred_element_type=f32)


def dot_first(left, right):
    return lax.dot_general(left, right, (((0,), (0,)), ((), ())), preferred_element_type=f32)


def gelu_of(v):
    return 0.5 * v * (1.0 + jnp.tanh(GELU_C * (v + GELU_A * v * v * v)))


def gelu_both(v):
    square = v * v
    th = jnp.tanh(GELU_C * (v + GELU_A * v * square))
    half = 0.5 * (1.0 + th)
    slope = half + 0.5 * v * (1.0 - th * th) * (GELU_C * (1.0 + 3.0 * GELU_A * square))
    return v * half, slope


def sigmoid(v):
    return 0.5 * jnp.tanh(0.5 * v) + 0.5


def split(values):
    high = values.astype(bf16)
    return high, (values - high.astype(f32)).astype(bf16)


def rows_of(index, rows):
    return pl.ds(pl.multiple_of(index * rows, rows), rows)


def pick_rows(order_col, count):
    places = lax.broadcasted_iota(jnp.int32, (order_col.shape[0], count), 1)
    return (places == order_col).astype(f32).astype(bf16)


def put_rows(order_row, first, rows):
    places = lax.broadcasted_iota(jnp.int32, (rows, order_row.shape[1]), 0) + first
    return (places == order_row).astype(f32).astype(bf16)


def mixer_forward(tokens, ocol, orow, pos, w_in, w_gate, chan, blocks, w_out_far, *rest):
    far, rest = rest[:8], rest[8:]
    packed, rate, prod, before, low, w_out, *near, late_sem, held_sem = rest
    gate_ref, branch_ref, conv_ref, gin_ref, grec_ref, state_ref, mixed_ref, out_ref = near
    (late_out,) = late_all([w_out_far], [w_out], late_sem)
    leaving = [
        pltpu.make_async_copy(source, target, held_sem.at[i, 0])
        for i, (source, target) in enumerate(zip(near, far))
    ]
    count, _ = tokens.shape
    width = w_in.shape[1]
    steps = count // SUB
    heads = width // LANE

    def project(b, carry):
        at = rows_of(b, ROWS)
        packed[...] = dot(pick_rows(ocol[at, :], count), tokens[...]).astype(bf16)
        branch_ref[at, :] = dot(packed[...], w_in[...])
        gate_ref[at, :] = dot(packed[...], w_gate[...])
        return carry

    lax.fori_loop(0, count // ROWS, project, 0)
    leaving[0].start()
    leaving[1].start()

    for k in range(TAIL // SUB):
        last = branch_ref[pl.ds(count - TAIL + k * SUB, SUB), :]
        before[pl.ds(k * SUB, SUB), :] = pltpu.roll(last, 1, 0)
    before[pl.ds(TAIL, ROWS), :] = branch_ref[pl.ds(0, ROWS), :]

    def gates(b, carry):
        at = rows_of(b, ROWS)

        @pl.when(b > 0)
        def _():
            before[...] = branch_ref[pl.ds(pl.multiple_of(b * ROWS - TAIL, SUB), ROWS + TAIL), :]

        place = pos[at, :]
        for h in range(heads):
            lanes = pl.ds(h * LANE, LANE)
            par = chan[:, lanes]
            conv = par[4:5] + par[0:1] * before[pl.ds(TAIL, ROWS), lanes]
            for k in range(1, 4):
                earlier = before[pl.ds(TAIL - SUB * k, ROWS), lanes]
                conv = conv + par[k : k + 1] * jnp.where(place >= k, earlier, 0.0)
            high, rest = split(conv)
            pair = jnp.concatenate([blocks[h], blocks[heads + h]], axis=1)
            pre = dot(
                jnp.concatenate([high, rest], axis=1), jnp.concatenate([pair, pair], axis=0)
            )
            gate_in = sigmoid(pre[:, :LANE] + par[5:6])
            gate_rec = sigmoid(pre[:, LANE:] + par[6:7])
            kept = jnp.exp(-8.0 * gate_rec * par[7:8])
            drive = jnp.sqrt(1.0 - kept * kept + 0.01) * gate_in * conv
            conv_ref[at, lanes] = conv
            gin_ref[at, lanes] = gate_in
            grec_ref[at, lanes] = gate_rec
            rate[at, lanes] = jnp.where(place >= 1, kept, 0.0)
            state_ref[at, lanes] = drive
        return carry

    lax.fori_loop(0, count // ROWS, gates, 0)
    for copy in leaving[2:5]:
        copy.start()

    def scan(i, carry):
        held, passed = carry
        at = rows_of(i, SUB)
        a = rate[at, :]
        held = a * held + state_ref[at, :]
        passed = a * passed
        state_ref[at, :] = held
        prod[at, :] = passed
        return held, passed

    ends = lax.fori_loop(
        0, steps, scan, (jnp.zeros((SUB, width), f32), jnp.ones((SUB, width), f32)), unroll=8
    )
    first = lax.broadcasted_iota(jnp.int32, (SUB, width), 0) == 0
    carry_in = jnp.zeros((SUB, width), f32)
    for _ in range(SUB - 1):
        carry_in = jnp.where(first, 0.0, pltpu.roll(ends[0] + ends[1] * carry_in, 1, 0))

    def finish(i, carry):
        at = rows_of(i, 2 * SUB)
        twice = jnp.concatenate([carry_in, carry_in], axis=0)
        value = state_ref[at, :] + prod[at, :] * twice
        state_ref[at, :] = value
        low[at, :] = (gelu_of(gate_ref[at, :]) * value).astype(bf16)
        return carry

    lax.fori_loop(0, steps // 2, finish, 0, unroll=2)
    leaving[5].start()
    late_out.ready()

    def leave(b, carry):
        at = rows_of(b, ROWS)
        mixed = dot(put_rows(orow[...], b * ROWS, ROWS), low[...]).astype(bf16)
        mixed_ref[at, :] = mixed
        out_ref[at, :] = dot_last(mixed, w_out[...]).astype(bf16)
        return carry

    lax.fori_loop(0, count // ROWS, leave, 0)
    for copy in leaving[6:]:
        copy.start()
    for copy in leaving:
        copy.wait()


def mixer_backward(back, w_out, ocol, orow, pos, gain, chan, blocks, *rest):
    far, (dcat_ref, dnorm_ref, little_ref, dgain_ref), rest = rest[:9], rest[9:13], rest[13:]
    dmix_arr, dmix, adj, prod, after, before, low, small_ref, dblocks_ref, *rest = rest
    gate_ref, grec_ref, state_ref, conv_ref, gin_ref, branch_ref, norm, w_in, w_gate, late_sem = rest
    late = late_all(far, rest[:9], late_sem)
    count, _ = back.shape
    width = w_in.shape[1]
    steps = count // SUB
    heads = width // LANE
    blocks_of = count // ROWS

    def enter(b, carry):
        at = rows_of(b, ROWS)
        dmix_arr[at, :] = dot(back[at, :], w_out[...]).astype(bf16)
        return carry

    lax.fori_loop(0, blocks_of, enter, 0)
    for array in late[:3]:
        array.ready()

    def pack(b, carry):
        at = rows_of(b, ROWS)
        d_mixed = dot(pick_rows(ocol[at, :], count), dmix_arr[...])
        value, slope = gelu_both(gate_ref[at, :])
        adj[at, :] = d_mixed * value
        low[at, pl.ds(width, width)] = (d_mixed * state_ref[at, :] * slope).astype(bf16)
        kept = jnp.exp(-8.0 * grec_ref[at, :] * chan[7:8, :])
        dmix[at, :] = jnp.where(pos[at, :] >= 1, kept, 0.0)
        return carry

    lax.fori_loop(0, blocks_of, pack, 0)
    for array in late:
        array.ready()

    def scan(i, carry):
        held, passed, following = carry
        at = rows_of(steps - 1 - i, SUB)
        held = following * held + adj[at, :]
        passed = following * passed
        adj[at, :] = held
        prod[at, :] = passed
        return held, passed, dmix[at, :]

    last = lax.broadcasted_iota(jnp.int32, (SUB, width), 0) == SUB - 1
    wrapped = jnp.where(last, 0.0, pltpu.roll(dmix[pl.ds(0, SUB), :], SUB - 1, 0))
    ends = lax.fori_loop(
        0,
        steps,
        scan,
        (jnp.zeros((SUB, width), f32), jnp.ones((SUB, width), f32), wrapped),
        unroll=8,
    )
    carry_in = jnp.zeros((SUB, width), f32)
    for _ in range(SUB - 1):
        carry_in = jnp.where(last, 0.0, pltpu.roll(ends[0] + ends[1] * carry_in, SUB - 1, 0))

    small_ref[...] = jnp.zeros_like(small_ref)
    dblocks_ref[...] = jnp.zeros_like(dblocks_ref)
    first = lax.broadcasted_iota(jnp.int32, (SUB, width), 0) == 0
    state_last = state_ref[pl.ds(count - SUB, SUB), :]
    before[pl.ds(TAIL - SUB, SUB), :] = jnp.where(first, 0.0, pltpu.roll(state_last, 1, 0))
    before[pl.ds(TAIL, ROWS), :] = state_ref[pl.ds(0, ROWS), :]
    wide_carry = jnp.concatenate([carry_in] * (ROWS // SUB), axis=0)

    def point(b, carry):
        at = rows_of(b, ROWS)

        @pl.when(b > 0)
        def _():
            before[...] = state_ref[pl.ds(pl.multiple_of(b * ROWS - TAIL, SUB), ROWS + TAIL), :]

        place = pos[at, :]
        for h in range(heads):
            lanes = pl.ds(h * LANE, LANE)
            par = chan[:, lanes]
            adjoint = adj[at, lanes] + prod[at, lanes] * wide_carry[:, h * LANE : (h + 1) * LANE]
            conv = conv_ref[at, lanes]
            gate_in = gin_ref[at, lanes]
            gate_rec = grec_ref[at, lanes]
            kept = jnp.exp(-8.0 * gate_rec * par[7:8])
            square = kept * kept
            inside = 1.0 - square + 0.01
            inverse = lax.rsqrt(inside)
            root = inside * inverse
            previous = before[pl.ds(TAIL - SUB, ROWS), lanes]
            d_log = adjoint * previous * dmix[at, lanes]
            scaled = adjoint * gate_in
            d_log = d_log - scaled * conv * square * inverse
            d_in = adjoint * root * conv * gate_in * (1.0 - gate_in)
            d_rec = d_log * (-8.0 * par[7:8]) * gate_rec * (1.0 - gate_rec)
            both = jnp.concatenate([d_in, d_rec], axis=1)
            high, rest = split(both)
            pair = jnp.concatenate([blocks[h], blocks[heads + h]], axis=1)
            d_conv = scaled * root + dot_last(high, pair) + dot_last(rest, pair)
            dblocks_ref[h] += dot_first(conv.astype(bf16), high)
            after[at, lanes] = d_conv
            small_ref[4:5, lanes] += jnp.sum(d_conv, axis=0, keepdims=True)
            small_ref[5:6, lanes] += jnp.sum(d_in, axis=0, keepdims=True)
            small_ref[6:7, lanes] += jnp.sum(d_rec, axis=0, keepdims=True)
            small_ref[7:8, lanes] += (
                jnp.sum(d_log * gate_rec, axis=0, keepdims=True) * (-8.0) * par[8:9]
            )
        return carry

    lax.fori_loop(0, blocks_of, point, 0)

    for k in range(TAIL // SUB):
        head = after[pl.ds(k * SUB, SUB), :]
        after[pl.ds(count + k * SUB, SUB), :] = pltpu.roll(head, SUB - 1, 0)
        tail = branch_ref[pl.ds(count - TAIL + k * SUB, SUB), :]
        before[pl.ds(k * SUB, SUB), :] = pltpu.roll(tail, 1, 0)
    before[pl.ds(TAIL, ROWS), :] = branch_ref[pl.ds(0, ROWS), :]

    def unmix(b, carry):
        at = rows_of(b, ROWS)

        @pl.when(b > 0)
        def _():
            before[...] = branch_ref[pl.ds(pl.multiple_of(b * ROWS - TAIL, SUB), ROWS + TAIL), :]

        place = pos[at, :]
        for h in range(heads):
            lanes = pl.ds(h * LANE, LANE)
            par = chan[:, lanes]
            d_conv = after[at, lanes]
            d_branch = par[0:1] * d_conv
            small_ref[0:1, lanes] += jnp.sum(
                d_conv * before[pl.ds(TAIL, ROWS), lanes], axis=0, keepdims=True
            )
            for k in range(1, 4):
                later = pl.ds(pl.multiple_of(b * ROWS + SUB * k, SUB), ROWS)
                d_branch = d_branch + par[k : k + 1] * jnp.where(
                    pos[later, :] >= k, after[later, lanes], 0.0
                )
                earlier = before[pl.ds(TAIL - SUB * k, ROWS), lanes]
                small_ref[k : k + 1, lanes] += jnp.sum(
                    jnp.where(place >= k, d_conv * earlier, 0.0), axis=0, keepdims=True
                )
            low[at, lanes] = d_branch.astype(bf16)
        return carry

    lax.fori_loop(0, blocks_of, unmix, 0)
    lines = [small_ref[0:SUB, h * LANE : (h + 1) * LANE] for h in range(heads)]
    lines.append(jnp.zeros((LANE - SUB * heads, LANE), f32))
    little_ref[:, pl.ds(2 * width, LANE)] = jnp.concatenate(lines, axis=0).T
    for h in range(heads):
        little_ref[:, pl.ds(2 * h * LANE, 2 * LANE)] = dblocks_ref[h]
    dgain_ref[...] = jnp.zeros_like(dgain_ref)

    def leave(b, carry):
        at = rows_of(b, ROWS)
        cat = dot(put_rows(orow[...], b * ROWS, ROWS), low[...]).astype(bf16)
        dcat_ref[at, :] = cat
        d_norm = dot_last(cat[:, :width], w_in[...]) + dot_last(cat[:, width:], w_gate[...])
        dgain_ref[...] += jnp.sum(d_norm * norm[at, :].astype(f32), axis=0, keepdims=True)
        dnorm_ref[at, :] = d_norm.astype(bf16)
        return carry

    lax.fori_loop(0, blocks_of, leave, 0)
    dgain_ref[...] = dgain_ref[...] / gain[...]


MESH = pl.DeviceIdType.MESH
TILE = 16
PIECES = 8
HOP = 1
AFTER = 1


def cut_rows(rows, parts):
    tiles = rows // TILE
    ends = [tiles * (k + 1) // parts for k in range(parts)]
    return [(TILE * a, TILE * (b - a)) for a, b in zip([0] + ends[:-1], ends)]


class Line:
    def __init__(self, n, local, part, arrived, whole, sums, alls):
        self.n, self.local, self.part, self.arrived, self.whole = n, local, part, arrived, whole
        self.sums, self.alls = sums, alls
        self.me = lax.axis_index("mp")
        self.pieces = cut_rows(local, PIECES)
        self.has = (self.me > 0, self.me < n - 1)

    def greet(self, plane=None):
        barrier = pltpu.get_barrier_semaphore()
        more = 0
        if plane is not None:
            for bit in plane.bits:
                more += 1
                pl.semaphore_signal(
                    barrier, inc=1, device_id={"dp": plane.other(bit)}, device_id_type=MESH
                )
        for away in range(1, self.n):
            more += 1
            pl.semaphore_signal(
                barrier,
                inc=1,
                device_id={"mp": lax.rem(self.me + away, self.n)},
                device_id_type=MESH,
            )
        pl.semaphore_wait(barrier, more)

    def rows_at(self, owner, k):
        first, rows = self.pieces[k]
        return pl.ds(pl.multiple_of(owner * self.local + first, TILE), rows)

    def copy(self, source, target, sems, way, owner, k):
        return pltpu.make_async_remote_copy(
            src_ref=source,
            dst_ref=target,
            send_sem=sems[0].at[way, owner, k],
            recv_sem=sems[1].at[way, owner, k],
            device_id={"mp": self.me + 1 - 2 * way},
            device_id_type=MESH,
        )

    def sum_copy(self, way, owner, k, first=False):
        at = self.rows_at(owner, k)
        landed = self.arrived[way].at[at]
        return self.copy(self.part.at[at] if first else landed, landed, self.sums, way, owner, k)

    def all_copy(self, way, owner, k):
        block = self.whole.at[self.rows_at(owner, k)]
        return self.copy(block, block, self.alls, way, owner, k)

    def first(self, k):
        for away in range(self.n - 1):
            for way in range(2):
                owner = away if way else self.n - 1 - away

                @pl.when(jnp.logical_not(self.has[way]))
                def _():
                    self.sum_copy(way, owner, k, True).start()

    def relay(self, k, stage):
        for way in range(2):
            late = stage - (self.n - 1 - self.me if way else self.me)
            owner = late if way else self.n - 1 - late

            @pl.when(self.has[way] & (late >= 0))
            def _():
                self.sum_copy(way, owner, k).wait_recv()
                at = self.rows_at(owner, k)
                landed = self.arrived[way]
                landed[at, :] = (landed[at, :].astype(f32) + self.part[at, :].astype(f32)).astype(bf16)
                self.sum_copy(way, owner, k).start()

    def total(self, k, into):
        at = self.rows_at(self.me, k)
        rows = pl.ds(0, self.pieces[k][1])
        into[rows, :] = self.part[at, :].astype(f32)
        for way in range(2):

            @pl.when(self.has[way])
            def _():
                self.sum_copy(way, self.me, k).wait_recv()
                into[rows, :] += self.arrived[way][at, :].astype(f32)

    def spread(self, k):
        for way in range(2):

            @pl.when(self.has[1 - way])
            def _():
                self.all_copy(way, self.me, k).start()

    def forward(self, k, stage):
        for way in range(2):
            owner = self.me + stage if way else self.me - stage
            there = owner < self.n if way else owner >= 0

            @pl.when(there)
            def _():
                self.all_copy(way, owner, k).wait_recv()

            @pl.when(there & self.has[1 - way])
            def _():
                self.all_copy(way, owner, k).start()

    def sent(self, k):
        for owner in range(self.n):
            for way in range(2):

                @pl.when(self.me > owner if way else self.me < owner)
                def _():
                    self.sum_copy(way, owner, k).wait_send()

    def finish(self):
        for k in range(PIECES):
            for owner in range(self.n):
                for way in range(2):
                    if self.whole is not None:
                        reached = self.me <= owner if way else self.me >= owner

                        @pl.when(reached & self.has[1 - way])
                        def _():
                            self.all_copy(way, owner, k).wait_send()

    def run(self, point, tasks=()):
        sums, alls = self.part is not None, self.whole is not None
        slots = [[] for _ in range(PIECES + (HOP + AFTER) * (self.n - 1) + 1)]
        for k in range(PIECES):
            done = k + HOP * (self.n - 1) if sums else 0
            if sums:
                slots[k].append((0, functools.partial(self.first, k)))
                for stage in range(1, self.n - 1):
                    slots[k + HOP * stage].append((2, functools.partial(self.relay, k, stage)))
                slots[done].append((3, functools.partial(self.sent, k)))
            slots[done].append((3, functools.partial(point, k)))
            if alls:
                slots[done].append((4, functools.partial(self.spread, k)))
                for stage in range(1, self.n):
                    at = (done if sums else k) + AFTER * stage
                    slots[at].append((1, functools.partial(self.forward, k, stage)))
        tasks = iter(tasks)
        for slot in slots:
            for step, (_, work) in enumerate(sorted(slot, key=lambda entry: entry[0])):
                if step in (0, 1, 3):
                    next(tasks, idle)()
                work()
        for task in tasks:
            task()
        self.finish()

    def tiles(self, k, body):
        first, rows = self.pieces[k]

        def one(i, carry):
            body(
                pl.ds(pl.multiple_of(i * TILE, TILE), TILE),
                pl.ds(pl.multiple_of(first + i * TILE, TILE), TILE),
                pl.ds(pl.multiple_of(self.me * self.local + first + i * TILE, TILE), TILE),
            )
            return carry

        lax.fori_loop(0, rows // TILE, one, 0)


def idle():
    pass


class Late:
    def __init__(self, source, ref, sem):
        self.ref = ref
        self.copy = pltpu.make_async_copy(source, ref, sem)
        self.pending = True

    def begin(self):
        self.copy.start()

    def ready(self):
        if self.pending:
            self.copy.wait()
        self.pending = False


class Here:
    def __init__(self, ref):
        self.ref = ref

    def ready(self):
        pass


def late_all(sources, refs, sems):
    arrays = [Late(source, ref, sems.at[i]) for i, (source, ref) in enumerate(zip(sources, refs))]
    for array in arrays:
        array.begin()
    return arrays


class Plane:
    bits = (1, 2, 4)
    orders = ((4, 2, 1), (2, 4, 1))

    def __init__(self):
        self.me = lax.axis_index("dp")

    def bit(self, bit):
        return lax.rem(self.me // bit, 2)

    def other(self, *bits):
        return self.me + sum(bit * (1 - 2 * self.bit(bit)) for bit in bits)

    def gather_copies(self, item, view, halves, stage, sems):
        copies = []
        for half in halves:
            order = self.orders[half]
            for combo in range(1 << stage):
                flipped = [bit for i, bit in enumerate(order[:stage]) if combo >> i & 1]
                block = view(self.other(*flipped), half)
                slot = (1 << stage) - 1 + combo
                copies.append(
                    pltpu.make_async_remote_copy(
                        src_ref=block,
                        dst_ref=block,
                        send_sem=sems[0].at[item, half, slot],
                        recv_sem=sems[1].at[item, half, slot],
                        device_id={"dp": self.other(order[stage])},
                        device_id_type=MESH,
                    )
                )
        return copies


class Reduce(Plane):
    def __init__(self, index, left, right, lanes, sent, mine, theirs, got, second, third, out, sems):
        super().__init__()
        self.sent, self.theirs = sent, theirs
        self.index, self.left, self.right, self.lanes = index, left, right, lanes
        self.mine, self.got = mine, got
        self.second, self.third, self.out = second, third, out
        self.sems = sems
        self.rows = out.shape[0]
        self.half = self.rows // 2

    def copy(self, source, target, slot, bit):
        return pltpu.make_async_remote_copy(
            src_ref=source,
            dst_ref=target,
            send_sem=self.sems[0].at[self.index, slot],
            recv_sem=self.sems[1].at[self.index, slot],
            device_id={"dp": self.other(bit)},
            device_id_type=MESH,
        )

    def core_copy(self, t):
        return self.copy(self.theirs.at[(4 * self.index + t) % 2], self.got.at[t], t, 1)

    def second_copy(self, half, j):
        x, y = self.bit(2), self.bit(4)
        block = (1 - y) * 2 + j if half else j * 2 + 1 - x
        rows = self.mine.at[block, pl.ds(half * self.half, self.half)]
        return self.copy(rows, self.second(half, j), 4 + 2 * half + j, 4 if half else 2)

    def third_block(self, half):
        x, y = self.bit(2), self.bit(4)
        return y * 2 + 1 - x if half else (1 - y) * 2 + x

    def third_copy(self, half):
        rows = self.mine.at[self.third_block(half), pl.ds(half * self.half, self.half)]
        return self.copy(rows, self.third(half), 8 + half, 2 if half else 4)

    def product(self, t):
        def task():
            core = self.bit(1)
            pair = pl.ds(t * 2 * self.rows, 2 * self.rows)
            if t == 0:
                self.left.ready()
                self.right.ready()
            if len(self.sent) > 1:
                self.sent[-2].wait_send()
            both = dot_first(self.left.ref[:, pair], self.right.ref[:, self.lanes])
            low, high = both[: self.rows], both[self.rows :]
            self.mine[t] = jnp.where(core == 0, low, high).astype(bf16)
            self.theirs[(4 * self.index + t) % 2] = jnp.where(core == 0, high, low).astype(bf16)
            self.sent.append(self.core_copy(t))
            self.sent[-1].start()

        return task

    def keep(self, t):
        return self.mine[t]

    def add_core(self):
        for t in range(4):
            self.core_copy(t).wait_recv()
            self.mine[t] = (self.keep(t).astype(f32) + self.got[t].astype(f32)).astype(self.mine.dtype)
        for half in range(2):
            for j in range(2):
                self.second_copy(half, j).start()

    def add_second(self):
        for half in range(2):
            for j in range(2):
                self.second_copy(half, j).wait_recv()
        for half in range(2):
            block, at = self.third_block(half), pl.ds(half * self.half, self.half)
            far = 1 - self.bit(2 if half else 4)
            self.mine[block, at] = (
                self.mine[block, at].astype(f32) + self.second(half, far)[...].astype(f32)
            ).astype(self.mine.dtype)
            self.third_copy(half).start()

    def add_third(self):
        own = self.bit(4) * 2 + self.bit(2)
        for half in range(2):
            self.third_copy(half).wait_recv()
            at = pl.ds(half * self.half, self.half)
            near = self.bit(2 if half else 4)
            self.out[at, :] = (
                self.mine[own, at].astype(f32)
                + self.second(half, near)[...].astype(f32)
                + self.third(half)[...].astype(f32)
            )

    def finish(self):
        for half in range(2):
            for j in range(2):
                self.second_copy(half, j).wait_send()
            self.third_copy(half).wait_send()


class Given(Reduce):
    def __init__(self, given, mine, got, second, third, out, sems):
        super().__init__(0, None, None, None, None, *views(0, mine, None, got, second, third), out, sems)
        self.given = given

    def rows_of(self, t, core):
        return pl.ds(pl.multiple_of((2 * t + core) * self.rows, self.rows), self.rows)

    def core_copy(self, t):
        return self.copy(self.given.at[self.rows_of(t, 1 - self.bit(1))], self.got.at[t], t, 1)

    def start(self):
        for t in range(4):
            self.core_copy(t).start()

    def finish(self):
        for t in range(4):
            self.core_copy(t).wait_send()
        super().finish()

    def keep(self, t):
        return self.given[self.rows_of(t, self.bit(1)), :]


def views(index, mine, theirs, got, second, third):
    return (
        mine.at[index],
        theirs,
        got.at[index],
        lambda half, j: second.at[index, half, j],
        lambda half: third.at[index, half],
    )


def blocks_views(index, both, spare):
    half_rows = spare.shape[1] // 2

    def halves(block, j):
        return spare.at[block, pl.ds(pl.multiple_of(j * half_rows, TILE), half_rows)]

    return (
        both.at[pl.ds(0, 4)],
        spare.at[pl.ds(6, 2)],
        both.at[pl.ds(4, 4)],
        lambda half, j: halves(3 * index + half, j),
        lambda half: halves(3 * index + 2, half),
    )


def reduce_tasks(parts, given=()):
    tasks = [part.product(t) for part in parts for t in range(4)]

    def also(at, extra):
        while len(tasks) <= at:
            tasks.append(idle)
        before = tasks[at]

        def both():
            extra()
            before()

        tasks[at] = both

    for i, part in enumerate(parts):
        also(4 * i + 5, part.add_core)
        also(4 * i + 8, part.add_second)
        also(4 * i + 10, part.add_third)

    for part in given:
        also(0, part.start)
        also(2, part.add_core)
        also(4, part.add_second)
        also(6, part.add_third)

    def finish():
        for ring in {id(part.sent): part.sent for part in parts}.values():
            for copy in ring[-2:]:
                copy.wait_send()
        for part in [*parts, *given]:
            part.finish()

    return tasks, finish


def given_scratch(rows, width):
    sem = pltpu.SemaphoreType.DMA((1, 10))
    return [
        pltpu.VMEM((1, 4, rows, width), f32),
        pltpu.VMEM((1, 4, rows, width), f32),
        pltpu.VMEM((1, 2, 2, rows // 2, width), f32),
        pltpu.VMEM((1, 2, rows // 2, width), f32),
        sem,
        sem,
    ]


def reduce_scratch(arrays, rows, width):
    block = pltpu.VMEM((arrays, 4, rows, width), bf16)
    sem = pltpu.SemaphoreType.DMA((arrays, 10))
    return [
        block,
        pltpu.VMEM((2, rows, width), bf16),
        block,
        pltpu.VMEM((arrays, 2, 2, rows // 2, width), bf16),
        pltpu.VMEM((arrays, 2, rows // 2, width), bf16),
        sem,
        sem,
    ]


def gather_norm(n, x, gain, whole, send, recv):
    line = Line(n, x.shape[0], None, None, whole, None, (send, recv))
    line.greet()

    def point(k):
        def one(_, own, at):
            v = x[own, :].astype(f32)
            whole[at, :] = (v * rms_scale(v) * gain[...]).astype(bf16)

        line.tiles(k, one)

    line.run(point)


def row_view(array, rows):
    def view(owner, half):
        first = owner * rows + half * (rows // 2)
        return array.at[pl.ds(pl.multiple_of(first, TILE), rows // 2)]

    return view


def gather_tasks(plane, items, sems):
    def copies(stage):
        return [
            copy
            for item, (view, halves) in enumerate(items)
            for copy in plane.gather_copies(item, view, halves, stage, sems)
        ]

    def stage_task(stage):
        def task():
            if stage:
                for copy in copies(stage - 1):
                    copy.wait_recv()
            for copy in copies(stage):
                copy.start()

        return task

    def last():
        for copy in copies(2):
            copy.wait_recv()
        for stage in range(3):
            for copy in copies(stage):
                copy.wait_send()

    return stage_task(0), stage_task(1), stage_task(2), last


def gather_weights(
    n,
    x,
    gain,
    w_in,
    w_gate,
    w_out,
    blocks,
    chan,
    whole,
    all_in,
    all_gate,
    all_out,
    all_blocks,
    all_chan,
    send,
    recv,
    raw,
    plane_send,
    plane_recv,
):
    line = Line(n, x.shape[0], None, None, whole, None, (send, recv))
    plane = Plane()
    line.greet(plane)
    sems = plane_send, plane_recv
    rows, piece = w_in.shape[0], blocks.shape[1]
    lines = chan.shape[0]

    def blocks_view(owner, half):
        return all_blocks.at[:, pl.ds(pl.multiple_of(owner * piece, TILE), piece)]

    def chan_view(owner, half):
        return raw.at[pl.ds(pl.multiple_of(owner * lines, TILE), lines)]

    items = [(row_view(array, rows), (0, 1)) for array in (all_in, all_gate, all_out)]
    items += [(blocks_view, (0,)), (chan_view, (1,))]

    first, second, third, finish = gather_tasks(plane, items, sems)

    def last():
        finish()
        lane = lax.broadcasted_iota(jnp.int32, (LANE, LANE), 1)
        row = lax.broadcasted_iota(jnp.int32, (LANE, LANE), 0)
        total = jnp.zeros((lines, LANE), f32)
        for owner in range(LANE // piece):
            moved = ((row < piece) & (row + owner * piece == lane)).astype(f32).astype(bf16)
            total = total + dot(raw[pl.ds(owner * lines, lines), :], moved)
        for h in range(lines // SUB):
            par = total[h * SUB : (h + 1) * SUB]
            lanes = pl.ds(h * LANE, LANE)
            all_chan[0:SUB, lanes] = par
            decay = par[SUB - 1 : SUB]
            small = jnp.exp(-jnp.abs(decay))
            one_more = 1.0 + small
            rest = jnp.where(one_more == 1.0, 1.0, one_more - 1.0)
            log_one_more = jnp.where(one_more == 1.0, small, jnp.log(one_more) * (small / rest))
            all_chan[SUB - 1 : SUB, lanes] = jnp.maximum(decay, 0.0) + log_one_more
            all_chan[SUB : 2 * SUB, lanes] = jnp.broadcast_to(sigmoid(decay), (SUB, LANE))

    own = pl.ds(pl.multiple_of(plane.me * rows, TILE), rows)
    all_in[own, :] = w_in[...]
    all_gate[own, :] = w_gate[...]
    all_out[own, :] = w_out[...]
    all_blocks[:, pl.ds(pl.multiple_of(plane.me * piece, TILE), piece), :] = blocks[...]
    raw[pl.ds(pl.multiple_of(plane.me * lines, TILE), lines), :] = chan[...]

    def point(k):
        def one(_, own, at):
            v = x[own, :].astype(f32)
            whole[at, :] = (v * rms_scale(v) * gain[...]).astype(bf16)

        line.tiles(k, one)

    first()
    line.run(point, [idle] * 4 + [second] + [idle] * 3 + [third] + [idle] * 3 + [last])


def norm_back(value, gain, grad):
    scale = rms_scale(value)
    e = gain * grad
    slope = scale * scale * scale * jnp.mean(value * e, axis=-1, keepdims=True)
    return scale * e - value * slope, grad * value * scale


def middle(n, x, gain, cot, part, *rest):
    (*shares, cot_first), rest = rest[:4], rest[4:]
    grads = len(rest) > 45 and 2 or 0
    (d_resid, gain_grad, back, high_sum), rest = rest[:4], rest[4:]
    weight_grads, far, rest = rest[:grads], rest[grads : grads + 7], rest[grads + 7 :]
    left, right, total, ss, sr, send, recv, part2, ss2, sr2, send2, recv2, csend, crecv, *rest = rest
    up_s, value_s, grad_s, high_part, left3, right3, total3, ss3, sr3, cot_sem, *rest = rest
    *rest, held_sem = rest
    near, rest = rest[-7:], rest[:-7]
    whole, cots, resid, hidden, d_up, d_gate, low_part = near
    plane = Plane() if rest else None
    w_up, w_gate, w_down = weights = rest[:3] if rest else shares

    def whole_of(weight):
        return weight[...].reshape(-1, weight.shape[-1])

    local = x.shape[0]
    line = Line(n, local, part, (left, right), whole, (ss, sr), (send, recv))
    back_line = Line(n, local, part2, (left, right), back, (ss2, sr2), (send2, recv2))
    early = cot_first.shape[1]
    later = pl.ds(early, cot.shape[1] - early)
    cot_line = Line(n, local, None, None, cots.at[:, later], None, (csend, crecv))
    high_line = Line(n, local, high_part, (left3, right3), None, (ss3, sr3), None)
    line.greet(plane)
    arriving = pltpu.make_async_copy(cot_first, cots.at[:, pl.ds(0, early)], cot_sem)
    arriving.start()
    gain_grad[...] = jnp.zeros_like(gain_grad)
    leaving = [
        pltpu.make_async_copy(source, target, held_sem.at[i])
        for i, (source, target) in enumerate(zip(near, far))
    ]

    def keep_cot(_, own, at):
        cots[at, later] = cot[own, later]

    def point(k):
        line.total(k, total)

        def one(here, own, at):
            v = x[own, :].astype(f32) + total[here, :]
            resid[own, :] = v
            whole[at, :] = (v * rms_scale(v) * gain[...]).astype(bf16)

        line.tiles(k, one)

    def back_point(k):
        back_line.total(k, total)

        def one(here, own, at):
            grad, terms = norm_back(resid[own, :], gain[...], total[here, :])
            gain_grad[...] += jnp.sum(terms, axis=0, keepdims=True)
            value = cot[own, :].astype(f32) + grad
            d_resid[own, :] = value
            back[at, :] = value.astype(bf16)

        line.tiles(k, one)

    def high_point(k):
        high_line.total(k, total3)
        first, rows = line.pieces[k]
        high_sum[pl.ds(first, rows), :] = total3[pl.ds(0, rows), :].astype(bf16)

    def pair_steps(j):
        first = line.pieces[2 * j][0]
        rows = line.pieces[2 * j][1] + line.pieces[2 * j + 1][1]
        at = [pl.ds(owner * local + first, rows) for owner in range(n)]
        here = pl.ds(0, n * rows)

        def read(array):
            return jnp.concatenate([array[rows_at, :] for rows_at in at], axis=0)

        def write(array, value):
            for owner, rows_at in enumerate(at):
                array[rows_at, :] = value[owner * rows : (owner + 1) * rows]

        def up():
            up_s[here, :] = dot(read(whole), whole_of(w_up))

        def gate():
            value, slope = gelu_both(dot(read(whole), whole_of(w_gate)))
            write(hidden, (value * up_s[here, :]).astype(bf16))
            value_s[here, :] = value
            up_s[here, :] = up_s[here, :] * slope

        def into_hidden():
            d_hidden = dot(read(cots), whole_of(w_down))
            write(d_up, (d_hidden * value_s[here, :]).astype(bf16))
            write(d_gate, (d_hidden * up_s[here, :]).astype(bf16))

        def through_up():
            grad_s[here, :] = dot_last(read(d_up), whole_of(w_up))

        def through_gate():
            write(part2, (grad_s[here, :] + dot_last(read(d_gate), whole_of(w_gate))).astype(bf16))

        def project():
            value = dot_last(read(hidden), whole_of(w_down)).astype(bf16)
            write(low_part, value[:, : value.shape[1] // 2])
            write(high_part, value[:, value.shape[1] // 2 :])

        return up, gate, into_hidden, through_up, through_gate, project

    hops = n - 1
    slots = [[] for _ in range(PIECES + 5 * hops)]

    def put(slot, order, work, *args):
        slots[slot].append((order, functools.partial(work, *args)))

    for k in range(PIECES):
        put(k, 0, line.first, k)
        for stage in range(1, hops):
            put(k + stage, 2, line.relay, k, stage)
        met = k + hops
        put(met, 3, line.sent, k)
        put(met, 3, point, k)
        put(met, 3, line.spread, k)
        given = k if 2 * k < PIECES else min(2 * k - PIECES // 2 + 1, PIECES + 2)
        put(given, 0, cot_line.tiles, k, keep_cot)
        put(given, 0, cot_line.spread, k)
        for stage in range(1, n):
            put(met + stage, 5, line.forward, k, stage)
            put(given + stage, 5, cot_line.forward, k, stage)
    for j in range(PIECES // 2):
        slot = 2 * j + 2 + 2 * hops
        steps = pair_steps(j)
        for at, order, step in zip((0, 0, 0, 1, 1, 1), (0.5, 1.5, 2.5, 0.5, 1.5, 3.5), steps):
            put(slot + at, order, step)
        for k in (2 * j, 2 * j + 1):
            begun = slot + 1 + k % 2
            put(begun, 2 if begun == slot + 1 else 0, back_line.first, k)
            for stage in range(1, hops):
                put(begun + stage, 2, back_line.relay, k, stage)
            put(begun + hops, 3, back_line.sent, k)
            put(begun + hops, 3, back_point, k)
            put(begun + hops, 3, back_line.spread, k)
            for stage in range(1, n):
                put(begun + hops + stage, 5, back_line.forward, k, stage)
            begun += 1
            put(begun, 4, high_line.first, k)
            for stage in range(1, hops):
                put(begun + stage, 4, high_line.relay, k, stage)
            put(begun + hops, 4, high_line.sent, k)
            put(begun + hops, 4, high_point, k)
    put(2 * hops + 2, 0, arriving.wait)
    done = PIECES + 2 * hops + 2
    for copy in leaving:
        put(done, 0, copy.start)
    if plane is not None:
        *plane_sems, wide_send, wide_recv, free = rest[3:]
        half_rows = shares[0].shape[0] // 2
        for share, array in zip(shares, weights):
            array[plane.me] = share[...]

        def weight_view(array):
            return lambda owner, half: array.at[owner, pl.ds(half * half_rows, half_rows)]

        items = [(weight_view(array), (0, 1)) for array in weights]
        stages = gather_tasks(plane, items, plane_sems)
        for slot, stage in zip((0, 3, 6, 2 * hops + 2), stages):
            put(slot, 0, stage)

        def leave_weights():
            for bit in plane.bits:
                pl.semaphore_signal(
                    free, inc=1, device_id={"dp": plane.other(bit)}, device_id_type=MESH
                )

        sent = []
        tokens = Here(whole)
        tasks, end = reduce_tasks(
            [
                Reduce(
                    i,
                    tokens,
                    Here(right),
                    slice(None),
                    sent,
                    *blocks_views(i, both, w_down),
                    out,
                    (wide_send, wide_recv),
                )
                for i, (right, both, out) in enumerate(
                    zip((d_up, d_gate), (w_up, w_gate), weight_grads)
                )
            ]
        )
        put(done - 1, 4, leave_weights)
        put(done, 0, pl.semaphore_wait, free, len(plane.bits))
        at = [(slot, order) for slot in range(done, len(slots)) for order in (0.5, 2.5, 3.5)]
        for (slot, order), task in zip(at, tasks):
            put(slot, order, task)
        rest_tasks = tasks[len(at) :]
    else:
        rest_tasks = []
    for slot in slots:
        for _, work in sorted(slot, key=lambda entry: entry[0]):
            work()
    for task in rest_tasks:
        task()
    for each in (line, back_line, cot_line):
        each.finish()
    if plane is not None:
        end()
    for copy in leaving:
        copy.wait()


def sum_back(n, x, d_resid, gain, part, *rest):
    if len(rest) > 6:
        little, gains, *rest = rest
        sources, rest = rest[:6], rest[6:]
        grad_x, *outs, little_out, gains_out = rest[:7]
        left, right, total, ss, sr, *reduce = rest[7:]
        wide, late_refs, late_sems = reduce[22:29], reduce[29:35], reduce[35]
        given = [
            Given(little, *reduce[7:11], little_out, reduce[11:13]),
            Given(gains, *reduce[13:17], gains_out, reduce[17:19]),
        ]
        met, met_send, met_recv = reduce[19:22]
    else:
        grad_x, left, right, total, ss, sr = rest
        sources = ()
    line = Line(n, x.shape[0], part, (left, right), None, (ss, sr), None)
    line.greet(Plane() if sources else None)

    def point(k):
        line.total(k, total)

        def one(here, own, at):
            back, _ = norm_back(x[own, :].astype(f32), gain[...], total[here, :])
            grad_x[own, :] = (d_resid[own, :] + back).astype(bf16)

        line.tiles(k, one)

    if not sources:
        line.run(point)
        return
    width = sources[5].shape[1]
    cots, hidden, norm, back_all, cat, mixed = late_all(sources, late_refs, late_sems)
    every, sent, sent_wide = slice(None), [], []
    wide_sides = ((cots, hidden, every),)
    sides = (
        (norm, cat, slice(0, width)),
        (norm, cat, slice(width, 2 * width)),
        (back_all, mixed, every),
    )
    parts = [
        Reduce(i, *side, sent_wide, *views(i, *wide[:5]), out, wide[5:7])
        for i, (side, out) in enumerate(zip(wide_sides, outs))
    ]
    parts += [
        Reduce(i, *side, sent, *views(i, *reduce[:5]), out, reduce[5:7])
        for i, (side, out) in enumerate(zip(sides, outs[1:]))
    ]
    tasks, finish = reduce_tasks(parts, given)

    me = lax.axis_index("mp")

    def meet(away):
        return pltpu.make_async_remote_copy(
            src_ref=gains_out,
            dst_ref=met.at[away - 1],
            send_sem=met_send.at[away - 1],
            recv_sem=met_recv.at[away - 1],
            device_id={"mp": lax.rem(me + away, n)},
            device_id_type=MESH,
        )

    def send_gains():
        for away in range(1, n):
            meet(away).start()

    def add_gains():
        for away in range(1, n):
            meet(away).wait()
        gains_out[...] += sum(met[away] for away in range(n - 1))

    tasks[7:7] = [send_gains]
    line.run(point, tasks)
    finish()
    add_gains()


def line_call(body, n, identity, outs, sums, alls, args, more=(), late=0, held=0):
    whole = pl.BlockSpec(memory_space=pltpu.VMEM)
    local, model = args[0].shape
    sem = pltpu.SemaphoreType.DMA((2, n, PIECES))
    scratch = []
    if sums:
        scratch += [pltpu.VMEM((n * local, model), bf16)] * 2
        scratch += [pltpu.VMEM((max(rows for _, rows in cut_rows(local, PIECES)), model), f32)]
        scratch += [sem, sem]
    if alls:
        scratch += [sem, sem]
    scratch += more
    if held:
        scratch += [pltpu.VMEM(o.shape, o.dtype) for o in outs[len(outs) - held :]]
        scratch += [pltpu.SemaphoreType.DMA((held,))]
    away = pl.BlockSpec(memory_space=pl.ANY)
    moved = sum(a.size * a.dtype.itemsize for a in args)
    return pl.pallas_call(
        functools.partial(body, n),
        out_shape=outs,
        in_specs=[whole] * (len(args) - late) + [away] * late,
        out_specs=[whole] * (len(outs) - held) + [away] * held,
        scratch_shapes=scratch,
        compiler_params=pltpu.CompilerParams(
            vmem_limit_bytes=VMEM_MB << 20, collective_id=identity, has_side_effects=True
        ),
        cost_estimate=pl.CostEstimate(flops=0, bytes_accessed=100 * moved, transcendentals=0),
    )(*args)


def finish(heads, piece, share, resid, low, high, gains, little, *rest):
    count = (len(rest) - 6) // 2
    sources, rest = rest[:count], rest[count:]
    output, grad_gains, grad_conv, grad_bias, grad_decay, grad_blocks, *targets = rest
    for source, target in zip(sources, targets):
        target[...] = source[...]
    half = low.shape[1]
    output[:, :half] = (resid[:, :half] + low[...].astype(f32)).astype(bf16)
    output[:, half:] = (resid[:, half:] + high[...].astype(f32)).astype(bf16)
    for position in range(gains.shape[0] // 2):

        @pl.when(lax.axis_index("mp") == position)
        def _():
            grad_gains[...] = gains[2 * position : 2 * position + 2, :share]

    for h in range(heads):
        for gate in range(2):
            first = (2 * h + gate) * LANE
            grad_blocks[gate, h] = little[:, first : first + LANE]
    first = 2 * heads * LANE
    lines = little[:, first : first + LANE]
    lines = jnp.concatenate([lines, jnp.zeros((LANE - piece, LANE), f32)], axis=0).T
    for h in range(heads):
        for k in range(SUB):
            row = lines[h * SUB + k : h * SUB + k + 1, :piece]
            if k < 4:
                grad_conv[k, h : h + 1, :] = row
            elif k < SUB - 1:
                grad_bias[k - 4, h : h + 1, :] = row
            else:
                grad_decay[h : h + 1, :] = row


def local_call(body, outs, scratch, flops, args, late=0, held=0):
    whole, away = pl.BlockSpec(memory_space=pltpu.VMEM), pl.BlockSpec(memory_space=pl.ANY)
    twins = list(args[len(args) - late :]) + list(outs[len(outs) - held :])
    scratch = scratch + [pltpu.VMEM(a.shape, a.dtype) for a in twins]
    if late:
        scratch.append(pltpu.SemaphoreType.DMA((late,)))
    if held:
        scratch.append(pltpu.SemaphoreType.DMA((held, 4)))
    moved = sum(a.size * a.dtype.itemsize for a in args)
    moved += sum(o.size * o.dtype.itemsize for o in outs)
    return pl.pallas_call(
        body,
        out_shape=outs,
        in_specs=[whole] * (len(args) - late) + [away] * late,
        out_specs=[whole] * (len(outs) - held) + [away] * held,
        scratch_shapes=scratch,
        compiler_params=pltpu.CompilerParams(vmem_limit_bytes=VMEM_MB << 20),
        cost_estimate=pl.CostEstimate(flops=flops, bytes_accessed=moved, transcendentals=0),
    )(*args)


def shape_of(dtype, *shape):
    return jax.ShapeDtypeStruct(shape, dtype)


def shards(
    inputs,
    cotangent,
    token_mask,
    order,
    lengths,
    gains,
    w_in,
    w_gate,
    w_out,
    conv_weight,
    chan_bias,
    decay,
    gate_blocks,
    w_up,
    w_gate_ff,
    w_down,
):
    n_dp = lax.axis_size("dp")
    local_rows, model = inputs.shape
    count = local_rows * lax.axis_size("mp")
    heads, piece = decay.shape
    width = heads * piece * n_dp
    hidden_width = w_up.shape[1]

    fused = n_dp == 8
    rows = model // n_dp
    out_rows, down_rows = w_out.T, w_down.T
    lines = jnp.concatenate([conv_weight, chan_bias, decay[None]], axis=0).transpose(1, 0, 2)
    lines = lines.reshape(SUB * heads, piece)

    steps = count // SUB
    ends = jnp.cumsum(lengths[0], dtype=jnp.int32)
    starts = ends - lengths[0]
    places = jnp.arange(count, dtype=jnp.int32)
    own_start = jnp.max(
        jnp.where(places[:, None] >= starts[None, :], starts[None, :], 0), axis=1
    )
    pos = (places - own_start).reshape(SUB, steps).T
    wrap = jnp.concatenate([pos[: TAIL // SUB, 1:], jnp.full((TAIL // SUB, 1), -1, jnp.int32)], axis=1)
    pos_col = jnp.concatenate([pos, wrap], axis=0).reshape(count + TAIL, 1)
    order_int = order[0].reshape(SUB, steps).T.reshape(count)
    ocol, orow = order_int.reshape(count, 1), order_int.reshape(1, count)

    gain_f = gains.astype(f32)
    n_mp = lax.axis_size("mp")
    tok = shape_of(bf16, count, model)
    own = shape_of(f32, local_rows, model)
    if fused:
        grown = shape_of(bf16, model, width)
        norm_group, full_in, full_gate, full_out, blocks, chan = line_call(
            gather_weights,
            n_mp,
            0,
            [tok, grown, grown, grown, shape_of(bf16, 2 * heads, LANE, LANE), shape_of(f32, 16, width)],
            False,
            True,
            (
                inputs,
                gain_f[0:1],
                w_in,
                w_gate,
                out_rows,
                gate_blocks.reshape(2 * heads, piece, LANE),
                jnp.pad(lines, ((0, 0), (0, LANE - piece))),
            ),
            [pltpu.VMEM((n_dp * SUB * heads, LANE), bf16)] + [pltpu.SemaphoreType.DMA((5, 2, 7))] * 2,
        )
    else:
        (norm_group,) = line_call(gather_norm, n_mp, 0, [tok], False, True, (inputs, gain_f[0:1]))
        full_in = lax.all_gather(w_in, "dp", axis=0, tiled=True)
        full_gate = lax.all_gather(w_gate, "dp", axis=0, tiled=True)
        full_out = lax.all_gather(out_rows, "dp", axis=0, tiled=True)
        blocks = lax.all_gather(gate_blocks, "dp", axis=2, tiled=True).reshape(2 * heads, LANE, LANE)
        params = lax.all_gather(lines, "dp", axis=1, tiled=True).astype(f32)
        params = params.reshape(heads, SUB, LANE).transpose(1, 0, 2).reshape(SUB, width)
        decay_row = params[7:8]
        chan = jnp.concatenate(
            [params[:7], jax.nn.softplus(decay_row)] + [jax.nn.sigmoid(decay_row)] * SUB, axis=0
        )
    cot = cotangent * token_mask.astype(bf16)[:, None]

    cot_first, norm_group = lax.optimization_barrier((cot[:, : model // 3], norm_group))
    cot_first = lax.all_gather(cot_first, "mp", axis=0, tiled=True)

    wide = pltpu.VMEM((count, width), f32)
    saved = [shape_of(f32, count, width)] * 6
    gate_pre, branch, conv, gate_in, gate_rec, state, mixed, back_part = local_call(
        mixer_forward,
        saved + [shape_of(bf16, count, width), shape_of(bf16, count, model)],
        [
            pltpu.VMEM((ROWS, model), bf16),
            wide,
            wide,
            pltpu.VMEM((ROWS + TAIL, width), f32),
            pltpu.VMEM((count, width), bf16),
        ],
        2 * count * (count * model + 3 * model * width),
        (norm_group, ocol, orow, pos_col, full_in, full_gate, chan, blocks, full_out),
        1,
        8,
    )
    shares = (w_up, w_gate_ff, down_rows)
    if not fused:
        shares = [lax.all_gather(share, "dp", axis=0, tiled=True) for share in shares]
    hid = shape_of(bf16, count, hidden_width)
    half = shape_of(bf16, count, model // 2)
    half_twin = pltpu.VMEM(half.shape, bf16)
    pieces = cut_rows(local_rows, PIECES)
    most = n_mp * max(pieces[k][1] + pieces[k + 1][1] for k in range(0, PIECES, 2))
    pair = pltpu.VMEM((most, hidden_width), f32)
    flow = pltpu.SemaphoreType.DMA((2, n_mp, PIECES))
    plane_scratch = [pltpu.VMEM((n_dp, rows, hidden_width), bf16)] * 3
    plane_scratch += [pltpu.SemaphoreType.DMA((3, 2, 7))] * 2 + [pltpu.SemaphoreType.DMA((2, 10))] * 2
    plane_scratch += [pltpu.SemaphoreType.REGULAR]
    (
        d_resid,
        gain_mid,
        back_group,
        ffn_high,
        *ffn_grads,
        norm_mid_group,
        cot_group,
        resid,
        hidden,
        d_up,
        d_gate_ff,
        ffn_part,
    ) = line_call(
        middle,
        n_mp,
        1,
        [own, shape_of(f32, 1, model), tok, shape_of(bf16, local_rows, model // 2)]
        + [shape_of(f32, rows, hidden_width)] * (2 * fused)
        + [tok, tok, own, hid, hid, hid, half],
        True,
        True,
        (inputs, gain_f[1:2], cot, back_part, *shares, cot_first),
        [pltpu.VMEM((count, model), bf16)]
        + [flow] * 6
        + [pair, pair, pltpu.VMEM((most, model), f32)]
        + [half_twin] * 3
        + [pltpu.VMEM((max(rows for _, rows in pieces), model // 2), f32), flow, flow]
        + [pltpu.SemaphoreType.DMA(())]
        + plane_scratch * fused,
        late=1,
        held=7,
    )

    def reduced(left, right):
        grad = dot_first(left, right).astype(bf16)
        return lax.psum_scatter(grad, "dp", scatter_dimension=0, tiled=True).astype(f32)

    d_cat, d_norm_back, little, gain_in = local_call(
        mixer_backward,
        [
            shape_of(bf16, count, 2 * width),
            tok,
            shape_of(f32, LANE, 2 * width + LANE),
            shape_of(f32, 1, model),
        ],
        [
            pltpu.VMEM((count, width), bf16),
            wide,
            wide,
            wide,
            pltpu.VMEM((count + TAIL, width), f32),
            pltpu.VMEM((ROWS + TAIL, width), f32),
            pltpu.VMEM((count, 2 * width), bf16),
            pltpu.VMEM((SUB, width), f32),
            pltpu.VMEM((heads, LANE, 2 * LANE), f32),
        ],
        2 * count * (3 * count * width + 3 * model * width),
        (
            back_group,
            full_out,
            ocol,
            orow,
            pos_col,
            gain_f[0:1],
            chan,
            blocks,
            gate_pre,
            gate_rec,
            state,
            conv,
            gate_in,
            branch,
            norm_group,
            full_in,
            full_gate,
        ),
        9,
    )
    share = model // (n_dp * n_mp)
    gain_parts = jnp.concatenate([gain_in, gain_mid], axis=0).reshape(2, n_dp, n_mp, share)
    gain_parts = gain_parts.transpose(1, 2, 0, 3).reshape(n_dp, 2 * n_mp, share)
    gain_parts = jnp.pad(gain_parts, ((0, 0), (0, 2 * SUB - 2 * n_mp), (0, LANE - share)))
    gain_parts = gain_parts.reshape(2 * SUB * n_dp, LANE)
    ffn_low = lax.psum_scatter(ffn_part, "mp", scatter_dimension=0, tiled=True)
    ffn_low, d_norm_back = lax.optimization_barrier((ffn_low, d_norm_back))
    grad_inputs, *mix_grads = line_call(
        sum_back,
        n_mp,
        3,
        [shape_of(bf16, local_rows, model)]
        + (
            [shape_of(f32, rows, hidden_width)]
            + [shape_of(f32, rows, width)] * 3
            + [shape_of(f32, piece, little.shape[1]), shape_of(f32, 2 * SUB, LANE)]
        )
        * fused,
        True,
        False,
        (inputs, d_resid, gain_f[0:1], d_norm_back)
        + (
            (
                little,
                gain_parts,
                cot_group,
                hidden,
                norm_group,
                back_group,
                d_cat,
                mixed,
            )
            if fused
            else ()
        ),
        reduce_scratch(3, rows, width)
        + given_scratch(piece, little.shape[1])
        + given_scratch(2 * SUB, LANE)
        + [pltpu.VMEM((n_mp - 1, 2 * SUB, LANE), f32)]
        + [pltpu.SemaphoreType.DMA((n_mp - 1,))] * 2
        + reduce_scratch(1, rows, hidden_width)
        + [pltpu.VMEM(a.shape, a.dtype) for a in (cot_group, hidden, norm_group, back_group, d_cat, mixed)]
        + [pltpu.SemaphoreType.DMA((6,))]
        if fused
        else (),
        6 * fused,
    )
    if fused:
        up_grad, gate_ff_grad = ffn_grads
        down_grad, *mix_grads, little_own, gain_own = mix_grads
    else:
        up_grad = reduced(norm_mid_group, d_up)
        gate_ff_grad = reduced(norm_mid_group, d_gate_ff)
        down_grad = reduced(cot_group, hidden)
        mix_grads = [
            reduced(norm_group, d_cat[:, :width]),
            reduced(norm_group, d_cat[:, width:]),
            reduced(back_group, mixed),
        ]
        little_own = lax.psum_scatter(little, "dp", scatter_dimension=0, tiled=True)
        gain_own = lax.psum(lax.psum_scatter(gain_parts, "dp", scatter_dimension=0, tiled=True), "mp")
    outs = [
        shape_of(bf16, local_rows, model),
        shape_of(f32, 2, share),
        shape_of(f32, 4, heads, piece),
        shape_of(f32, 3, heads, piece),
        shape_of(f32, heads, piece),
        shape_of(f32, 2, heads, piece, LANE),
    ]
    copied = [grad_inputs, mix_grads[0], mix_grads[1], up_grad, gate_ff_grad] if fused else []
    output, grad_gains, grad_conv, grad_bias, grad_decay, grad_blocks, *copied = local_call(
        functools.partial(finish, heads, piece, share),
        outs + [shape_of(a.dtype, *a.shape) for a in copied],
        [],
        0,
        (resid, ffn_low, ffn_high, gain_own, little_own, *copied),
    )
    if fused:
        grad_inputs, grad_in, grad_gate, up_grad, gate_ff_grad = copied
    else:
        grad_in, grad_gate, _ = mix_grads
    return (
        output,
        grad_inputs,
        grad_gains,
        grad_in,
        grad_gate,
        mix_grads[2].T,
        grad_conv,
        grad_bias,
        grad_decay,
        grad_blocks,
        up_grad,
        gate_ff_grad,
        down_grad.T,
    )


def solution(mesh):
    row, col = P("dp", "mp"), P("mp", "dp")
    tok = P(("dp", "mp"), None)
    chan = P(None, "mp", "dp")
    gate = P(None, "mp", "dp", None)
    return jax.shard_map(
        shards,
        mesh=mesh,
        in_specs=(
            tok, tok, P(("dp", "mp")), P("dp", None), P("dp", None), P(),
            row, row, col, chan, chan, col, gate, row, row, col,
        ),
        out_specs=(
            tok, tok, P(None, ("dp", "mp")), row, row, col, chan, chan, col, gate, row, row, col,
        ),
        check_vma=False,
    )
```

```python
import functools

import jax
import jax.numpy as jnp
from jax import lax
from jax.experimental import pallas as pl
from jax.experimental.pallas import tpu as pltpu
from jax.sharding import PartitionSpec as P

epsilon = 1e-06
LANE = 128
SUB = 8
TAIL = 24
ROWS = 272
VMEM_MB = 62
f32 = jnp.float32
bf16 = jnp.bfloat16
GELU_C = 0.7978845608028654
GELU_A = 0.044715


def rms_scale(values):
    return lax.rsqrt(jnp.mean(values * values, axis=-1, keepdims=True) + epsilon)


def dot(left, right):
    return lax.dot_general(left, right, (((1,), (0,)), ((), ())), preferred_element_type=f32)


def dot_last(left, right):
    return lax.dot_general(left, right, (((1,), (1,)), ((), ())), preferred_element_type=f32)


def dot_first(left, right):
    return lax.dot_general(left, right, (((0,), (0,)), ((), ())), preferred_element_type=f32)


def gelu_of(v):
    return 0.5 * v * (1.0 + jnp.tanh(GELU_C * (v + GELU_A * v * v * v)))


def gelu_both(v):
    square = v * v
    th = jnp.tanh(GELU_C * (v + GELU_A * v * square))
    half = 0.5 * (1.0 + th)
    slope = half + 0.5 * v * (1.0 - th * th) * (GELU_C * (1.0 + 3.0 * GELU_A * square))
    return v * half, slope


def sigmoid(v):
    return 0.5 * jnp.tanh(0.5 * v) + 0.5


def split(values):
    high = values.astype(bf16)
    return high, (values - high.astype(f32)).astype(bf16)


def rows_of(index, rows):
    return pl.ds(pl.multiple_of(index * rows, rows), rows)


def pick_rows(order_col, count):
    places = lax.broadcasted_iota(jnp.int32, (order_col.shape[0], count), 1)
    return (places == order_col).astype(f32).astype(bf16)


def put_rows(order_row, first, rows):
    places = lax.broadcasted_iota(jnp.int32, (rows, order_row.shape[1]), 0) + first
    return (places == order_row).astype(f32).astype(bf16)


def mixer_forward(tokens, ocol, orow, pos, w_in, w_gate, chan, blocks, w_out_far, *rest):
    far, rest = rest[:8], rest[8:]
    packed, rate, prod, before, low, w_out, *near, late_sem, held_sem = rest
    gate_ref, branch_ref, conv_ref, gin_ref, grec_ref, state_ref, mixed_ref, out_ref = near
    (late_out,) = late_all([w_out_far], [w_out], late_sem)
    leaving = [
        pltpu.make_async_copy(source, target, held_sem.at[i, 0])
        for i, (source, target) in enumerate(zip(near, far))
    ]
    count, _ = tokens.shape
    width = w_in.shape[1]
    steps = count // SUB
    heads = width // LANE

    def project(b, carry):
        at = rows_of(b, ROWS)
        packed[...] = dot(pick_rows(ocol[at, :], count), tokens[...]).astype(bf16)
        branch_ref[at, :] = dot(packed[...], w_in[...])
        gate_ref[at, :] = dot(packed[...], w_gate[...])
        return carry

    lax.fori_loop(0, count // ROWS, project, 0)
    leaving[0].start()
    leaving[1].start()

    for k in range(TAIL // SUB):
        last = branch_ref[pl.ds(count - TAIL + k * SUB, SUB), :]
        before[pl.ds(k * SUB, SUB), :] = pltpu.roll(last, 1, 0)
    before[pl.ds(TAIL, ROWS), :] = branch_ref[pl.ds(0, ROWS), :]

    def gates(b, carry):
        at = rows_of(b, ROWS)

        @pl.when(b > 0)
        def _():
            before[...] = branch_ref[pl.ds(pl.multiple_of(b * ROWS - TAIL, SUB), ROWS + TAIL), :]

        place = pos[at, :]
        for h in range(heads):
            lanes = pl.ds(h * LANE, LANE)
            par = chan[:, lanes]
            conv = par[4:5] + par[0:1] * before[pl.ds(TAIL, ROWS), lanes]
            for k in range(1, 4):
                earlier = before[pl.ds(TAIL - SUB * k, ROWS), lanes]
                conv = conv + par[k : k + 1] * jnp.where(place >= k, earlier, 0.0)
            high, rest = split(conv)
            pair = jnp.concatenate([blocks[h], blocks[heads + h]], axis=1)
            pre = dot(
                jnp.concatenate([high, rest], axis=1), jnp.concatenate([pair, pair], axis=0)
            )
            gate_in = sigmoid(pre[:, :LANE] + par[5:6])
            gate_rec = sigmoid(pre[:, LANE:] + par[6:7])
            kept = jnp.exp(-8.0 * gate_rec * par[7:8])
            drive = jnp.sqrt(1.0 - kept * kept + 0.01) * gate_in * conv
            conv_ref[at, lanes] = conv
            gin_ref[at, lanes] = gate_in
            grec_ref[at, lanes] = gate_rec
            rate[at, lanes] = jnp.where(place >= 1, kept, 0.0)
            state_ref[at, lanes] = drive
        return carry

    lax.fori_loop(0, count // ROWS, gates, 0)
    for copy in leaving[2:5]:
        copy.start()

    def scan(i, carry):
        held, passed = carry
        at = rows_of(i, SUB)
        a = rate[at, :]
        held = a * held + state_ref[at, :]
        passed = a * passed
        state_ref[at, :] = held
        prod[at, :] = passed
        return held, passed

    ends = lax.fori_loop(
        0, steps, scan, (jnp.zeros((SUB, width), f32), jnp.ones((SUB, width), f32)), unroll=8
    )
    first = lax.broadcasted_iota(jnp.int32, (SUB, width), 0) == 0
    carry_in = jnp.zeros((SUB, width), f32)
    for _ in range(SUB - 1):
        carry_in = jnp.where(first, 0.0, pltpu.roll(ends[0] + ends[1] * carry_in, 1, 0))

    def finish(i, carry):
        at = rows_of(i, 2 * SUB)
        twice = jnp.concatenate([carry_in, carry_in], axis=0)
        value = state_ref[at, :] + prod[at, :] * twice
        state_ref[at, :] = value
        low[at, :] = (gelu_of(gate_ref[at, :]) * value).astype(bf16)
        return carry

    lax.fori_loop(0, steps // 2, finish, 0, unroll=2)
    leaving[5].start()
    late_out.ready()

    def leave(b, carry):
        at = rows_of(b, ROWS)
        mixed = dot(put_rows(orow[...], b * ROWS, ROWS), low[...]).astype(bf16)
        mixed_ref[at, :] = mixed
        out_ref[at, :] = dot_last(mixed, w_out[...]).astype(bf16)
        return carry

    lax.fori_loop(0, count // ROWS, leave, 0)
    for copy in leaving[6:]:
        copy.start()
    for copy in leaving:
        copy.wait()


def mixer_backward(back, w_out, ocol, orow, pos, gain, chan, blocks, *rest):
    more = 2 if len(rest) > 36 else 0
    far, rest = rest[: 9 + more], rest[9 + more :]
    (dcat_ref, dnorm_ref, little_ref, dgain_ref), rest = rest[:4], rest[4:]
    passed_on, rest = rest[:more], rest[more:]
    dmix_arr, dmix, adj, prod, after, before, low, small_ref, dblocks_ref, *rest = rest
    gate_ref, grec_ref, state_ref, conv_ref, gin_ref, branch_ref, norm, w_in, w_gate, *extra = rest[: 9 + more]
    late_sem = rest[9 + 2 * more]
    late = late_all(far, rest[: 9 + more], late_sem)
    leaving = [
        pltpu.make_async_copy(source, target, rest[-1].at[i, 0])
        for i, (source, target) in enumerate(zip(extra, passed_on))
    ]
    count, _ = back.shape
    width = w_in.shape[1]
    steps = count // SUB
    heads = width // LANE
    blocks_of = count // ROWS

    def enter(b, carry):
        at = rows_of(b, ROWS)
        dmix_arr[at, :] = dot(back[at, :], w_out[...]).astype(bf16)
        return carry

    lax.fori_loop(0, blocks_of, enter, 0)
    for array in late[:3]:
        array.ready()

    def pack(b, carry):
        at = rows_of(b, ROWS)
        d_mixed = dot(pick_rows(ocol[at, :], count), dmix_arr[...])
        value, slope = gelu_both(gate_ref[at, :])
        adj[at, :] = d_mixed * value
        low[at, pl.ds(width, width)] = (d_mixed * state_ref[at, :] * slope).astype(bf16)
        kept = jnp.exp(-8.0 * grec_ref[at, :] * chan[7:8, :])
        dmix[at, :] = jnp.where(pos[at, :] >= 1, kept, 0.0)
        return carry

    lax.fori_loop(0, blocks_of, pack, 0)
    for array in late:
        array.ready()
    for copy in leaving:
        copy.start()

    def scan(i, carry):
        held, passed, following = carry
        at = rows_of(steps - 1 - i, SUB)
        held = following * held + adj[at, :]
        passed = following * passed
        adj[at, :] = held
        prod[at, :] = passed
        return held, passed, dmix[at, :]

    last = lax.broadcasted_iota(jnp.int32, (SUB, width), 0) == SUB - 1
    wrapped = jnp.where(last, 0.0, pltpu.roll(dmix[pl.ds(0, SUB), :], SUB - 1, 0))
    ends = lax.fori_loop(
        0,
        steps,
        scan,
        (jnp.zeros((SUB, width), f32), jnp.ones((SUB, width), f32), wrapped),
        unroll=8,
    )
    carry_in = jnp.zeros((SUB, width), f32)
    for _ in range(SUB - 1):
        carry_in = jnp.where(last, 0.0, pltpu.roll(ends[0] + ends[1] * carry_in, SUB - 1, 0))

    small_ref[...] = jnp.zeros_like(small_ref)
    dblocks_ref[...] = jnp.zeros_like(dblocks_ref)
    first = lax.broadcasted_iota(jnp.int32, (SUB, width), 0) == 0
    state_last = state_ref[pl.ds(count - SUB, SUB), :]
    before[pl.ds(TAIL - SUB, SUB), :] = jnp.where(first, 0.0, pltpu.roll(state_last, 1, 0))
    before[pl.ds(TAIL, ROWS), :] = state_ref[pl.ds(0, ROWS), :]
    wide_carry = jnp.concatenate([carry_in] * (ROWS // SUB), axis=0)

    def point(b, carry):
        at = rows_of(b, ROWS)

        @pl.when(b > 0)
        def _():
            before[...] = state_ref[pl.ds(pl.multiple_of(b * ROWS - TAIL, SUB), ROWS + TAIL), :]

        place = pos[at, :]
        for h in range(heads):
            lanes = pl.ds(h * LANE, LANE)
            par = chan[:, lanes]
            adjoint = adj[at, lanes] + prod[at, lanes] * wide_carry[:, h * LANE : (h + 1) * LANE]
            conv = conv_ref[at, lanes]
            gate_in = gin_ref[at, lanes]
            gate_rec = grec_ref[at, lanes]
            kept = jnp.exp(-8.0 * gate_rec * par[7:8])
            square = kept * kept
            inside = 1.0 - square + 0.01
            inverse = lax.rsqrt(inside)
            root = inside * inverse
            previous = before[pl.ds(TAIL - SUB, ROWS), lanes]
            d_log = adjoint * previous * dmix[at, lanes]
            scaled = adjoint * gate_in
            d_log = d_log - scaled * conv * square * inverse
            d_in = adjoint * root * conv * gate_in * (1.0 - gate_in)
            d_rec = d_log * (-8.0 * par[7:8]) * gate_rec * (1.0 - gate_rec)
            both = jnp.concatenate([d_in, d_rec], axis=1)
            high, rest = split(both)
            pair = jnp.concatenate([blocks[h], blocks[heads + h]], axis=1)
            d_conv = scaled * root + dot_last(high, pair) + dot_last(rest, pair)
            dblocks_ref[h] += dot_first(conv.astype(bf16), high)
            after[at, lanes] = d_conv
            small_ref[4:5, lanes] += jnp.sum(d_conv, axis=0, keepdims=True)
            small_ref[5:6, lanes] += jnp.sum(d_in, axis=0, keepdims=True)
            small_ref[6:7, lanes] += jnp.sum(d_rec, axis=0, keepdims=True)
            small_ref[7:8, lanes] += (
                jnp.sum(d_log * gate_rec, axis=0, keepdims=True) * (-8.0) * par[8:9]
            )
        return carry

    lax.fori_loop(0, blocks_of, point, 0)

    for k in range(TAIL // SUB):
        head = after[pl.ds(k * SUB, SUB), :]
        after[pl.ds(count + k * SUB, SUB), :] = pltpu.roll(head, SUB - 1, 0)
        tail = branch_ref[pl.ds(count - TAIL + k * SUB, SUB), :]
        before[pl.ds(k * SUB, SUB), :] = pltpu.roll(tail, 1, 0)
    before[pl.ds(TAIL, ROWS), :] = branch_ref[pl.ds(0, ROWS), :]

    def unmix(b, carry):
        at = rows_of(b, ROWS)

        @pl.when(b > 0)
        def _():
            before[...] = branch_ref[pl.ds(pl.multiple_of(b * ROWS - TAIL, SUB), ROWS + TAIL), :]

        place = pos[at, :]
        for h in range(heads):
            lanes = pl.ds(h * LANE, LANE)
            par = chan[:, lanes]
            d_conv = after[at, lanes]
            d_branch = par[0:1] * d_conv
            small_ref[0:1, lanes] += jnp.sum(
                d_conv * before[pl.ds(TAIL, ROWS), lanes], axis=0, keepdims=True
            )
            for k in range(1, 4):
                later = pl.ds(pl.multiple_of(b * ROWS + SUB * k, SUB), ROWS)
                d_branch = d_branch + par[k : k + 1] * jnp.where(
                    pos[later, :] >= k, after[later, lanes], 0.0
                )
                earlier = before[pl.ds(TAIL - SUB * k, ROWS), lanes]
                small_ref[k : k + 1, lanes] += jnp.sum(
                    jnp.where(place >= k, d_conv * earlier, 0.0), axis=0, keepdims=True
                )
            low[at, lanes] = d_branch.astype(bf16)
        return carry

    lax.fori_loop(0, blocks_of, unmix, 0)
    lines = [small_ref[0:SUB, h * LANE : (h + 1) * LANE] for h in range(heads)]
    lines.append(jnp.zeros((LANE - SUB * heads, LANE), f32))
    little_ref[:, pl.ds(2 * width, LANE)] = jnp.concatenate(lines, axis=0).T
    for h in range(heads):
        little_ref[:, pl.ds(2 * h * LANE, 2 * LANE)] = dblocks_ref[h]
    dgain_ref[...] = jnp.zeros_like(dgain_ref)

    def leave(b, carry):
        at = rows_of(b, ROWS)
        cat = dot(put_rows(orow[...], b * ROWS, ROWS), low[...]).astype(bf16)
        dcat_ref[at, :] = cat
        d_norm = dot_last(cat[:, :width], w_in[...]) + dot_last(cat[:, width:], w_gate[...])
        dgain_ref[...] += jnp.sum(d_norm * norm[at, :].astype(f32), axis=0, keepdims=True)
        dnorm_ref[at, :] = d_norm.astype(bf16)
        return carry

    lax.fori_loop(0, blocks_of, leave, 0)
    dgain_ref[...] = dgain_ref[...] / gain[...]
    for copy in leaving:
        copy.wait()


MESH = pl.DeviceIdType.MESH
TILE = 16
PIECES = 8
HOP = 1
AFTER = 1


def cut_rows(rows, parts):
    tiles = rows // TILE
    ends = [tiles * (k + 1) // parts for k in range(parts)]
    return [(TILE * a, TILE * (b - a)) for a, b in zip([0] + ends[:-1], ends)]


class Line:
    def __init__(self, n, local, part, arrived, whole, sums, alls):
        self.n, self.local, self.part, self.arrived, self.whole = n, local, part, arrived, whole
        self.sums, self.alls = sums, alls
        self.me = lax.axis_index("mp")
        self.pieces = cut_rows(local, PIECES)
        self.has = (self.me > 0, self.me < n - 1)

    def greet(self, plane=None):
        barrier = pltpu.get_barrier_semaphore()
        more = 0
        if plane is not None:
            for bit in plane.bits:
                more += 1
                pl.semaphore_signal(
                    barrier, inc=1, device_id={"dp": plane.other(bit)}, device_id_type=MESH
                )
        for away in range(1, self.n):
            more += 1
            pl.semaphore_signal(
                barrier,
                inc=1,
                device_id={"mp": lax.rem(self.me + away, self.n)},
                device_id_type=MESH,
            )
        pl.semaphore_wait(barrier, more)

    def rows_at(self, owner, k):
        first, rows = self.pieces[k]
        return pl.ds(pl.multiple_of(owner * self.local + first, TILE), rows)

    def copy(self, source, target, sems, way, owner, k):
        return pltpu.make_async_remote_copy(
            src_ref=source,
            dst_ref=target,
            send_sem=sems[0].at[way, owner, k],
            recv_sem=sems[1].at[way, owner, k],
            device_id={"mp": self.me + 1 - 2 * way},
            device_id_type=MESH,
        )

    def sum_copy(self, way, owner, k, first=False):
        at = self.rows_at(owner, k)
        landed = self.arrived[way].at[at]
        return self.copy(self.part.at[at] if first else landed, landed, self.sums, way, owner, k)

    def all_copy(self, way, owner, k):
        block = self.whole.at[self.rows_at(owner, k)]
        return self.copy(block, block, self.alls, way, owner, k)

    def first(self, k):
        for away in range(self.n - 1):
            for way in range(2):
                owner = away if way else self.n - 1 - away

                @pl.when(jnp.logical_not(self.has[way]))
                def _():
                    self.sum_copy(way, owner, k, True).start()

    def relay(self, k, stage):
        for way in range(2):
            late = stage - (self.n - 1 - self.me if way else self.me)
            owner = late if way else self.n - 1 - late

            @pl.when(self.has[way] & (late >= 0))
            def _():
                self.sum_copy(way, owner, k).wait_recv()
                at = self.rows_at(owner, k)
                landed = self.arrived[way]
                landed[at, :] = (landed[at, :].astype(f32) + self.part[at, :].astype(f32)).astype(bf16)
                self.sum_copy(way, owner, k).start()

    def total(self, k, into):
        at = self.rows_at(self.me, k)
        rows = pl.ds(0, self.pieces[k][1])
        into[rows, :] = self.part[at, :].astype(f32)
        for way in range(2):

            @pl.when(self.has[way])
            def _():
                self.sum_copy(way, self.me, k).wait_recv()
                into[rows, :] += self.arrived[way][at, :].astype(f32)

    def spread(self, k):
        for way in range(2):

            @pl.when(self.has[1 - way])
            def _():
                self.all_copy(way, self.me, k).start()

    def forward(self, k, stage):
        for way in range(2):
            owner = self.me + stage if way else self.me - stage
            there = owner < self.n if way else owner >= 0

            @pl.when(there)
            def _():
                self.all_copy(way, owner, k).wait_recv()

            @pl.when(there & self.has[1 - way])
            def _():
                self.all_copy(way, owner, k).start()

    def sent(self, k):
        for owner in range(self.n):
            for way in range(2):

                @pl.when(self.me > owner if way else self.me < owner)
                def _():
                    self.sum_copy(way, owner, k).wait_send()

    def finish(self):
        for k in range(PIECES):
            for owner in range(self.n):
                for way in range(2):
                    if self.whole is not None:
                        reached = self.me <= owner if way else self.me >= owner

                        @pl.when(reached & self.has[1 - way])
                        def _():
                            self.all_copy(way, owner, k).wait_send()

    def run(self, point, tasks=()):
        sums, alls = self.part is not None, self.whole is not None
        slots = [[] for _ in range(PIECES + (HOP + AFTER) * (self.n - 1) + 1)]
        for k in range(PIECES):
            done = k + HOP * (self.n - 1) if sums else 0
            if sums:
                slots[k].append((0, functools.partial(self.first, k)))
                for stage in range(1, self.n - 1):
                    slots[k + HOP * stage].append((2, functools.partial(self.relay, k, stage)))
                slots[done].append((3, functools.partial(self.sent, k)))
            slots[done].append((3, functools.partial(point, k)))
            if alls:
                slots[done].append((4, functools.partial(self.spread, k)))
                for stage in range(1, self.n):
                    at = (done if sums else k) + AFTER * stage
                    slots[at].append((1, functools.partial(self.forward, k, stage)))
        tasks = iter(tasks)
        for slot in slots:
            for step, (_, work) in enumerate(sorted(slot, key=lambda entry: entry[0])):
                if step in (0, 1, 3):
                    next(tasks, idle)()
                work()
        for task in tasks:
            task()
        self.finish()

    def tiles(self, k, body):
        first, rows = self.pieces[k]

        def one(i, carry):
            body(
                pl.ds(pl.multiple_of(i * TILE, TILE), TILE),
                pl.ds(pl.multiple_of(first + i * TILE, TILE), TILE),
                pl.ds(pl.multiple_of(self.me * self.local + first + i * TILE, TILE), TILE),
            )
            return carry

        lax.fori_loop(0, rows // TILE, one, 0)


def idle():
    pass


class Late:
    def __init__(self, source, ref, sem):
        self.ref = ref
        self.copy = pltpu.make_async_copy(source, ref, sem)
        self.pending = True

    def begin(self):
        self.copy.start()

    def ready(self):
        if self.pending:
            self.copy.wait()
        self.pending = False


class Here:
    def __init__(self, ref):
        self.ref = ref

    def ready(self):
        pass


def late_all(sources, refs, sems):
    arrays = [Late(source, ref, sems.at[i]) for i, (source, ref) in enumerate(zip(sources, refs))]
    for array in arrays:
        array.begin()
    return arrays


class Plane:
    bits = (1, 2, 4)
    orders = ((4, 2, 1), (2, 4, 1))

    def __init__(self):
        self.me = lax.axis_index("dp")

    def bit(self, bit):
        return lax.rem(self.me // bit, 2)

    def other(self, *bits):
        return self.me + sum(bit * (1 - 2 * self.bit(bit)) for bit in bits)

    def gather_copies(self, item, view, halves, stage, sems):
        copies = []
        for half in halves:
            order = self.orders[half]
            for combo in range(1 << stage):
                flipped = [bit for i, bit in enumerate(order[:stage]) if combo >> i & 1]
                block = view(self.other(*flipped), half)
                slot = (1 << stage) - 1 + combo
                copies.append(
                    pltpu.make_async_remote_copy(
                        src_ref=block,
                        dst_ref=block,
                        send_sem=sems[0].at[item, half, slot],
                        recv_sem=sems[1].at[item, half, slot],
                        device_id={"dp": self.other(order[stage])},
                        device_id_type=MESH,
                    )
                )
        return copies


class Reduce(Plane):
    def __init__(self, index, left, right, lanes, sent, mine, theirs, got, second, third, out, sems):
        super().__init__()
        self.sent, self.theirs = sent, theirs
        self.index, self.left, self.right, self.lanes = index, left, right, lanes
        self.mine, self.got = mine, got
        self.second, self.third, self.out = second, third, out
        self.sems = sems
        self.rows = out.shape[0]
        self.half = self.rows // 2

    def copy(self, source, target, slot, bit):
        return pltpu.make_async_remote_copy(
            src_ref=source,
            dst_ref=target,
            send_sem=self.sems[0].at[self.index, slot],
            recv_sem=self.sems[1].at[self.index, slot],
            device_id={"dp": self.other(bit)},
            device_id_type=MESH,
        )

    def core_copy(self, t):
        return self.copy(self.theirs.at[(4 * self.index + t) % 2], self.got.at[t], t, 1)

    def second_copy(self, half, j):
        x, y = self.bit(2), self.bit(4)
        block = (1 - y) * 2 + j if half else j * 2 + 1 - x
        rows = self.mine.at[block, pl.ds(half * self.half, self.half)]
        return self.copy(rows, self.second(half, j), 4 + 2 * half + j, 4 if half else 2)

    def third_block(self, half):
        x, y = self.bit(2), self.bit(4)
        return y * 2 + 1 - x if half else (1 - y) * 2 + x

    def third_copy(self, half):
        rows = self.mine.at[self.third_block(half), pl.ds(half * self.half, self.half)]
        return self.copy(rows, self.third(half), 8 + half, 2 if half else 4)

    def product(self, t):
        def task():
            core = self.bit(1)
            pair = pl.ds(t * 2 * self.rows, 2 * self.rows)
            if t == 0:
                self.left.ready()
                self.right.ready()
            if len(self.sent) > 1:
                self.sent[-2].wait_send()
            both = dot_first(self.left.ref[:, pair], self.right.ref[:, self.lanes])
            low, high = both[: self.rows], both[self.rows :]
            self.mine[t] = jnp.where(core == 0, low, high).astype(bf16)
            self.theirs[(4 * self.index + t) % 2] = jnp.where(core == 0, high, low).astype(bf16)
            self.sent.append(self.core_copy(t))
            self.sent[-1].start()

        return task

    def keep(self, t):
        return self.mine[t]

    def add_core(self):
        for t in range(4):
            self.core_copy(t).wait_recv()
            self.mine[t] = (self.keep(t).astype(f32) + self.got[t].astype(f32)).astype(self.mine.dtype)
        for half in range(2):
            for j in range(2):
                self.second_copy(half, j).start()

    def add_second(self):
        for half in range(2):
            for j in range(2):
                self.second_copy(half, j).wait_recv()
        for half in range(2):
            block, at = self.third_block(half), pl.ds(half * self.half, self.half)
            far = 1 - self.bit(2 if half else 4)
            self.mine[block, at] = (
                self.mine[block, at].astype(f32) + self.second(half, far)[...].astype(f32)
            ).astype(self.mine.dtype)
            self.third_copy(half).start()

    def add_third(self):
        own = self.bit(4) * 2 + self.bit(2)
        for half in range(2):
            self.third_copy(half).wait_recv()
            at = pl.ds(half * self.half, self.half)
            near = self.bit(2 if half else 4)
            self.out[at, :] = (
                self.mine[own, at].astype(f32)
                + self.second(half, near)[...].astype(f32)
                + self.third(half)[...].astype(f32)
            )

    def finish(self):
        for half in range(2):
            for j in range(2):
                self.second_copy(half, j).wait_send()
            self.third_copy(half).wait_send()


class Given(Reduce):
    def __init__(self, given, mine, got, second, third, out, sems):
        super().__init__(0, None, None, None, None, *views(0, mine, None, got, second, third), out, sems)
        self.given = given

    def rows_of(self, t, core):
        return pl.ds(pl.multiple_of((2 * t + core) * self.rows, self.rows), self.rows)

    def core_copy(self, t):
        return self.copy(self.given.at[self.rows_of(t, 1 - self.bit(1))], self.got.at[t], t, 1)

    def start(self):
        for t in range(4):
            self.core_copy(t).start()

    def finish(self):
        for t in range(4):
            self.core_copy(t).wait_send()
        super().finish()

    def keep(self, t):
        return self.given[self.rows_of(t, self.bit(1)), :]


def views(index, mine, theirs, got, second, third):
    return (
        mine.at[index],
        theirs,
        got.at[index],
        lambda half, j: second.at[index, half, j],
        lambda half: third.at[index, half],
    )


def blocks_views(index, both, spare):
    half_rows = spare.shape[1] // 2

    def halves(block, j):
        return spare.at[block, pl.ds(pl.multiple_of(j * half_rows, TILE), half_rows)]

    return (
        both.at[pl.ds(0, 4)],
        spare.at[pl.ds(6, 2)],
        both.at[pl.ds(4, 4)],
        lambda half, j: halves(3 * index + half, j),
        lambda half: halves(3 * index + 2, half),
    )


def reduce_tasks(parts, given=()):
    tasks = [part.product(t) for part in parts for t in range(4)]

    def also(at, extra):
        while len(tasks) <= at:
            tasks.append(idle)
        before = tasks[at]

        def both():
            extra()
            before()

        tasks[at] = both

    for i, part in enumerate(parts):
        also(4 * i + 5, part.add_core)
        also(4 * i + 8, part.add_second)
        also(4 * i + 10, part.add_third)

    for part in given:
        also(0, part.start)
        also(2, part.add_core)
        also(4, part.add_second)
        also(6, part.add_third)

    def finish():
        for ring in {id(part.sent): part.sent for part in parts}.values():
            for copy in ring[-2:]:
                copy.wait_send()
        for part in [*parts, *given]:
            part.finish()

    return tasks, finish


def given_scratch(rows, width):
    sem = pltpu.SemaphoreType.DMA((1, 10))
    return [
        pltpu.VMEM((1, 4, rows, width), f32),
        pltpu.VMEM((1, 4, rows, width), f32),
        pltpu.VMEM((1, 2, 2, rows // 2, width), f32),
        pltpu.VMEM((1, 2, rows // 2, width), f32),
        sem,
        sem,
    ]


def reduce_scratch(arrays, rows, width):
    block = pltpu.VMEM((arrays, 4, rows, width), bf16)
    sem = pltpu.SemaphoreType.DMA((arrays, 10))
    return [
        block,
        pltpu.VMEM((2, rows, width), bf16),
        block,
        pltpu.VMEM((arrays, 2, 2, rows // 2, width), bf16),
        pltpu.VMEM((arrays, 2, rows // 2, width), bf16),
        sem,
        sem,
    ]


def gather_norm(n, x, gain, whole, send, recv):
    line = Line(n, x.shape[0], None, None, whole, None, (send, recv))
    line.greet()

    def point(k):
        def one(_, own, at):
            v = x[own, :].astype(f32)
            whole[at, :] = (v * rms_scale(v) * gain[...]).astype(bf16)

        line.tiles(k, one)

    line.run(point)


def row_view(array, rows):
    def view(owner, half):
        first = owner * rows + half * (rows // 2)
        return array.at[pl.ds(pl.multiple_of(first, TILE), rows // 2)]

    return view


def gather_tasks(plane, items, sems):
    def copies(stage):
        return [
            copy
            for item, (view, halves) in enumerate(items)
            for copy in plane.gather_copies(item, view, halves, stage, sems)
        ]

    def stage_task(stage):
        def task():
            if stage:
                for copy in copies(stage - 1):
                    copy.wait_recv()
            for copy in copies(stage):
                copy.start()

        return task

    def last():
        for copy in copies(2):
            copy.wait_recv()
        for stage in range(3):
            for copy in copies(stage):
                copy.wait_send()

    return stage_task(0), stage_task(1), stage_task(2), last


def gather_weights(
    n,
    x,
    gain,
    w_in,
    w_gate,
    w_out,
    blocks,
    chan,
    order,
    lengths,
    whole,
    all_in,
    all_gate,
    all_out,
    all_blocks,
    all_chan,
    ocol,
    orow,
    pos,
    send,
    recv,
    raw,
    plane_send,
    plane_recv,
):
    line = Line(n, x.shape[0], None, None, whole, None, (send, recv))
    plane = Plane()
    line.greet(plane)
    sems = plane_send, plane_recv
    rows, piece = w_in.shape[0], blocks.shape[1]
    lines = chan.shape[0]

    def blocks_view(owner, half):
        return all_blocks.at[:, pl.ds(pl.multiple_of(owner * piece, TILE), piece)]

    def chan_view(owner, half):
        return raw.at[pl.ds(pl.multiple_of(owner * lines, TILE), lines)]

    items = [(row_view(array, rows), (0, 1)) for array in (all_in, all_gate, all_out)]
    items += [(blocks_view, (0,)), (chan_view, (1,))]

    first, second, third, finish = gather_tasks(plane, items, sems)

    def last():
        finish()
        lane = lax.broadcasted_iota(jnp.int32, (LANE, LANE), 1)
        row = lax.broadcasted_iota(jnp.int32, (LANE, LANE), 0)
        total = jnp.zeros((lines, LANE), f32)
        for owner in range(LANE // piece):
            moved = ((row < piece) & (row + owner * piece == lane)).astype(f32).astype(bf16)
            total = total + dot(raw[pl.ds(owner * lines, lines), :], moved)
        for h in range(lines // SUB):
            par = total[h * SUB : (h + 1) * SUB]
            lanes = pl.ds(h * LANE, LANE)
            all_chan[0:SUB, lanes] = par
            decay = par[SUB - 1 : SUB]
            small = jnp.exp(-jnp.abs(decay))
            one_more = 1.0 + small
            rest = jnp.where(one_more == 1.0, 1.0, one_more - 1.0)
            log_one_more = jnp.where(one_more == 1.0, small, jnp.log(one_more) * (small / rest))
            all_chan[SUB - 1 : SUB, lanes] = jnp.maximum(decay, 0.0) + log_one_more
            all_chan[SUB : 2 * SUB, lanes] = jnp.broadcast_to(sigmoid(decay), (SUB, LANE))

    own = pl.ds(pl.multiple_of(plane.me * rows, TILE), rows)
    all_in[own, :] = w_in[...]
    all_gate[own, :] = w_gate[...]
    all_out[own, :] = w_out[...]
    all_blocks[:, pl.ds(pl.multiple_of(plane.me * piece, TILE), piece), :] = blocks[...]
    raw[pl.ds(pl.multiple_of(plane.me * lines, TILE), lines), :] = chan[...]

    def point(k):
        def one(_, own, at):
            v = x[own, :].astype(f32)
            whole[at, :] = (v * rms_scale(v) * gain[...]).astype(bf16)

        line.tiles(k, one)

    def indices():
        count = whole.shape[0]
        steps = count // SUB
        tokens = order[...].astype(f32)
        across = lax.broadcasted_iota(jnp.int32, (ROWS, count), 1)
        line_total = jnp.zeros((1, count), f32)
        for b in range(count // ROWS):
            row = lax.broadcasted_iota(jnp.int32, (ROWS, 1), 0) + b * ROWS
            token = lax.rem(row, SUB) * steps + lax.div(row, SUB)
            picked = jnp.sum(jnp.where(across == token, tokens, 0.0), axis=1, keepdims=True)
            ocol[pl.ds(b * ROWS, ROWS), :] = picked.astype(jnp.int32)
            line_total += jnp.sum(jnp.where(across == row, picked, 0.0), axis=0, keepdims=True)
        orow[...] = line_total.astype(jnp.int32)
        row = lax.broadcasted_iota(jnp.int32, pos.shape, 0)
        token = lax.rem(row, SUB) * steps + lax.div(row, SUB)
        start, own_start = jnp.zeros((1, 1), jnp.int32), jnp.zeros(pos.shape, jnp.int32)
        for k in range(lengths.shape[1]):
            own_start = jnp.where(token >= start, start, own_start)
            start = start + lengths[:, k : k + 1]
        pos[...] = jnp.where(token >= count, -1, token - own_start)

    first()
    line.run(point, [idle] * 4 + [second, indices] + [idle] * 2 + [third] + [idle] * 3 + [last])


def norm_back(value, gain, grad):
    scale = rms_scale(value)
    e = gain * grad
    slope = scale * scale * scale * jnp.mean(value * e, axis=-1, keepdims=True)
    return scale * e - value * slope, grad * value * scale


def middle(n, x, gain, cot, part, *rest):
    (*shares, cot_first), rest = rest[:4], rest[4:]
    grads = len(rest) > 45 and 2 or 0
    (d_resid, gain_grad, back, high_sum), rest = rest[:4], rest[4:]
    weight_grads, far, rest = rest[:grads], rest[grads : grads + 7], rest[grads + 7 :]
    left, right, total, ss, sr, send, recv, part2, ss2, sr2, send2, recv2, csend, crecv, *rest = rest
    up_s, value_s, grad_s, high_part, left3, right3, total3, ss3, sr3, cot_sem, *rest = rest
    *rest, held_sem = rest
    near, rest = rest[-7:], rest[:-7]
    whole, cots, resid, hidden, d_up, d_gate, low_part = near
    plane = Plane() if rest else None
    w_up, w_gate, w_down = weights = rest[:3] if rest else shares

    def whole_of(weight):
        return weight[...].reshape(-1, weight.shape[-1])

    local = x.shape[0]
    line = Line(n, local, part, (left, right), whole, (ss, sr), (send, recv))
    back_line = Line(n, local, part2, (left, right), back, (ss2, sr2), (send2, recv2))
    early = cot_first.shape[1]
    later = pl.ds(early, cot.shape[1] - early)
    cot_line = Line(n, local, None, None, cots.at[:, later], None, (csend, crecv))
    high_line = Line(n, local, high_part, (left3, right3), None, (ss3, sr3), None)
    line.greet(plane)
    arriving = pltpu.make_async_copy(cot_first, cots.at[:, pl.ds(0, early)], cot_sem)
    arriving.start()
    gain_grad[...] = jnp.zeros_like(gain_grad)
    leaving = [
        pltpu.make_async_copy(source, target, held_sem.at[i])
        for i, (source, target) in enumerate(zip(near, far))
    ]

    def keep_cot(_, own, at):
        cots[at, later] = cot[own, later]

    def point(k):
        line.total(k, total)

        def one(here, own, at):
            v = x[own, :].astype(f32) + total[here, :]
            resid[own, :] = v
            whole[at, :] = (v * rms_scale(v) * gain[...]).astype(bf16)

        line.tiles(k, one)

    def back_point(k):
        back_line.total(k, total)

        def one(here, own, at):
            grad, terms = norm_back(resid[own, :], gain[...], total[here, :])
            gain_grad[...] += jnp.sum(terms, axis=0, keepdims=True)
            value = cot[own, :].astype(f32) + grad
            d_resid[own, :] = value
            back[at, :] = value.astype(bf16)

        line.tiles(k, one)

    def high_point(k):
        high_line.total(k, total3)
        first, rows = line.pieces[k]
        high_sum[pl.ds(first, rows), :] = total3[pl.ds(0, rows), :].astype(bf16)

    def pair_steps(j):
        first = line.pieces[2 * j][0]
        rows = line.pieces[2 * j][1] + line.pieces[2 * j + 1][1]
        at = [pl.ds(owner * local + first, rows) for owner in range(n)]
        here = pl.ds(0, n * rows)

        def read(array):
            return jnp.concatenate([array[rows_at, :] for rows_at in at], axis=0)

        def write(array, value):
            for owner, rows_at in enumerate(at):
                array[rows_at, :] = value[owner * rows : (owner + 1) * rows]

        def up():
            up_s[here, :] = dot(read(whole), whole_of(w_up))

        def gate():
            value, slope = gelu_both(dot(read(whole), whole_of(w_gate)))
            write(hidden, (value * up_s[here, :]).astype(bf16))
            value_s[here, :] = value
            up_s[here, :] = up_s[here, :] * slope

        def into_hidden():
            d_hidden = dot(read(cots), whole_of(w_down))
            write(d_up, (d_hidden * value_s[here, :]).astype(bf16))
            write(d_gate, (d_hidden * up_s[here, :]).astype(bf16))

        def through_up():
            grad_s[here, :] = dot_last(read(d_up), whole_of(w_up))

        def through_gate():
            write(part2, (grad_s[here, :] + dot_last(read(d_gate), whole_of(w_gate))).astype(bf16))

        def project():
            value = dot_last(read(hidden), whole_of(w_down)).astype(bf16)
            write(low_part, value[:, : low_part.shape[1]])
            write(high_part, value[:, low_part.shape[1] :])

        return up, gate, into_hidden, through_up, through_gate, project

    hops = n - 1
    slots = [[] for _ in range(PIECES + 5 * hops)]

    def put(slot, order, work, *args):
        slots[slot].append((order, functools.partial(work, *args)))

    for k in range(PIECES):
        put(k, 0, line.first, k)
        for stage in range(1, hops):
            put(k + stage, 2, line.relay, k, stage)
        met = k + hops
        put(met, 3, line.sent, k)
        put(met, 3, point, k)
        put(met, 3, line.spread, k)
        given = k if 2 * k < PIECES else min(2 * k - PIECES // 2 + 1, PIECES + 2)
        put(given, 0, cot_line.tiles, k, keep_cot)
        put(given, 0, cot_line.spread, k)
        for stage in range(1, n):
            put(met + stage, 5, line.forward, k, stage)
            put(given + stage, 5, cot_line.forward, k, stage)
    for j in range(PIECES // 2):
        slot = 2 * j + 2 + 2 * hops
        steps = pair_steps(j)
        for at, order, step in zip((0, 0, 0, 1, 1, 1), (0.5, 1.5, 2.5, 0.5, 1.5, 3.5), steps):
            put(slot + at, order, step)
        for k in (2 * j, 2 * j + 1):
            begun = slot + 1 + k % 2
            put(begun, 2 if begun == slot + 1 else 0, back_line.first, k)
            for stage in range(1, hops):
                put(begun + stage, 2, back_line.relay, k, stage)
            put(begun + hops, 3, back_line.sent, k)
            put(begun + hops, 3, back_point, k)
            put(begun + hops, 3, back_line.spread, k)
            for stage in range(1, n):
                put(begun + hops + stage, 5, back_line.forward, k, stage)
            begun += 1
            put(begun, 4, high_line.first, k)
            for stage in range(1, hops):
                put(begun + stage, 4, high_line.relay, k, stage)
            put(begun + hops, 4, high_line.sent, k)
            put(begun + hops, 4, high_point, k)
    put(2 * hops + 2, 0, arriving.wait)
    done = PIECES + 2 * hops + 2
    for copy in leaving:
        put(done, 0, copy.start)
    if plane is not None:
        *plane_sems, wide_send, wide_recv, free = rest[3:]
        half_rows = shares[0].shape[0] // 2
        for share, array in zip(shares, weights):
            array[plane.me] = share[...]

        def weight_view(array):
            return lambda owner, half: array.at[owner, pl.ds(half * half_rows, half_rows)]

        items = [(weight_view(array), (0, 1)) for array in weights]
        stages = gather_tasks(plane, items, plane_sems)
        for slot, stage in zip((0, 3, 6, 2 * hops + 2), stages):
            put(slot, 0, stage)

        def leave_weights():
            for bit in plane.bits:
                pl.semaphore_signal(
                    free, inc=1, device_id={"dp": plane.other(bit)}, device_id_type=MESH
                )

        sent = []
        tokens = Here(whole)
        tasks, end = reduce_tasks(
            [
                Reduce(
                    i,
                    tokens,
                    Here(right),
                    slice(None),
                    sent,
                    *blocks_views(i, both, w_down),
                    out,
                    (wide_send, wide_recv),
                )
                for i, (right, both, out) in enumerate(
                    zip((d_up, d_gate), (w_up, w_gate), weight_grads)
                )
            ]
        )
        put(done - 1, 4, leave_weights)
        put(done, 0, pl.semaphore_wait, free, len(plane.bits))
        at = [(slot, order) for slot in range(done, len(slots)) for order in (0.5, 2.5, 3.5)]
        for (slot, order), task in zip(at, tasks):
            put(slot, order, task)
        rest_tasks = tasks[len(at) :]
    else:
        rest_tasks = []
    for slot in slots:
        for _, work in sorted(slot, key=lambda entry: entry[0]):
            work()
    for task in rest_tasks:
        task()
    for each in (line, back_line, cot_line):
        each.finish()
    if plane is not None:
        end()
    for copy in leaving:
        copy.wait()


def sum_back(n, x, d_resid, gain, part, *rest):
    if len(rest) > 6:
        little, gains, *rest = rest
        sources, rest = rest[:6], rest[6:]
        grad_x, *outs, little_out, gains_out = rest[:7]
        left, right, total, ss, sr, *reduce = rest[7:]
        wide, late_refs, late_sems = reduce[22:29], reduce[29:35], reduce[35]
        given = [
            Given(little, *reduce[7:11], little_out, reduce[11:13]),
            Given(gains, *reduce[13:17], gains_out, reduce[17:19]),
        ]
        met, met_send, met_recv = reduce[19:22]
    else:
        grad_x, left, right, total, ss, sr = rest
        sources = ()
    line = Line(n, x.shape[0], part, (left, right), None, (ss, sr), None)
    line.greet(Plane() if sources else None)

    def point(k):
        line.total(k, total)

        def one(here, own, at):
            back, _ = norm_back(x[own, :].astype(f32), gain[...], total[here, :])
            grad_x[own, :] = (d_resid[own, :] + back).astype(bf16)

        line.tiles(k, one)

    if not sources:
        line.run(point)
        return
    width = sources[5].shape[1]
    cots, hidden, norm, back_all, cat, mixed = late_all(sources, late_refs, late_sems)
    every, sent, sent_wide = slice(None), [], []
    wide_sides = ((cots, hidden, every),)
    sides = (
        (norm, cat, slice(0, width)),
        (norm, cat, slice(width, 2 * width)),
        (back_all, mixed, every),
    )
    parts = [
        Reduce(i, *side, sent_wide, *views(i, *wide[:5]), out, wide[5:7])
        for i, (side, out) in enumerate(zip(wide_sides, outs))
    ]
    parts += [
        Reduce(i, *side, sent, *views(i, *reduce[:5]), out, reduce[5:7])
        for i, (side, out) in enumerate(zip(sides, outs[1:]))
    ]
    tasks, finish = reduce_tasks(parts, given)

    me = lax.axis_index("mp")

    def meet(away):
        return pltpu.make_async_remote_copy(
            src_ref=gains_out,
            dst_ref=met.at[away - 1],
            send_sem=met_send.at[away - 1],
            recv_sem=met_recv.at[away - 1],
            device_id={"mp": lax.rem(me + away, n)},
            device_id_type=MESH,
        )

    def send_gains():
        for away in range(1, n):
            meet(away).start()

    def add_gains():
        for away in range(1, n):
            meet(away).wait()
        gains_out[...] += sum(met[away] for away in range(n - 1))

    tasks[7:7] = [send_gains]
    line.run(point, tasks)
    finish()
    add_gains()


def line_call(body, n, identity, outs, sums, alls, args, more=(), late=0, held=0):
    whole = pl.BlockSpec(memory_space=pltpu.VMEM)
    local, model = args[0].shape
    sem = pltpu.SemaphoreType.DMA((2, n, PIECES))
    scratch = []
    if sums:
        scratch += [pltpu.VMEM((n * local, model), bf16)] * 2
        scratch += [pltpu.VMEM((max(rows for _, rows in cut_rows(local, PIECES)), model), f32)]
        scratch += [sem, sem]
    if alls:
        scratch += [sem, sem]
    scratch += more
    if held:
        scratch += [pltpu.VMEM(o.shape, o.dtype) for o in outs[len(outs) - held :]]
        scratch += [pltpu.SemaphoreType.DMA((held,))]
    away = pl.BlockSpec(memory_space=pl.ANY)
    moved = sum(a.size * a.dtype.itemsize for a in args)
    return pl.pallas_call(
        functools.partial(body, n),
        out_shape=outs,
        in_specs=[whole] * (len(args) - late) + [away] * late,
        out_specs=[whole] * (len(outs) - held) + [away] * held,
        scratch_shapes=scratch,
        compiler_params=pltpu.CompilerParams(
            vmem_limit_bytes=VMEM_MB << 20, collective_id=identity, has_side_effects=True
        ),
        cost_estimate=pl.CostEstimate(flops=0, bytes_accessed=100 * moved, transcendentals=0),
    )(*args)


def finish(heads, piece, share, resid, low, high, gains, little, *rest):
    count = (len(rest) - 6) // 2
    sources, rest = rest[:count], rest[count:]
    output, grad_gains, grad_conv, grad_bias, grad_decay, grad_blocks, *targets = rest
    for source, target in zip(sources, targets):
        target[...] = source[...]
    half = low.shape[1]
    output[:, :half] = (resid[:, :half] + low[...].astype(f32)).astype(bf16)
    output[:, half:] = (resid[:, half:] + high[...].astype(f32)).astype(bf16)
    for position in range(gains.shape[0] // 2):

        @pl.when(lax.axis_index("mp") == position)
        def _():
            grad_gains[...] = gains[2 * position : 2 * position + 2, :share]

    for h in range(heads):
        for gate in range(2):
            first = (2 * h + gate) * LANE
            grad_blocks[gate, h] = little[:, first : first + LANE]
    first = 2 * heads * LANE
    lines = little[:, first : first + LANE]
    lines = jnp.concatenate([lines, jnp.zeros((LANE - piece, LANE), f32)], axis=0).T
    for h in range(heads):
        for k in range(SUB):
            row = lines[h * SUB + k : h * SUB + k + 1, :piece]
            if k < 4:
                grad_conv[k, h : h + 1, :] = row
            elif k < SUB - 1:
                grad_bias[k - 4, h : h + 1, :] = row
            else:
                grad_decay[h : h + 1, :] = row


def local_call(body, outs, scratch, flops, args, late=0, held=0):
    whole, away = pl.BlockSpec(memory_space=pltpu.VMEM), pl.BlockSpec(memory_space=pl.ANY)
    twins = list(args[len(args) - late :]) + list(outs[len(outs) - held :])
    scratch = scratch + [pltpu.VMEM(a.shape, a.dtype) for a in twins]
    if late:
        scratch.append(pltpu.SemaphoreType.DMA((late,)))
    if held:
        scratch.append(pltpu.SemaphoreType.DMA((held, 4)))
    moved = sum(a.size * a.dtype.itemsize for a in args)
    moved += sum(o.size * o.dtype.itemsize for o in outs)
    return pl.pallas_call(
        body,
        out_shape=outs,
        in_specs=[whole] * (len(args) - late) + [away] * late,
        out_specs=[whole] * (len(outs) - held) + [away] * held,
        scratch_shapes=scratch,
        compiler_params=pltpu.CompilerParams(vmem_limit_bytes=VMEM_MB << 20),
        cost_estimate=pl.CostEstimate(flops=flops, bytes_accessed=moved, transcendentals=0),
    )(*args)


def shape_of(dtype, *shape):
    return jax.ShapeDtypeStruct(shape, dtype)


def shards(
    inputs,
    cotangent,
    token_mask,
    order,
    lengths,
    gains,
    w_in,
    w_gate,
    w_out,
    conv_weight,
    chan_bias,
    decay,
    gate_blocks,
    w_up,
    w_gate_ff,
    w_down,
):
    n_dp = lax.axis_size("dp")
    local_rows, model = inputs.shape
    count = local_rows * lax.axis_size("mp")
    heads, piece = decay.shape
    width = heads * piece * n_dp
    hidden_width = w_up.shape[1]

    fused = n_dp == 8
    rows = model // n_dp
    out_rows, down_rows = w_out.T, w_down.T
    lines = jnp.concatenate([conv_weight, chan_bias, decay[None]], axis=0).transpose(1, 0, 2)
    lines = lines.reshape(SUB * heads, piece)

    gain_f = gains.astype(f32)
    n_mp = lax.axis_size("mp")
    tok = shape_of(bf16, count, model)
    own = shape_of(f32, local_rows, model)
    if fused:
        grown = shape_of(bf16, model, width)
        norm_group, full_in, full_gate, full_out, blocks, chan, ocol, orow, pos_col = line_call(
            gather_weights,
            n_mp,
            0,
            [tok, grown, grown, grown, shape_of(bf16, 2 * heads, LANE, LANE), shape_of(f32, 16, width)]
            + [shape_of(jnp.int32, *at) for at in ((count, 1), (1, count), (count + TAIL, 1))],
            False,
            True,
            (
                inputs,
                gain_f[0:1],
                w_in,
                w_gate,
                out_rows,
                gate_blocks.reshape(2 * heads, piece, LANE),
                jnp.pad(lines, ((0, 0), (0, LANE - piece))),
                order,
                lengths,
            ),
            [pltpu.VMEM((n_dp * SUB * heads, LANE), bf16)] + [pltpu.SemaphoreType.DMA((5, 2, 7))] * 2,
        )
    else:
        steps = count // SUB
        ends = jnp.cumsum(lengths[0], dtype=jnp.int32)
        starts = ends - lengths[0]
        places = jnp.arange(count, dtype=jnp.int32)
        own_start = jnp.max(
            jnp.where(places[:, None] >= starts[None, :], starts[None, :], 0), axis=1
        )
        pos = (places - own_start).reshape(SUB, steps).T
        wrap = jnp.concatenate([pos[: TAIL // SUB, 1:], jnp.full((TAIL // SUB, 1), -1, jnp.int32)], axis=1)
        pos_col = jnp.concatenate([pos, wrap], axis=0).reshape(count + TAIL, 1)
        order_int = order[0].reshape(SUB, steps).T.reshape(count)
        ocol, orow = order_int.reshape(count, 1), order_int.reshape(1, count)
        (norm_group,) = line_call(gather_norm, n_mp, 0, [tok], False, True, (inputs, gain_f[0:1]))
        full_in = lax.all_gather(w_in, "dp", axis=0, tiled=True)
        full_gate = lax.all_gather(w_gate, "dp", axis=0, tiled=True)
        full_out = lax.all_gather(out_rows, "dp", axis=0, tiled=True)
        blocks = lax.all_gather(gate_blocks, "dp", axis=2, tiled=True).reshape(2 * heads, LANE, LANE)
        params = lax.all_gather(lines, "dp", axis=1, tiled=True).astype(f32)
        params = params.reshape(heads, SUB, LANE).transpose(1, 0, 2).reshape(SUB, width)
        decay_row = params[7:8]
        chan = jnp.concatenate(
            [params[:7], jax.nn.softplus(decay_row)] + [jax.nn.sigmoid(decay_row)] * SUB, axis=0
        )
    cot = cotangent * token_mask.astype(bf16)[:, None]

    cot_first, norm_group = lax.optimization_barrier((cot[:, : model // 3], norm_group))
    cot_first = lax.all_gather(cot_first, "mp", axis=0, tiled=True)

    wide = pltpu.VMEM((count, width), f32)
    saved = [shape_of(f32, count, width)] * 6
    gate_pre, branch, conv, gate_in, gate_rec, state, mixed, back_part = local_call(
        mixer_forward,
        saved + [shape_of(bf16, count, width), shape_of(bf16, count, model)],
        [
            pltpu.VMEM((ROWS, model), bf16),
            wide,
            wide,
            pltpu.VMEM((ROWS + TAIL, width), f32),
            pltpu.VMEM((count, width), bf16),
        ],
        2 * count * (count * model + 3 * model * width),
        (norm_group, ocol, orow, pos_col, full_in, full_gate, chan, blocks, full_out),
        1,
        8,
    )
    shares = (w_up, w_gate_ff, down_rows)
    if not fused:
        shares = [lax.all_gather(share, "dp", axis=0, tiled=True) for share in shares]
    hid = shape_of(bf16, count, hidden_width)
    low_width = model * 5 // 12
    low_shape = shape_of(bf16, count, low_width)
    high_twin = pltpu.VMEM((count, model - low_width), bf16)
    pieces = cut_rows(local_rows, PIECES)
    most = n_mp * max(pieces[k][1] + pieces[k + 1][1] for k in range(0, PIECES, 2))
    pair = pltpu.VMEM((most, hidden_width), f32)
    flow = pltpu.SemaphoreType.DMA((2, n_mp, PIECES))
    plane_scratch = [pltpu.VMEM((n_dp, rows, hidden_width), bf16)] * 3
    plane_scratch += [pltpu.SemaphoreType.DMA((3, 2, 7))] * 2 + [pltpu.SemaphoreType.DMA((2, 10))] * 2
    plane_scratch += [pltpu.SemaphoreType.REGULAR]
    (
        d_resid,
        gain_mid,
        back_group,
        ffn_high,
        *ffn_grads,
        norm_mid_group,
        cot_group,
        resid,
        hidden,
        d_up,
        d_gate_ff,
        ffn_part,
    ) = line_call(
        middle,
        n_mp,
        1,
        [own, shape_of(f32, 1, model), tok, shape_of(bf16, local_rows, model - low_width)]
        + [shape_of(f32, rows, hidden_width)] * (2 * fused)
        + [tok, tok, own, hid, hid, hid, low_shape],
        True,
        True,
        (inputs, gain_f[1:2], cot, back_part, *shares, cot_first),
        [pltpu.VMEM((count, model), bf16)]
        + [flow] * 6
        + [pair, pair, pltpu.VMEM((most, model), f32)]
        + [high_twin] * 3
        + [pltpu.VMEM((max(rows for _, rows in pieces), model - low_width), f32), flow, flow]
        + [pltpu.SemaphoreType.DMA(())]
        + plane_scratch * fused,
        late=1,
        held=7,
    )

    def reduced(left, right):
        grad = dot_first(left, right).astype(bf16)
        return lax.psum_scatter(grad, "dp", scatter_dimension=0, tiled=True).astype(f32)

    d_cat, d_norm_back, little, gain_in, *ffn_grads = local_call(
        mixer_backward,
        [
            shape_of(bf16, count, 2 * width),
            tok,
            shape_of(f32, LANE, 2 * width + LANE),
            shape_of(f32, 1, model),
        ]
        + [shape_of(f32, *a.shape) for a in ffn_grads],
        [
            pltpu.VMEM((count, width), bf16),
            wide,
            wide,
            wide,
            pltpu.VMEM((count + TAIL, width), f32),
            pltpu.VMEM((ROWS + TAIL, width), f32),
            pltpu.VMEM((count, 2 * width), bf16),
            pltpu.VMEM((SUB, width), f32),
            pltpu.VMEM((heads, LANE, 2 * LANE), f32),
        ],
        2 * count * (3 * count * width + 3 * model * width),
        (
            back_group,
            full_out,
            ocol,
            orow,
            pos_col,
            gain_f[0:1],
            chan,
            blocks,
            gate_pre,
            gate_rec,
            state,
            conv,
            gate_in,
            branch,
            norm_group,
            full_in,
            full_gate,
            *ffn_grads,
        ),
        9 + len(ffn_grads),
        len(ffn_grads),
    )
    share = model // (n_dp * n_mp)
    gain_parts = jnp.concatenate([gain_in, gain_mid], axis=0).reshape(2, n_dp, n_mp, share)
    gain_parts = gain_parts.transpose(1, 2, 0, 3).reshape(n_dp, 2 * n_mp, share)
    gain_parts = jnp.pad(gain_parts, ((0, 0), (0, 2 * SUB - 2 * n_mp), (0, LANE - share)))
    gain_parts = gain_parts.reshape(2 * SUB * n_dp, LANE)
    ffn_low = lax.psum_scatter(ffn_part, "mp", scatter_dimension=0, tiled=True)
    ffn_low, d_norm_back = lax.optimization_barrier((ffn_low, d_norm_back))
    grad_inputs, *mix_grads = line_call(
        sum_back,
        n_mp,
        3,
        [shape_of(bf16, local_rows, model)]
        + (
            [shape_of(f32, rows, hidden_width)]
            + [shape_of(f32, rows, width)] * 3
            + [shape_of(f32, piece, little.shape[1]), shape_of(f32, 2 * SUB, LANE)]
        )
        * fused,
        True,
        False,
        (inputs, d_resid, gain_f[0:1], d_norm_back)
        + (
            (
                little,
                gain_parts,
                cot_group,
                hidden,
                norm_group,
                back_group,
                d_cat,
                mixed,
            )
            if fused
            else ()
        ),
        reduce_scratch(3, rows, width)
        + given_scratch(piece, little.shape[1])
        + given_scratch(2 * SUB, LANE)
        + [pltpu.VMEM((n_mp - 1, 2 * SUB, LANE), f32)]
        + [pltpu.SemaphoreType.DMA((n_mp - 1,))] * 2
        + reduce_scratch(1, rows, hidden_width)
        + [pltpu.VMEM(a.shape, a.dtype) for a in (cot_group, hidden, norm_group, back_group, d_cat, mixed)]
        + [pltpu.SemaphoreType.DMA((6,))]
        if fused
        else (),
        6 * fused,
    )
    if fused:
        up_grad, gate_ff_grad = ffn_grads
        down_grad, *mix_grads, little_own, gain_own = mix_grads
    else:
        up_grad = reduced(norm_mid_group, d_up)
        gate_ff_grad = reduced(norm_mid_group, d_gate_ff)
        down_grad = reduced(cot_group, hidden)
        mix_grads = [
            reduced(norm_group, d_cat[:, :width]),
            reduced(norm_group, d_cat[:, width:]),
            reduced(back_group, mixed),
        ]
        little_own = lax.psum_scatter(little, "dp", scatter_dimension=0, tiled=True)
        gain_own = lax.psum(lax.psum_scatter(gain_parts, "dp", scatter_dimension=0, tiled=True), "mp")
    outs = [
        shape_of(bf16, local_rows, model),
        shape_of(f32, 2, share),
        shape_of(f32, 4, heads, piece),
        shape_of(f32, 3, heads, piece),
        shape_of(f32, heads, piece),
        shape_of(f32, 2, heads, piece, LANE),
    ]
    copied = [grad_inputs, mix_grads[0], mix_grads[1]] if fused else []
    output, grad_gains, grad_conv, grad_bias, grad_decay, grad_blocks, *copied = local_call(
        functools.partial(finish, heads, piece, share),
        outs + [shape_of(a.dtype, *a.shape) for a in copied],
        [],
        0,
        (resid, ffn_low, ffn_high, gain_own, little_own, *copied),
    )
    if fused:
        grad_inputs, grad_in, grad_gate = copied
    else:
        grad_in, grad_gate, _ = mix_grads
    return (
        output,
        grad_inputs,
        grad_gains,
        grad_in,
        grad_gate,
        mix_grads[2].T,
        grad_conv,
        grad_bias,
        grad_decay,
        grad_blocks,
        up_grad,
        gate_ff_grad,
        down_grad.T,
    )


def solution(mesh):
    row, col = P("dp", "mp"), P("mp", "dp")
    tok = P(("dp", "mp"), None)
    chan = P(None, "mp", "dp")
    gate = P(None, "mp", "dp", None)
    return jax.shard_map(
        shards,
        mesh=mesh,
        in_specs=(
            tok, tok, P(("dp", "mp")), P("dp", None), P("dp", None), P(),
            row, row, col, chan, chan, col, gate, row, row, col,
        ),
        out_specs=(
            tok, tok, P(None, ("dp", "mp")), row, row, col, chan, chan, col, gate, row, row, col,
        ),
        check_vma=False,
    )
```

```python
import functools

import jax
import jax.numpy as jnp
from jax import lax
from jax.experimental import pallas as pl
from jax.experimental.pallas import tpu as pltpu
from jax.sharding import PartitionSpec as P

epsilon = 1e-06
LANE = 128
SUB = 8
TAIL = 24
ROWS = 272
VMEM_MB = 62
f32 = jnp.float32
bf16 = jnp.bfloat16
GELU_C = 0.7978845608028654
GELU_A = 0.044715


def rms_scale(values):
    return lax.rsqrt(jnp.mean(values * values, axis=-1, keepdims=True) + epsilon)


def dot(left, right):
    return lax.dot_general(left, right, (((1,), (0,)), ((), ())), preferred_element_type=f32)


def dot_last(left, right):
    return lax.dot_general(left, right, (((1,), (1,)), ((), ())), preferred_element_type=f32)


def dot_first(left, right):
    return lax.dot_general(left, right, (((0,), (0,)), ((), ())), preferred_element_type=f32)


def gelu_of(v):
    return 0.5 * v * (1.0 + jnp.tanh(GELU_C * (v + GELU_A * v * v * v)))


def gelu_both(v):
    square = v * v
    th = jnp.tanh(GELU_C * (v + GELU_A * v * square))
    half = 0.5 * (1.0 + th)
    slope = half + 0.5 * v * (1.0 - th * th) * (GELU_C * (1.0 + 3.0 * GELU_A * square))
    return v * half, slope


def sigmoid(v):
    return 0.5 * jnp.tanh(0.5 * v) + 0.5


def split(values):
    high = values.astype(bf16)
    return high, (values - high.astype(f32)).astype(bf16)


def rows_of(index, rows):
    return pl.ds(pl.multiple_of(index * rows, rows), rows)


def pick_rows(order_col, count):
    places = lax.broadcasted_iota(jnp.int32, (order_col.shape[0], count), 1)
    return (places == order_col).astype(f32).astype(bf16)


def put_rows(order_row, first, rows):
    places = lax.broadcasted_iota(jnp.int32, (rows, order_row.shape[1]), 0) + first
    return (places == order_row).astype(f32).astype(bf16)


def mixer_forward(tokens, ocol, orow, pos, w_in, w_gate, chan, blocks, w_out_far, *rest):
    far, rest = rest[:8], rest[8:]
    packed, rate, prod, before, low, w_out, *near, late_sem, held_sem = rest
    gate_ref, branch_ref, conv_ref, gin_ref, grec_ref, state_ref, mixed_ref, out_ref = near
    (late_out,) = late_all([w_out_far], [w_out], late_sem)
    leaving = [
        pltpu.make_async_copy(source, target, held_sem.at[i, 0])
        for i, (source, target) in enumerate(zip(near, far))
    ]
    count, _ = tokens.shape
    width = w_in.shape[1]
    steps = count // SUB
    heads = width // LANE

    def project(b, carry):
        at = rows_of(b, ROWS)
        packed[...] = dot(pick_rows(ocol[at, :], count), tokens[...]).astype(bf16)
        branch_ref[at, :] = dot(packed[...], w_in[...])
        gate_ref[at, :] = dot(packed[...], w_gate[...])
        return carry

    lax.fori_loop(0, count // ROWS, project, 0)
    leaving[0].start()
    leaving[1].start()

    for k in range(TAIL // SUB):
        last = branch_ref[pl.ds(count - TAIL + k * SUB, SUB), :]
        before[pl.ds(k * SUB, SUB), :] = pltpu.roll(last, 1, 0)
    before[pl.ds(TAIL, ROWS), :] = branch_ref[pl.ds(0, ROWS), :]

    def gates(b, carry):
        at = rows_of(b, ROWS)

        @pl.when(b > 0)
        def _():
            before[...] = branch_ref[pl.ds(pl.multiple_of(b * ROWS - TAIL, SUB), ROWS + TAIL), :]

        place = pos[at, :]
        for h in range(heads):
            lanes = pl.ds(h * LANE, LANE)
            par = chan[:, lanes]
            conv = par[4:5] + par[0:1] * before[pl.ds(TAIL, ROWS), lanes]
            for k in range(1, 4):
                earlier = before[pl.ds(TAIL - SUB * k, ROWS), lanes]
                conv = conv + par[k : k + 1] * jnp.where(place >= k, earlier, 0.0)
            high, rest = split(conv)
            pair = jnp.concatenate([blocks[h], blocks[heads + h]], axis=1)
            pre = dot(
                jnp.concatenate([high, rest], axis=1), jnp.concatenate([pair, pair], axis=0)
            )
            gate_in = sigmoid(pre[:, :LANE] + par[5:6])
            gate_rec = sigmoid(pre[:, LANE:] + par[6:7])
            kept = jnp.exp(-8.0 * gate_rec * par[7:8])
            drive = jnp.sqrt(1.0 - kept * kept + 0.01) * gate_in * conv
            conv_ref[at, lanes] = conv
            gin_ref[at, lanes] = gate_in
            grec_ref[at, lanes] = gate_rec
            rate[at, lanes] = jnp.where(place >= 1, kept, 0.0)
            state_ref[at, lanes] = drive
        return carry

    lax.fori_loop(0, count // ROWS, gates, 0)
    for copy in leaving[2:5]:
        copy.start()

    def scan(i, carry):
        held, passed = carry
        at = rows_of(i, SUB)
        a = rate[at, :]
        held = a * held + state_ref[at, :]
        passed = a * passed
        state_ref[at, :] = held
        prod[at, :] = passed
        return held, passed

    ends = lax.fori_loop(
        0, steps, scan, (jnp.zeros((SUB, width), f32), jnp.ones((SUB, width), f32)), unroll=8
    )
    first = lax.broadcasted_iota(jnp.int32, (SUB, width), 0) == 0
    carry_in = jnp.zeros((SUB, width), f32)
    for _ in range(SUB - 1):
        carry_in = jnp.where(first, 0.0, pltpu.roll(ends[0] + ends[1] * carry_in, 1, 0))

    def finish(i, carry):
        at = rows_of(i, 2 * SUB)
        twice = jnp.concatenate([carry_in, carry_in], axis=0)
        value = state_ref[at, :] + prod[at, :] * twice
        state_ref[at, :] = value
        low[at, :] = (gelu_of(gate_ref[at, :]) * value).astype(bf16)
        return carry

    lax.fori_loop(0, steps // 2, finish, 0, unroll=2)
    leaving[5].start()
    late_out.ready()

    def leave(b, carry):
        at = rows_of(b, ROWS)
        mixed = dot(put_rows(orow[...], b * ROWS, ROWS), low[...]).astype(bf16)
        mixed_ref[at, :] = mixed
        out_ref[at, :] = dot_last(mixed, w_out[...]).astype(bf16)
        return carry

    lax.fori_loop(0, count // ROWS, leave, 0)
    for copy in leaving[6:]:
        copy.start()
    for copy in leaving:
        copy.wait()


def mixer_backward(back, w_out, ocol, orow, pos, gain, chan, blocks, *rest):
    more = 2 if len(rest) > 36 else 0
    far, rest = rest[: 9 + more], rest[9 + more :]
    (dcat_ref, dnorm_ref, little_ref, dgain_ref), rest = rest[:4], rest[4:]
    passed_on, rest = rest[:more], rest[more:]
    dmix_arr, dmix, adj, prod, after, before, low, small_ref, dblocks_ref, *rest = rest
    gate_ref, grec_ref, state_ref, conv_ref, gin_ref, branch_ref, norm, w_in, w_gate, *extra = rest[: 9 + more]
    late_sem = rest[9 + 2 * more]
    late = late_all(far, rest[: 9 + more], late_sem)
    leaving = [
        pltpu.make_async_copy(source, target, rest[-1].at[i, 0])
        for i, (source, target) in enumerate(zip(extra, passed_on))
    ]
    count, _ = back.shape
    width = w_in.shape[1]
    steps = count // SUB
    heads = width // LANE
    blocks_of = count // ROWS

    def enter(b, carry):
        at = rows_of(b, ROWS)
        dmix_arr[at, :] = dot(back[at, :], w_out[...]).astype(bf16)
        return carry

    lax.fori_loop(0, blocks_of, enter, 0)
    for array in late[:3]:
        array.ready()

    def pack(b, carry):
        at = rows_of(b, ROWS)
        d_mixed = dot(pick_rows(ocol[at, :], count), dmix_arr[...])
        value, slope = gelu_both(gate_ref[at, :])
        adj[at, :] = d_mixed * value
        low[at, pl.ds(width, width)] = (d_mixed * state_ref[at, :] * slope).astype(bf16)
        kept = jnp.exp(-8.0 * grec_ref[at, :] * chan[7:8, :])
        dmix[at, :] = jnp.where(pos[at, :] >= 1, kept, 0.0)
        return carry

    lax.fori_loop(0, blocks_of, pack, 0)
    for array in late:
        array.ready()
    for copy in leaving:
        copy.start()

    def scan(i, carry):
        held, passed, following = carry
        at = rows_of(steps - 1 - i, SUB)
        held = following * held + adj[at, :]
        passed = following * passed
        adj[at, :] = held
        prod[at, :] = passed
        return held, passed, dmix[at, :]

    last = lax.broadcasted_iota(jnp.int32, (SUB, width), 0) == SUB - 1
    wrapped = jnp.where(last, 0.0, pltpu.roll(dmix[pl.ds(0, SUB), :], SUB - 1, 0))
    ends = lax.fori_loop(
        0,
        steps,
        scan,
        (jnp.zeros((SUB, width), f32), jnp.ones((SUB, width), f32), wrapped),
        unroll=8,
    )
    carry_in = jnp.zeros((SUB, width), f32)
    for _ in range(SUB - 1):
        carry_in = jnp.where(last, 0.0, pltpu.roll(ends[0] + ends[1] * carry_in, SUB - 1, 0))

    small_ref[...] = jnp.zeros_like(small_ref)
    dblocks_ref[...] = jnp.zeros_like(dblocks_ref)
    first = lax.broadcasted_iota(jnp.int32, (SUB, width), 0) == 0
    state_last = state_ref[pl.ds(count - SUB, SUB), :]
    before[pl.ds(TAIL - SUB, SUB), :] = jnp.where(first, 0.0, pltpu.roll(state_last, 1, 0))
    before[pl.ds(TAIL, ROWS), :] = state_ref[pl.ds(0, ROWS), :]
    wide_carry = jnp.concatenate([carry_in] * (ROWS // SUB), axis=0)

    def point(b, carry):
        at = rows_of(b, ROWS)

        @pl.when(b > 0)
        def _():
            before[...] = state_ref[pl.ds(pl.multiple_of(b * ROWS - TAIL, SUB), ROWS + TAIL), :]

        place = pos[at, :]
        for h in range(heads):
            lanes = pl.ds(h * LANE, LANE)
            par = chan[:, lanes]
            adjoint = adj[at, lanes] + prod[at, lanes] * wide_carry[:, h * LANE : (h + 1) * LANE]
            conv = conv_ref[at, lanes]
            gate_in = gin_ref[at, lanes]
            gate_rec = grec_ref[at, lanes]
            kept = jnp.exp(-8.0 * gate_rec * par[7:8])
            square = kept * kept
            inside = 1.0 - square + 0.01
            inverse = lax.rsqrt(inside)
            root = inside * inverse
            previous = before[pl.ds(TAIL - SUB, ROWS), lanes]
            d_log = adjoint * previous * dmix[at, lanes]
            scaled = adjoint * gate_in
            d_log = d_log - scaled * conv * square * inverse
            d_in = adjoint * root * conv * gate_in * (1.0 - gate_in)
            d_rec = d_log * (-8.0 * par[7:8]) * gate_rec * (1.0 - gate_rec)
            both = jnp.concatenate([d_in, d_rec], axis=1)
            high, rest = split(both)
            pair = jnp.concatenate([blocks[h], blocks[heads + h]], axis=1)
            d_conv = scaled * root + dot_last(high, pair) + dot_last(rest, pair)
            dblocks_ref[h] += dot_first(conv.astype(bf16), high)
            after[at, lanes] = d_conv
            small_ref[4:5, lanes] += jnp.sum(d_conv, axis=0, keepdims=True)
            small_ref[5:6, lanes] += jnp.sum(d_in, axis=0, keepdims=True)
            small_ref[6:7, lanes] += jnp.sum(d_rec, axis=0, keepdims=True)
            small_ref[7:8, lanes] += (
                jnp.sum(d_log * gate_rec, axis=0, keepdims=True) * (-8.0) * par[8:9]
            )
        return carry

    lax.fori_loop(0, blocks_of, point, 0)

    for k in range(TAIL // SUB):
        head = after[pl.ds(k * SUB, SUB), :]
        after[pl.ds(count + k * SUB, SUB), :] = pltpu.roll(head, SUB - 1, 0)
        tail = branch_ref[pl.ds(count - TAIL + k * SUB, SUB), :]
        before[pl.ds(k * SUB, SUB), :] = pltpu.roll(tail, 1, 0)
    before[pl.ds(TAIL, ROWS), :] = branch_ref[pl.ds(0, ROWS), :]

    def unmix(b, carry):
        at = rows_of(b, ROWS)

        @pl.when(b > 0)
        def _():
            before[...] = branch_ref[pl.ds(pl.multiple_of(b * ROWS - TAIL, SUB), ROWS + TAIL), :]

        place = pos[at, :]
        for h in range(heads):
            lanes = pl.ds(h * LANE, LANE)
            par = chan[:, lanes]
            d_conv = after[at, lanes]
            d_branch = par[0:1] * d_conv
            small_ref[0:1, lanes] += jnp.sum(
                d_conv * before[pl.ds(TAIL, ROWS), lanes], axis=0, keepdims=True
            )
            for k in range(1, 4):
                later = pl.ds(pl.multiple_of(b * ROWS + SUB * k, SUB), ROWS)
                d_branch = d_branch + par[k : k + 1] * jnp.where(
                    pos[later, :] >= k, after[later, lanes], 0.0
                )
                earlier = before[pl.ds(TAIL - SUB * k, ROWS), lanes]
                small_ref[k : k + 1, lanes] += jnp.sum(
                    jnp.where(place >= k, d_conv * earlier, 0.0), axis=0, keepdims=True
                )
            low[at, lanes] = d_branch.astype(bf16)
        return carry

    lax.fori_loop(0, blocks_of, unmix, 0)
    lines = [small_ref[0:SUB, h * LANE : (h + 1) * LANE] for h in range(heads)]
    lines.append(jnp.zeros((LANE - SUB * heads, LANE), f32))
    little_ref[:, pl.ds(2 * width, LANE)] = jnp.concatenate(lines, axis=0).T
    for h in range(heads):
        little_ref[:, pl.ds(2 * h * LANE, 2 * LANE)] = dblocks_ref[h]
    dgain_ref[...] = jnp.zeros_like(dgain_ref)

    def leave(b, carry):
        at = rows_of(b, ROWS)
        cat = dot(put_rows(orow[...], b * ROWS, ROWS), low[...]).astype(bf16)
        dcat_ref[at, :] = cat
        d_norm = dot_last(cat[:, :width], w_in[...]) + dot_last(cat[:, width:], w_gate[...])
        dgain_ref[...] += jnp.sum(d_norm * norm[at, :].astype(f32), axis=0, keepdims=True)
        dnorm_ref[at, :] = d_norm.astype(bf16)
        return carry

    lax.fori_loop(0, blocks_of, leave, 0)
    dgain_ref[...] = dgain_ref[...] / gain[...]
    for copy in leaving:
        copy.wait()


MESH = pl.DeviceIdType.MESH
TILE = 16
PIECES = 8
HOP = 1
AFTER = 1


def cut_rows(rows, parts):
    tiles = rows // TILE
    ends = [tiles * (k + 1) // parts for k in range(parts)]
    return [(TILE * a, TILE * (b - a)) for a, b in zip([0] + ends[:-1], ends)]


class Line:
    def __init__(self, n, local, part, arrived, whole, sums, alls):
        self.n, self.local, self.part, self.arrived, self.whole = n, local, part, arrived, whole
        self.sums, self.alls = sums, alls
        self.me = lax.axis_index("mp")
        self.pieces = cut_rows(local, PIECES)
        self.has = (self.me > 0, self.me < n - 1)

    def greet(self, plane=None):
        barrier = pltpu.get_barrier_semaphore()
        more = 0
        if plane is not None:
            for bit in plane.bits:
                more += 1
                pl.semaphore_signal(
                    barrier, inc=1, device_id={"dp": plane.other(bit)}, device_id_type=MESH
                )
        for away in range(1, self.n):
            more += 1
            pl.semaphore_signal(
                barrier,
                inc=1,
                device_id={"mp": lax.rem(self.me + away, self.n)},
                device_id_type=MESH,
            )
        pl.semaphore_wait(barrier, more)

    def rows_at(self, owner, k):
        first, rows = self.pieces[k]
        return pl.ds(pl.multiple_of(owner * self.local + first, TILE), rows)

    def copy(self, source, target, sems, way, owner, k):
        return pltpu.make_async_remote_copy(
            src_ref=source,
            dst_ref=target,
            send_sem=sems[0].at[way, owner, k],
            recv_sem=sems[1].at[way, owner, k],
            device_id={"mp": self.me + 1 - 2 * way},
            device_id_type=MESH,
        )

    def sum_copy(self, way, owner, k, first=False):
        at = self.rows_at(owner, k)
        landed = self.arrived[way].at[at]
        return self.copy(self.part.at[at] if first else landed, landed, self.sums, way, owner, k)

    def all_copy(self, way, owner, k):
        block = self.whole.at[self.rows_at(owner, k)]
        return self.copy(block, block, self.alls, way, owner, k)

    def first(self, k):
        for away in range(self.n - 1):
            for way in range(2):
                owner = away if way else self.n - 1 - away

                @pl.when(jnp.logical_not(self.has[way]))
                def _():
                    self.sum_copy(way, owner, k, True).start()

    def relay(self, k, stage):
        for way in range(2):
            late = stage - (self.n - 1 - self.me if way else self.me)
            owner = late if way else self.n - 1 - late

            @pl.when(self.has[way] & (late >= 0))
            def _():
                self.sum_copy(way, owner, k).wait_recv()
                at = self.rows_at(owner, k)
                landed = self.arrived[way]
                landed[at, :] = (landed[at, :].astype(f32) + self.part[at, :].astype(f32)).astype(bf16)
                self.sum_copy(way, owner, k).start()

    def total(self, k, into):
        at = self.rows_at(self.me, k)
        rows = pl.ds(0, self.pieces[k][1])
        into[rows, :] = self.part[at, :].astype(f32)
        for way in range(2):

            @pl.when(self.has[way])
            def _():
                self.sum_copy(way, self.me, k).wait_recv()
                into[rows, :] += self.arrived[way][at, :].astype(f32)

    def spread(self, k):
        for way in range(2):

            @pl.when(self.has[1 - way])
            def _():
                self.all_copy(way, self.me, k).start()

    def forward(self, k, stage):
        for way in range(2):
            owner = self.me + stage if way else self.me - stage
            there = owner < self.n if way else owner >= 0

            @pl.when(there)
            def _():
                self.all_copy(way, owner, k).wait_recv()

            @pl.when(there & self.has[1 - way])
            def _():
                self.all_copy(way, owner, k).start()

    def sent(self, k):
        for owner in range(self.n):
            for way in range(2):

                @pl.when(self.me > owner if way else self.me < owner)
                def _():
                    self.sum_copy(way, owner, k).wait_send()

    def finish(self):
        for k in range(PIECES):
            for owner in range(self.n):
                for way in range(2):
                    if self.whole is not None:
                        reached = self.me <= owner if way else self.me >= owner

                        @pl.when(reached & self.has[1 - way])
                        def _():
                            self.all_copy(way, owner, k).wait_send()

    def run(self, point, tasks=()):
        sums, alls = self.part is not None, self.whole is not None
        slots = [[] for _ in range(PIECES + (HOP + AFTER) * (self.n - 1) + 1)]
        for k in range(PIECES):
            done = k + HOP * (self.n - 1) if sums else 0
            if sums:
                slots[k].append((0, functools.partial(self.first, k)))
                for stage in range(1, self.n - 1):
                    slots[k + HOP * stage].append((2, functools.partial(self.relay, k, stage)))
                slots[done].append((3, functools.partial(self.sent, k)))
            slots[done].append((3, functools.partial(point, k)))
            if alls:
                slots[done].append((4, functools.partial(self.spread, k)))
                for stage in range(1, self.n):
                    at = (done if sums else k) + AFTER * stage
                    slots[at].append((1, functools.partial(self.forward, k, stage)))
        tasks = iter(tasks)
        for slot in slots:
            for step, (_, work) in enumerate(sorted(slot, key=lambda entry: entry[0])):
                if step in (0, 1, 3):
                    next(tasks, idle)()
                work()
        for task in tasks:
            task()
        self.finish()

    def tiles(self, k, body):
        first, rows = self.pieces[k]

        def one(i, carry):
            body(
                pl.ds(pl.multiple_of(i * TILE, TILE), TILE),
                pl.ds(pl.multiple_of(first + i * TILE, TILE), TILE),
                pl.ds(pl.multiple_of(self.me * self.local + first + i * TILE, TILE), TILE),
            )
            return carry

        lax.fori_loop(0, rows // TILE, one, 0)


def idle():
    pass


class Late:
    def __init__(self, source, ref, sem):
        self.ref = ref
        self.copy = pltpu.make_async_copy(source, ref, sem)
        self.pending = True

    def begin(self):
        self.copy.start()

    def ready(self):
        if self.pending:
            self.copy.wait()
        self.pending = False


class Here:
    def __init__(self, ref):
        self.ref = ref

    def ready(self):
        pass


def late_all(sources, refs, sems):
    arrays = [Late(source, ref, sems.at[i]) for i, (source, ref) in enumerate(zip(sources, refs))]
    for array in arrays:
        array.begin()
    return arrays


class Plane:
    bits = (1, 2, 4)
    orders = ((4, 2, 1), (2, 4, 1))

    def __init__(self):
        self.me = lax.axis_index("dp")

    def bit(self, bit):
        return lax.rem(self.me // bit, 2)

    def other(self, *bits):
        return self.me + sum(bit * (1 - 2 * self.bit(bit)) for bit in bits)

    def gather_copies(self, item, view, halves, stage, sems):
        copies = []
        for half in halves:
            order = self.orders[half]
            for combo in range(1 << stage):
                flipped = [bit for i, bit in enumerate(order[:stage]) if combo >> i & 1]
                block = view(self.other(*flipped), half)
                slot = (1 << stage) - 1 + combo
                copies.append(
                    pltpu.make_async_remote_copy(
                        src_ref=block,
                        dst_ref=block,
                        send_sem=sems[0].at[item, half, slot],
                        recv_sem=sems[1].at[item, half, slot],
                        device_id={"dp": self.other(order[stage])},
                        device_id_type=MESH,
                    )
                )
        return copies


class Reduce(Plane):
    def __init__(self, index, left, right, lanes, sent, mine, theirs, got, second, third, out, sems):
        super().__init__()
        self.sent, self.theirs = sent, theirs
        self.index, self.left, self.right, self.lanes = index, left, right, lanes
        self.mine, self.got = mine, got
        self.second, self.third, self.out = second, third, out
        self.sems = sems
        self.rows = out.shape[0]
        self.half = self.rows // 2

    def copy(self, source, target, slot, bit):
        return pltpu.make_async_remote_copy(
            src_ref=source,
            dst_ref=target,
            send_sem=self.sems[0].at[self.index, slot],
            recv_sem=self.sems[1].at[self.index, slot],
            device_id={"dp": self.other(bit)},
            device_id_type=MESH,
        )

    def core_copy(self, t):
        return self.copy(self.theirs.at[(4 * self.index + t) % 2], self.got.at[t], t, 1)

    def second_copy(self, half, j):
        x, y = self.bit(2), self.bit(4)
        block = (1 - y) * 2 + j if half else j * 2 + 1 - x
        rows = self.mine.at[block, pl.ds(half * self.half, self.half)]
        return self.copy(rows, self.second(half, j), 4 + 2 * half + j, 4 if half else 2)

    def third_block(self, half):
        x, y = self.bit(2), self.bit(4)
        return y * 2 + 1 - x if half else (1 - y) * 2 + x

    def third_copy(self, half):
        rows = self.mine.at[self.third_block(half), pl.ds(half * self.half, self.half)]
        return self.copy(rows, self.third(half), 8 + half, 2 if half else 4)

    def product(self, t):
        def task():
            core = self.bit(1)
            pair = pl.ds(t * 2 * self.rows, 2 * self.rows)
            if t == 0:
                self.left.ready()
                self.right.ready()
            if len(self.sent) > 1:
                self.sent[-2].wait_send()
            both = dot_first(self.left.ref[:, pair], self.right.ref[:, self.lanes])
            low, high = both[: self.rows], both[self.rows :]
            self.mine[t] = jnp.where(core == 0, low, high).astype(bf16)
            self.theirs[(4 * self.index + t) % 2] = jnp.where(core == 0, high, low).astype(bf16)
            self.sent.append(self.core_copy(t))
            self.sent[-1].start()

        return task

    def keep(self, t):
        return self.mine[t]

    def add_core(self):
        for t in range(4):
            self.core_copy(t).wait_recv()
            self.mine[t] = (self.keep(t).astype(f32) + self.got[t].astype(f32)).astype(self.mine.dtype)
        for half in range(2):
            for j in range(2):
                self.second_copy(half, j).start()

    def add_second(self):
        for half in range(2):
            for j in range(2):
                self.second_copy(half, j).wait_recv()
        for half in range(2):
            block, at = self.third_block(half), pl.ds(half * self.half, self.half)
            far = 1 - self.bit(2 if half else 4)
            self.mine[block, at] = (
                self.mine[block, at].astype(f32) + self.second(half, far)[...].astype(f32)
            ).astype(self.mine.dtype)
            self.third_copy(half).start()

    def add_third(self):
        own = self.bit(4) * 2 + self.bit(2)
        for half in range(2):
            self.third_copy(half).wait_recv()
            at = pl.ds(half * self.half, self.half)
            near = self.bit(2 if half else 4)
            self.out[at, :] = (
                self.mine[own, at].astype(f32)
                + self.second(half, near)[...].astype(f32)
                + self.third(half)[...].astype(f32)
            )

    def finish(self):
        for half in range(2):
            for j in range(2):
                self.second_copy(half, j).wait_send()
            self.third_copy(half).wait_send()


class Given(Reduce):
    def __init__(self, given, mine, got, second, third, out, sems):
        super().__init__(0, None, None, None, None, *views(0, mine, None, got, second, third), out, sems)
        self.given = given

    def rows_of(self, t, core):
        return pl.ds(pl.multiple_of((2 * t + core) * self.rows, self.rows), self.rows)

    def core_copy(self, t):
        return self.copy(self.given.at[self.rows_of(t, 1 - self.bit(1))], self.got.at[t], t, 1)

    def start(self):
        for t in range(4):
            self.core_copy(t).start()

    def finish(self):
        for t in range(4):
            self.core_copy(t).wait_send()
        super().finish()

    def keep(self, t):
        return self.given[self.rows_of(t, self.bit(1)), :]


def views(index, mine, theirs, got, second, third):
    return (
        mine.at[index],
        theirs,
        got.at[index],
        lambda half, j: second.at[index, half, j],
        lambda half: third.at[index, half],
    )


def blocks_views(index, both, spare):
    half_rows = spare.shape[1] // 2

    def halves(block, j):
        return spare.at[block, pl.ds(pl.multiple_of(j * half_rows, TILE), half_rows)]

    return (
        both.at[pl.ds(0, 4)],
        spare.at[pl.ds(6, 2)],
        both.at[pl.ds(4, 4)],
        lambda half, j: halves(3 * index + half, j),
        lambda half: halves(3 * index + 2, half),
    )


def reduce_tasks(parts, given=()):
    tasks = [part.product(t) for part in parts for t in range(4)]

    def also(at, extra):
        while len(tasks) <= at:
            tasks.append(idle)
        before = tasks[at]

        def both():
            extra()
            before()

        tasks[at] = both

    for i, part in enumerate(parts):
        also(4 * i + 5, part.add_core)
        also(4 * i + 8, part.add_second)
        also(4 * i + 10, part.add_third)

    for part in given:
        also(0, part.start)
        also(2, part.add_core)
        also(4, part.add_second)
        also(6, part.add_third)

    def finish():
        for ring in {id(part.sent): part.sent for part in parts}.values():
            for copy in ring[-2:]:
                copy.wait_send()
        for part in [*parts, *given]:
            part.finish()

    return tasks, finish


def given_scratch(rows, width):
    sem = pltpu.SemaphoreType.DMA((1, 10))
    return [
        pltpu.VMEM((1, 4, rows, width), f32),
        pltpu.VMEM((1, 4, rows, width), f32),
        pltpu.VMEM((1, 2, 2, rows // 2, width), f32),
        pltpu.VMEM((1, 2, rows // 2, width), f32),
        sem,
        sem,
    ]


def reduce_scratch(arrays, rows, width):
    block = pltpu.VMEM((arrays, 4, rows, width), bf16)
    sem = pltpu.SemaphoreType.DMA((arrays, 10))
    return [
        block,
        pltpu.VMEM((2, rows, width), bf16),
        block,
        pltpu.VMEM((arrays, 2, 2, rows // 2, width), bf16),
        pltpu.VMEM((arrays, 2, rows // 2, width), bf16),
        sem,
        sem,
    ]


def gather_norm(n, x, gain, whole, send, recv):
    line = Line(n, x.shape[0], None, None, whole, None, (send, recv))
    line.greet()

    def point(k):
        def one(_, own, at):
            v = x[own, :].astype(f32)
            whole[at, :] = (v * rms_scale(v) * gain[...]).astype(bf16)

        line.tiles(k, one)

    line.run(point)


def row_view(array, rows):
    def view(owner, half):
        first = owner * rows + half * (rows // 2)
        return array.at[pl.ds(pl.multiple_of(first, TILE), rows // 2)]

    return view


def gather_tasks(plane, items, sems):
    def copies(stage):
        return [
            copy
            for item, (view, halves) in enumerate(items)
            for copy in plane.gather_copies(item, view, halves, stage, sems)
        ]

    def stage_task(stage):
        def task():
            if stage:
                for copy in copies(stage - 1):
                    copy.wait_recv()
            for copy in copies(stage):
                copy.start()

        return task

    def last():
        for copy in copies(2):
            copy.wait_recv()
        for stage in range(3):
            for copy in copies(stage):
                copy.wait_send()

    return stage_task(0), stage_task(1), stage_task(2), last


def gather_weights(
    n,
    x,
    gain,
    w_in,
    w_gate,
    w_out,
    blocks,
    chan,
    order,
    lengths,
    cotangent,
    mask,
    whole,
    all_in,
    all_gate,
    all_out,
    all_blocks,
    all_chan,
    ocol,
    orow,
    pos,
    cot,
    cot_first,
    send,
    recv,
    raw,
    plane_send,
    plane_recv,
):
    line = Line(n, x.shape[0], None, None, whole, None, (send, recv))
    plane = Plane()
    line.greet(plane)
    sems = plane_send, plane_recv
    rows, piece = w_in.shape[0], blocks.shape[1]
    lines = chan.shape[0]

    def blocks_view(owner, half):
        return all_blocks.at[:, pl.ds(pl.multiple_of(owner * piece, TILE), piece)]

    def chan_view(owner, half):
        return raw.at[pl.ds(pl.multiple_of(owner * lines, TILE), lines)]

    items = [(row_view(array, rows), (0, 1)) for array in (all_in, all_gate, all_out)]
    items += [(blocks_view, (0,)), (chan_view, (1,))]

    first, second, third, finish = gather_tasks(plane, items, sems)

    def last():
        finish()
        lane = lax.broadcasted_iota(jnp.int32, (LANE, LANE), 1)
        row = lax.broadcasted_iota(jnp.int32, (LANE, LANE), 0)
        total = jnp.zeros((lines, LANE), f32)
        for owner in range(LANE // piece):
            moved = ((row < piece) & (row + owner * piece == lane)).astype(f32).astype(bf16)
            total = total + dot(raw[pl.ds(owner * lines, lines), :], moved)
        for h in range(lines // SUB):
            par = total[h * SUB : (h + 1) * SUB]
            lanes = pl.ds(h * LANE, LANE)
            all_chan[0:SUB, lanes] = par
            decay = par[SUB - 1 : SUB]
            small = jnp.exp(-jnp.abs(decay))
            one_more = 1.0 + small
            rest = jnp.where(one_more == 1.0, 1.0, one_more - 1.0)
            log_one_more = jnp.where(one_more == 1.0, small, jnp.log(one_more) * (small / rest))
            all_chan[SUB - 1 : SUB, lanes] = jnp.maximum(decay, 0.0) + log_one_more
            all_chan[SUB : 2 * SUB, lanes] = jnp.broadcast_to(sigmoid(decay), (SUB, LANE))

    own = pl.ds(pl.multiple_of(plane.me * rows, TILE), rows)
    all_in[own, :] = w_in[...]
    all_gate[own, :] = w_gate[...]
    all_out[own, :] = w_out[...]
    all_blocks[:, pl.ds(pl.multiple_of(plane.me * piece, TILE), piece), :] = blocks[...]
    raw[pl.ds(pl.multiple_of(plane.me * lines, TILE), lines), :] = chan[...]

    def point(k):
        def one(_, own, at):
            v = x[own, :].astype(f32)
            whole[at, :] = (v * rms_scale(v) * gain[...]).astype(bf16)

        line.tiles(k, one)

    def indices():
        count = whole.shape[0]
        steps = count // SUB
        tokens = order[...].astype(f32)
        across = lax.broadcasted_iota(jnp.int32, (ROWS, count), 1)
        line_total = jnp.zeros((1, count), f32)
        for b in range(count // ROWS):
            row = lax.broadcasted_iota(jnp.int32, (ROWS, 1), 0) + b * ROWS
            token = lax.rem(row, SUB) * steps + lax.div(row, SUB)
            picked = jnp.sum(jnp.where(across == token, tokens, 0.0), axis=1, keepdims=True)
            ocol[pl.ds(b * ROWS, ROWS), :] = picked.astype(jnp.int32)
            line_total += jnp.sum(jnp.where(across == row, picked, 0.0), axis=0, keepdims=True)
        orow[...] = line_total.astype(jnp.int32)
        row = lax.broadcasted_iota(jnp.int32, pos.shape, 0)
        token = lax.rem(row, SUB) * steps + lax.div(row, SUB)
        start, own_start = jnp.zeros((1, 1), jnp.int32), jnp.zeros(pos.shape, jnp.int32)
        for k in range(lengths.shape[1]):
            own_start = jnp.where(token >= start, start, own_start)
            start = start + lengths[:, k : k + 1]
        pos[...] = jnp.where(token >= count, -1, token - own_start)

    def masked():
        count = cotangent.shape[0]
        row = lax.broadcasted_iota(jnp.int32, (count, count), 0)
        column = lax.broadcasted_iota(jnp.int32, (count, count), 1)
        kept = jnp.where(row == column, mask[...].astype(f32), 0.0)
        kept = jnp.sum(kept, axis=1, keepdims=True)
        value = (cotangent[...].astype(f32) * kept).astype(bf16)
        cot[...] = value
        cot_first[...] = value[:, : cot_first.shape[1]]

    first()
    line.run(point, [idle] * 4 + [second, indices, masked, idle, third] + [idle] * 3 + [last])


def norm_back(value, gain, grad):
    scale = rms_scale(value)
    e = gain * grad
    slope = scale * scale * scale * jnp.mean(value * e, axis=-1, keepdims=True)
    return scale * e - value * slope, grad * value * scale


def middle(n, x, gain, cot, part, *rest):
    (*shares, cot_first), rest = rest[:4], rest[4:]
    grads = len(rest) > 45 and 2 or 0
    (d_resid, gain_grad, back, high_sum), rest = rest[:4], rest[4:]
    weight_grads, far, rest = rest[:grads], rest[grads : grads + 7], rest[grads + 7 :]
    left, right, total, ss, sr, send, recv, part2, ss2, sr2, send2, recv2, csend, crecv, *rest = rest
    up_s, value_s, grad_s, high_part, left3, right3, total3, ss3, sr3, cot_sem, *rest = rest
    *rest, held_sem = rest
    near, rest = rest[-7:], rest[:-7]
    whole, cots, resid, hidden, d_up, d_gate, low_part = near
    plane = Plane() if rest else None
    w_up, w_gate, w_down = weights = rest[:3] if rest else shares

    def whole_of(weight):
        return weight[...].reshape(-1, weight.shape[-1])

    local = x.shape[0]
    line = Line(n, local, part, (left, right), whole, (ss, sr), (send, recv))
    back_line = Line(n, local, part2, (left, right), back, (ss2, sr2), (send2, recv2))
    early = cot_first.shape[1]
    later = pl.ds(early, cot.shape[1] - early)
    cot_line = Line(n, local, None, None, cots.at[:, later], None, (csend, crecv))
    high_line = Line(n, local, high_part, (left3, right3), None, (ss3, sr3), None)
    line.greet(plane)
    arriving = pltpu.make_async_copy(cot_first, cots.at[:, pl.ds(0, early)], cot_sem)
    arriving.start()
    gain_grad[...] = jnp.zeros_like(gain_grad)
    leaving = [
        pltpu.make_async_copy(source, target, held_sem.at[i])
        for i, (source, target) in enumerate(zip(near, far))
    ]

    def keep_cot(_, own, at):
        cots[at, later] = cot[own, later]

    def point(k):
        line.total(k, total)

        def one(here, own, at):
            v = x[own, :].astype(f32) + total[here, :]
            resid[own, :] = v
            whole[at, :] = (v * rms_scale(v) * gain[...]).astype(bf16)

        line.tiles(k, one)

    def back_point(k):
        back_line.total(k, total)

        def one(here, own, at):
            grad, terms = norm_back(resid[own, :], gain[...], total[here, :])
            gain_grad[...] += jnp.sum(terms, axis=0, keepdims=True)
            value = cot[own, :].astype(f32) + grad
            d_resid[own, :] = value
            back[at, :] = value.astype(bf16)

        line.tiles(k, one)

    def high_point(k):
        high_line.total(k, total3)
        first, rows = line.pieces[k]
        high_sum[pl.ds(first, rows), :] = total3[pl.ds(0, rows), :].astype(bf16)

    def pair_steps(j):
        first = line.pieces[2 * j][0]
        rows = line.pieces[2 * j][1] + line.pieces[2 * j + 1][1]
        at = [pl.ds(owner * local + first, rows) for owner in range(n)]
        here = pl.ds(0, n * rows)

        def read(array):
            return jnp.concatenate([array[rows_at, :] for rows_at in at], axis=0)

        def write(array, value):
            for owner, rows_at in enumerate(at):
                array[rows_at, :] = value[owner * rows : (owner + 1) * rows]

        def up():
            up_s[here, :] = dot(read(whole), whole_of(w_up))

        def gate():
            value, slope = gelu_both(dot(read(whole), whole_of(w_gate)))
            write(hidden, (value * up_s[here, :]).astype(bf16))
            value_s[here, :] = value
            up_s[here, :] = up_s[here, :] * slope

        def into_hidden():
            d_hidden = dot(read(cots), whole_of(w_down))
            write(d_up, (d_hidden * value_s[here, :]).astype(bf16))
            write(d_gate, (d_hidden * up_s[here, :]).astype(bf16))

        def through_up():
            grad_s[here, :] = dot_last(read(d_up), whole_of(w_up))

        def through_gate():
            write(part2, (grad_s[here, :] + dot_last(read(d_gate), whole_of(w_gate))).astype(bf16))

        def project():
            value = dot_last(read(hidden), whole_of(w_down)).astype(bf16)
            write(low_part, value[:, : low_part.shape[1]])
            write(high_part, value[:, low_part.shape[1] :])

        return up, gate, into_hidden, through_up, through_gate, project

    hops = n - 1
    slots = [[] for _ in range(PIECES + 5 * hops)]

    def put(slot, order, work, *args):
        slots[slot].append((order, functools.partial(work, *args)))

    for k in range(PIECES):
        put(k, 0, line.first, k)
        for stage in range(1, hops):
            put(k + stage, 2, line.relay, k, stage)
        met = k + hops
        put(met, 3, line.sent, k)
        put(met, 3, point, k)
        put(met, 3, line.spread, k)
        given = max(k - 2, 0) if 2 * k <= PIECES else min(2 * k - 3, PIECES + 2)
        put(given, 0, cot_line.tiles, k, keep_cot)
        put(given, 0, cot_line.spread, k)
        for stage in range(1, n):
            put(met + stage, 5, line.forward, k, stage)
            put(given + stage, 5, cot_line.forward, k, stage)
    for j in range(PIECES // 2):
        slot = 2 * j + 2 + 2 * hops
        steps = pair_steps(j)
        for at, order, step in zip((0, 0, 0, 1, 1, 1), (0.5, 1.5, 2.5, 0.5, 1.5, 3.5), steps):
            put(slot + at, order, step)
        for k in (2 * j, 2 * j + 1):
            begun = slot + 1 + k % 2
            put(begun, 2 if begun == slot + 1 else 0, back_line.first, k)
            for stage in range(1, hops):
                put(begun + stage, 2, back_line.relay, k, stage)
            put(begun + hops, 3, back_line.sent, k)
            put(begun + hops, 3, back_point, k)
            put(begun + hops, 3, back_line.spread, k)
            for stage in range(1, n):
                put(begun + hops + stage, 5, back_line.forward, k, stage)
            begun += hops
            put(begun, 4, high_line.first, k)
            for stage in range(1, hops):
                put(begun + stage, 4, high_line.relay, k, stage)
            put(begun + hops, 4, high_line.sent, k)
            put(begun + hops, 4, high_point, k)
    put(2 * hops + 2, 0, arriving.wait)
    done = PIECES + 2 * hops + 2
    for copy in leaving:
        put(done, 0, copy.start)
    if plane is not None:
        *plane_sems, wide_send, wide_recv, free = rest[3:]
        half_rows = shares[0].shape[0] // 2
        for share, array in zip(shares, weights):
            array[plane.me] = share[...]

        def weight_view(array):
            return lambda owner, half: array.at[owner, pl.ds(half * half_rows, half_rows)]

        items = [(weight_view(array), (0, 1)) for array in weights]
        stages = gather_tasks(plane, items, plane_sems)
        for slot, stage in zip((0, 3, 6, 2 * hops + 2), stages):
            put(slot, 0, stage)

        def leave_weights():
            for bit in plane.bits:
                pl.semaphore_signal(
                    free, inc=1, device_id={"dp": plane.other(bit)}, device_id_type=MESH
                )

        sent = []
        tokens = Here(whole)
        tasks, end = reduce_tasks(
            [
                Reduce(
                    i,
                    tokens,
                    Here(right),
                    slice(None),
                    sent,
                    *blocks_views(i, both, w_down),
                    out,
                    (wide_send, wide_recv),
                )
                for i, (right, both, out) in enumerate(
                    zip((d_up, d_gate), (w_up, w_gate), weight_grads)
                )
            ]
        )
        put(done - 1, 4, leave_weights)
        put(done, 0, pl.semaphore_wait, free, len(plane.bits))
        at = [(slot, order) for slot in range(done, len(slots)) for order in (0.5, 2.5, 3.5)]
        for (slot, order), task in zip(at, tasks):
            put(slot, order, task)
        rest_tasks = tasks[len(at) :]
    else:
        rest_tasks = []
    for slot in slots:
        for _, work in sorted(slot, key=lambda entry: entry[0]):
            work()
    for task in rest_tasks:
        task()
    for each in (line, back_line, cot_line):
        each.finish()
    if plane is not None:
        end()
    for copy in leaving:
        copy.wait()


def sum_back(n, x, d_resid, gain, part, *rest):
    if len(rest) > 6:
        little, gains, *rest = rest
        sources, rest = rest[:6], rest[6:]
        grad_x, *outs, little_out, gains_out = rest[:7]
        left, right, total, ss, sr, *reduce = rest[7:]
        wide, late_refs, late_sems = reduce[22:29], reduce[29:35], reduce[35]
        given = [
            Given(little, *reduce[7:11], little_out, reduce[11:13]),
            Given(gains, *reduce[13:17], gains_out, reduce[17:19]),
        ]
        met, met_send, met_recv = reduce[19:22]
    else:
        grad_x, left, right, total, ss, sr = rest
        sources = ()
    line = Line(n, x.shape[0], part, (left, right), None, (ss, sr), None)
    line.greet(Plane() if sources else None)

    def point(k):
        line.total(k, total)

        def one(here, own, at):
            back, _ = norm_back(x[own, :].astype(f32), gain[...], total[here, :])
            grad_x[own, :] = (d_resid[own, :] + back).astype(bf16)

        line.tiles(k, one)

    if not sources:
        line.run(point)
        return
    width = sources[5].shape[1]
    cots, hidden, norm, back_all, cat, mixed = late_all(sources, late_refs, late_sems)
    every, sent, sent_wide = slice(None), [], []
    wide_sides = ((cots, hidden, every),)
    sides = (
        (norm, cat, slice(0, width)),
        (norm, cat, slice(width, 2 * width)),
        (back_all, mixed, every),
    )
    parts = [
        Reduce(i, *side, sent_wide, *views(i, *wide[:5]), out, wide[5:7])
        for i, (side, out) in enumerate(zip(wide_sides, outs))
    ]
    parts += [
        Reduce(i, *side, sent, *views(i, *reduce[:5]), out, reduce[5:7])
        for i, (side, out) in enumerate(zip(sides, outs[1:]))
    ]
    tasks, finish = reduce_tasks(parts, given)

    me = lax.axis_index("mp")

    def meet(away):
        return pltpu.make_async_remote_copy(
            src_ref=gains_out,
            dst_ref=met.at[away - 1],
            send_sem=met_send.at[away - 1],
            recv_sem=met_recv.at[away - 1],
            device_id={"mp": lax.rem(me + away, n)},
            device_id_type=MESH,
        )

    def send_gains():
        for away in range(1, n):
            meet(away).start()

    def add_gains():
        for away in range(1, n):
            meet(away).wait()
        gains_out[...] += sum(met[away] for away in range(n - 1))

    tasks[7:7] = [send_gains]
    line.run(point, tasks)
    finish()
    add_gains()


def line_call(body, n, identity, outs, sums, alls, args, more=(), late=0, held=0):
    whole = pl.BlockSpec(memory_space=pltpu.VMEM)
    local, model = args[0].shape
    sem = pltpu.SemaphoreType.DMA((2, n, PIECES))
    scratch = []
    if sums:
        scratch += [pltpu.VMEM((n * local, model), bf16)] * 2
        scratch += [pltpu.VMEM((max(rows for _, rows in cut_rows(local, PIECES)), model), f32)]
        scratch += [sem, sem]
    if alls:
        scratch += [sem, sem]
    scratch += more
    if held:
        scratch += [pltpu.VMEM(o.shape, o.dtype) for o in outs[len(outs) - held :]]
        scratch += [pltpu.SemaphoreType.DMA((held,))]
    away = pl.BlockSpec(memory_space=pl.ANY)
    moved = sum(a.size * a.dtype.itemsize for a in args)
    return pl.pallas_call(
        functools.partial(body, n),
        out_shape=outs,
        in_specs=[whole] * (len(args) - late) + [away] * late,
        out_specs=[whole] * (len(outs) - held) + [away] * held,
        scratch_shapes=scratch,
        compiler_params=pltpu.CompilerParams(
            vmem_limit_bytes=VMEM_MB << 20, collective_id=identity, has_side_effects=True
        ),
        cost_estimate=pl.CostEstimate(flops=0, bytes_accessed=100 * moved, transcendentals=0),
    )(*args)


def finish(heads, piece, share, resid, low, high, gains, little, *rest):
    count = (len(rest) - 6) // 2
    sources, rest = rest[:count], rest[count:]
    output, grad_gains, grad_conv, grad_bias, grad_decay, grad_blocks, *targets = rest
    for source, target in zip(sources, targets):
        target[...] = source[...]
    half = low.shape[1]
    output[:, :half] = (resid[:, :half] + low[...].astype(f32)).astype(bf16)
    output[:, half:] = (resid[:, half:] + high[...].astype(f32)).astype(bf16)
    for position in range(gains.shape[0] // 2):

        @pl.when(lax.axis_index("mp") == position)
        def _():
            grad_gains[...] = gains[2 * position : 2 * position + 2, :share]

    for h in range(heads):
        for gate in range(2):
            first = (2 * h + gate) * LANE
            grad_blocks[gate, h] = little[:, first : first + LANE]
    first = 2 * heads * LANE
    lines = little[:, first : first + LANE]
    lines = jnp.concatenate([lines, jnp.zeros((LANE - piece, LANE), f32)], axis=0).T
    for h in range(heads):
        for k in range(SUB):
            row = lines[h * SUB + k : h * SUB + k + 1, :piece]
            if k < 4:
                grad_conv[k, h : h + 1, :] = row
            elif k < SUB - 1:
                grad_bias[k - 4, h : h + 1, :] = row
            else:
                grad_decay[h : h + 1, :] = row


def local_call(body, outs, scratch, flops, args, late=0, held=0):
    whole, away = pl.BlockSpec(memory_space=pltpu.VMEM), pl.BlockSpec(memory_space=pl.ANY)
    twins = list(args[len(args) - late :]) + list(outs[len(outs) - held :])
    scratch = scratch + [pltpu.VMEM(a.shape, a.dtype) for a in twins]
    if late:
        scratch.append(pltpu.SemaphoreType.DMA((late,)))
    if held:
        scratch.append(pltpu.SemaphoreType.DMA((held, 4)))
    moved = sum(a.size * a.dtype.itemsize for a in args)
    moved += sum(o.size * o.dtype.itemsize for o in outs)
    return pl.pallas_call(
        body,
        out_shape=outs,
        in_specs=[whole] * (len(args) - late) + [away] * late,
        out_specs=[whole] * (len(outs) - held) + [away] * held,
        scratch_shapes=scratch,
        compiler_params=pltpu.CompilerParams(vmem_limit_bytes=VMEM_MB << 20),
        cost_estimate=pl.CostEstimate(flops=flops, bytes_accessed=moved, transcendentals=0),
    )(*args)


def shape_of(dtype, *shape):
    return jax.ShapeDtypeStruct(shape, dtype)


def shards(
    inputs,
    cotangent,
    token_mask,
    order,
    lengths,
    gains,
    w_in,
    w_gate,
    w_out,
    conv_weight,
    chan_bias,
    decay,
    gate_blocks,
    w_up,
    w_gate_ff,
    w_down,
):
    n_dp = lax.axis_size("dp")
    local_rows, model = inputs.shape
    count = local_rows * lax.axis_size("mp")
    heads, piece = decay.shape
    width = heads * piece * n_dp
    hidden_width = w_up.shape[1]

    fused = n_dp == 8
    rows = model // n_dp
    out_rows, down_rows = w_out.T, w_down.T
    lines = jnp.concatenate([conv_weight, chan_bias, decay[None]], axis=0).transpose(1, 0, 2)
    lines = lines.reshape(SUB * heads, piece)

    gain_f = gains.astype(f32)
    n_mp = lax.axis_size("mp")
    tok = shape_of(bf16, count, model)
    own = shape_of(f32, local_rows, model)
    if fused:
        grown = shape_of(bf16, model, width)
        norm_group, full_in, full_gate, full_out, blocks, chan, ocol, orow, pos_col, cot, cot_first = (
            line_call(
            gather_weights,
            n_mp,
            0,
            [tok, grown, grown, grown, shape_of(bf16, 2 * heads, LANE, LANE), shape_of(f32, 16, width)]
            + [shape_of(jnp.int32, *at) for at in ((count, 1), (1, count), (count + TAIL, 1))]
            + [shape_of(bf16, local_rows, model), shape_of(bf16, local_rows, model // 3)],
            False,
            True,
            (
                inputs,
                gain_f[0:1],
                w_in,
                w_gate,
                out_rows,
                gate_blocks.reshape(2 * heads, piece, LANE),
                jnp.pad(lines, ((0, 0), (0, LANE - piece))),
                order,
                lengths,
                cotangent,
                token_mask.reshape(1, -1),
            ),
            [pltpu.VMEM((n_dp * SUB * heads, LANE), bf16)] + [pltpu.SemaphoreType.DMA((5, 2, 7))] * 2,
        )
        )
    else:
        steps = count // SUB
        ends = jnp.cumsum(lengths[0], dtype=jnp.int32)
        starts = ends - lengths[0]
        places = jnp.arange(count, dtype=jnp.int32)
        own_start = jnp.max(
            jnp.where(places[:, None] >= starts[None, :], starts[None, :], 0), axis=1
        )
        pos = (places - own_start).reshape(SUB, steps).T
        wrap = jnp.concatenate([pos[: TAIL // SUB, 1:], jnp.full((TAIL // SUB, 1), -1, jnp.int32)], axis=1)
        pos_col = jnp.concatenate([pos, wrap], axis=0).reshape(count + TAIL, 1)
        order_int = order[0].reshape(SUB, steps).T.reshape(count)
        ocol, orow = order_int.reshape(count, 1), order_int.reshape(1, count)
        (norm_group,) = line_call(gather_norm, n_mp, 0, [tok], False, True, (inputs, gain_f[0:1]))
        full_in = lax.all_gather(w_in, "dp", axis=0, tiled=True)
        full_gate = lax.all_gather(w_gate, "dp", axis=0, tiled=True)
        full_out = lax.all_gather(out_rows, "dp", axis=0, tiled=True)
        blocks = lax.all_gather(gate_blocks, "dp", axis=2, tiled=True).reshape(2 * heads, LANE, LANE)
        params = lax.all_gather(lines, "dp", axis=1, tiled=True).astype(f32)
        params = params.reshape(heads, SUB, LANE).transpose(1, 0, 2).reshape(SUB, width)
        decay_row = params[7:8]
        chan = jnp.concatenate(
            [params[:7], jax.nn.softplus(decay_row)] + [jax.nn.sigmoid(decay_row)] * SUB, axis=0
        )

    if not fused:
        cot = cotangent * token_mask.astype(bf16)[:, None]
        cot_first = cot[:, : model // 3]
    cot_first = lax.all_gather(cot_first, "mp", axis=0, tiled=True)

    wide = pltpu.VMEM((count, width), f32)
    saved = [shape_of(f32, count, width)] * 6
    gate_pre, branch, conv, gate_in, gate_rec, state, mixed, back_part = local_call(
        mixer_forward,
        saved + [shape_of(bf16, count, width), shape_of(bf16, count, model)],
        [
            pltpu.VMEM((ROWS, model), bf16),
            wide,
            wide,
            pltpu.VMEM((ROWS + TAIL, width), f32),
            pltpu.VMEM((count, width), bf16),
        ],
        2 * count * (count * model + 3 * model * width),
        (norm_group, ocol, orow, pos_col, full_in, full_gate, chan, blocks, full_out),
        1,
        8,
    )
    shares = (w_up, w_gate_ff, down_rows)
    if not fused:
        shares = [lax.all_gather(share, "dp", axis=0, tiled=True) for share in shares]
    hid = shape_of(bf16, count, hidden_width)
    low_width = model * 5 // 12
    low_shape = shape_of(bf16, count, low_width)
    high_twin = pltpu.VMEM((count, model - low_width), bf16)
    pieces = cut_rows(local_rows, PIECES)
    most = n_mp * max(pieces[k][1] + pieces[k + 1][1] for k in range(0, PIECES, 2))
    pair = pltpu.VMEM((most, hidden_width), f32)
    flow = pltpu.SemaphoreType.DMA((2, n_mp, PIECES))
    plane_scratch = [pltpu.VMEM((n_dp, rows, hidden_width), bf16)] * 3
    plane_scratch += [pltpu.SemaphoreType.DMA((3, 2, 7))] * 2 + [pltpu.SemaphoreType.DMA((2, 10))] * 2
    plane_scratch += [pltpu.SemaphoreType.REGULAR]
    (
        d_resid,
        gain_mid,
        back_group,
        ffn_high,
        *ffn_grads,
        norm_mid_group,
        cot_group,
        resid,
        hidden,
        d_up,
        d_gate_ff,
        ffn_part,
    ) = line_call(
        middle,
        n_mp,
        1,
        [own, shape_of(f32, 1, model), tok, shape_of(bf16, local_rows, model - low_width)]
        + [shape_of(f32, rows, hidden_width)] * (2 * fused)
        + [tok, tok, own, hid, hid, hid, low_shape],
        True,
        True,
        (inputs, gain_f[1:2], cot, back_part, *shares, cot_first),
        [pltpu.VMEM((count, model), bf16)]
        + [flow] * 6
        + [pair, pair, pltpu.VMEM((most, model), f32)]
        + [high_twin] * 3
        + [pltpu.VMEM((max(rows for _, rows in pieces), model - low_width), f32), flow, flow]
        + [pltpu.SemaphoreType.DMA(())]
        + plane_scratch * fused,
        late=1,
        held=7,
    )

    def reduced(left, right):
        grad = dot_first(left, right).astype(bf16)
        return lax.psum_scatter(grad, "dp", scatter_dimension=0, tiled=True).astype(f32)

    d_cat, d_norm_back, little, gain_in, *ffn_grads = local_call(
        mixer_backward,
        [
            shape_of(bf16, count, 2 * width),
            tok,
            shape_of(f32, LANE, 2 * width + LANE),
            shape_of(f32, 1, model),
        ]
        + [shape_of(f32, *a.shape) for a in ffn_grads],
        [
            pltpu.VMEM((count, width), bf16),
            wide,
            wide,
            wide,
            pltpu.VMEM((count + TAIL, width), f32),
            pltpu.VMEM((ROWS + TAIL, width), f32),
            pltpu.VMEM((count, 2 * width), bf16),
            pltpu.VMEM((SUB, width), f32),
            pltpu.VMEM((heads, LANE, 2 * LANE), f32),
        ],
        2 * count * (3 * count * width + 3 * model * width),
        (
            back_group,
            full_out,
            ocol,
            orow,
            pos_col,
            gain_f[0:1],
            chan,
            blocks,
            gate_pre,
            gate_rec,
            state,
            conv,
            gate_in,
            branch,
            norm_group,
            full_in,
            full_gate,
            *ffn_grads,
        ),
        9 + len(ffn_grads),
        len(ffn_grads),
    )
    share = model // (n_dp * n_mp)
    gain_parts = jnp.concatenate([gain_in, gain_mid], axis=0).reshape(2, n_dp, n_mp, share)
    gain_parts = gain_parts.transpose(1, 2, 0, 3).reshape(n_dp, 2 * n_mp, share)
    gain_parts = jnp.pad(gain_parts, ((0, 0), (0, 2 * SUB - 2 * n_mp), (0, LANE - share)))
    gain_parts = gain_parts.reshape(2 * SUB * n_dp, LANE)
    ffn_low = lax.psum_scatter(ffn_part, "mp", scatter_dimension=0, tiled=True)
    ffn_low, d_norm_back = lax.optimization_barrier((ffn_low, d_norm_back))
    grad_inputs, *mix_grads = line_call(
        sum_back,
        n_mp,
        3,
        [shape_of(bf16, local_rows, model)]
        + (
            [shape_of(f32, rows, hidden_width)]
            + [shape_of(f32, rows, width)] * 3
            + [shape_of(f32, piece, little.shape[1]), shape_of(f32, 2 * SUB, LANE)]
        )
        * fused,
        True,
        False,
        (inputs, d_resid, gain_f[0:1], d_norm_back)
        + (
            (
                little,
                gain_parts,
                cot_group,
                hidden,
                norm_group,
                back_group,
                d_cat,
                mixed,
            )
            if fused
            else ()
        ),
        reduce_scratch(3, rows, width)
        + given_scratch(piece, little.shape[1])
        + given_scratch(2 * SUB, LANE)
        + [pltpu.VMEM((n_mp - 1, 2 * SUB, LANE), f32)]
        + [pltpu.SemaphoreType.DMA((n_mp - 1,))] * 2
        + reduce_scratch(1, rows, hidden_width)
        + [pltpu.VMEM(a.shape, a.dtype) for a in (cot_group, hidden, norm_group, back_group, d_cat, mixed)]
        + [pltpu.SemaphoreType.DMA((6,))]
        if fused
        else (),
        6 * fused,
    )
    if fused:
        up_grad, gate_ff_grad = ffn_grads
        down_grad, *mix_grads, little_own, gain_own = mix_grads
    else:
        up_grad = reduced(norm_mid_group, d_up)
        gate_ff_grad = reduced(norm_mid_group, d_gate_ff)
        down_grad = reduced(cot_group, hidden)
        mix_grads = [
            reduced(norm_group, d_cat[:, :width]),
            reduced(norm_group, d_cat[:, width:]),
            reduced(back_group, mixed),
        ]
        little_own = lax.psum_scatter(little, "dp", scatter_dimension=0, tiled=True)
        gain_own = lax.psum(lax.psum_scatter(gain_parts, "dp", scatter_dimension=0, tiled=True), "mp")
    outs = [
        shape_of(bf16, local_rows, model),
        shape_of(f32, 2, share),
        shape_of(f32, 4, heads, piece),
        shape_of(f32, 3, heads, piece),
        shape_of(f32, heads, piece),
        shape_of(f32, 2, heads, piece, LANE),
    ]
    copied = [grad_inputs, mix_grads[0], mix_grads[1]] if fused else []
    output, grad_gains, grad_conv, grad_bias, grad_decay, grad_blocks, *copied = local_call(
        functools.partial(finish, heads, piece, share),
        outs + [shape_of(a.dtype, *a.shape) for a in copied],
        [],
        0,
        (resid, ffn_low, ffn_high, gain_own, little_own, *copied),
    )
    if fused:
        grad_inputs, grad_in, grad_gate = copied
    else:
        grad_in, grad_gate, _ = mix_grads
    return (
        output,
        grad_inputs,
        grad_gains,
        grad_in,
        grad_gate,
        mix_grads[2].T,
        grad_conv,
        grad_bias,
        grad_decay,
        grad_blocks,
        up_grad,
        gate_ff_grad,
        down_grad.T,
    )


def solution(mesh):
    row, col = P("dp", "mp"), P("mp", "dp")
    tok = P(("dp", "mp"), None)
    chan = P(None, "mp", "dp")
    gate = P(None, "mp", "dp", None)
    return jax.shard_map(
        shards,
        mesh=mesh,
        in_specs=(
            tok, tok, P(("dp", "mp")), P("dp", None), P("dp", None), P(),
            row, row, col, chan, chan, col, gate, row, row, col,
        ),
        out_specs=(
            tok, tok, P(None, ("dp", "mp")), row, row, col, chan, chan, col, gate, row, row, col,
        ),
        check_vma=False,
    )
```

```python
import functools

import jax
import jax.numpy as jnp
from jax import lax
from jax.experimental import pallas as pl
from jax.experimental.pallas import tpu as pltpu
from jax.sharding import PartitionSpec as P

epsilon = 1e-06
LANE = 128
SUB = 8
TAIL = 24
ROWS = 272
VMEM_MB = 62
f32 = jnp.float32
bf16 = jnp.bfloat16
GELU_C = 0.7978845608028654
GELU_A = 0.044715


def rms_scale(values):
    return lax.rsqrt(jnp.mean(values * values, axis=-1, keepdims=True) + epsilon)


def dot(left, right):
    return lax.dot_general(left, right, (((1,), (0,)), ((), ())), preferred_element_type=f32)


def dot_last(left, right):
    return lax.dot_general(left, right, (((1,), (1,)), ((), ())), preferred_element_type=f32)


def dot_first(left, right):
    return lax.dot_general(left, right, (((0,), (0,)), ((), ())), preferred_element_type=f32)


def gelu_of(v):
    return 0.5 * v * (1.0 + jnp.tanh(GELU_C * (v + GELU_A * v * v * v)))


def gelu_both(v):
    square = v * v
    th = jnp.tanh(GELU_C * (v + GELU_A * v * square))
    half = 0.5 * (1.0 + th)
    slope = half + 0.5 * v * (1.0 - th * th) * (GELU_C * (1.0 + 3.0 * GELU_A * square))
    return v * half, slope


def sigmoid(v):
    return 0.5 * jnp.tanh(0.5 * v) + 0.5


def split(values):
    high = values.astype(bf16)
    return high, (values - high.astype(f32)).astype(bf16)


def rows_of(index, rows):
    return pl.ds(pl.multiple_of(index * rows, rows), rows)


def pick_rows(order_col, count):
    places = lax.broadcasted_iota(jnp.int32, (order_col.shape[0], count), 1)
    return (places == order_col).astype(f32).astype(bf16)


def put_rows(order_row, first, rows):
    places = lax.broadcasted_iota(jnp.int32, (rows, order_row.shape[1]), 0) + first
    return (places == order_row).astype(f32).astype(bf16)


def mixer_forward(tokens, ocol, orow, pos, w_in, w_gate, chan, blocks, w_out_far, *rest):
    far, rest = rest[:8], rest[8:]
    packed, rate, prod, before, low, w_out, *near, late_sem, held_sem = rest
    gate_ref, branch_ref, conv_ref, gin_ref, grec_ref, state_ref, mixed_ref, out_ref = near
    (late_out,) = late_all([w_out_far], [w_out], late_sem)
    leaving = [
        pltpu.make_async_copy(source, target, held_sem.at[i, 0])
        for i, (source, target) in enumerate(zip(near, far))
    ]
    count, _ = tokens.shape
    width = w_in.shape[1]
    steps = count // SUB
    heads = width // LANE

    def project(b, carry):
        at = rows_of(b, ROWS)
        packed[...] = dot(pick_rows(ocol[at, :], count), tokens[...]).astype(bf16)
        branch_ref[at, :] = dot(packed[...], w_in[...])
        gate_ref[at, :] = dot(packed[...], w_gate[...])
        return carry

    lax.fori_loop(0, count // ROWS, project, 0)
    leaving[0].start()
    leaving[1].start()

    for k in range(TAIL // SUB):
        last = branch_ref[pl.ds(count - TAIL + k * SUB, SUB), :]
        before[pl.ds(k * SUB, SUB), :] = pltpu.roll(last, 1, 0)
    before[pl.ds(TAIL, ROWS), :] = branch_ref[pl.ds(0, ROWS), :]

    def gates(b, carry):
        at = rows_of(b, ROWS)

        @pl.when(b > 0)
        def _():
            before[...] = branch_ref[pl.ds(pl.multiple_of(b * ROWS - TAIL, SUB), ROWS + TAIL), :]

        place = pos[at, :]
        for h in range(heads):
            lanes = pl.ds(h * LANE, LANE)
            par = chan[:, lanes]
            conv = par[4:5] + par[0:1] * before[pl.ds(TAIL, ROWS), lanes]
            for k in range(1, 4):
                earlier = before[pl.ds(TAIL - SUB * k, ROWS), lanes]
                conv = conv + par[k : k + 1] * jnp.where(place >= k, earlier, 0.0)
            high, rest = split(conv)
            pair = jnp.concatenate([blocks[h], blocks[heads + h]], axis=1)
            pre = dot(
                jnp.concatenate([high, rest], axis=1), jnp.concatenate([pair, pair], axis=0)
            )
            gate_in = sigmoid(pre[:, :LANE] + par[5:6])
            gate_rec = sigmoid(pre[:, LANE:] + par[6:7])
            kept = jnp.exp(-8.0 * gate_rec * par[7:8])
            drive = jnp.sqrt(1.0 - kept * kept + 0.01) * gate_in * conv
            conv_ref[at, lanes] = conv
            gin_ref[at, lanes] = gate_in
            grec_ref[at, lanes] = gate_rec
            rate[at, lanes] = jnp.where(place >= 1, kept, 0.0)
            state_ref[at, lanes] = drive
        return carry

    lax.fori_loop(0, count // ROWS, gates, 0)
    for copy in leaving[2:5]:
        copy.start()

    def scan(i, carry):
        held, passed = carry
        at = rows_of(i, SUB)
        a = rate[at, :]
        held = a * held + state_ref[at, :]
        passed = a * passed
        state_ref[at, :] = held
        prod[at, :] = passed
        return held, passed

    ends = lax.fori_loop(
        0, steps, scan, (jnp.zeros((SUB, width), f32), jnp.ones((SUB, width), f32)), unroll=8
    )
    first = lax.broadcasted_iota(jnp.int32, (SUB, width), 0) == 0
    carry_in = jnp.zeros((SUB, width), f32)
    for _ in range(SUB - 1):
        carry_in = jnp.where(first, 0.0, pltpu.roll(ends[0] + ends[1] * carry_in, 1, 0))

    def finish(i, carry):
        at = rows_of(i, 2 * SUB)
        twice = jnp.concatenate([carry_in, carry_in], axis=0)
        value = state_ref[at, :] + prod[at, :] * twice
        state_ref[at, :] = value
        low[at, :] = (gelu_of(gate_ref[at, :]) * value).astype(bf16)
        return carry

    lax.fori_loop(0, steps // 2, finish, 0, unroll=2)
    leaving[5].start()
    late_out.ready()

    def leave(b, carry):
        at = rows_of(b, ROWS)
        mixed = dot(put_rows(orow[...], b * ROWS, ROWS), low[...]).astype(bf16)
        mixed_ref[at, :] = mixed
        out_ref[at, :] = dot_last(mixed, w_out[...]).astype(bf16)
        return carry

    lax.fori_loop(0, count // ROWS, leave, 0)
    for copy in leaving[6:]:
        copy.start()
    for copy in leaving:
        copy.wait()


def mixer_backward(back, w_out, ocol, orow, pos, gain, chan, blocks, *rest):
    more = 2 if len(rest) > 36 else 0
    far, rest = rest[: 9 + more], rest[9 + more :]
    (dcat_ref, dnorm_ref, little_ref, dgain_ref), rest = rest[:4], rest[4:]
    passed_on, rest = rest[:more], rest[more:]
    dmix_arr, dmix, adj, prod, after, before, low, small_ref, dblocks_ref, *rest = rest
    gate_ref, grec_ref, state_ref, conv_ref, gin_ref, branch_ref, norm, w_in, w_gate, *extra = rest[: 9 + more]
    late_sem = rest[9 + 2 * more]
    late = late_all(far, rest[: 9 + more], late_sem)
    leaving = [
        pltpu.make_async_copy(source, target, rest[-1].at[i, 0])
        for i, (source, target) in enumerate(zip(extra, passed_on))
    ]
    count, _ = back.shape
    width = w_in.shape[1]
    steps = count // SUB
    heads = width // LANE
    blocks_of = count // ROWS

    def enter(b, carry):
        at = rows_of(b, ROWS)
        dmix_arr[at, :] = dot(back[at, :], w_out[...]).astype(bf16)
        return carry

    lax.fori_loop(0, blocks_of, enter, 0)
    for array in late[:3]:
        array.ready()

    def pack(b, carry):
        at = rows_of(b, ROWS)
        d_mixed = dot(pick_rows(ocol[at, :], count), dmix_arr[...])
        value, slope = gelu_both(gate_ref[at, :])
        adj[at, :] = d_mixed * value
        low[at, pl.ds(width, width)] = (d_mixed * state_ref[at, :] * slope).astype(bf16)
        kept = jnp.exp(-8.0 * grec_ref[at, :] * chan[7:8, :])
        dmix[at, :] = jnp.where(pos[at, :] >= 1, kept, 0.0)
        return carry

    lax.fori_loop(0, blocks_of, pack, 0)
    for array in late:
        array.ready()
    for copy in leaving:
        copy.start()

    def scan(i, carry):
        held, passed, following = carry
        at = rows_of(steps - 1 - i, SUB)
        held = following * held + adj[at, :]
        passed = following * passed
        adj[at, :] = held
        prod[at, :] = passed
        return held, passed, dmix[at, :]

    last = lax.broadcasted_iota(jnp.int32, (SUB, width), 0) == SUB - 1
    wrapped = jnp.where(last, 0.0, pltpu.roll(dmix[pl.ds(0, SUB), :], SUB - 1, 0))
    ends = lax.fori_loop(
        0,
        steps,
        scan,
        (jnp.zeros((SUB, width), f32), jnp.ones((SUB, width), f32), wrapped),
        unroll=8,
    )
    carry_in = jnp.zeros((SUB, width), f32)
    for _ in range(SUB - 1):
        carry_in = jnp.where(last, 0.0, pltpu.roll(ends[0] + ends[1] * carry_in, SUB - 1, 0))

    small_ref[...] = jnp.zeros_like(small_ref)
    dblocks_ref[...] = jnp.zeros_like(dblocks_ref)
    first = lax.broadcasted_iota(jnp.int32, (SUB, width), 0) == 0
    state_last = state_ref[pl.ds(count - SUB, SUB), :]
    before[pl.ds(TAIL - SUB, SUB), :] = jnp.where(first, 0.0, pltpu.roll(state_last, 1, 0))
    before[pl.ds(TAIL, ROWS), :] = state_ref[pl.ds(0, ROWS), :]
    wide_carry = jnp.concatenate([carry_in] * (ROWS // SUB), axis=0)

    def point(b, carry):
        at = rows_of(b, ROWS)

        @pl.when(b > 0)
        def _():
            before[...] = state_ref[pl.ds(pl.multiple_of(b * ROWS - TAIL, SUB), ROWS + TAIL), :]

        place = pos[at, :]
        for h in range(heads):
            lanes = pl.ds(h * LANE, LANE)
            par = chan[:, lanes]
            adjoint = adj[at, lanes] + prod[at, lanes] * wide_carry[:, h * LANE : (h + 1) * LANE]
            conv = conv_ref[at, lanes]
            gate_in = gin_ref[at, lanes]
            gate_rec = grec_ref[at, lanes]
            kept = jnp.exp(-8.0 * gate_rec * par[7:8])
            square = kept * kept
            inside = 1.0 - square + 0.01
            inverse = lax.rsqrt(inside)
            root = inside * inverse
            previous = before[pl.ds(TAIL - SUB, ROWS), lanes]
            d_log = adjoint * previous * dmix[at, lanes]
            scaled = adjoint * gate_in
            d_log = d_log - scaled * conv * square * inverse
            d_in = adjoint * root * conv * gate_in * (1.0 - gate_in)
            d_rec = d_log * (-8.0 * par[7:8]) * gate_rec * (1.0 - gate_rec)
            both = jnp.concatenate([d_in, d_rec], axis=1)
            high, rest = split(both)
            pair = jnp.concatenate([blocks[h], blocks[heads + h]], axis=1)
            d_conv = scaled * root + dot_last(high, pair) + dot_last(rest, pair)
            dblocks_ref[h] += dot_first(conv.astype(bf16), high)
            after[at, lanes] = d_conv
            small_ref[4:5, lanes] += jnp.sum(d_conv, axis=0, keepdims=True)
            small_ref[5:6, lanes] += jnp.sum(d_in, axis=0, keepdims=True)
            small_ref[6:7, lanes] += jnp.sum(d_rec, axis=0, keepdims=True)
            small_ref[7:8, lanes] += (
                jnp.sum(d_log * gate_rec, axis=0, keepdims=True) * (-8.0) * par[8:9]
            )
        return carry

    lax.fori_loop(0, blocks_of, point, 0)

    for k in range(TAIL // SUB):
        head = after[pl.ds(k * SUB, SUB), :]
        after[pl.ds(count + k * SUB, SUB), :] = pltpu.roll(head, SUB - 1, 0)
        tail = branch_ref[pl.ds(count - TAIL + k * SUB, SUB), :]
        before[pl.ds(k * SUB, SUB), :] = pltpu.roll(tail, 1, 0)
    before[pl.ds(TAIL, ROWS), :] = branch_ref[pl.ds(0, ROWS), :]

    def unmix(b, carry):
        at = rows_of(b, ROWS)

        @pl.when(b > 0)
        def _():
            before[...] = branch_ref[pl.ds(pl.multiple_of(b * ROWS - TAIL, SUB), ROWS + TAIL), :]

        place = pos[at, :]
        for h in range(heads):
            lanes = pl.ds(h * LANE, LANE)
            par = chan[:, lanes]
            d_conv = after[at, lanes]
            d_branch = par[0:1] * d_conv
            small_ref[0:1, lanes] += jnp.sum(
                d_conv * before[pl.ds(TAIL, ROWS), lanes], axis=0, keepdims=True
            )
            for k in range(1, 4):
                later = pl.ds(pl.multiple_of(b * ROWS + SUB * k, SUB), ROWS)
                d_branch = d_branch + par[k : k + 1] * jnp.where(
                    pos[later, :] >= k, after[later, lanes], 0.0
                )
                earlier = before[pl.ds(TAIL - SUB * k, ROWS), lanes]
                small_ref[k : k + 1, lanes] += jnp.sum(
                    jnp.where(place >= k, d_conv * earlier, 0.0), axis=0, keepdims=True
                )
            low[at, lanes] = d_branch.astype(bf16)
        return carry

    lax.fori_loop(0, blocks_of, unmix, 0)
    lines = [small_ref[0:SUB, h * LANE : (h + 1) * LANE] for h in range(heads)]
    lines.append(jnp.zeros((LANE - SUB * heads, LANE), f32))
    little_ref[:, pl.ds(2 * width, LANE)] = jnp.concatenate(lines, axis=0).T
    for h in range(heads):
        little_ref[:, pl.ds(2 * h * LANE, 2 * LANE)] = dblocks_ref[h]
    dgain_ref[...] = jnp.zeros_like(dgain_ref)

    def leave(b, carry):
        at = rows_of(b, ROWS)
        cat = dot(put_rows(orow[...], b * ROWS, ROWS), low[...]).astype(bf16)
        dcat_ref[at, :] = cat
        d_norm = dot_last(cat[:, :width], w_in[...]) + dot_last(cat[:, width:], w_gate[...])
        dgain_ref[...] += jnp.sum(d_norm * norm[at, :].astype(f32), axis=0, keepdims=True)
        dnorm_ref[at, :] = d_norm.astype(bf16)
        return carry

    lax.fori_loop(0, blocks_of, leave, 0)
    dgain_ref[...] = dgain_ref[...] / gain[...]
    for copy in leaving:
        copy.wait()


MESH = pl.DeviceIdType.MESH
TILE = 16
PIECES = 8
HOP = 1
AFTER = 1


def cut_rows(rows, parts):
    tiles = rows // TILE
    ends = [tiles * (k + 1) // parts for k in range(parts)]
    return [(TILE * a, TILE * (b - a)) for a, b in zip([0] + ends[:-1], ends)]


class Line:
    def __init__(self, n, local, part, arrived, whole, sums, alls):
        self.n, self.local, self.part, self.arrived, self.whole = n, local, part, arrived, whole
        self.sums, self.alls = sums, alls
        self.me = lax.axis_index("mp")
        self.pieces = cut_rows(local, PIECES)
        self.has = (self.me > 0, self.me < n - 1)

    def greet(self, plane=None):
        barrier = pltpu.get_barrier_semaphore()
        more = 0
        if plane is not None:
            for bit in plane.bits:
                more += 1
                pl.semaphore_signal(
                    barrier, inc=1, device_id={"dp": plane.other(bit)}, device_id_type=MESH
                )
        for away in range(1, self.n):
            more += 1
            pl.semaphore_signal(
                barrier,
                inc=1,
                device_id={"mp": lax.rem(self.me + away, self.n)},
                device_id_type=MESH,
            )
        pl.semaphore_wait(barrier, more)

    def rows_at(self, owner, k):
        first, rows = self.pieces[k]
        return pl.ds(pl.multiple_of(owner * self.local + first, TILE), rows)

    def copy(self, source, target, sems, way, owner, k):
        return pltpu.make_async_remote_copy(
            src_ref=source,
            dst_ref=target,
            send_sem=sems[0].at[way, owner, k],
            recv_sem=sems[1].at[way, owner, k],
            device_id={"mp": self.me + 1 - 2 * way},
            device_id_type=MESH,
        )

    def sum_copy(self, way, owner, k, first=False):
        at = self.rows_at(owner, k)
        landed = self.arrived[way].at[at]
        return self.copy(self.part.at[at] if first else landed, landed, self.sums, way, owner, k)

    def all_copy(self, way, owner, k):
        block = self.whole.at[self.rows_at(owner, k)]
        return self.copy(block, block, self.alls, way, owner, k)

    def first(self, k):
        for away in range(self.n - 1):
            for way in range(2):
                owner = away if way else self.n - 1 - away

                @pl.when(jnp.logical_not(self.has[way]))
                def _():
                    self.sum_copy(way, owner, k, True).start()

    def relay(self, k, stage):
        for way in range(2):
            late = stage - (self.n - 1 - self.me if way else self.me)
            owner = late if way else self.n - 1 - late

            @pl.when(self.has[way] & (late >= 0))
            def _():
                self.sum_copy(way, owner, k).wait_recv()
                at = self.rows_at(owner, k)
                landed = self.arrived[way]
                landed[at, :] = (landed[at, :].astype(f32) + self.part[at, :].astype(f32)).astype(bf16)
                self.sum_copy(way, owner, k).start()

    def total(self, k, into):
        at = self.rows_at(self.me, k)
        rows = pl.ds(0, self.pieces[k][1])
        into[rows, :] = self.part[at, :].astype(f32)
        for way in range(2):

            @pl.when(self.has[way])
            def _():
                self.sum_copy(way, self.me, k).wait_recv()
                into[rows, :] += self.arrived[way][at, :].astype(f32)

    def spread(self, k):
        for way in range(2):

            @pl.when(self.has[1 - way])
            def _():
                self.all_copy(way, self.me, k).start()

    def forward(self, k, stage):
        for way in range(2):
            owner = self.me + stage if way else self.me - stage
            there = owner < self.n if way else owner >= 0

            @pl.when(there)
            def _():
                self.all_copy(way, owner, k).wait_recv()

            @pl.when(there & self.has[1 - way])
            def _():
                self.all_copy(way, owner, k).start()

    def sent(self, k):
        for owner in range(self.n):
            for way in range(2):

                @pl.when(self.me > owner if way else self.me < owner)
                def _():
                    self.sum_copy(way, owner, k).wait_send()

    def finish(self):
        for k in range(PIECES):
            for owner in range(self.n):
                for way in range(2):
                    if self.whole is not None:
                        reached = self.me <= owner if way else self.me >= owner

                        @pl.when(reached & self.has[1 - way])
                        def _():
                            self.all_copy(way, owner, k).wait_send()

    def run(self, point, tasks=()):
        sums, alls = self.part is not None, self.whole is not None
        slots = [[] for _ in range(PIECES + (HOP + AFTER) * (self.n - 1) + 1)]
        for k in range(PIECES):
            done = k + HOP * (self.n - 1) if sums else 0
            if sums:
                slots[k].append((0, functools.partial(self.first, k)))
                for stage in range(1, self.n - 1):
                    slots[k + HOP * stage].append((2, functools.partial(self.relay, k, stage)))
                slots[done].append((3, functools.partial(self.sent, k)))
            slots[done].append((3, functools.partial(point, k)))
            if alls:
                slots[done].append((4, functools.partial(self.spread, k)))
                for stage in range(1, self.n):
                    at = (done if sums else k) + AFTER * stage
                    slots[at].append((1, functools.partial(self.forward, k, stage)))
        tasks = iter(tasks)
        for slot in slots:
            for step, (_, work) in enumerate(sorted(slot, key=lambda entry: entry[0])):
                if step in (0, 1, 3):
                    next(tasks, idle)()
                work()
        for task in tasks:
            task()
        self.finish()

    def tiles(self, k, body):
        first, rows = self.pieces[k]

        def one(i, carry):
            body(
                pl.ds(pl.multiple_of(i * TILE, TILE), TILE),
                pl.ds(pl.multiple_of(first + i * TILE, TILE), TILE),
                pl.ds(pl.multiple_of(self.me * self.local + first + i * TILE, TILE), TILE),
            )
            return carry

        lax.fori_loop(0, rows // TILE, one, 0)


def idle():
    pass


class Late:
    def __init__(self, source, ref, sem):
        self.ref = ref
        self.copy = pltpu.make_async_copy(source, ref, sem)
        self.pending = True

    def begin(self):
        self.copy.start()

    def ready(self):
        if self.pending:
            self.copy.wait()
        self.pending = False


class Here:
    def __init__(self, ref):
        self.ref = ref

    def ready(self):
        pass


def late_all(sources, refs, sems):
    arrays = [Late(source, ref, sems.at[i]) for i, (source, ref) in enumerate(zip(sources, refs))]
    for array in arrays:
        array.begin()
    return arrays


class Plane:
    bits = (1, 2, 4)
    orders = ((4, 2, 1), (2, 4, 1))

    def __init__(self):
        self.me = lax.axis_index("dp")

    def bit(self, bit):
        return lax.rem(self.me // bit, 2)

    def other(self, *bits):
        return self.me + sum(bit * (1 - 2 * self.bit(bit)) for bit in bits)

    def gather_copies(self, item, view, halves, stage, sems):
        copies = []
        for half in halves:
            order = self.orders[half]
            for combo in range(1 << stage):
                flipped = [bit for i, bit in enumerate(order[:stage]) if combo >> i & 1]
                block = view(self.other(*flipped), half)
                slot = (1 << stage) - 1 + combo
                copies.append(
                    pltpu.make_async_remote_copy(
                        src_ref=block,
                        dst_ref=block,
                        send_sem=sems[0].at[item, half, slot],
                        recv_sem=sems[1].at[item, half, slot],
                        device_id={"dp": self.other(order[stage])},
                        device_id_type=MESH,
                    )
                )
        return copies


class Reduce(Plane):
    def __init__(self, index, left, right, lanes, sent, mine, theirs, got, second, third, out, sems):
        super().__init__()
        self.sent, self.theirs = sent, theirs
        self.index, self.left, self.right, self.lanes = index, left, right, lanes
        self.mine, self.got = mine, got
        self.second, self.third, self.out = second, third, out
        self.sems = sems
        self.rows = out.shape[0]
        self.half = self.rows // 2

    def copy(self, source, target, slot, bit):
        return pltpu.make_async_remote_copy(
            src_ref=source,
            dst_ref=target,
            send_sem=self.sems[0].at[self.index, slot],
            recv_sem=self.sems[1].at[self.index, slot],
            device_id={"dp": self.other(bit)},
            device_id_type=MESH,
        )

    def core_copy(self, t):
        return self.copy(self.theirs.at[(4 * self.index + t) % 2], self.got.at[t], t, 1)

    def second_copy(self, half, j):
        x, y = self.bit(2), self.bit(4)
        block = (1 - y) * 2 + j if half else j * 2 + 1 - x
        rows = self.mine.at[block, pl.ds(half * self.half, self.half)]
        return self.copy(rows, self.second(half, j), 4 + 2 * half + j, 4 if half else 2)

    def third_block(self, half):
        x, y = self.bit(2), self.bit(4)
        return y * 2 + 1 - x if half else (1 - y) * 2 + x

    def third_copy(self, half):
        rows = self.mine.at[self.third_block(half), pl.ds(half * self.half, self.half)]
        return self.copy(rows, self.third(half), 8 + half, 2 if half else 4)

    def product(self, t):
        def task():
            core = self.bit(1)
            pair = pl.ds(t * 2 * self.rows, 2 * self.rows)
            if t == 0:
                self.left.ready()
                self.right.ready()
            if len(self.sent) > 1:
                self.sent[-2].wait_send()
            both = dot_first(self.left.ref[:, pair], self.right.ref[:, self.lanes])
            low, high = both[: self.rows], both[self.rows :]
            self.mine[t] = jnp.where(core == 0, low, high).astype(bf16)
            self.theirs[(4 * self.index + t) % 2] = jnp.where(core == 0, high, low).astype(bf16)
            self.sent.append(self.core_copy(t))
            self.sent[-1].start()

        return task

    def keep(self, t):
        return self.mine[t]

    def add_core(self):
        for t in range(4):
            self.core_copy(t).wait_recv()
            self.mine[t] = (self.keep(t).astype(f32) + self.got[t].astype(f32)).astype(self.mine.dtype)
        for half in range(2):
            for j in range(2):
                self.second_copy(half, j).start()

    def add_second(self):
        for half in range(2):
            for j in range(2):
                self.second_copy(half, j).wait_recv()
        for half in range(2):
            block, at = self.third_block(half), pl.ds(half * self.half, self.half)
            far = 1 - self.bit(2 if half else 4)
            self.mine[block, at] = (
                self.mine[block, at].astype(f32) + self.second(half, far)[...].astype(f32)
            ).astype(self.mine.dtype)
            self.third_copy(half).start()

    def add_third(self):
        own = self.bit(4) * 2 + self.bit(2)
        for half in range(2):
            self.third_copy(half).wait_recv()
            at = pl.ds(half * self.half, self.half)
            near = self.bit(2 if half else 4)
            self.out[at, :] = (
                self.mine[own, at].astype(f32)
                + self.second(half, near)[...].astype(f32)
                + self.third(half)[...].astype(f32)
            )

    def finish(self):
        for half in range(2):
            for j in range(2):
                self.second_copy(half, j).wait_send()
            self.third_copy(half).wait_send()


class Given(Reduce):
    def __init__(self, given, mine, got, second, third, out, sems):
        super().__init__(0, None, None, None, None, *views(0, mine, None, got, second, third), out, sems)
        self.given = given

    def rows_of(self, t, core):
        return pl.ds(pl.multiple_of((2 * t + core) * self.rows, self.rows), self.rows)

    def core_copy(self, t):
        return self.copy(self.given.at[self.rows_of(t, 1 - self.bit(1))], self.got.at[t], t, 1)

    def start(self):
        for t in range(4):
            self.core_copy(t).start()

    def finish(self):
        for t in range(4):
            self.core_copy(t).wait_send()
        super().finish()

    def keep(self, t):
        return self.given[self.rows_of(t, self.bit(1)), :]


def views(index, mine, theirs, got, second, third):
    return (
        mine.at[index],
        theirs,
        got.at[index],
        lambda half, j: second.at[index, half, j],
        lambda half: third.at[index, half],
    )


def blocks_views(index, both, spare):
    half_rows = spare.shape[1] // 2

    def halves(block, j):
        return spare.at[block, pl.ds(pl.multiple_of(j * half_rows, TILE), half_rows)]

    return (
        both.at[pl.ds(0, 4)],
        spare.at[pl.ds(6, 2)],
        both.at[pl.ds(4, 4)],
        lambda half, j: halves(3 * index + half, j),
        lambda half: halves(3 * index + 2, half),
    )


def reduce_tasks(parts, given=()):
    tasks = [part.product(t) for part in parts for t in range(4)]

    def also(at, extra):
        while len(tasks) <= at:
            tasks.append(idle)
        before = tasks[at]

        def both():
            extra()
            before()

        tasks[at] = both

    for i, part in enumerate(parts):
        also(4 * i + 5, part.add_core)
        also(4 * i + 8, part.add_second)
        also(4 * i + 10, part.add_third)

    for part in given:
        also(0, part.start)
        also(2, part.add_core)
        also(4, part.add_second)
        also(6, part.add_third)

    def finish():
        for ring in {id(part.sent): part.sent for part in parts}.values():
            for copy in ring[-2:]:
                copy.wait_send()
        for part in [*parts, *given]:
            part.finish()

    return tasks, finish


def given_scratch(rows, width):
    sem = pltpu.SemaphoreType.DMA((1, 10))
    return [
        pltpu.VMEM((1, 4, rows, width), f32),
        pltpu.VMEM((1, 4, rows, width), f32),
        pltpu.VMEM((1, 2, 2, rows // 2, width), f32),
        pltpu.VMEM((1, 2, rows // 2, width), f32),
        sem,
        sem,
    ]


def reduce_scratch(arrays, rows, width):
    block = pltpu.VMEM((arrays, 4, rows, width), bf16)
    sem = pltpu.SemaphoreType.DMA((arrays, 10))
    return [
        block,
        pltpu.VMEM((2, rows, width), bf16),
        block,
        pltpu.VMEM((arrays, 2, 2, rows // 2, width), bf16),
        pltpu.VMEM((arrays, 2, rows // 2, width), bf16),
        sem,
        sem,
    ]


def gather_norm(n, x, gain, whole, send, recv):
    line = Line(n, x.shape[0], None, None, whole, None, (send, recv))
    line.greet()

    def point(k):
        def one(_, own, at):
            v = x[own, :].astype(f32)
            whole[at, :] = (v * rms_scale(v) * gain[...]).astype(bf16)

        line.tiles(k, one)

    line.run(point)


def row_view(array, rows):
    def view(owner, half):
        first = owner * rows + half * (rows // 2)
        return array.at[pl.ds(pl.multiple_of(first, TILE), rows // 2)]

    return view


def gather_tasks(plane, items, sems):
    def copies(stage):
        return [
            copy
            for item, (view, halves) in enumerate(items)
            for copy in plane.gather_copies(item, view, halves, stage, sems)
        ]

    def stage_task(stage):
        def task():
            if stage:
                for copy in copies(stage - 1):
                    copy.wait_recv()
            for copy in copies(stage):
                copy.start()

        return task

    def last():
        for copy in copies(2):
            copy.wait_recv()
        for stage in range(3):
            for copy in copies(stage):
                copy.wait_send()

    return stage_task(0), stage_task(1), stage_task(2), last


def gather_weights(
    n,
    x,
    gain,
    w_in,
    w_gate,
    w_out,
    blocks,
    chan,
    order,
    lengths,
    cotangent,
    mask,
    whole,
    all_in,
    all_gate,
    all_out,
    all_blocks,
    all_chan,
    ocol,
    orow,
    pos,
    cot,
    cot_first,
    send,
    recv,
    raw,
    plane_send,
    plane_recv,
):
    line = Line(n, x.shape[0], None, None, whole, None, (send, recv))
    plane = Plane()
    line.greet(plane)
    sems = plane_send, plane_recv
    rows, piece = w_in.shape[0], blocks.shape[1]
    lines = chan.shape[0]

    def blocks_view(owner, half):
        return all_blocks.at[:, pl.ds(pl.multiple_of(owner * piece, TILE), piece)]

    def chan_view(owner, half):
        return raw.at[pl.ds(pl.multiple_of(owner * lines, TILE), lines)]

    items = [(row_view(array, rows), (0, 1)) for array in (all_in, all_gate, all_out)]
    items += [(blocks_view, (0,)), (chan_view, (1,))]

    first, second, third, finish = gather_tasks(plane, items, sems)

    def last():
        finish()
        lane = lax.broadcasted_iota(jnp.int32, (LANE, LANE), 1)
        row = lax.broadcasted_iota(jnp.int32, (LANE, LANE), 0)
        total = jnp.zeros((lines, LANE), f32)
        for owner in range(LANE // piece):
            moved = ((row < piece) & (row + owner * piece == lane)).astype(f32).astype(bf16)
            total = total + dot(raw[pl.ds(owner * lines, lines), :], moved)
        for h in range(lines // SUB):
            par = total[h * SUB : (h + 1) * SUB]
            lanes = pl.ds(h * LANE, LANE)
            all_chan[0:SUB, lanes] = par
            decay = par[SUB - 1 : SUB]
            small = jnp.exp(-jnp.abs(decay))
            one_more = 1.0 + small
            rest = jnp.where(one_more == 1.0, 1.0, one_more - 1.0)
            log_one_more = jnp.where(one_more == 1.0, small, jnp.log(one_more) * (small / rest))
            all_chan[SUB - 1 : SUB, lanes] = jnp.maximum(decay, 0.0) + log_one_more
            all_chan[SUB : 2 * SUB, lanes] = jnp.broadcast_to(sigmoid(decay), (SUB, LANE))

    own = pl.ds(pl.multiple_of(plane.me * rows, TILE), rows)
    all_in[own, :] = w_in[...]
    all_gate[own, :] = w_gate[...]
    all_out[own, :] = w_out[...]
    all_blocks[:, pl.ds(pl.multiple_of(plane.me * piece, TILE), piece), :] = blocks[...]
    raw[pl.ds(pl.multiple_of(plane.me * lines, TILE), lines), :] = chan[...]

    def point(k):
        def one(_, own, at):
            v = x[own, :].astype(f32)
            whole[at, :] = (v * rms_scale(v) * gain[...]).astype(bf16)

        line.tiles(k, one)

    def indices():
        count = whole.shape[0]
        steps = count // SUB
        tokens = order[...].astype(f32)
        across = lax.broadcasted_iota(jnp.int32, (ROWS, count), 1)
        line_total = jnp.zeros((1, count), f32)
        for b in range(count // ROWS):
            row = lax.broadcasted_iota(jnp.int32, (ROWS, 1), 0) + b * ROWS
            token = lax.rem(row, SUB) * steps + lax.div(row, SUB)
            picked = jnp.sum(jnp.where(across == token, tokens, 0.0), axis=1, keepdims=True)
            ocol[pl.ds(b * ROWS, ROWS), :] = picked.astype(jnp.int32)
            line_total += jnp.sum(jnp.where(across == row, picked, 0.0), axis=0, keepdims=True)
        orow[...] = line_total.astype(jnp.int32)
        row = lax.broadcasted_iota(jnp.int32, pos.shape, 0)
        token = lax.rem(row, SUB) * steps + lax.div(row, SUB)
        start, own_start = jnp.zeros((1, 1), jnp.int32), jnp.zeros(pos.shape, jnp.int32)
        for k in range(lengths.shape[1]):
            own_start = jnp.where(token >= start, start, own_start)
            start = start + lengths[:, k : k + 1]
        pos[...] = jnp.where(token >= count, -1, token - own_start)

    def masked():
        count = cotangent.shape[0]
        row = lax.broadcasted_iota(jnp.int32, (count, count), 0)
        column = lax.broadcasted_iota(jnp.int32, (count, count), 1)
        kept = jnp.where(row == column, mask[...].astype(f32), 0.0)
        kept = jnp.sum(kept, axis=1, keepdims=True)
        value = (cotangent[...].astype(f32) * kept).astype(bf16)
        cot[...] = value
        cot_first[...] = value[:, : cot_first.shape[1]]

    first()
    line.run(point, [idle] * 4 + [second, indices, masked, idle, third] + [idle] * 3 + [last])


def norm_back(value, gain, grad):
    scale = rms_scale(value)
    e = gain * grad
    slope = scale * scale * scale * jnp.mean(value * e, axis=-1, keepdims=True)
    return scale * e - value * slope, grad * value * scale


def middle(n, x, gain, cot, part, *rest):
    (*shares, cot_first), rest = rest[:4], rest[4:]
    grads = len(rest) > 45 and 2 or 0
    (d_resid, gain_grad, back, high_sum), rest = rest[:4], rest[4:]
    weight_grads, far, rest = rest[:grads], rest[grads : grads + 7], rest[grads + 7 :]
    left, right, total, ss, sr, send, recv, part2, ss2, sr2, send2, recv2, csend, crecv, *rest = rest
    up_s, value_s, grad_s, high_part, left3, right3, total3, ss3, sr3, cot_sem, *rest = rest
    *rest, held_sem = rest
    near, rest = rest[-7:], rest[:-7]
    whole, cots, resid, hidden, d_up, d_gate, low_part = near
    plane = Plane() if rest else None
    w_up, w_gate, w_down = weights = rest[:3] if rest else shares

    def whole_of(weight):
        return weight[...].reshape(-1, weight.shape[-1])

    local = x.shape[0]
    line = Line(n, local, part, (left, right), whole, (ss, sr), (send, recv))
    back_line = Line(n, local, part2, (left, right), back, (ss2, sr2), (send2, recv2))
    early = cot_first.shape[1]
    later = pl.ds(early, cot.shape[1] - early)
    cot_line = Line(n, local, None, None, cots.at[:, later], None, (csend, crecv))
    high_line = Line(n, local, high_part, (left3, right3), None, (ss3, sr3), None)
    line.greet(plane)
    arriving = pltpu.make_async_copy(cot_first, cots.at[:, pl.ds(0, early)], cot_sem)
    arriving.start()
    gain_grad[...] = jnp.zeros_like(gain_grad)
    leaving = [
        pltpu.make_async_copy(source, target, held_sem.at[i])
        for i, (source, target) in enumerate(zip(near, far))
    ]

    def keep_cot(_, own, at):
        cots[at, later] = cot[own, later]

    def point(k):
        line.total(k, total)

        def one(here, own, at):
            v = x[own, :].astype(f32) + total[here, :]
            resid[own, :] = v
            whole[at, :] = (v * rms_scale(v) * gain[...]).astype(bf16)

        line.tiles(k, one)

    def back_point(k):
        back_line.total(k, total)

        def one(here, own, at):
            grad, terms = norm_back(resid[own, :], gain[...], total[here, :])
            gain_grad[...] += jnp.sum(terms, axis=0, keepdims=True)
            value = cot[own, :].astype(f32) + grad
            d_resid[own, :] = value
            back[at, :] = value.astype(bf16)

        line.tiles(k, one)

    def high_point(k):
        high_line.total(k, total3)
        first, rows = line.pieces[k]
        high_sum[pl.ds(first, rows), :] = total3[pl.ds(0, rows), :].astype(bf16)

    def pair_steps(j):
        first = line.pieces[2 * j][0]
        rows = line.pieces[2 * j][1] + line.pieces[2 * j + 1][1]
        at = [pl.ds(owner * local + first, rows) for owner in range(n)]
        here = pl.ds(0, n * rows)

        def read(array):
            return jnp.concatenate([array[rows_at, :] for rows_at in at], axis=0)

        def write(array, value):
            for owner, rows_at in enumerate(at):
                array[rows_at, :] = value[owner * rows : (owner + 1) * rows]

        def up():
            up_s[here, :] = dot(read(whole), whole_of(w_up))

        def gate():
            value, slope = gelu_both(dot(read(whole), whole_of(w_gate)))
            write(hidden, (value * up_s[here, :]).astype(bf16))
            value_s[here, :] = value
            up_s[here, :] = up_s[here, :] * slope

        def into_hidden():
            d_hidden = dot(read(cots), whole_of(w_down))
            write(d_up, (d_hidden * value_s[here, :]).astype(bf16))
            write(d_gate, (d_hidden * up_s[here, :]).astype(bf16))

        def through_up():
            grad_s[here, :] = dot_last(read(d_up), whole_of(w_up))

        def through_gate():
            write(part2, (grad_s[here, :] + dot_last(read(d_gate), whole_of(w_gate))).astype(bf16))

        def project():
            value = dot_last(read(hidden), whole_of(w_down)).astype(bf16)
            write(low_part, value[:, : low_part.shape[1]])
            write(high_part, value[:, low_part.shape[1] :])

        return up, gate, into_hidden, through_up, through_gate, project

    hops = n - 1
    slots = [[] for _ in range(PIECES + 5 * hops)]

    def put(slot, order, work, *args):
        slots[slot].append((order, functools.partial(work, *args)))

    for k in range(PIECES):
        put(k, 0, line.first, k)
        for stage in range(1, hops):
            put(k + stage, 2, line.relay, k, stage)
        met = k + hops
        put(met, 3, line.sent, k)
        put(met, 3, point, k)
        put(met, 3, line.spread, k)
        given = max(k - 2, 0) if 2 * k <= PIECES else min(2 * k - 3, PIECES + 2)
        put(given, 0, cot_line.tiles, k, keep_cot)
        put(given, 0, cot_line.spread, k)
        for stage in range(1, n):
            put(met + stage, 5, line.forward, k, stage)
            put(given + stage, 5, cot_line.forward, k, stage)
    for j in range(PIECES // 2):
        slot = 2 * j + 2 + 2 * hops
        steps = pair_steps(j)
        for at, order, step in zip((0, 0, 0, 1, 1, 1), (0.5, 1.5, 2.5, 0.5, 1.5, 3.5), steps):
            put(slot + at, order, step)
        for k in (2 * j, 2 * j + 1):
            begun = slot + 1 + k % 2
            put(begun, 2 if begun == slot + 1 else 0, back_line.first, k)
            for stage in range(1, hops):
                put(begun + stage, 2, back_line.relay, k, stage)
            put(begun + hops, 3, back_line.sent, k)
            put(begun + hops, 3, back_point, k)
            put(begun + hops, 3, back_line.spread, k)
            for stage in range(1, n):
                put(begun + hops + stage, 5, back_line.forward, k, stage)
            begun += hops
            put(begun, 4, high_line.first, k)
            for stage in range(1, hops):
                put(begun + stage, 4, high_line.relay, k, stage)
            put(begun + hops, 4, high_line.sent, k)
            put(begun + hops, 4, high_point, k)
    put(2 * hops + 2, 0, arriving.wait)
    done = PIECES + 2 * hops + 2
    for copy in leaving:
        put(done, 0, copy.start)
    if plane is not None:
        *plane_sems, wide_send, wide_recv, free = rest[3:]
        half_rows = shares[0].shape[0] // 2
        for share, array in zip(shares, weights):
            array[plane.me] = share[...]

        def weight_view(array):
            return lambda owner, half: array.at[owner, pl.ds(half * half_rows, half_rows)]

        items = [(weight_view(array), (0, 1)) for array in weights]
        stages = gather_tasks(plane, items, plane_sems)
        for slot, stage in zip((0, 3, 6, 2 * hops + 2), stages):
            put(slot, 0, stage)

        def leave_weights():
            for bit in plane.bits:
                pl.semaphore_signal(
                    free, inc=1, device_id={"dp": plane.other(bit)}, device_id_type=MESH
                )

        sent = []
        tokens = Here(whole)
        tasks, end = reduce_tasks(
            [
                Reduce(
                    i,
                    tokens,
                    Here(right),
                    slice(None),
                    sent,
                    *blocks_views(i, both, w_down),
                    out,
                    (wide_send, wide_recv),
                )
                for i, (right, both, out) in enumerate(
                    zip((d_up, d_gate), (w_up, w_gate), weight_grads)
                )
            ]
        )
        put(done - 1, 4, leave_weights)
        put(done, 0, pl.semaphore_wait, free, len(plane.bits))
        at = [(slot, order) for slot in range(done, len(slots)) for order in (0.5, 2.5, 3.5)]
        for (slot, order), task in zip(at, tasks):
            put(slot, order, task)
        rest_tasks = tasks[len(at) :]
    else:
        rest_tasks = []
    for slot in slots:
        for _, work in sorted(slot, key=lambda entry: entry[0]):
            work()
    for task in rest_tasks:
        task()
    for each in (line, back_line, cot_line):
        each.finish()
    if plane is not None:
        end()
    for copy in leaving:
        copy.wait()


def sum_back(n, x, d_resid, gain, part, *rest):
    if len(rest) > 6:
        little, gains, *rest = rest
        sources, rest = rest[:6], rest[6:]
        grad_x, *outs, little_out, gains_out = rest[:7]
        left, right, total, ss, sr, *reduce = rest[7:]
        wide, late_refs, late_sems = reduce[22:29], reduce[29:35], reduce[35]
        given = [
            Given(little, *reduce[7:11], little_out, reduce[11:13]),
            Given(gains, *reduce[13:17], gains_out, reduce[17:19]),
        ]
        met, met_send, met_recv = reduce[19:22]
    else:
        grad_x, left, right, total, ss, sr = rest
        sources = ()
    line = Line(n, x.shape[0], part, (left, right), None, (ss, sr), None)
    line.greet(Plane() if sources else None)

    def point(k):
        line.total(k, total)

        def one(here, own, at):
            back, _ = norm_back(x[own, :].astype(f32), gain[...], total[here, :])
            grad_x[own, :] = (d_resid[own, :] + back).astype(bf16)

        line.tiles(k, one)

    if not sources:
        line.run(point)
        return
    width = sources[5].shape[1]
    cots, hidden, norm, back_all, cat, mixed = late_all(sources, late_refs, late_sems)
    every, sent, sent_wide = slice(None), [], []
    wide_sides = ((cots, hidden, every),)
    sides = (
        (norm, cat, slice(0, width)),
        (norm, cat, slice(width, 2 * width)),
        (back_all, mixed, every),
    )
    parts = [
        Reduce(i, *side, sent_wide, *views(i, *wide[:5]), out, wide[5:7])
        for i, (side, out) in enumerate(zip(wide_sides, outs))
    ]
    parts += [
        Reduce(i, *side, sent, *views(i, *reduce[:5]), out, reduce[5:7])
        for i, (side, out) in enumerate(zip(sides, outs[1:]))
    ]
    tasks, finish = reduce_tasks(parts, given)

    me = lax.axis_index("mp")

    def meet(away):
        return pltpu.make_async_remote_copy(
            src_ref=gains_out,
            dst_ref=met.at[away - 1],
            send_sem=met_send.at[away - 1],
            recv_sem=met_recv.at[away - 1],
            device_id={"mp": lax.rem(me + away, n)},
            device_id_type=MESH,
        )

    def send_gains():
        for away in range(1, n):
            meet(away).start()

    def add_gains():
        for away in range(1, n):
            meet(away).wait()
        gains_out[...] += sum(met[away] for away in range(n - 1))

    tasks[7:7] = [send_gains]
    line.run(point, tasks)
    finish()
    add_gains()


def line_call(body, n, identity, outs, sums, alls, args, more=(), late=0, held=0):
    whole = pl.BlockSpec(memory_space=pltpu.VMEM)
    local, model = args[0].shape
    sem = pltpu.SemaphoreType.DMA((2, n, PIECES))
    scratch = []
    if sums:
        scratch += [pltpu.VMEM((n * local, model), bf16)] * 2
        scratch += [pltpu.VMEM((max(rows for _, rows in cut_rows(local, PIECES)), model), f32)]
        scratch += [sem, sem]
    if alls:
        scratch += [sem, sem]
    scratch += more
    if held:
        scratch += [pltpu.VMEM(o.shape, o.dtype) for o in outs[len(outs) - held :]]
        scratch += [pltpu.SemaphoreType.DMA((held,))]
    away = pl.BlockSpec(memory_space=pl.ANY)
    moved = sum(a.size * a.dtype.itemsize for a in args)
    return pl.pallas_call(
        functools.partial(body, n),
        out_shape=outs,
        in_specs=[whole] * (len(args) - late) + [away] * late,
        out_specs=[whole] * (len(outs) - held) + [away] * held,
        scratch_shapes=scratch,
        compiler_params=pltpu.CompilerParams(
            vmem_limit_bytes=VMEM_MB << 20, collective_id=identity, has_side_effects=True
        ),
        cost_estimate=pl.CostEstimate(flops=0, bytes_accessed=100 * moved, transcendentals=0),
    )(*args)


def finish(heads, piece, share, resid, low, high, gains, little, *rest):
    count = (len(rest) - 6) // 2
    sources, rest = rest[:count], rest[count:]
    output, grad_gains, grad_conv, grad_bias, grad_decay, grad_blocks, *targets = rest
    for source, target in zip(sources, targets):
        target[...] = source[...]
    half = low.shape[1]
    output[:, :half] = (resid[:, :half] + low[...].astype(f32)).astype(bf16)
    output[:, half:] = (resid[:, half:] + high[...].astype(f32)).astype(bf16)
    for position in range(gains.shape[0] // 2):

        @pl.when(lax.axis_index("mp") == position)
        def _():
            grad_gains[...] = gains[2 * position : 2 * position + 2, :share]

    for h in range(heads):
        for gate in range(2):
            first = (2 * h + gate) * LANE
            grad_blocks[gate, h] = little[:, first : first + LANE]
    first = 2 * heads * LANE
    lines = little[:, first : first + LANE]
    lines = jnp.concatenate([lines, jnp.zeros((LANE - piece, LANE), f32)], axis=0).T
    for h in range(heads):
        for k in range(SUB):
            row = lines[h * SUB + k : h * SUB + k + 1, :piece]
            if k < 4:
                grad_conv[k, h : h + 1, :] = row
            elif k < SUB - 1:
                grad_bias[k - 4, h : h + 1, :] = row
            else:
                grad_decay[h : h + 1, :] = row


def local_call(body, outs, scratch, flops, args, late=0, held=0):
    whole, away = pl.BlockSpec(memory_space=pltpu.VMEM), pl.BlockSpec(memory_space=pl.ANY)
    twins = list(args[len(args) - late :]) + list(outs[len(outs) - held :])
    scratch = scratch + [pltpu.VMEM(a.shape, a.dtype) for a in twins]
    if late:
        scratch.append(pltpu.SemaphoreType.DMA((late,)))
    if held:
        scratch.append(pltpu.SemaphoreType.DMA((held, 4)))
    moved = sum(a.size * a.dtype.itemsize for a in args)
    moved += sum(o.size * o.dtype.itemsize for o in outs)
    return pl.pallas_call(
        body,
        out_shape=outs,
        in_specs=[whole] * (len(args) - late) + [away] * late,
        out_specs=[whole] * (len(outs) - held) + [away] * held,
        scratch_shapes=scratch,
        compiler_params=pltpu.CompilerParams(vmem_limit_bytes=VMEM_MB << 20),
        cost_estimate=pl.CostEstimate(flops=flops, bytes_accessed=moved, transcendentals=0),
    )(*args)


def shape_of(dtype, *shape):
    return jax.ShapeDtypeStruct(shape, dtype)


def shards(
    inputs,
    cotangent,
    token_mask,
    order,
    lengths,
    gains,
    w_in,
    w_gate,
    w_out,
    conv_weight,
    chan_bias,
    decay,
    gate_blocks,
    w_up,
    w_gate_ff,
    w_down,
):
    n_dp = lax.axis_size("dp")
    local_rows, model = inputs.shape
    count = local_rows * lax.axis_size("mp")
    heads, piece = decay.shape
    width = heads * piece * n_dp
    hidden_width = w_up.shape[1]

    fused = n_dp == 8
    rows = model // n_dp
    out_rows, down_rows = w_out.T, w_down.T
    lines = jnp.concatenate([conv_weight, chan_bias, decay[None]], axis=0).transpose(1, 0, 2)
    lines = lines.reshape(SUB * heads, piece)

    gain_f = gains.astype(f32)
    n_mp = lax.axis_size("mp")
    tok = shape_of(bf16, count, model)
    own = shape_of(f32, local_rows, model)
    if fused:
        grown = shape_of(bf16, model, width)
        norm_group, full_in, full_gate, full_out, blocks, chan, ocol, orow, pos_col, cot, cot_first = (
            line_call(
            gather_weights,
            n_mp,
            0,
            [tok, grown, grown, grown, shape_of(bf16, 2 * heads, LANE, LANE), shape_of(f32, 16, width)]
            + [shape_of(jnp.int32, *at) for at in ((count, 1), (1, count), (count + TAIL, 1))]
            + [shape_of(bf16, local_rows, model), shape_of(bf16, local_rows, model // 4)],
            False,
            True,
            (
                inputs,
                gain_f[0:1],
                w_in,
                w_gate,
                out_rows,
                gate_blocks.reshape(2 * heads, piece, LANE),
                jnp.pad(lines, ((0, 0), (0, LANE - piece))),
                order,
                lengths,
                cotangent,
                token_mask.reshape(1, -1),
            ),
            [pltpu.VMEM((n_dp * SUB * heads, LANE), bf16)] + [pltpu.SemaphoreType.DMA((5, 2, 7))] * 2,
        )
        )
    else:
        steps = count // SUB
        ends = jnp.cumsum(lengths[0], dtype=jnp.int32)
        starts = ends - lengths[0]
        places = jnp.arange(count, dtype=jnp.int32)
        own_start = jnp.max(
            jnp.where(places[:, None] >= starts[None, :], starts[None, :], 0), axis=1
        )
        pos = (places - own_start).reshape(SUB, steps).T
        wrap = jnp.concatenate([pos[: TAIL // SUB, 1:], jnp.full((TAIL // SUB, 1), -1, jnp.int32)], axis=1)
        pos_col = jnp.concatenate([pos, wrap], axis=0).reshape(count + TAIL, 1)
        order_int = order[0].reshape(SUB, steps).T.reshape(count)
        ocol, orow = order_int.reshape(count, 1), order_int.reshape(1, count)
        (norm_group,) = line_call(gather_norm, n_mp, 0, [tok], False, True, (inputs, gain_f[0:1]))
        full_in = lax.all_gather(w_in, "dp", axis=0, tiled=True)
        full_gate = lax.all_gather(w_gate, "dp", axis=0, tiled=True)
        full_out = lax.all_gather(out_rows, "dp", axis=0, tiled=True)
        blocks = lax.all_gather(gate_blocks, "dp", axis=2, tiled=True).reshape(2 * heads, LANE, LANE)
        params = lax.all_gather(lines, "dp", axis=1, tiled=True).astype(f32)
        params = params.reshape(heads, SUB, LANE).transpose(1, 0, 2).reshape(SUB, width)
        decay_row = params[7:8]
        chan = jnp.concatenate(
            [params[:7], jax.nn.softplus(decay_row)] + [jax.nn.sigmoid(decay_row)] * SUB, axis=0
        )

    if not fused:
        cot = cotangent * token_mask.astype(bf16)[:, None]
        cot_first = cot[:, : model // 4]
    cot_first = lax.all_gather(cot_first, "mp", axis=0, tiled=True)

    wide = pltpu.VMEM((count, width), f32)
    saved = [shape_of(f32, count, width)] * 6
    gate_pre, branch, conv, gate_in, gate_rec, state, mixed, back_part = local_call(
        mixer_forward,
        saved + [shape_of(bf16, count, width), shape_of(bf16, count, model)],
        [
            pltpu.VMEM((ROWS, model), bf16),
            wide,
            wide,
            pltpu.VMEM((ROWS + TAIL, width), f32),
            pltpu.VMEM((count, width), bf16),
        ],
        2 * count * (count * model + 3 * model * width),
        (norm_group, ocol, orow, pos_col, full_in, full_gate, chan, blocks, full_out),
        1,
        8,
    )
    shares = (w_up, w_gate_ff, down_rows)
    if not fused:
        shares = [lax.all_gather(share, "dp", axis=0, tiled=True) for share in shares]
    hid = shape_of(bf16, count, hidden_width)
    low_width = model * 5 // 12
    low_shape = shape_of(bf16, count, low_width)
    high_twin = pltpu.VMEM((count, model - low_width), bf16)
    pieces = cut_rows(local_rows, PIECES)
    most = n_mp * max(pieces[k][1] + pieces[k + 1][1] for k in range(0, PIECES, 2))
    pair = pltpu.VMEM((most, hidden_width), f32)
    flow = pltpu.SemaphoreType.DMA((2, n_mp, PIECES))
    plane_scratch = [pltpu.VMEM((n_dp, rows, hidden_width), bf16)] * 3
    plane_scratch += [pltpu.SemaphoreType.DMA((3, 2, 7))] * 2 + [pltpu.SemaphoreType.DMA((2, 10))] * 2
    plane_scratch += [pltpu.SemaphoreType.REGULAR]
    (
        d_resid,
        gain_mid,
        back_group,
        ffn_high,
        *ffn_grads,
        norm_mid_group,
        cot_group,
        resid,
        hidden,
        d_up,
        d_gate_ff,
        ffn_part,
    ) = line_call(
        middle,
        n_mp,
        1,
        [own, shape_of(f32, 1, model), tok, shape_of(bf16, local_rows, model - low_width)]
        + [shape_of(f32, rows, hidden_width)] * (2 * fused)
        + [tok, tok, own, hid, hid, hid, low_shape],
        True,
        True,
        (inputs, gain_f[1:2], cot, back_part, *shares, cot_first),
        [pltpu.VMEM((count, model), bf16)]
        + [flow] * 6
        + [pair, pair, pltpu.VMEM((most, model), f32)]
        + [high_twin] * 3
        + [pltpu.VMEM((max(rows for _, rows in pieces), model - low_width), f32), flow, flow]
        + [pltpu.SemaphoreType.DMA(())]
        + plane_scratch * fused,
        late=1,
        held=7,
    )

    def reduced(left, right):
        grad = dot_first(left, right).astype(bf16)
        return lax.psum_scatter(grad, "dp", scatter_dimension=0, tiled=True).astype(f32)

    d_cat, d_norm_back, little, gain_in, *ffn_grads = local_call(
        mixer_backward,
        [
            shape_of(bf16, count, 2 * width),
            tok,
            shape_of(f32, LANE, 2 * width + LANE),
            shape_of(f32, 1, model),
        ]
        + [shape_of(f32, *a.shape) for a in ffn_grads],
        [
            pltpu.VMEM((count, width), bf16),
            wide,
            wide,
            wide,
            pltpu.VMEM((count + TAIL, width), f32),
            pltpu.VMEM((ROWS + TAIL, width), f32),
            pltpu.VMEM((count, 2 * width), bf16),
            pltpu.VMEM((SUB, width), f32),
            pltpu.VMEM((heads, LANE, 2 * LANE), f32),
        ],
        2 * count * (3 * count * width + 3 * model * width),
        (
            back_group,
            full_out,
            ocol,
            orow,
            pos_col,
            gain_f[0:1],
            chan,
            blocks,
            gate_pre,
            gate_rec,
            state,
            conv,
            gate_in,
            branch,
            norm_group,
            full_in,
            full_gate,
            *ffn_grads,
        ),
        9 + len(ffn_grads),
        len(ffn_grads),
    )
    share = model // (n_dp * n_mp)
    gain_parts = jnp.concatenate([gain_in, gain_mid], axis=0).reshape(2, n_dp, n_mp, share)
    gain_parts = gain_parts.transpose(1, 2, 0, 3).reshape(n_dp, 2 * n_mp, share)
    gain_parts = jnp.pad(gain_parts, ((0, 0), (0, 2 * SUB - 2 * n_mp), (0, LANE - share)))
    gain_parts = gain_parts.reshape(2 * SUB * n_dp, LANE)
    ffn_low = lax.psum_scatter(ffn_part, "mp", scatter_dimension=0, tiled=True)
    ffn_low, d_norm_back = lax.optimization_barrier((ffn_low, d_norm_back))
    grad_inputs, *mix_grads = line_call(
        sum_back,
        n_mp,
        3,
        [shape_of(bf16, local_rows, model)]
        + (
            [shape_of(f32, rows, hidden_width)]
            + [shape_of(f32, rows, width)] * 3
            + [shape_of(f32, piece, little.shape[1]), shape_of(f32, 2 * SUB, LANE)]
        )
        * fused,
        True,
        False,
        (inputs, d_resid, gain_f[0:1], d_norm_back)
        + (
            (
                little,
                gain_parts,
                cot_group,
                hidden,
                norm_group,
                back_group,
                d_cat,
                mixed,
            )
            if fused
            else ()
        ),
        reduce_scratch(3, rows, width)
        + given_scratch(piece, little.shape[1])
        + given_scratch(2 * SUB, LANE)
        + [pltpu.VMEM((n_mp - 1, 2 * SUB, LANE), f32)]
        + [pltpu.SemaphoreType.DMA((n_mp - 1,))] * 2
        + reduce_scratch(1, rows, hidden_width)
        + [pltpu.VMEM(a.shape, a.dtype) for a in (cot_group, hidden, norm_group, back_group, d_cat, mixed)]
        + [pltpu.SemaphoreType.DMA((6,))]
        if fused
        else (),
        6 * fused,
    )
    if fused:
        up_grad, gate_ff_grad = ffn_grads
        down_grad, *mix_grads, little_own, gain_own = mix_grads
    else:
        up_grad = reduced(norm_mid_group, d_up)
        gate_ff_grad = reduced(norm_mid_group, d_gate_ff)
        down_grad = reduced(cot_group, hidden)
        mix_grads = [
            reduced(norm_group, d_cat[:, :width]),
            reduced(norm_group, d_cat[:, width:]),
            reduced(back_group, mixed),
        ]
        little_own = lax.psum_scatter(little, "dp", scatter_dimension=0, tiled=True)
        gain_own = lax.psum(lax.psum_scatter(gain_parts, "dp", scatter_dimension=0, tiled=True), "mp")
    outs = [
        shape_of(bf16, local_rows, model),
        shape_of(f32, 2, share),
        shape_of(f32, 4, heads, piece),
        shape_of(f32, 3, heads, piece),
        shape_of(f32, heads, piece),
        shape_of(f32, 2, heads, piece, LANE),
    ]
    copied = [grad_inputs, mix_grads[0], mix_grads[1]] if fused else []
    output, grad_gains, grad_conv, grad_bias, grad_decay, grad_blocks, *copied = local_call(
        functools.partial(finish, heads, piece, share),
        outs + [shape_of(a.dtype, *a.shape) for a in copied],
        [],
        0,
        (resid, ffn_low, ffn_high, gain_own, little_own, *copied),
    )
    if fused:
        grad_inputs, grad_in, grad_gate = copied
    else:
        grad_in, grad_gate, _ = mix_grads
    return (
        output,
        grad_inputs,
        grad_gains,
        grad_in,
        grad_gate,
        mix_grads[2].T,
        grad_conv,
        grad_bias,
        grad_decay,
        grad_blocks,
        up_grad,
        gate_ff_grad,
        down_grad.T,
    )


def solution(mesh):
    row, col = P("dp", "mp"), P("mp", "dp")
    tok = P(("dp", "mp"), None)
    chan = P(None, "mp", "dp")
    gate = P(None, "mp", "dp", None)
    return jax.shard_map(
        shards,
        mesh=mesh,
        in_specs=(
            tok, tok, P(("dp", "mp")), P("dp", None), P("dp", None), P(),
            row, row, col, chan, chan, col, gate, row, row, col,
        ),
        out_specs=(
            tok, tok, P(None, ("dp", "mp")), row, row, col, chan, chan, col, gate, row, row, col,
        ),
        check_vma=False,
    )
```
